32 devices in a mesh: groups: 2 (over x), ctx: 16 (over z, y, core).
Axes of the slice: x: 2, y: 2, z: 4, core: 2. Of those that a mesh axis runs over, the one named last changes fastest.
Arguments:
- queries: bfloat16 [512, 4096], P(('groups', 'ctx')), parts along dimension 0, may hold values from -12 to 12
- new_key: bfloat16 [512, 512], P(('groups', 'ctx')), parts along dimension 0, may hold values from -8 to 8
- new_value: bfloat16 [512, 512], P(('groups', 'ctx')), parts along dimension 0, may hold values from -6 to 6
- key_cache: bfloat16 [32768, 512], P(('groups', 'ctx')), parts along dimension 0, may hold values from -8 to 8
- value_cache: bfloat16 [32768, 512], P(('groups', 'ctx')), parts along dimension 0, may hold values from -6 to 6
- cache_len: int32 [512], P('groups'), parts along dimension 0, may hold values from 1 to 16384
- out_weight: bfloat16 [4096, 2048], P('ctx'), may hold values from -0.09375 to 0.09375
- residual: bfloat16 [512, 2048], P(('groups', 'ctx')), parts along dimension 0, may hold values from -8 to 8
- norm_gain: bfloat16 [2048], replicated, may hold values from 0.099609375 to 1.8984375
- expert_ids: int32 [512, 8], P(('groups', 'ctx')), parts along dimension 0, may hold values from 0 to 31, all different within a row; in each aligned block of 16 rows (0 to 15, 16 to 31, ...) at most 4 rows name the same one
- route_weight: float32 [512, 8], P(('groups', 'ctx')), parts along dimension 0, may hold values from 0.1 to 1
- w_gate: bfloat16 [32, 2048, 768], P('ctx'), may hold values from -0.125 to 0.125
- w_up: bfloat16 [32, 2048, 768], P('ctx'), may hold values from -0.125 to 0.125
- w_down: bfloat16 [32, 768, 2048], P('ctx'), may hold values from -0.21875 to 0.21875
Outputs:
- layer_out: bfloat16 [512, 2048], P(('groups', 'ctx')), parts along dimension 0
The draws below stay inside these ranges and needn't reach their ends.
There are 2 independent parts, one for each index of `groups`. The reference program is written for one: setup_inputs(seed, part) draws one part's arguments, and reference() takes and returns one part's arrays. A program takes and returns all parts, laid end to end along the dimension named above; an argument that names none is the same for every part. Nothing has to cross between parts.
Inputs may be any that keep to these rules, and one draw needn't show every extreme that they name: `expert_ids`: among the rows of one device no expert is named more than 4 times.
All inputs are finite; a program needn't handle non-finite values.
Results may differ from the reference program's by a relative error of at most 0.018.
Values may be sent and summed in bfloat16 or wider, within the bound.
No kernel may reach another device: no remote copies, remote signals or barrier semaphores. Data moves between devices by JAX's collectives and lax.ppermute only.
A program may use at most 192 MiB of HBM per device.

```python
import math
import jax
import jax.numpy as jnp
import numpy as np
from jax import lax

D = 2048
HEADS = 32
KVH = 4
HD = 128
FF = 768
TOP = 8
ROWS_DEV = 16
EXPERTS = 32
ROWS = 256
CTX = 16384
MOST = 4


def draw_queries(key, part):
    own_key = jax.random.fold_in(key, 11)
    values = jnp.clip(2.0 * jax.random.normal(own_key, (ROWS, HEADS * HD)), -8.0, 8.0)
    return values.astype(jnp.bfloat16)


def draw_key_cache(key, part):
    own_key = jax.random.fold_in(key, 12)
    values = jnp.clip(1.5 * jax.random.normal(own_key, (CTX, KVH * HD)), -8.0, 8.0)
    return values.astype(jnp.bfloat16)


def draw_new_key(key, part):
    own_key = jax.random.fold_in(key, 13)
    values = jnp.clip(2.5 * jax.random.normal(own_key, (ROWS, KVH * HD)), -8.0, 8.0)
    return values.astype(jnp.bfloat16)


def draw_residual(key, part):
    own_key = jax.random.fold_in(key, 14)
    noise_key = jax.random.fold_in(own_key, 0)
    values = jax.random.normal(noise_key, (ROWS, D))
    values = jnp.clip(values, -6.0, 6.0)
    return values.astype(jnp.bfloat16)


def with_ends(drawn, stream_key, least, top_value):
    dims = drawn.shape
    spot = [jax.random.randint(jax.random.fold_in(stream_key, axis), (), 0, dims[axis]) for axis in range(len(dims))]
    drawn = drawn.at[tuple(spot)].set(least)
    longest = dims.index(max(dims))
    spot[longest] = (spot[longest] + 1) % dims[longest]
    return drawn.at[tuple(spot)].set(top_value)


def block_levels(stream_key, dims, cuts, least, top_value):
    level = 1.0
    for dim, parts in cuts:
        steps = jax.random.uniform(jax.random.fold_in(jax.random.fold_in(stream_key, 6), dim), (parts,), jnp.float32, least / len(cuts), top_value / len(cuts))
        level = level * jnp.repeat(jnp.exp(steps), dims[dim] // parts).reshape((-1,) + (1,) * (len(dims) - 1 - dim))
    return level


def routed_block(key, own, number, rows, count, top, reach, lean):
    order = jax.random.permutation(key, count)
    packed, ordinary = load_shares(count, rows * top, reach, lean, True), load_shares(count, rows * top, reach, lean, False)
    places = jnp.arange(count)

    def named(sizes, turn):
        used = int((sizes > 0).sum())
        fixed = max(1, used // 4)
        moved = fixed + (places - fixed + turn * (used - fixed)) % max(1, count - fixed)
        return jnp.zeros((count,), jnp.int32).at[order[jnp.where(places < fixed, places, moved)]].set(jnp.asarray(sizes, jnp.int32))

    sizes = jnp.where(number % 4 == 0, named(packed, number // 4), named(ordinary, number - number // 4 - 1))
    mixed = jax.random.permutation(jax.random.fold_in(own, 3), count)
    donor, taker = mixed[0:count // 2 * 2:2], mixed[1:count // 2 * 2:2]
    slack = jnp.minimum(sizes[donor] - 1, reach - sizes[taker]) // 2
    slack = jnp.where((donor == order[0]) | (taker == order[0]) | (sizes[taker] == 0), 0, jnp.maximum(slack, 0))
    moved = jax.random.randint(jax.random.fold_in(own, 4), (count // 2,), 0, 1 << 20) % (slack + 1)
    sizes = sizes.at[donor].add(-moved).at[taker].add(moved)
    labels = jnp.searchsorted(jnp.cumsum(sizes), jnp.arange(rows * top), side="right").astype(jnp.int32)
    table = labels.reshape(top, rows).T
    table = table[jax.random.permutation(jax.random.fold_in(own, 1), rows)]
    turn = jax.random.randint(jax.random.fold_in(own, 2), (rows, 1), 0, top)
    return jnp.take_along_axis(table, (jnp.arange(top)[None, :] + turn) % top, axis=1)


def load_shares(amount, total, limit, skew, full):
    loads = [(1 << 20) // math.isqrt(rank ** skew) + 1 for rank in range(1, amount + 1)]
    largest = limit if full else min(limit, max(-(-total // amount), total * loads[0] // sum(loads)))
    least = 1 if total - largest >= amount - 1 else 0
    holding, spare = [largest] + [least] * (amount - 1), total - largest - least * (amount - 1)
    while spare > 0:
        free = [i for i in range(1, amount) if holding[i] < largest] or [i for i in range(1, amount) if holding[i] < limit]
        mass, left = sum([loads[i] for i in free]), spare
        for i in free:
            addition = min(limit - holding[i], max(1, left * loads[i] // mass), spare)
            holding[i] = holding[i] + addition
            spare = spare - addition
    return np.array(holding)


def centred(stream_key, extent, scale, limit, cuts=(), kind=jnp.bfloat16):
    entries = jax.random.normal(stream_key, extent, jnp.float32) * scale
    if len(cuts) > 0:
        entries = block_levels(stream_key, extent, cuts, -0.22, 0.18) * entries
    return jnp.clip(entries, min=-limit, max=limit).astype(kind)


def setup_inputs(seed: int = 0, part: int = 0) -> dict:
    splits = jax.random.split(jax.random.key(seed), 15)
    part_splits = jax.random.split(jax.random.fold_in(splits[14], part), 15)
    queries = draw_queries(jax.random.fold_in(jax.random.fold_in(splits[14], part), 71), part)
    new_key = draw_new_key(jax.random.fold_in(jax.random.fold_in(splits[14], part), 71), part)
    new_value = centred(part_splits[2], (ROWS, KVH * HD), 1.0, 6.0, ((0, 16),))
    key_cache = draw_key_cache(jax.random.fold_in(jax.random.fold_in(splits[14], part), 71), part)
    value_cache = centred(part_splits[4], (CTX, KVH * HD), 1.0, 6.0, ((0, 16),))
    cache_len = with_ends(jax.random.randint(part_splits[5], (ROWS,), 1, CTX + 1), jax.random.fold_in(part_splits[5], 1), 1, CTX).astype(jnp.int32)
    out_weight = centred(splits[6], (HEADS * HD, D), (HEADS * HD) ** -0.5, 0.09375, ((0, 16),))
    residual = draw_residual(jax.random.fold_in(jax.random.fold_in(splits[14], part), 71), part)
    norm_gain = jnp.clip(1.0 + 0.18 * jax.random.normal(splits[8], (D,), jnp.float32), 0.099609375, 1.8984375).astype(jnp.bfloat16)
    expert_ids_keys = jax.random.split(jax.random.fold_in(part_splits[9], 1), ROWS // ROWS_DEV)
    expert_ids_turns = jax.random.permutation(jax.random.fold_in(part_splits[9], 3), ROWS // ROWS_DEV)
    expert_ids = jax.vmap(lambda own, number: routed_block(jax.random.fold_in(part_splits[9], 2), own, number, ROWS_DEV, EXPERTS, TOP, MOST, 2))(expert_ids_keys, expert_ids_turns).reshape((ROWS, TOP))
    route_weight = jnp.clip(jnp.exp(math.log(1.0) - 2.3025851 * jax.random.uniform(part_splits[10], (ROWS, TOP), jnp.float32) ** block_levels(part_splits[10], (ROWS, TOP), ((0, 16),), -0.2, 0.2)), 0.1, 1.0)
    w_gate = centred(splits[11], (EXPERTS, D, FF), D ** -0.5, 0.125, ((0, 16),))
    w_up = centred(splits[12], (EXPERTS, D, FF), D ** -0.5, 0.125, ((0, 16),))
    w_down = centred(splits[13], (EXPERTS, FF, D), FF ** -0.5, 0.21875, ((0, 16),))
    return {"queries": queries, "new_key": new_key, "new_value": new_value, "key_cache": key_cache, "value_cache": value_cache, "cache_len": cache_len, "out_weight": out_weight, "residual": residual, "norm_gain": norm_gain, "expert_ids": expert_ids, "route_weight": route_weight, "w_gate": w_gate, "w_up": w_up, "w_down": w_down}


def reference(queries, new_key, new_value, key_cache, value_cache, cache_len, out_weight, residual, norm_gain, expert_ids, route_weight, w_gate, w_up, w_down):
    total_rows = queries.shape[0]
    cache_total = key_cache.shape[0]
    group_size = HEADS // KVH
    score_scale = 1.0 / math.sqrt(HD)
    query_heads = queries.astype(jnp.float32).reshape(total_rows, KVH, group_size, HD)
    fresh_keys = new_key.astype(jnp.float32).reshape(total_rows, KVH, HD)
    fresh_values = new_value.astype(jnp.float32).reshape(total_rows, KVH, HD)
    cached_keys = key_cache.astype(jnp.float32).reshape(cache_total, KVH, HD)
    cached_values = value_cache.astype(jnp.float32).reshape(cache_total, KVH, HD)
    fresh_scores = jnp.einsum('rgqd,rgd->rgq', query_heads, fresh_keys) * score_scale
    block_rows = 16

    def attend(block_index):
        first_row = (block_index * block_rows).astype(jnp.int32)
        query_block = lax.dynamic_slice_in_dim(query_heads, first_row, block_rows, 0)
        fresh_block = lax.dynamic_slice_in_dim(fresh_scores, first_row, block_rows, 0)
        value_block = lax.dynamic_slice_in_dim(fresh_values, first_row, block_rows, 0)
        length_block = lax.dynamic_slice_in_dim(cache_len, first_row, block_rows, 0)
        scores = jnp.einsum('rgqd,pgd->rgqp', query_block, cached_keys) * score_scale
        visible = jnp.arange(cache_total, dtype=jnp.int32)[None, :] < length_block[:, None]
        scores = jnp.where(visible[:, None, None, :], scores, -jnp.inf)
        row_peak = jnp.maximum(fresh_block, lax.optimization_barrier(jnp.max(scores, axis=-1)))
        weights = lax.optimization_barrier(jnp.exp(scores - row_peak[..., None]).astype(jnp.bfloat16)).astype(jnp.float32)
        numerator = jnp.einsum('rgqp,pgd->rgqd', weights, cached_values)
        denominator = lax.optimization_barrier(jnp.sum(weights, axis=-1))
        fresh_weight = lax.optimization_barrier(jnp.exp(fresh_block - row_peak).astype(jnp.bfloat16)).astype(jnp.float32)
        numerator = numerator + fresh_weight[..., None] * value_block[:, :, None, :]
        denominator = denominator + fresh_weight
        return (numerator / denominator[..., None]).astype(jnp.bfloat16).reshape(block_rows, HEADS * HD)
    attended = lax.map(attend, jnp.arange(total_rows // block_rows, dtype=jnp.int32)).reshape(total_rows, HEADS * HD)
    attn_out = jnp.dot(attended, out_weight, preferred_element_type=jnp.float32)
    after_attention = lax.optimization_barrier((residual.astype(jnp.float32) + attn_out).astype(jnp.bfloat16))
    middle = after_attention.astype(jnp.float32)
    inv_rms = lax.rsqrt(lax.optimization_barrier(jnp.mean(middle * middle, axis=-1, keepdims=True)) + 1e-06)
    normed = (middle * inv_rms * norm_gain.astype(jnp.float32)[None, :]).astype(jnp.bfloat16)
    expert_total = w_gate.shape[0]

    def add_expert(carry, inputs):
        gate_matrix, up_matrix, down_matrix, expert_number = inputs
        gate_proj = jnp.dot(normed, gate_matrix, preferred_element_type=jnp.float32)
        upward = jnp.dot(normed, up_matrix, preferred_element_type=jnp.float32)
        hidden = (jax.nn.silu(gate_proj) * upward).astype(jnp.bfloat16)
        produced = lax.optimization_barrier(jnp.dot(hidden, down_matrix, preferred_element_type=jnp.float32).astype(jnp.bfloat16))
        coefficient = lax.optimization_barrier(jnp.sum(jnp.where(expert_ids == expert_number, route_weight, 0.0), axis=1))
        return (carry + coefficient[:, None] * produced.astype(jnp.float32), None)
    mixed, _ = lax.scan(add_expert, jnp.zeros((total_rows, D), jnp.float32), (w_gate, w_up, w_down, jnp.arange(expert_total, dtype=jnp.int32)))
    return (middle + mixed).astype(jnp.bfloat16)
```

```python
import functools
import math

import jax
import jax.numpy as jnp
from jax import lax
from jax.experimental import pallas as pl
from jax.experimental.pallas import tpu as pltpu
from jax.sharding import PartitionSpec as P

HD = 128
MOST = 4
CORES = 2
STATS = 16
MASKED = -1e30
FLOOR = -1e20
LOG2E = math.log2(math.e)
MIB = 1024 * 1024
F32 = jnp.float32
BF16 = jnp.bfloat16


def nt_dot(a, b):
    return lax.dot_general(a, b, (((1,), (1,)), ((), ())), preferred_element_type=F32)


def nn_dot(a, b):
    return lax.dot_general(a, b, (((1,), (0,)), ((), ())), preferred_element_type=F32)


def attention_body(chips, heads_chip, spare, place, *refs):
    query_refs = refs[:chips]
    key_own, key_other, value_own, value_other, key_fresh, value_fresh, lens, out, q_rows, v_turned, hidden = refs[chips:]
    owner = pl.program_id(0)
    chip, start_own, start_other = place[0], place[1], place[2]
    home_rows = query_refs[0].shape[0]
    rows = chips * home_rows
    cache_here = key_own.shape[0]

    @pl.when(owner == 0)
    def _():
        for part, start in enumerate((start_own, start_other)):
            positions = start + lax.broadcasted_iota(jnp.int32, (cache_here, rows), 0)
            hidden[part * cache_here : (part + 1) * cache_here, :] = jnp.where(
                positions < lens[...], 0.0, MASKED
            )
        token = lax.broadcasted_iota(jnp.int32, (home_rows, rows), 0)
        column = lax.broadcasted_iota(jnp.int32, (home_rows, rows), 1)
        hidden[2 * cache_here :, :] = jnp.where(token + chip * home_rows == column, 0.0, MASKED)

    @pl.when(owner % spare == 0)
    def _():
        v_turned[:HD, :cache_here] = value_own[...].T
        v_turned[:HD, cache_here : 2 * cache_here] = value_other[...].T
        v_turned[HD:, :] = jnp.ones_like(v_turned[HD:, :])

    for shift in range(chips):
        source = lax.rem(chip + chips - shift, chips)
        q_rows[pl.ds(pl.multiple_of(source * home_rows, home_rows), home_rows), :] = query_refs[shift][...]

    value_new = value_fresh[...].astype(F32).T.astype(BF16)
    peaks, highs, lows = [], [], []
    pair = min(2, heads_chip)
    for first in range(0, heads_chip, pair):
        q = jnp.concatenate(
            [q_rows[:, h * HD : (h + 1) * HD] for h in range(first, first + pair)], axis=0
        )
        mask = jnp.concatenate([hidden[...]] * pair, axis=1)
        s_own = nt_dot(key_own[...], q) + mask[:cache_here]
        s_other = nt_dot(key_other[...], q) + mask[cache_here : 2 * cache_here]
        s_new = nt_dot(key_fresh[...], q) + mask[2 * cache_here :]
        peak = jnp.maximum(
            jnp.maximum(jnp.max(s_own, axis=0, keepdims=True), jnp.max(s_other, axis=0, keepdims=True)),
            jnp.max(s_new, axis=0, keepdims=True),
        )
        scale = 1.0 / math.sqrt(HD)
        peak = jnp.maximum(peak * scale, FLOOR).astype(BF16).astype(F32)
        lift = peak * LOG2E
        p_own = jnp.exp2(s_own * (scale * LOG2E) - lift).astype(BF16)
        p_other = jnp.exp2(s_other * (scale * LOG2E) - lift).astype(BF16)
        p_new = jnp.exp2(s_new * (scale * LOG2E) - lift).astype(BF16)
        total = nn_dot(v_turned[:, :cache_here], p_own) + nn_dot(v_turned[:, cache_here:], p_other)
        numer = total[:HD] + nn_dot(value_new, p_new)
        denom = total[HD : HD + 1] + jnp.sum(p_new.astype(F32), axis=0, keepdims=True)
        for k in range(pair):
            cols = slice(k * rows, (k + 1) * rows)
            out[0, (first + k) * HD : (first + k + 1) * HD, :] = numer[:, cols].astype(BF16)
            high = denom[:, cols].astype(BF16).astype(F32)
            peaks.append(peak[:, cols])
            highs.append(high)
            lows.append(denom[:, cols] - high)
    stats = peaks + highs + lows
    stats = stats + [jnp.zeros_like(stats[0])] * (STATS - len(stats))
    out[0, heads_chip * HD :, :] = jnp.concatenate(stats, axis=0).astype(BF16)


def attention(place, query_parts, keys, values, new_key, new_value, lens, heads_chip, group_size):
    chips = len(query_parts)
    home_rows = query_parts[0].shape[0]
    rows = chips * home_rows
    cache_here = keys[0].shape[0]
    spare = max(1, group_size // heads_chip)
    kv = lambda j, place: (0, j * heads_chip // group_size)
    height = heads_chip * HD + STATS
    total_positions = 2 * cache_here + home_rows
    work = rows * heads_chip * chips * total_positions
    return pl.pallas_call(
        functools.partial(attention_body, chips, heads_chip, spare),
        grid_spec=pltpu.PrefetchScalarGridSpec(
            num_scalar_prefetch=1,
            grid=(chips,),
            in_specs=[pl.BlockSpec((home_rows, heads_chip * HD), lambda j, place: (0, j))] * chips
            + [pl.BlockSpec((cache_here, HD), kv)] * 4
            + [pl.BlockSpec((home_rows, HD), kv)] * 2
            + [pl.BlockSpec((1, rows), lambda j, place: (0, 0))],
            out_specs=pl.BlockSpec((1, height, rows), lambda j, place: (j, 0, 0)),
            scratch_shapes=[
                pltpu.VMEM((rows, heads_chip * HD), BF16),
                pltpu.VMEM((HD + STATS, 2 * cache_here), BF16),
                pltpu.VMEM((total_positions, rows), F32),
            ],
        ),
        out_shape=jax.ShapeDtypeStruct((chips, height, rows), BF16),
        compiler_params=pltpu.CompilerParams(vmem_limit_bytes=40 * MIB),
        cost_estimate=pl.CostEstimate(
            flops=4 * work * HD, bytes_accessed=8 * MIB, transcendentals=work
        ),
        name="attention",
    )(place, *query_parts, *keys, *values, new_key, new_value, lens)


def project_body(heads_chip, place, parts, weight_own, weight_other, out, turned):
    core = place[3]
    chips = parts.shape[0]
    base = heads_chip * HD
    stats = parts[:, base:, :].astype(F32)
    peaks = stats[:, :heads_chip]
    top = jnp.max(peaks, axis=0, keepdims=True)
    share = jnp.exp(peaks - top)
    totals = stats[:, heads_chip : 2 * heads_chip] + stats[:, 2 * heads_chip : 3 * heads_chip]
    denom = jnp.sum(share * totals, axis=0)
    half = heads_chip // CORES
    for h in range(heads_chip):
        numer = None
        for s in range(chips):
            term = parts[s, h * HD : (h + 1) * HD, :].astype(F32) * share[s, h : h + 1, :]
            numer = term if numer is None else numer + term
        attended = (numer / denom[h : h + 1, :]).T.astype(BF16)
        turned[h // half, :, (h % half) * HD : (h % half + 1) * HD] = attended
    product = nn_dot(turned[core], weight_own[...]) + nn_dot(turned[1 - core], weight_other[...])
    out[...] = product.astype(BF16)


def project(place, parts, weight_own, weight_other, heads_chip):
    rows = parts.shape[2]
    width = weight_own.shape[1]
    vmem = pl.BlockSpec(memory_space=pltpu.VMEM)
    return pl.pallas_call(
        functools.partial(project_body, heads_chip),
        in_specs=[pl.BlockSpec(memory_space=pltpu.SMEM), vmem, vmem, vmem],
        out_specs=vmem,
        out_shape=jax.ShapeDtypeStruct((rows, width), BF16),
        scratch_shapes=[pltpu.VMEM((CORES, rows, weight_own.shape[0]), BF16)],
        compiler_params=pltpu.CompilerParams(vmem_limit_bytes=32 * MIB),
        cost_estimate=pl.CostEstimate(
            flops=2 * rows * width * heads_chip * HD, bytes_accessed=4 * MIB, transcendentals=0
        ),
        name="project",
    )(place, parts, weight_own, weight_other)


def norm_body(parts, residual, gain, chooser, middle_out, sent):
    total = parts[0].astype(F32)
    for s in range(1, parts.shape[0]):
        total = total + parts[s].astype(F32)
    middle = (residual[...].astype(F32) + total).astype(BF16)
    middle_out[...] = middle
    middle = middle.astype(F32)
    inv_rms = lax.rsqrt(jnp.mean(middle * middle, axis=-1, keepdims=True) + 1e-06)
    normed = (middle * inv_rms * gain[...].astype(F32)).astype(BF16)
    sent[...] = nn_dot(chooser[...], normed).astype(BF16)


def norm_and_dispatch(parts, residual, gain, chooser):
    vmem = pl.BlockSpec(memory_space=pltpu.VMEM)
    rows, width = residual.shape
    return pl.pallas_call(
        norm_body,
        in_specs=[vmem] * 4,
        out_specs=[vmem] * 2,
        out_shape=[
            jax.ShapeDtypeStruct((rows, width), BF16),
            jax.ShapeDtypeStruct((chooser.shape[0], width), BF16),
        ],
        compiler_params=pltpu.CompilerParams(vmem_limit_bytes=24 * MIB),
        cost_estimate=pl.CostEstimate(
            flops=2 * chooser.shape[0] * rows * width, bytes_accessed=2 * MIB, transcendentals=0
        ),
        name="norm_and_dispatch",
    )(parts, residual, gain, chooser)


def experts_body(experts, arrived, w_gate, w_up, w_down, out, total):
    expert, chunk = pl.program_id(0), pl.program_id(1)
    rows = arrived.shape[0]
    gate = nn_dot(arrived[...], w_gate[0])
    upward = nn_dot(arrived[...], w_up[0])
    hidden = gate / (1.0 + jnp.exp(-gate)) * upward
    slot = lax.broadcasted_iota(jnp.int32, hidden.shape, 0)
    mine = lax.rem(slot, experts * MOST) // MOST == expert
    hidden = jnp.where(mine, hidden, 0.0).astype(BF16)
    product = nn_dot(hidden, w_down[0])
    first = (expert == 0) & (chunk == 0)
    last = (expert == pl.num_programs(0) - 1) & (chunk == pl.num_programs(1) - 1)

    @pl.when(first)
    def _():
        total[...] = product

    @pl.when(jnp.logical_not(first))
    def _():
        total[...] += product

    @pl.when(last)
    def _():
        out[...] = total[...].astype(BF16)


def run_experts(arrived, w_gate, w_up, w_down):
    rows, width = arrived.shape
    experts, _, hidden = w_gate.shape
    block = 256
    return pl.pallas_call(
        functools.partial(experts_body, experts),
        grid=(experts, hidden // block),
        in_specs=[
            pl.BlockSpec((rows, width), lambda e, f: (0, 0)),
            pl.BlockSpec((1, width, block), lambda e, f: (e, 0, f)),
            pl.BlockSpec((1, width, block), lambda e, f: (e, 0, f)),
            pl.BlockSpec((1, block, width), lambda e, f: (e, f, 0)),
        ],
        out_specs=pl.BlockSpec((rows, width), lambda e, f: (0, 0)),
        out_shape=jax.ShapeDtypeStruct((rows, width), BF16),
        scratch_shapes=[pltpu.VMEM((rows, width), F32)],
        compiler_params=pltpu.CompilerParams(vmem_limit_bytes=32 * MIB),
        cost_estimate=pl.CostEstimate(
            flops=6 * rows * width * experts * hidden,
            bytes_accessed=6 * width * experts * hidden,
            transcendentals=rows * experts * hidden,
        ),
        name="experts",
    )(arrived, w_gate, w_up, w_down)


def mix_body(returned, coarse, fine, middle, out):
    values = returned[...]
    mixed = nn_dot(coarse[...], values) + nn_dot(fine[...], values)
    out[...] = (middle[...].astype(F32) + mixed).astype(BF16)


def mix(returned, coarse, fine, middle):
    vmem = pl.BlockSpec(memory_space=pltpu.VMEM)
    return pl.pallas_call(
        mix_body,
        in_specs=[vmem] * 4,
        out_specs=vmem,
        out_shape=jax.ShapeDtypeStruct(middle.shape, BF16),
        compiler_params=pltpu.CompilerParams(vmem_limit_bytes=16 * MIB),
        name="mix",
    )(returned, coarse, fine, middle)


def on_device(
    queries,
    new_key,
    new_value,
    key_cache,
    value_cache,
    cache_len,
    out_weight,
    residual,
    norm_gain,
    expert_ids,
    route_weight,
    w_gate,
    w_up,
    w_down,
):
    devices = lax.axis_size("ctx")
    chips = devices // CORES
    index = lax.axis_index("ctx")
    chip, core = index // CORES, index % CORES
    home_rows, width = residual.shape
    top = expert_ids.shape[1]
    heads = queries.shape[1] // HD
    group_size = heads // (key_cache.shape[1] // HD)
    heads_chip = heads // chips
    cache_here = key_cache.shape[0]
    same_core = [[CORES * j + c for j in range(chips)] for c in range(CORES)]
    swap = [(i, i ^ 1) for i in range(devices)]

    query_parts = [queries] + [
        lax.ppermute(
            queries,
            "ctx",
            [(i, (i + CORES * shift) % devices) for i in range(devices)],
        )
        for shift in range(1, chips)
    ]
    key_other = lax.ppermute(key_cache, "ctx", swap)
    value_other = lax.ppermute(value_cache, "ctx", swap)
    weight_other = lax.ppermute(out_weight, "ctx", swap)

    place = jnp.stack([chip, index * cache_here, (index ^ 1) * cache_here, core]).astype(jnp.int32)
    lens = lax.dynamic_index_in_dim(
        cache_len.reshape(chips, CORES, home_rows), core, axis=1, keepdims=False
    ).reshape(1, chips * home_rows)

    flat_ids = expert_ids.reshape(-1)
    picks = jnp.arange(flat_ids.shape[0])
    earlier = (flat_ids[:, None] == flat_ids[None, :]) & (picks[None, :] < picks[:, None])
    target = (flat_ids * MOST + jnp.sum(earlier, axis=1, dtype=jnp.int32)).reshape(home_rows, top)
    experts = w_gate.shape[0]
    slots = experts * devices * MOST
    takes = target[:, :, None] == jnp.arange(slots, dtype=jnp.int32)
    chooser = jnp.any(takes, axis=1).T.astype(BF16)
    spread = jnp.sum(jnp.where(takes, route_weight[:, :, None], 0.0), axis=1)
    coarse = spread.astype(BF16)
    fine = (spread - coarse.astype(F32)).astype(BF16)

    sums = attention(
        place,
        query_parts,
        (key_cache, key_other),
        (value_cache, value_other),
        new_key,
        new_value,
        lens,
        heads_chip,
        group_size,
    )
    gathered = lax.all_to_all(
        sums, "ctx", split_axis=0, concat_axis=0, axis_index_groups=same_core, tiled=True
    )
    share = project(place, gathered, out_weight, weight_other, heads_chip)
    shares = lax.all_to_all(
        share.reshape(chips, home_rows, width),
        "ctx",
        split_axis=0,
        concat_axis=0,
        axis_index_groups=same_core,
        tiled=True,
    )
    middle, outgoing = norm_and_dispatch(shares, residual, norm_gain.reshape(1, width), chooser)
    arrived = lax.all_to_all(
        outgoing.reshape(devices, experts * MOST, width), "ctx", split_axis=0, concat_axis=0, tiled=True
    )
    produced = run_experts(arrived.reshape(slots, width), w_gate, w_up, w_down)
    returned = lax.all_to_all(
        produced.reshape(devices, experts * MOST, width), "ctx", split_axis=0, concat_axis=0, tiled=True
    )
    return mix(returned.reshape(slots, width), coarse, fine, middle)


def solution(mesh):
    placed = (
        P(("groups", "ctx"), None),
        P(("groups", "ctx"), None),
        P(("groups", "ctx"), None),
        P(("groups", "ctx"), None),
        P(("groups", "ctx"), None),
        P("groups"),
        P("ctx", None),
        P(("groups", "ctx"), None),
        P(),
        P(("groups", "ctx"), None),
        P(("groups", "ctx"), None),
        P("ctx", None, None),
        P("ctx", None, None),
        P("ctx", None, None),
    )
    return jax.shard_map(
        on_device, mesh=mesh, in_specs=placed, out_specs=P(("groups", "ctx"), None), check_vma=False
    )
```

```python
import functools
import math

import jax
import jax.numpy as jnp
from jax import lax
from jax.experimental import pallas as pl
from jax.experimental.pallas import tpu as pltpu
from jax.sharding import PartitionSpec as P

HD = 128
MOST = 4
CORES = 2
STATS = 16
MASKED = -1e30
FLOOR = -1e20
LOG2E = math.log2(math.e)
MIB = 1024 * 1024
F32 = jnp.float32
BF16 = jnp.bfloat16


def nt_dot(a, b):
    return lax.dot_general(a, b, (((1,), (1,)), ((), ())), preferred_element_type=F32)


def nn_dot(a, b):
    return lax.dot_general(a, b, (((1,), (0,)), ((), ())), preferred_element_type=F32)


def attention_body(shape, place, own_q, other_q, key_own, key_other, value_own, value_other, key_fresh, value_fresh, lens, out, *scratch):
    owners, heads_owner, home_rows, rows, cache_here, step = shape
    q_rows, v_turned, hidden, scores, probs = scratch
    chip, start_own, start_other, pair_place = place[0], place[1], place[2], place[4]
    rings = rows // home_rows // 2

    @pl.when(pl.program_id(0) == 0)
    def _():
        for part, start in enumerate((start_own, start_other)):
            positions = start + lax.broadcasted_iota(jnp.int32, (cache_here, rows), 0)
            hidden[part * cache_here : (part + 1) * cache_here, :] = jnp.where(
                positions < lens[...], 0.0, MASKED
            )
        token = lax.broadcasted_iota(jnp.int32, (home_rows, rows), 0)
        column = lax.broadcasted_iota(jnp.int32, (home_rows, rows), 1)
        hidden[2 * cache_here :, :] = jnp.where(token + chip * home_rows == column, 0.0, MASKED)
        v_turned[HD:, :] = jnp.ones_like(v_turned[HD:, :])

    v_turned[:HD, :cache_here] = value_own[...].T
    v_turned[:HD, cache_here:] = value_other[...].T
    value_new = value_fresh[...].astype(F32).T.astype(BF16)
    for ring in range(rings):
        taken = slice(ring * home_rows, (ring + 1) * home_rows)
        for piece, side in ((own_q, pair_place), (other_q, 1 - pair_place)):
            spot = pl.multiple_of((2 * ring + side) * home_rows, home_rows)
            q_rows[pl.ds(spot, home_rows), :] = piece[taken, :]

    heads = owners * heads_owner
    wide = min(2, heads)
    groups = heads // wide
    factor = LOG2E / math.sqrt(HD)
    pieces = [(key_own, 0, i) for i in range(0, cache_here, step)]
    pieces += [(key_other, cache_here, i) for i in range(0, cache_here, step)]
    queries, highest, fresh = [], [], []
    for group in range(groups):
        scaled = jnp.concatenate(
            [q_rows[:, (group * wide + k) * HD : (group * wide + k + 1) * HD] for k in range(wide)], axis=0
        ).astype(F32) * factor
        coarse = scaled.astype(BF16)
        fine = (scaled - coarse.astype(F32)).astype(BF16)
        queries.append(jnp.concatenate([coarse, fine], axis=1))

    def score(group, piece):
        source, base, i = piece
        keys = source[i : i + step, :]
        s = nt_dot(jnp.concatenate([keys, keys], axis=1), queries[group])
        s = s + jnp.concatenate([hidden[base + i : base + i + step, :]] * wide, axis=1)
        scores[group % 2, base + i : base + i + step, :] = s
        return jnp.max(s.reshape(step // 8, 8, wide * rows), axis=0)

    def weigh(group, piece, lift):
        _, base, i = piece
        s = scores[group % 2, base + i : base + i + step, :]
        probs[group % 2, base + i : base + i + step, :] = jnp.exp2(s - lift).astype(BF16)

    def finish_peak(group, run):
        keys = key_fresh[...]
        s = nt_dot(jnp.concatenate([keys, keys], axis=1), queries[group])
        s = s + jnp.concatenate([hidden[2 * cache_here :, :]] * wide, axis=1)
        peak = jnp.maximum(jnp.max(run, axis=0, keepdims=True), jnp.max(s, axis=0, keepdims=True))
        peak = jnp.maximum(peak, FLOOR).astype(BF16).astype(F32)
        return peak, jnp.exp2(s - peak).astype(BF16)

    stats = [[None] * (3 * heads_owner) for _ in range(owners)]

    def total(group, peak, p_new):
        sums = nn_dot(v_turned[...], probs[group % 2])
        numer = sums[:HD] + nn_dot(value_new, p_new)
        denom = sums[HD : HD + 1] + jnp.sum(p_new.astype(F32), axis=0, keepdims=True)
        for k in range(wide):
            owner, h = divmod(group * wide + k, heads_owner)
            cols = slice(k * rows, (k + 1) * rows)
            out[owner, h * HD : (h + 1) * HD, :] = numer[:, cols].astype(BF16)
            high = denom[:, cols].astype(BF16).astype(F32)
            stats[owner][h] = peak[:, cols]
            stats[owner][heads_owner + h] = high
            stats[owner][2 * heads_owner + h] = denom[:, cols] - high

    previous = None
    for group in range(groups + 1):
        run = None
        for piece in pieces:
            if group < groups:
                top = score(group, piece)
                run = top if run is None else jnp.maximum(run, top)
            if previous is not None:
                weigh(group - 1, piece, previous[0])
        if previous is not None:
            total(group - 1, *previous)
        if group < groups:
            previous = finish_peak(group, run)
    for owner in range(owners):
        filled = stats[owner] + [jnp.zeros_like(stats[owner][0])] * (STATS - len(stats[owner]))
        out[owner, heads_owner * HD :, :] = jnp.concatenate(filled, axis=0).astype(BF16)


def attention(place, own_q, other_q, keys, values, new_key, new_value, lens, chips, kv_heads):
    rows = lens.shape[1]
    home_rows = new_key.shape[0]
    cache_here = keys[0].shape[0]
    heads_owner = own_q.shape[1] // HD // chips
    owners = chips // kv_heads
    height = heads_owner * HD + STATS
    step = 256
    wide = min(2, owners * heads_owner)
    kv = lambda g, place: (0, g)
    shape = (owners, heads_owner, home_rows, rows, cache_here, step)
    work = rows * heads_owner * chips * 2 * cache_here
    return pl.pallas_call(
        functools.partial(attention_body, shape),
        grid_spec=pltpu.PrefetchScalarGridSpec(
            num_scalar_prefetch=1,
            grid=(kv_heads,),
            in_specs=[pl.BlockSpec((own_q.shape[0], owners * heads_owner * HD), kv)] * 2
            + [pl.BlockSpec((cache_here, HD), kv)] * 4
            + [pl.BlockSpec((home_rows, HD), kv)] * 2
            + [pl.BlockSpec((1, rows), lambda g, place: (0, 0))],
            out_specs=pl.BlockSpec((owners, height, rows), lambda g, place: (g, 0, 0)),
            scratch_shapes=[
                pltpu.VMEM((rows, owners * heads_owner * HD), BF16),
                pltpu.VMEM((HD + STATS, 2 * cache_here), BF16),
                pltpu.VMEM((2 * cache_here + home_rows, rows), F32),
                pltpu.VMEM((2, 2 * cache_here, wide * rows), F32),
                pltpu.VMEM((2, 2 * cache_here, wide * rows), BF16),
            ],
        ),
        out_shape=jax.ShapeDtypeStruct((chips, height, rows), BF16),
        compiler_params=pltpu.CompilerParams(vmem_limit_bytes=56 * MIB),
        cost_estimate=pl.CostEstimate(
            flops=6 * work * HD, bytes_accessed=8 * MIB, transcendentals=work
        ),
        name="attention",
    )(place, own_q, other_q, *keys, *values, new_key, new_value, lens)


def project_body(place, *refs):
    *chunks, weight_own, weight_other, out, turned = refs
    core = place[3]
    for chunk, parts in enumerate(chunks):
        chips, height, _ = parts.shape
        base = height - STATS
        heads = base // HD
        stats = parts[:, base:, :].astype(F32)
        peaks = stats[:, :heads]
        share = jnp.exp2(peaks - jnp.max(peaks, axis=0, keepdims=True))
        totals = stats[:, heads : 2 * heads] + stats[:, 2 * heads : 3 * heads]
        denom = jnp.sum(share * totals, axis=0)
        for h in range(heads):
            numer = None
            for s in range(chips):
                term = parts[s, h * HD : (h + 1) * HD, :].astype(F32) * share[s, h : h + 1, :]
                numer = term if numer is None else numer + term
            turned[chunk, :, h * HD : (h + 1) * HD] = (numer / denom[h : h + 1, :]).T.astype(BF16)
    product = nn_dot(turned[core], weight_own[...]) + nn_dot(turned[1 - core], weight_other[...])
    out[...] = product.astype(BF16)


def project(place, chunks, weight_own, weight_other):
    rows = chunks[0].shape[2]
    depth, width = weight_own.shape
    vmem = pl.BlockSpec(memory_space=pltpu.VMEM)
    return pl.pallas_call(
        project_body,
        in_specs=[pl.BlockSpec(memory_space=pltpu.SMEM)] + [vmem] * (len(chunks) + 2),
        out_specs=vmem,
        out_shape=jax.ShapeDtypeStruct((rows, width), BF16),
        scratch_shapes=[pltpu.VMEM((CORES, rows, depth), BF16)],
        compiler_params=pltpu.CompilerParams(vmem_limit_bytes=32 * MIB),
        cost_estimate=pl.CostEstimate(
            flops=4 * rows * width * depth, bytes_accessed=4 * MIB, transcendentals=0
        ),
        name="project",
    )(place, *chunks, weight_own, weight_other)


def norm_body(parts, residual, gain, chooser, middle_out, sent):
    total = parts[0].astype(F32)
    for s in range(1, parts.shape[0]):
        total = total + parts[s].astype(F32)
    middle = (residual[...].astype(F32) + total).astype(BF16)
    middle_out[...] = middle
    middle = middle.astype(F32)
    inv_rms = lax.rsqrt(jnp.mean(middle * middle, axis=-1, keepdims=True) + 1e-06)
    normed = (middle * inv_rms * gain[...].astype(F32)).astype(BF16)
    sent[...] = nn_dot(chooser[...], normed).astype(BF16)


def norm_and_dispatch(parts, residual, gain, chooser):
    vmem = pl.BlockSpec(memory_space=pltpu.VMEM)
    rows, width = residual.shape
    return pl.pallas_call(
        norm_body,
        in_specs=[vmem] * 4,
        out_specs=[vmem] * 2,
        out_shape=[
            jax.ShapeDtypeStruct((rows, width), BF16),
            jax.ShapeDtypeStruct((chooser.shape[0], width), BF16),
        ],
        compiler_params=pltpu.CompilerParams(vmem_limit_bytes=24 * MIB),
        cost_estimate=pl.CostEstimate(
            flops=2 * chooser.shape[0] * rows * width, bytes_accessed=2 * MIB, transcendentals=0
        ),
        name="norm_and_dispatch",
    )(parts, residual, gain, chooser)


def experts_body(experts, arrived, w_gate, w_up, w_down, out, total):
    expert, chunk = pl.program_id(0), pl.program_id(1)
    rows = arrived.shape[0]
    gate = nn_dot(arrived[...], w_gate[0])
    upward = nn_dot(arrived[...], w_up[0])
    hidden = gate / (1.0 + jnp.exp(-gate)) * upward
    slot = lax.broadcasted_iota(jnp.int32, hidden.shape, 0)
    mine = lax.rem(slot, experts * MOST) // MOST == expert
    hidden = jnp.where(mine, hidden, 0.0).astype(BF16)
    product = nn_dot(hidden, w_down[0])
    first = (expert == 0) & (chunk == 0)
    last = (expert == pl.num_programs(0) - 1) & (chunk == pl.num_programs(1) - 1)

    @pl.when(first)
    def _():
        total[...] = product

    @pl.when(jnp.logical_not(first))
    def _():
        total[...] += product

    @pl.when(last)
    def _():
        out[...] = total[...].astype(BF16)


def run_experts(arrived, w_gate, w_up, w_down):
    rows, width = arrived.shape
    experts, _, hidden = w_gate.shape
    block = 256
    return pl.pallas_call(
        functools.partial(experts_body, experts),
        grid=(experts, hidden // block),
        in_specs=[
            pl.BlockSpec((rows, width), lambda e, f: (0, 0)),
            pl.BlockSpec((1, width, block), lambda e, f: (e, 0, f)),
            pl.BlockSpec((1, width, block), lambda e, f: (e, 0, f)),
            pl.BlockSpec((1, block, width), lambda e, f: (e, f, 0)),
        ],
        out_specs=pl.BlockSpec((rows, width), lambda e, f: (0, 0)),
        out_shape=jax.ShapeDtypeStruct((rows, width), BF16),
        scratch_shapes=[pltpu.VMEM((rows, width), F32)],
        compiler_params=pltpu.CompilerParams(vmem_limit_bytes=60 * MIB),
        cost_estimate=pl.CostEstimate(
            flops=6 * rows * width * experts * hidden,
            bytes_accessed=6 * width * experts * hidden,
            transcendentals=rows * experts * hidden,
        ),
        name="experts",
    )(arrived, w_gate, w_up, w_down)


def mix_body(returned, coarse, fine, middle, out):
    values = returned[...]
    mixed = nn_dot(coarse[...], values) + nn_dot(fine[...], values)
    out[...] = (middle[...].astype(F32) + mixed).astype(BF16)


def mix(returned, coarse, fine, middle):
    vmem = pl.BlockSpec(memory_space=pltpu.VMEM)
    return pl.pallas_call(
        mix_body,
        in_specs=[vmem] * 4,
        out_specs=vmem,
        out_shape=jax.ShapeDtypeStruct(middle.shape, BF16),
        compiler_params=pltpu.CompilerParams(vmem_limit_bytes=16 * MIB),
        name="mix",
    )(returned, coarse, fine, middle)


def on_device(
    queries,
    new_key,
    new_value,
    key_cache,
    value_cache,
    cache_len,
    out_weight,
    residual,
    norm_gain,
    expert_ids,
    route_weight,
    w_gate,
    w_up,
    w_down,
):
    devices = lax.axis_size("ctx")
    chips = devices // CORES
    index = lax.axis_index("ctx")
    chip, core = index // CORES, index % CORES
    home_rows, width = residual.shape
    top = expert_ids.shape[1]
    heads_here = out_weight.shape[0] // HD
    cache_here = key_cache.shape[0]
    same_core = [[CORES * j + c for j in range(chips)] for c in range(CORES)]
    swap = [(i, i ^ 1) for i in range(devices)]

    along = [
        [CORES * (2 * ring + side) + c for ring in range(chips // 2)]
        for side in range(2)
        for c in range(CORES)
    ]
    across = [(i, i ^ CORES) for i in range(devices)]

    key_other = lax.ppermute(key_cache, "ctx", swap)
    value_other = lax.ppermute(value_cache, "ctx", swap)
    by_owner = queries.reshape(home_rows, chips, CORES, heads_here * HD)
    query_chunks = []
    for chunk in range(CORES):
        part = by_owner[:, :, chunk].reshape(home_rows, chips * heads_here * HD)
        mine = lax.all_gather(part, "ctx", axis=0, axis_index_groups=along, tiled=True)
        query_chunks.append((mine, lax.ppermute(mine, "ctx", across)))
    weight_other = lax.ppermute(out_weight, "ctx", swap)

    place = jnp.stack([chip, index * cache_here, (index ^ 1) * cache_here, core, chip % 2]).astype(jnp.int32)
    lens = lax.dynamic_index_in_dim(
        cache_len.reshape(chips, CORES, home_rows), core, axis=1, keepdims=False
    ).reshape(1, chips * home_rows)

    flat_ids = expert_ids.reshape(-1)
    picks = jnp.arange(flat_ids.shape[0])
    earlier = (flat_ids[:, None] == flat_ids[None, :]) & (picks[None, :] < picks[:, None])
    target = (flat_ids * MOST + jnp.sum(earlier, axis=1, dtype=jnp.int32)).reshape(home_rows, top)
    experts = w_gate.shape[0]
    slots = experts * devices * MOST
    takes = target[:, :, None] == jnp.arange(slots, dtype=jnp.int32)
    chooser = jnp.any(takes, axis=1).T.astype(BF16)
    spread = jnp.sum(jnp.where(takes, route_weight[:, :, None], 0.0), axis=1)
    coarse = spread.astype(BF16)
    fine = (spread - coarse.astype(F32)).astype(BF16)

    gathered = []
    for own_q, other_q in query_chunks:
        sums = attention(
            place,
            own_q,
            other_q,
            (key_cache, key_other),
            (value_cache, value_other),
            new_key,
            new_value,
            lens,
            chips,
            key_cache.shape[1] // HD,
        )
        gathered.append(
            lax.all_to_all(
                sums, "ctx", split_axis=0, concat_axis=0, axis_index_groups=same_core, tiled=True
            )
        )
    share = project(place, gathered, out_weight, weight_other)
    shares = lax.all_to_all(
        share.reshape(chips, home_rows, width),
        "ctx",
        split_axis=0,
        concat_axis=0,
        axis_index_groups=same_core,
        tiled=True,
    )
    middle, outgoing = norm_and_dispatch(shares, residual, norm_gain.reshape(1, width), chooser)
    arrived = lax.all_to_all(
        outgoing.reshape(devices, experts * MOST, width), "ctx", split_axis=0, concat_axis=0, tiled=True
    )
    produced = run_experts(arrived.reshape(slots, width), w_gate, w_up, w_down)
    returned = lax.all_to_all(
        produced.reshape(devices, experts * MOST, width), "ctx", split_axis=0, concat_axis=0, tiled=True
    )
    return mix(returned.reshape(slots, width), coarse, fine, middle)


def solution(mesh):
    placed = (
        P(("groups", "ctx"), None),
        P(("groups", "ctx"), None),
        P(("groups", "ctx"), None),
        P(("groups", "ctx"), None),
        P(("groups", "ctx"), None),
        P("groups"),
        P("ctx", None),
        P(("groups", "ctx"), None),
        P(),
        P(("groups", "ctx"), None),
        P(("groups", "ctx"), None),
        P("ctx", None, None),
        P("ctx", None, None),
        P("ctx", None, None),
    )
    return jax.shard_map(
        on_device, mesh=mesh, in_specs=placed, out_specs=P(("groups", "ctx"), None), check_vma=False
    )
```

```python
import functools
import math

import jax
import jax.numpy as jnp
from jax import lax
from jax.experimental import pallas as pl
from jax.experimental.pallas import tpu as pltpu
from jax.sharding import PartitionSpec as P

HD = 128
MOST = 4
CORES = 2
STATS = 16
MASKED = -1e30
FLOOR = -1e20
LOG2E = math.log2(math.e)
MIB = 1024 * 1024
F32 = jnp.float32
BF16 = jnp.bfloat16


def nt_dot(a, b):
    return lax.dot_general(a, b, (((1,), (1,)), ((), ())), preferred_element_type=F32)


def nn_dot(a, b):
    return lax.dot_general(a, b, (((1,), (0,)), ((), ())), preferred_element_type=F32)


def attention_body(shape, place, own_q, other_q, key_own, key_other, value_own, value_other, key_fresh, value_fresh, lens, out, *scratch):
    owners, heads_owner, home_rows, rows, cache_here, step = shape
    q_rows, v_turned, hidden, scores, probs = scratch
    chip, start_own, start_other, pair_place, ring_place = place[0], place[1], place[2], place[4], place[5]
    rings = rows // home_rows // 2

    @pl.when(pl.program_id(0) == 0)
    def _():
        for part, start in enumerate((start_own, start_other)):
            positions = start + lax.broadcasted_iota(jnp.int32, (cache_here, rows), 0)
            hidden[part * cache_here : (part + 1) * cache_here, :] = jnp.where(
                positions < lens[...], 0.0, MASKED
            )
        token = lax.broadcasted_iota(jnp.int32, (home_rows, rows), 0)
        column = lax.broadcasted_iota(jnp.int32, (home_rows, rows), 1)
        hidden[2 * cache_here :, :] = jnp.where(token + chip * home_rows == column, 0.0, MASKED)
        v_turned[HD:, :] = jnp.ones_like(v_turned[HD:, :])

    v_turned[:HD, :cache_here] = value_own[...].T
    v_turned[:HD, cache_here:] = value_other[...].T
    value_new = value_fresh[...].astype(F32).T.astype(BF16)
    for ring in range(rings):
        taken = slice(ring * home_rows, (ring + 1) * home_rows)
        for piece, side in ((own_q, pair_place), (other_q, 1 - pair_place)):
            spot = pl.multiple_of((2 * (ring ^ ring_place) + side) * home_rows, home_rows)
            q_rows[pl.ds(spot, home_rows), :] = piece[taken, :]

    heads = owners * heads_owner
    wide = min(2, heads)
    groups = heads // wide
    factor = LOG2E / math.sqrt(HD)
    pieces = [(key_own, 0, i) for i in range(0, cache_here, step)]
    pieces += [(key_other, cache_here, i) for i in range(0, cache_here, step)]
    queries, highest, fresh = [], [], []
    for group in range(groups):
        scaled = jnp.concatenate(
            [q_rows[:, (group * wide + k) * HD : (group * wide + k + 1) * HD] for k in range(wide)], axis=0
        ).astype(F32) * factor
        coarse = scaled.astype(BF16)
        fine = (scaled - coarse.astype(F32)).astype(BF16)
        queries.append(jnp.concatenate([coarse, fine], axis=1))

    def score(group, piece):
        source, base, i = piece
        keys = source[i : i + step, :]
        s = nt_dot(jnp.concatenate([keys, keys], axis=1), queries[group])
        s = s + jnp.concatenate([hidden[base + i : base + i + step, :]] * wide, axis=1)
        scores[group % 2, base + i : base + i + step, :] = s
        return jnp.max(s.reshape(step // 8, 8, wide * rows), axis=0)

    def weigh(group, piece, lift):
        _, base, i = piece
        s = scores[group % 2, base + i : base + i + step, :]
        probs[group % 2, base + i : base + i + step, :] = jnp.exp2((s - lift).astype(BF16))

    def finish_peak(group, run):
        keys = key_fresh[...]
        s = nt_dot(jnp.concatenate([keys, keys], axis=1), queries[group])
        s = s + jnp.concatenate([hidden[2 * cache_here :, :]] * wide, axis=1)
        peak = jnp.maximum(jnp.max(run, axis=0, keepdims=True), jnp.max(s, axis=0, keepdims=True))
        peak = jnp.maximum(peak, FLOOR).astype(BF16).astype(F32)
        return peak, jnp.exp2((s - peak).astype(BF16))

    stats = [[None] * (3 * heads_owner) for _ in range(owners)]

    def total(group, peak, p_new):
        sums = nn_dot(v_turned[...], probs[group % 2])
        numer = sums[:HD] + nn_dot(value_new, p_new)
        denom = sums[HD : HD + 1] + jnp.sum(p_new.astype(F32), axis=0, keepdims=True)
        for k in range(wide):
            owner, h = divmod(group * wide + k, heads_owner)
            cols = slice(k * rows, (k + 1) * rows)
            out[owner, h * HD : (h + 1) * HD, :] = numer[:, cols].astype(BF16)
            high = denom[:, cols].astype(BF16).astype(F32)
            stats[owner][h] = peak[:, cols]
            stats[owner][heads_owner + h] = high
            stats[owner][2 * heads_owner + h] = denom[:, cols] - high

    previous = None
    for group in range(groups + 1):
        run = None
        for piece in pieces:
            if group < groups:
                top = score(group, piece)
                run = top if run is None else jnp.maximum(run, top)
            if previous is not None:
                weigh(group - 1, piece, previous[0])
        if previous is not None:
            total(group - 1, *previous)
        if group < groups:
            previous = finish_peak(group, run)
    for owner in range(owners):
        filled = stats[owner] + [jnp.zeros_like(stats[owner][0])] * (STATS - len(stats[owner]))
        out[owner, heads_owner * HD :, :] = jnp.concatenate(filled, axis=0).astype(BF16)


def attention(place, own_q, other_q, keys, values, new_key, new_value, lens, chips, kv_heads):
    rows = lens.shape[1]
    home_rows = new_key.shape[0]
    cache_here = keys[0].shape[0]
    heads_owner = own_q.shape[1] // HD // chips
    owners = chips // kv_heads
    height = heads_owner * HD + STATS
    step = 256
    wide = min(2, owners * heads_owner)
    kv = lambda g, place: (0, g)
    shape = (owners, heads_owner, home_rows, rows, cache_here, step)
    work = rows * heads_owner * chips * 2 * cache_here
    return pl.pallas_call(
        functools.partial(attention_body, shape),
        grid_spec=pltpu.PrefetchScalarGridSpec(
            num_scalar_prefetch=1,
            grid=(kv_heads,),
            in_specs=[pl.BlockSpec((own_q.shape[0], owners * heads_owner * HD), kv)] * 2
            + [pl.BlockSpec((cache_here, HD), kv)] * 4
            + [pl.BlockSpec((home_rows, HD), kv)] * 2
            + [pl.BlockSpec((1, rows), lambda g, place: (0, 0))],
            out_specs=pl.BlockSpec((owners, height, rows), lambda g, place: (g, 0, 0)),
            scratch_shapes=[
                pltpu.VMEM((rows, owners * heads_owner * HD), BF16),
                pltpu.VMEM((HD + STATS, 2 * cache_here), BF16),
                pltpu.VMEM((2 * cache_here + home_rows, rows), F32),
                pltpu.VMEM((2, 2 * cache_here, wide * rows), F32),
                pltpu.VMEM((2, 2 * cache_here, wide * rows), BF16),
            ],
        ),
        out_shape=jax.ShapeDtypeStruct((chips, height, rows), BF16),
        compiler_params=pltpu.CompilerParams(vmem_limit_bytes=56 * MIB),
        cost_estimate=pl.CostEstimate(
            flops=6 * work * HD, bytes_accessed=8 * MIB, transcendentals=work
        ),
        name="attention",
    )(place, own_q, other_q, *keys, *values, new_key, new_value, lens)


def project_body(place, *refs):
    *chunks, weight_own, weight_other, out, turned = refs
    core = place[3]
    for chunk, parts in enumerate(chunks):
        chips, height, _ = parts.shape
        base = height - STATS
        heads = base // HD
        stats = parts[:, base:, :].astype(F32)
        peaks = stats[:, :heads]
        share = jnp.exp2(peaks - jnp.max(peaks, axis=0, keepdims=True))
        totals = stats[:, heads : 2 * heads] + stats[:, 2 * heads : 3 * heads]
        denom = jnp.sum(share * totals, axis=0)
        for h in range(heads):
            numer = None
            for s in range(chips):
                term = parts[s, h * HD : (h + 1) * HD, :].astype(F32) * share[s, h : h + 1, :]
                numer = term if numer is None else numer + term
            turned[chunk, :, h * HD : (h + 1) * HD] = (numer / denom[h : h + 1, :]).T.astype(BF16)
    product = nn_dot(turned[core], weight_own[...]) + nn_dot(turned[1 - core], weight_other[...])
    out[...] = product.astype(BF16)


def project(place, chunks, weight_own, weight_other):
    rows = chunks[0].shape[2]
    depth, width = weight_own.shape
    vmem = pl.BlockSpec(memory_space=pltpu.VMEM)
    return pl.pallas_call(
        project_body,
        in_specs=[pl.BlockSpec(memory_space=pltpu.SMEM)] + [vmem] * (len(chunks) + 2),
        out_specs=vmem,
        out_shape=jax.ShapeDtypeStruct((rows, width), BF16),
        scratch_shapes=[pltpu.VMEM((CORES, rows, depth), BF16)],
        compiler_params=pltpu.CompilerParams(vmem_limit_bytes=32 * MIB),
        cost_estimate=pl.CostEstimate(
            flops=4 * rows * width * depth, bytes_accessed=4 * MIB, transcendentals=0
        ),
        name="project",
    )(place, *chunks, weight_own, weight_other)


def norm_body(parts, residual, gain, chooser, middle_out, sent):
    total = parts[0].astype(F32)
    for s in range(1, parts.shape[0]):
        total = total + parts[s].astype(F32)
    middle = (residual[...].astype(F32) + total).astype(BF16)
    middle_out[...] = middle
    middle = middle.astype(F32)
    inv_rms = lax.rsqrt(jnp.mean(middle * middle, axis=-1, keepdims=True) + 1e-06)
    normed = (middle * inv_rms * gain[...].astype(F32)).astype(BF16)
    sent[...] = nn_dot(chooser[...], normed).astype(BF16)


def norm_and_dispatch(parts, residual, gain, chooser):
    vmem = pl.BlockSpec(memory_space=pltpu.VMEM)
    rows, width = residual.shape
    return pl.pallas_call(
        norm_body,
        in_specs=[vmem] * 4,
        out_specs=[vmem] * 2,
        out_shape=[
            jax.ShapeDtypeStruct((rows, width), BF16),
            jax.ShapeDtypeStruct((chooser.shape[0], width), BF16),
        ],
        compiler_params=pltpu.CompilerParams(vmem_limit_bytes=24 * MIB),
        cost_estimate=pl.CostEstimate(
            flops=2 * chooser.shape[0] * rows * width, bytes_accessed=2 * MIB, transcendentals=0
        ),
        name="norm_and_dispatch",
    )(parts, residual, gain, chooser)


def experts_body(experts, arrived, w_gate, w_up, w_down, out, total):
    expert, chunk = pl.program_id(0), pl.program_id(1)
    rows = arrived.shape[0]
    gate = nn_dot(arrived[...], w_gate[0])
    upward = nn_dot(arrived[...], w_up[0])
    hidden = gate / (1.0 + jnp.exp(-gate)) * upward
    slot = lax.broadcasted_iota(jnp.int32, hidden.shape, 0)
    mine = lax.rem(slot, experts * MOST) // MOST == expert
    hidden = jnp.where(mine, hidden, 0.0).astype(BF16)
    product = nn_dot(hidden, w_down[0])
    first = (expert == 0) & (chunk == 0)
    last = (expert == pl.num_programs(0) - 1) & (chunk == pl.num_programs(1) - 1)

    @pl.when(first)
    def _():
        total[...] = product

    @pl.when(jnp.logical_not(first))
    def _():
        total[...] += product

    @pl.when(last)
    def _():
        out[...] = total[...].astype(BF16)


def run_experts(arrived, w_gate, w_up, w_down):
    rows, width = arrived.shape
    experts, _, hidden = w_gate.shape
    block = 256
    return pl.pallas_call(
        functools.partial(experts_body, experts),
        grid=(experts, hidden // block),
        in_specs=[
            pl.BlockSpec((rows, width), lambda e, f: (0, 0)),
            pl.BlockSpec((1, width, block), lambda e, f: (e, 0, f)),
            pl.BlockSpec((1, width, block), lambda e, f: (e, 0, f)),
            pl.BlockSpec((1, block, width), lambda e, f: (e, f, 0)),
        ],
        out_specs=pl.BlockSpec((rows, width), lambda e, f: (0, 0)),
        out_shape=jax.ShapeDtypeStruct((rows, width), BF16),
        scratch_shapes=[pltpu.VMEM((rows, width), F32)],
        compiler_params=pltpu.CompilerParams(vmem_limit_bytes=60 * MIB),
        cost_estimate=pl.CostEstimate(
            flops=6 * rows * width * experts * hidden,
            bytes_accessed=6 * width * experts * hidden,
            transcendentals=rows * experts * hidden,
        ),
        name="experts",
    )(arrived, w_gate, w_up, w_down)


def mix_body(returned, coarse, fine, middle, out):
    values = returned[...]
    mixed = nn_dot(coarse[...], values) + nn_dot(fine[...], values)
    out[...] = (middle[...].astype(F32) + mixed).astype(BF16)


def mix(returned, coarse, fine, middle):
    vmem = pl.BlockSpec(memory_space=pltpu.VMEM)
    return pl.pallas_call(
        mix_body,
        in_specs=[vmem] * 4,
        out_specs=vmem,
        out_shape=jax.ShapeDtypeStruct(middle.shape, BF16),
        compiler_params=pltpu.CompilerParams(vmem_limit_bytes=16 * MIB),
        name="mix",
    )(returned, coarse, fine, middle)


def on_device(
    queries,
    new_key,
    new_value,
    key_cache,
    value_cache,
    cache_len,
    out_weight,
    residual,
    norm_gain,
    expert_ids,
    route_weight,
    w_gate,
    w_up,
    w_down,
):
    devices = lax.axis_size("ctx")
    chips = devices // CORES
    index = lax.axis_index("ctx")
    chip, core = index // CORES, index % CORES
    home_rows, width = residual.shape
    top = expert_ids.shape[1]
    heads_here = out_weight.shape[0] // HD
    cache_here = key_cache.shape[0]
    same_core = [[CORES * j + c for j in range(chips)] for c in range(CORES)]
    swap = [(i, i ^ 1) for i in range(devices)]

    across = [(i, i ^ CORES) for i in range(devices)]

    by_owner = queries.reshape(home_rows, chips, CORES, heads_here * HD)
    query_chunks = []
    for chunk in range(CORES):
        mine = by_owner[:, :, chunk].reshape(home_rows, chips * heads_here * HD)
        stride = 2 * CORES
        while stride < devices:
            step = [(i, i ^ stride) for i in range(devices)]
            mine = jnp.concatenate([mine, lax.ppermute(mine, "ctx", step)], axis=0)
            stride *= 2
        query_chunks.append((mine, lax.ppermute(mine, "ctx", across)))
    key_other = lax.ppermute(key_cache, "ctx", swap)
    value_other = lax.ppermute(value_cache, "ctx", swap)
    weight_other = lax.ppermute(out_weight, "ctx", swap)

    place = jnp.stack([chip, index * cache_here, (index ^ 1) * cache_here, core, chip % 2, chip // 2]).astype(jnp.int32)
    lens = lax.dynamic_index_in_dim(
        cache_len.reshape(chips, CORES, home_rows), core, axis=1, keepdims=False
    ).reshape(1, chips * home_rows)

    flat_ids = expert_ids.reshape(-1)
    picks = jnp.arange(flat_ids.shape[0])
    earlier = (flat_ids[:, None] == flat_ids[None, :]) & (picks[None, :] < picks[:, None])
    target = (flat_ids * MOST + jnp.sum(earlier, axis=1, dtype=jnp.int32)).reshape(home_rows, top)
    experts = w_gate.shape[0]
    slots = experts * devices * MOST
    takes = target[:, :, None] == jnp.arange(slots, dtype=jnp.int32)
    chooser = jnp.any(takes, axis=1).T.astype(BF16)
    spread = jnp.sum(jnp.where(takes, route_weight[:, :, None], 0.0), axis=1)
    coarse = spread.astype(BF16)
    fine = (spread - coarse.astype(F32)).astype(BF16)

    gathered = []
    for own_q, other_q in query_chunks:
        sums = attention(
            place,
            own_q,
            other_q,
            (key_cache, key_other),
            (value_cache, value_other),
            new_key,
            new_value,
            lens,
            chips,
            key_cache.shape[1] // HD,
        )
        gathered.append(
            lax.all_to_all(
                sums, "ctx", split_axis=0, concat_axis=0, axis_index_groups=same_core, tiled=True
            )
        )
    share = project(place, gathered, out_weight, weight_other)
    shares = lax.all_to_all(
        share.reshape(chips, home_rows, width),
        "ctx",
        split_axis=0,
        concat_axis=0,
        axis_index_groups=same_core,
        tiled=True,
    )
    middle, outgoing = norm_and_dispatch(shares, residual, norm_gain.reshape(1, width), chooser)
    arrived = lax.all_to_all(
        outgoing.reshape(devices, experts * MOST, width), "ctx", split_axis=0, concat_axis=0, tiled=True
    )
    produced = run_experts(arrived.reshape(slots, width), w_gate, w_up, w_down)
    returned = lax.all_to_all(
        produced.reshape(devices, experts * MOST, width), "ctx", split_axis=0, concat_axis=0, tiled=True
    )
    return mix(returned.reshape(slots, width), coarse, fine, middle)


def solution(mesh):
    placed = (
        P(("groups", "ctx"), None),
        P(("groups", "ctx"), None),
        P(("groups", "ctx"), None),
        P(("groups", "ctx"), None),
        P(("groups", "ctx"), None),
        P("groups"),
        P("ctx", None),
        P(("groups", "ctx"), None),
        P(),
        P(("groups", "ctx"), None),
        P(("groups", "ctx"), None),
        P("ctx", None, None),
        P("ctx", None, None),
        P("ctx", None, None),
    )
    return jax.shard_map(
        on_device, mesh=mesh, in_specs=placed, out_specs=P(("groups", "ctx"), None), check_vma=False
    )
```

```python
import functools
import math

import jax
import jax.numpy as jnp
from jax import lax
from jax.experimental import pallas as pl
from jax.experimental.pallas import tpu as pltpu
from jax.sharding import PartitionSpec as P

HD = 128
MOST = 4
CORES = 2
STATS = 16
MASKED = -1e30
FLOOR = -1e20
LOG2E = math.log2(math.e)
MIB = 1024 * 1024
F32 = jnp.float32
BF16 = jnp.bfloat16


def nt_dot(a, b):
    return lax.dot_general(a, b, (((1,), (1,)), ((), ())), preferred_element_type=F32)


def nn_dot(a, b):
    return lax.dot_general(a, b, (((1,), (0,)), ((), ())), preferred_element_type=F32)


def attention_body(shape, place, own_q, other_q, key_own, key_other, value_own, value_other, key_fresh, value_fresh, lens, out, *scratch):
    owners, heads_owner, home_rows, rows, cache_here, step = shape
    q_rows, v_turned, hidden, scores = scratch
    chip, start_own, start_other, pair_place, ring_place = place[0], place[1], place[2], place[4], place[5]
    rings = rows // home_rows // 2

    @pl.when(pl.program_id(0) == 0)
    def _():
        for part, start in enumerate((start_own, start_other)):
            positions = start + lax.broadcasted_iota(jnp.int32, (cache_here, rows), 0)
            hidden[part * cache_here : (part + 1) * cache_here, :] = jnp.where(
                positions < lens[...], 0.0, MASKED
            )
        token = lax.broadcasted_iota(jnp.int32, (home_rows, rows), 0)
        column = lax.broadcasted_iota(jnp.int32, (home_rows, rows), 1)
        hidden[2 * cache_here :, :] = jnp.where(token + chip * home_rows == column, 0.0, MASKED)
        v_turned[HD:, :] = jnp.ones_like(v_turned[HD:, :])

    v_turned[:HD, :cache_here] = value_own[...].T
    v_turned[:HD, cache_here:] = value_other[...].T
    value_new = value_fresh[...].astype(F32).T.astype(BF16)
    for ring in range(rings):
        taken = slice(ring * home_rows, (ring + 1) * home_rows)
        for piece, side in ((own_q, pair_place), (other_q, 1 - pair_place)):
            spot = pl.multiple_of((2 * (ring ^ ring_place) + side) * home_rows, home_rows)
            q_rows[pl.ds(spot, home_rows), :] = piece[taken, :]

    heads = owners * heads_owner
    factor = LOG2E / math.sqrt(HD)
    pieces = [(key_own, 0, i) for i in range(0, cache_here, step)]
    pieces += [(key_other, cache_here, i) for i in range(0, cache_here, step)]
    scaled = jnp.concatenate([q_rows[:, h * HD : (h + 1) * HD] for h in range(heads)], axis=0)
    scaled = scaled.astype(F32) * factor
    coarse = scaled.astype(BF16)
    fine = (scaled - coarse.astype(F32)).astype(BF16)
    queries = jnp.concatenate([coarse, fine], axis=1)

    def score(keys, mask):
        s = nt_dot(jnp.concatenate([keys, keys], axis=1), queries)
        return s + jnp.concatenate([mask] * heads, axis=1)

    s_new = score(key_fresh[...], hidden[2 * cache_here :, :])
    run = jnp.max(s_new.reshape(home_rows // 8, 8, heads * rows), axis=0)
    for source, base, i in pieces:
        s = score(source[i : i + step, :], hidden[base + i : base + i + step, :])
        scores[base + i : base + i + step, :] = s
        run = jnp.maximum(run, jnp.max(s.reshape(step // 8, 8, heads * rows), axis=0))
    peak = jnp.maximum(jnp.max(run, axis=0, keepdims=True), FLOOR).astype(BF16).astype(F32)
    p_new = jnp.exp2((s_new - peak).astype(BF16))
    sums = None
    for _, base, i in pieces:
        at = slice(base + i, base + i + step)
        p = jnp.exp2((scores[at, :] - peak).astype(BF16))
        term = nn_dot(v_turned[:, at], p)
        sums = term if sums is None else sums + term
    numer = sums[:HD] + nn_dot(value_new, p_new)
    denom = sums[HD : HD + 1] + jnp.sum(p_new.astype(F32), axis=0, keepdims=True)
    high = denom.astype(BF16).astype(F32)
    low = denom - high
    for owner in range(owners):
        across = [slice((owner * heads_owner + h) * rows, (owner * heads_owner + h + 1) * rows) for h in range(heads_owner)]
        for h, cols in enumerate(across):
            out[owner, h * HD : (h + 1) * HD, :] = numer[:, cols].astype(BF16)
        filled = [kind[:, cols] for kind in (peak, high, low) for cols in across]
        filled += [jnp.zeros_like(filled[0])] * (STATS - len(filled))
        out[owner, heads_owner * HD :, :] = jnp.concatenate(filled, axis=0).astype(BF16)


def attention(place, own_q, other_q, keys, values, new_key, new_value, lens, chips, kv_heads):
    rows = lens.shape[1]
    home_rows = new_key.shape[0]
    cache_here = keys[0].shape[0]
    heads_owner = own_q.shape[1] // HD // chips
    owners = chips // kv_heads
    height = heads_owner * HD + STATS
    step = 256
    kv = lambda g, place: (0, g)
    shape = (owners, heads_owner, home_rows, rows, cache_here, step)
    work = rows * heads_owner * chips * 2 * cache_here
    return pl.pallas_call(
        functools.partial(attention_body, shape),
        grid_spec=pltpu.PrefetchScalarGridSpec(
            num_scalar_prefetch=1,
            grid=(kv_heads,),
            in_specs=[pl.BlockSpec((own_q.shape[0], owners * heads_owner * HD), kv)] * 2
            + [pl.BlockSpec((cache_here, HD), kv)] * 4
            + [pl.BlockSpec((home_rows, HD), kv)] * 2
            + [pl.BlockSpec((1, rows), lambda g, place: (0, 0))],
            out_specs=pl.BlockSpec((owners, height, rows), lambda g, place: (g, 0, 0)),
            scratch_shapes=[
                pltpu.VMEM((rows, owners * heads_owner * HD), BF16),
                pltpu.VMEM((HD + STATS, 2 * cache_here), BF16),
                pltpu.VMEM((2 * cache_here + home_rows, rows), F32),
                pltpu.VMEM((2 * cache_here, owners * heads_owner * rows), F32),
            ],
        ),
        out_shape=jax.ShapeDtypeStruct((chips, height, rows), BF16),
        compiler_params=pltpu.CompilerParams(vmem_limit_bytes=56 * MIB),
        cost_estimate=pl.CostEstimate(
            flops=6 * work * HD, bytes_accessed=8 * MIB, transcendentals=work
        ),
        name="attention",
    )(place, own_q, other_q, *keys, *values, new_key, new_value, lens)


def project_body(place, *refs):
    *chunks, weight_own, weight_other, out, turned = refs
    core = place[3]
    for chunk, parts in enumerate(chunks):
        chips, height, _ = parts.shape
        base = height - STATS
        heads = base // HD
        stats = parts[:, base:, :].astype(F32)
        peaks = stats[:, :heads]
        share = jnp.exp2(peaks - jnp.max(peaks, axis=0, keepdims=True))
        totals = stats[:, heads : 2 * heads] + stats[:, 2 * heads : 3 * heads]
        denom = jnp.sum(share * totals, axis=0)
        for h in range(heads):
            numer = None
            for s in range(chips):
                term = parts[s, h * HD : (h + 1) * HD, :].astype(F32) * share[s, h : h + 1, :]
                numer = term if numer is None else numer + term
            turned[chunk, :, h * HD : (h + 1) * HD] = (numer / denom[h : h + 1, :]).T.astype(BF16)
    product = nn_dot(turned[core], weight_own[...]) + nn_dot(turned[1 - core], weight_other[...])
    out[...] = product.astype(BF16)


def project(place, chunks, weight_own, weight_other):
    rows = chunks[0].shape[2]
    depth, width = weight_own.shape
    vmem = pl.BlockSpec(memory_space=pltpu.VMEM)
    return pl.pallas_call(
        project_body,
        in_specs=[pl.BlockSpec(memory_space=pltpu.SMEM)] + [vmem] * (len(chunks) + 2),
        out_specs=vmem,
        out_shape=jax.ShapeDtypeStruct((rows, width), BF16),
        scratch_shapes=[pltpu.VMEM((CORES, rows, depth), BF16)],
        compiler_params=pltpu.CompilerParams(vmem_limit_bytes=32 * MIB),
        cost_estimate=pl.CostEstimate(
            flops=4 * rows * width * depth, bytes_accessed=4 * MIB, transcendentals=0
        ),
        name="project",
    )(place, *chunks, weight_own, weight_other)


def norm_body(parts, residual, gain, chooser, done, middle_out, sent):
    total = parts[0].astype(F32)
    for s in range(1, parts.shape[0]):
        total = total + parts[s].astype(F32)
    middle = (residual[...].astype(F32) + total).astype(BF16)
    middle_out[...] = middle
    middle = middle.astype(F32)
    inv_rms = lax.rsqrt(jnp.mean(middle * middle, axis=-1, keepdims=True) + 1e-06)
    normed = (middle * inv_rms * gain[...].astype(F32)).astype(BF16)
    sent[...] = nn_dot(chooser[...], normed).astype(BF16)


def norm_and_dispatch(parts, residual, gain, chooser, done):
    vmem = pl.BlockSpec(memory_space=pltpu.VMEM)
    rows, width = residual.shape
    return pl.pallas_call(
        norm_body,
        in_specs=[vmem] * 5,
        out_specs=[vmem] * 2,
        out_shape=[
            jax.ShapeDtypeStruct((rows, width), BF16),
            jax.ShapeDtypeStruct((chooser.shape[0], width), BF16),
        ],
        compiler_params=pltpu.CompilerParams(vmem_limit_bytes=24 * MIB),
        cost_estimate=pl.CostEstimate(
            flops=2 * chooser.shape[0] * rows * width, bytes_accessed=2 * MIB, transcendentals=0
        ),
        name="norm_and_dispatch",
    )(parts, residual, gain, chooser, done)


def fetch_body(after, gate, up, down, gate_out, up_out, down_out, done, sems):
    copies = [
        pltpu.make_async_copy(source, held, sems.at[k])
        for k, (source, held) in enumerate(((gate, gate_out), (up, up_out), (down, down_out)))
    ]
    for copy in copies:
        copy.start()
    for copy in copies:
        copy.wait()
    done[...] = jnp.zeros_like(done)


def fetch(after, weights):
    anywhere = pl.BlockSpec(memory_space=pl.ANY)
    return pl.pallas_call(
        fetch_body,
        in_specs=[anywhere] * (1 + len(weights)),
        out_specs=[pl.BlockSpec(memory_space=pltpu.VMEM)] * (1 + len(weights)),
        out_shape=[pltpu.VMEM(w.shape, w.dtype) for w in weights]
        + [jax.ShapeDtypeStruct((8, HD), F32)],
        scratch_shapes=[pltpu.SemaphoreType.DMA((len(weights),))],
        compiler_params=pltpu.CompilerParams(vmem_limit_bytes=1 * MIB),
        cost_estimate=pl.CostEstimate(
            flops=0, bytes_accessed=2 * sum(w.size * 2 for w in weights), transcendentals=0
        ),
        name="fetch",
    )(after, *weights)


def experts_body(arrived, w_gate, w_up, w_down, out):
    experts, _, depth = w_gate.shape
    rows, width = arrived.shape
    slot = lax.broadcasted_iota(jnp.int32, (rows, 1), 0)
    values = arrived[...]
    step = 256
    hidden = []
    for e in range(experts):
        mine = lax.rem(slot, experts * MOST) // MOST == e
        parts = []
        for f in range(0, depth, step):
            gate = nn_dot(values, w_gate[e, :, f : f + step])
            upward = nn_dot(values, w_up[e, :, f : f + step])
            part = gate / (1.0 + jnp.exp(-gate)) * upward
            parts.append(jnp.where(mine, part, 0.0).astype(BF16))
        hidden.append(jnp.concatenate(parts, axis=1))
    step = 512
    for c in range(0, width, step):
        total = nn_dot(hidden[0], w_down[0, :, c : c + step])
        for e in range(1, experts):
            total = total + nn_dot(hidden[e], w_down[e, :, c : c + step])
        out[:, c : c + step] = total.astype(BF16)


def run_experts(arrived, w_gate, w_up, w_down):
    rows, width = arrived.shape
    experts, _, hidden = w_gate.shape
    vmem = pl.BlockSpec(memory_space=pltpu.VMEM)
    return pl.pallas_call(
        experts_body,
        in_specs=[vmem] * 4,
        out_specs=vmem,
        out_shape=jax.ShapeDtypeStruct((rows, width), BF16),
        compiler_params=pltpu.CompilerParams(vmem_limit_bytes=24 * MIB),
        cost_estimate=pl.CostEstimate(
            flops=6 * rows * width * experts * hidden,
            bytes_accessed=2 * MIB,
            transcendentals=rows * experts * hidden,
        ),
        name="experts",
    )(arrived, w_gate, w_up, w_down)


def mix_body(returned, coarse, fine, middle, out):
    values = returned[...]
    mixed = nn_dot(coarse[...], values) + nn_dot(fine[...], values)
    out[...] = (middle[...].astype(F32) + mixed).astype(BF16)


def mix(returned, coarse, fine, middle):
    vmem = pl.BlockSpec(memory_space=pltpu.VMEM)
    return pl.pallas_call(
        mix_body,
        in_specs=[vmem] * 4,
        out_specs=vmem,
        out_shape=jax.ShapeDtypeStruct(middle.shape, BF16),
        compiler_params=pltpu.CompilerParams(vmem_limit_bytes=16 * MIB),
        name="mix",
    )(returned, coarse, fine, middle)


def on_device(
    queries,
    new_key,
    new_value,
    key_cache,
    value_cache,
    cache_len,
    out_weight,
    residual,
    norm_gain,
    expert_ids,
    route_weight,
    w_gate,
    w_up,
    w_down,
):
    devices = lax.axis_size("ctx")
    chips = devices // CORES
    index = lax.axis_index("ctx")
    chip, core = index // CORES, index % CORES
    home_rows, width = residual.shape
    top = expert_ids.shape[1]
    heads_here = out_weight.shape[0] // HD
    cache_here = key_cache.shape[0]
    same_core = [[CORES * j + c for j in range(chips)] for c in range(CORES)]
    swap = [(i, i ^ 1) for i in range(devices)]

    across = [(i, i ^ CORES) for i in range(devices)]

    by_owner = queries.reshape(home_rows, chips, CORES, heads_here * HD)
    query_chunks = []
    for chunk in range(CORES):
        mine = by_owner[:, :, chunk].reshape(home_rows, chips * heads_here * HD)
        stride = 2 * CORES
        while stride < devices:
            step = [(i, i ^ stride) for i in range(devices)]
            mine = jnp.concatenate([mine, lax.ppermute(mine, "ctx", step)], axis=0)
            stride *= 2
        query_chunks.append((mine, lax.ppermute(mine, "ctx", across)))
    key_other = lax.ppermute(key_cache, "ctx", swap)
    value_other = lax.ppermute(value_cache, "ctx", swap)
    weight_other = lax.ppermute(out_weight, "ctx", swap)

    place = jnp.stack([chip, index * cache_here, (index ^ 1) * cache_here, core, chip % 2, chip // 2]).astype(jnp.int32)
    lens = lax.dynamic_index_in_dim(
        cache_len.reshape(chips, CORES, home_rows), core, axis=1, keepdims=False
    ).reshape(1, chips * home_rows)

    flat_ids = expert_ids.reshape(-1)
    picks = jnp.arange(flat_ids.shape[0])
    earlier = (flat_ids[:, None] == flat_ids[None, :]) & (picks[None, :] < picks[:, None])
    target = (flat_ids * MOST + jnp.sum(earlier, axis=1, dtype=jnp.int32)).reshape(home_rows, top)
    experts = w_gate.shape[0]
    slots = experts * devices * MOST
    takes = target[:, :, None] == jnp.arange(slots, dtype=jnp.int32)
    chooser = jnp.any(takes, axis=1).T.astype(BF16)
    spread = jnp.sum(jnp.where(takes, route_weight[:, :, None], 0.0), axis=1)
    coarse = spread.astype(BF16)
    fine = (spread - coarse.astype(F32)).astype(BF16)

    gathered = []
    for chunk, (own_q, other_q) in enumerate(query_chunks):
        sums = attention(
            place,
            own_q,
            other_q,
            (key_cache, key_other),
            (value_cache, value_other),
            new_key,
            new_value,
            lens,
            chips,
            key_cache.shape[1] // HD,
        )
        if chunk + 1 < len(query_chunks):
            own_next, other_next = query_chunks[chunk + 1]
            sums, other_next = lax.optimization_barrier((sums, other_next))
            query_chunks[chunk + 1] = (own_next, other_next)
        gathered.append(
            lax.all_to_all(
                sums, "ctx", split_axis=0, concat_axis=0, axis_index_groups=same_core, tiled=True
            )
        )
    share = project(place, gathered, out_weight, weight_other)
    *held, done = fetch(share, (w_gate, w_up, w_down))
    shares = lax.all_to_all(
        share.reshape(chips, home_rows, width),
        "ctx",
        split_axis=0,
        concat_axis=0,
        axis_index_groups=same_core,
        tiled=True,
    )
    middle, outgoing = norm_and_dispatch(shares, residual, norm_gain.reshape(1, width), chooser, done)
    arrived = lax.all_to_all(
        outgoing.reshape(devices, experts * MOST, width), "ctx", split_axis=0, concat_axis=0, tiled=True
    )
    produced = run_experts(arrived.reshape(slots, width), *held)
    returned = lax.all_to_all(
        produced.reshape(devices, experts * MOST, width), "ctx", split_axis=0, concat_axis=0, tiled=True
    )
    return mix(returned.reshape(slots, width), coarse, fine, middle)


def solution(mesh):
    placed = (
        P(("groups", "ctx"), None),
        P(("groups", "ctx"), None),
        P(("groups", "ctx"), None),
        P(("groups", "ctx"), None),
        P(("groups", "ctx"), None),
        P("groups"),
        P("ctx", None),
        P(("groups", "ctx"), None),
        P(),
        P(("groups", "ctx"), None),
        P(("groups", "ctx"), None),
        P("ctx", None, None),
        P("ctx", None, None),
        P("ctx", None, None),
    )
    return jax.shard_map(
        on_device, mesh=mesh, in_specs=placed, out_specs=P(("groups", "ctx"), None), check_vma=False
    )
```

```python
import functools
import math

import jax
import jax.numpy as jnp
from jax import lax
from jax.experimental import pallas as pl
from jax.experimental.pallas import tpu as pltpu
from jax.sharding import PartitionSpec as P

HD = 128
MOST = 4
CORES = 2
STATS = 16
MASKED = -1e30
FLOOR = -1e20
LOG2E = math.log2(math.e)
MIB = 1024 * 1024
F32 = jnp.float32
BF16 = jnp.bfloat16


def nt_dot(a, b):
    return lax.dot_general(a, b, (((1,), (1,)), ((), ())), preferred_element_type=F32)


def nn_dot(a, b):
    return lax.dot_general(a, b, (((1,), (0,)), ((), ())), preferred_element_type=F32)


def attention_body(shape, place, own_q, other_q, key_own, key_other, value_own, value_other, key_fresh, value_fresh, lens, out, *scratch):
    owners, heads_owner, home_rows, rows, cache_here, step = shape
    q_rows, q_turned, hidden, scores = scratch
    chip, start_own, start_other, pair_place, ring_place = place[0], place[1], place[2], place[4], place[5]
    rings = rows // home_rows // 2

    @pl.when(pl.program_id(0) == 0)
    def _():
        for part, start in enumerate((start_own, start_other)):
            positions = start + lax.broadcasted_iota(jnp.int32, (cache_here, rows), 0)
            hidden[part * cache_here : (part + 1) * cache_here, :] = jnp.where(
                positions < lens[...], 0.0, MASKED
            )
        token = lax.broadcasted_iota(jnp.int32, (home_rows, rows), 0)
        column = lax.broadcasted_iota(jnp.int32, (home_rows, rows), 1)
        hidden[2 * cache_here :, :] = jnp.where(token + chip * home_rows == column, 0.0, MASKED)

    value_new = value_fresh[...].astype(F32).T.astype(BF16)
    for ring in range(rings):
        taken = slice(ring * home_rows, (ring + 1) * home_rows)
        for piece, side in ((own_q, pair_place), (other_q, 1 - pair_place)):
            spot = pl.multiple_of((2 * (ring ^ ring_place) + side) * home_rows, home_rows)
            q_rows[pl.ds(spot, home_rows), :] = piece[taken, :]

    heads = owners * heads_owner
    factor = LOG2E / math.sqrt(HD)
    pieces = [(key_own, value_own, 0, i) for i in range(0, cache_here, step)]
    pieces += [(key_other, value_other, cache_here, i) for i in range(0, cache_here, step)]
    for h in range(heads):
        scaled = q_rows[:, h * HD : (h + 1) * HD].T.astype(F32) * factor
        coarse = scaled.astype(BF16)
        q_turned[:HD, h * rows : (h + 1) * rows] = coarse
        q_turned[HD:, h * rows : (h + 1) * rows] = (scaled - coarse.astype(F32)).astype(BF16)

    def score(keys, mask):
        s = nn_dot(jnp.concatenate([keys, keys], axis=1), q_turned[...])
        return s + jnp.concatenate([mask] * heads, axis=1)

    s_new = score(key_fresh[...], hidden[2 * cache_here :, :])
    run = jnp.max(s_new.reshape(home_rows // 8, 8, heads * rows), axis=0)
    for source, _, base, i in pieces:
        s = score(source[i : i + step, :], hidden[base + i : base + i + step, :])
        scores[base + i : base + i + step, :] = s
        run = jnp.maximum(run, jnp.max(s.reshape(step // 8, 8, heads * rows), axis=0))
    peak = jnp.maximum(jnp.max(run, axis=0, keepdims=True), FLOOR).astype(BF16).astype(F32)
    p_new = jnp.exp2((s_new - peak).astype(BF16))
    sums = None
    ones = jnp.ones((STATS, step), BF16)
    for _, source, base, i in pieces:
        p = jnp.exp2((scores[base + i : base + i + step, :] - peak).astype(BF16))
        term = nn_dot(jnp.concatenate([source[:, i : i + step], ones], axis=0), p)
        sums = term if sums is None else sums + term
    numer = sums[:HD] + nn_dot(value_new, p_new)
    denom = sums[HD : HD + 1] + jnp.sum(p_new.astype(F32), axis=0, keepdims=True)
    high = denom.astype(BF16).astype(F32)
    low = denom - high
    for owner in range(owners):
        across = [slice((owner * heads_owner + h) * rows, (owner * heads_owner + h + 1) * rows) for h in range(heads_owner)]
        for h, cols in enumerate(across):
            out[owner, h * HD : (h + 1) * HD, :] = numer[:, cols].astype(BF16)
        filled = [kind[:, cols] for kind in (peak, high, low) for cols in across]
        filled += [jnp.zeros_like(filled[0])] * (STATS - len(filled))
        out[owner, heads_owner * HD :, :] = jnp.concatenate(filled, axis=0).astype(BF16)


def attention(place, own_q, other_q, keys, values, new_key, new_value, lens, chips, kv_heads):
    rows = lens.shape[1]
    home_rows = new_key.shape[0]
    cache_here = keys[0].shape[0]
    heads_owner = own_q.shape[1] // HD // chips
    owners = chips // kv_heads
    height = heads_owner * HD + STATS
    step = 512
    kv = lambda g, place: (0, g)
    shape = (owners, heads_owner, home_rows, rows, cache_here, step)
    work = rows * heads_owner * chips * 2 * cache_here
    return pl.pallas_call(
        functools.partial(attention_body, shape),
        grid_spec=pltpu.PrefetchScalarGridSpec(
            num_scalar_prefetch=1,
            grid=(kv_heads,),
            in_specs=[pl.BlockSpec((own_q.shape[0], owners * heads_owner * HD), kv)] * 2
            + [pl.BlockSpec((cache_here, HD), kv)] * 2
            + [pl.BlockSpec((HD, cache_here), lambda g, place: (g, 0))] * 2
            + [pl.BlockSpec((home_rows, HD), kv)] * 2
            + [pl.BlockSpec((1, rows), lambda g, place: (0, 0))],
            out_specs=pl.BlockSpec((owners, height, rows), lambda g, place: (g, 0, 0)),
            scratch_shapes=[
                pltpu.VMEM((rows, owners * heads_owner * HD), BF16),
                pltpu.VMEM((2 * HD, owners * heads_owner * rows), BF16),
                pltpu.VMEM((2 * cache_here + home_rows, rows), F32),
                pltpu.VMEM((2 * cache_here, owners * heads_owner * rows), F32),
            ],
        ),
        out_shape=jax.ShapeDtypeStruct((chips, height, rows), BF16),
        compiler_params=pltpu.CompilerParams(vmem_limit_bytes=24 * MIB),
        cost_estimate=pl.CostEstimate(
            flops=6 * work * HD, bytes_accessed=8 * MIB, transcendentals=work
        ),
        name="attention",
    )(place, own_q, other_q, pltpu.with_memory_space_constraint(keys[0], pltpu.HBM), keys[1], *values, new_key, new_value, lens)


def project_body(place, *refs):
    *chunks, weight_own, weight_other, out, turned = refs
    core = place[3]
    for chunk, parts in enumerate(chunks):
        chips, height, _ = parts.shape
        base = height - STATS
        heads = base // HD
        stats = parts[:, base:, :].astype(F32)
        peaks = stats[:, :heads]
        share = jnp.exp2(peaks - jnp.max(peaks, axis=0, keepdims=True))
        totals = stats[:, heads : 2 * heads] + stats[:, 2 * heads : 3 * heads]
        denom = jnp.sum(share * totals, axis=0)
        for h in range(heads):
            numer = None
            for s in range(chips):
                term = parts[s, h * HD : (h + 1) * HD, :].astype(F32) * share[s, h : h + 1, :]
                numer = term if numer is None else numer + term
            turned[chunk, :, h * HD : (h + 1) * HD] = (numer / denom[h : h + 1, :]).T.astype(BF16)
    product = nn_dot(turned[core], weight_own[...]) + nn_dot(turned[1 - core], weight_other[...])
    out[...] = product.astype(BF16)


def project(place, chunks, weight_own, weight_other):
    rows = chunks[0].shape[2]
    depth, width = weight_own.shape
    vmem = pl.BlockSpec(memory_space=pltpu.VMEM)
    return pl.pallas_call(
        project_body,
        in_specs=[pl.BlockSpec(memory_space=pltpu.SMEM)] + [vmem] * (len(chunks) + 2),
        out_specs=vmem,
        out_shape=jax.ShapeDtypeStruct((rows, width), BF16),
        scratch_shapes=[pltpu.VMEM((CORES, rows, depth), BF16)],
        compiler_params=pltpu.CompilerParams(vmem_limit_bytes=32 * MIB),
        cost_estimate=pl.CostEstimate(
            flops=4 * rows * width * depth, bytes_accessed=4 * MIB, transcendentals=0
        ),
        name="project",
    )(place, *chunks, weight_own, weight_other)


def norm_body(parts, residual, gain, chooser, middle_out, sent):
    total = parts[0].astype(F32)
    for s in range(1, parts.shape[0]):
        total = total + parts[s].astype(F32)
    middle = (residual[...].astype(F32) + total).astype(BF16)
    middle_out[...] = middle
    middle = middle.astype(F32)
    inv_rms = lax.rsqrt(jnp.mean(middle * middle, axis=-1, keepdims=True) + 1e-06)
    normed = (middle * inv_rms * gain[...].astype(F32)).astype(BF16)
    sent[...] = nn_dot(chooser[...], normed).astype(BF16)


def norm_and_dispatch(parts, residual, gain, chooser):
    vmem = pl.BlockSpec(memory_space=pltpu.VMEM)
    rows, width = residual.shape
    return pl.pallas_call(
        norm_body,
        in_specs=[vmem] * 4,
        out_specs=[vmem] * 2,
        out_shape=[
            jax.ShapeDtypeStruct((rows, width), BF16),
            jax.ShapeDtypeStruct((chooser.shape[0], width), BF16),
        ],
        compiler_params=pltpu.CompilerParams(vmem_limit_bytes=24 * MIB),
        cost_estimate=pl.CostEstimate(
            flops=2 * chooser.shape[0] * rows * width, bytes_accessed=2 * MIB, transcendentals=0
        ),
        name="norm_and_dispatch",
    )(parts, residual, gain, chooser)


def fetch_body(after, gate, up, down, gate_out, up_out, down_out, sems):
    copies = [
        pltpu.make_async_copy(source, held, sems.at[k])
        for k, (source, held) in enumerate(((gate, gate_out), (up, up_out), (down, down_out)))
    ]
    for copy in copies:
        copy.start()
    for copy in copies:
        copy.wait()


def fetch(after, weights):
    hbm = pl.BlockSpec(memory_space=pltpu.HBM)
    return pl.pallas_call(
        fetch_body,
        in_specs=[pl.BlockSpec(memory_space=pl.ANY)] + [hbm] * len(weights),
        out_specs=[pl.BlockSpec(memory_space=pltpu.VMEM)] * len(weights),
        out_shape=[pltpu.VMEM(w.shape, w.dtype) for w in weights],
        scratch_shapes=[pltpu.SemaphoreType.DMA((len(weights),))],
        compiler_params=pltpu.CompilerParams(vmem_limit_bytes=2 * MIB),
        cost_estimate=pl.CostEstimate(
            flops=0, bytes_accessed=2 * sum(w.size * 2 for w in weights), transcendentals=0
        ),
        name="fetch",
    )(after, *[pltpu.with_memory_space_constraint(w, pltpu.HBM) for w in weights])


def experts_body(arrived, w_gate, w_up, w_down, out):
    experts, _, depth = w_gate.shape
    rows, width = arrived.shape
    slot = lax.broadcasted_iota(jnp.int32, (rows, 1), 0)
    values = arrived[...]
    step = 256
    hidden = []
    for e in range(experts):
        mine = lax.rem(slot, experts * MOST) // MOST == e
        parts = []
        for f in range(0, depth, step):
            gate = nn_dot(values, w_gate[e, :, f : f + step])
            upward = nn_dot(values, w_up[e, :, f : f + step])
            part = gate / (1.0 + jnp.exp(-gate)) * upward
            parts.append(jnp.where(mine, part, 0.0).astype(BF16))
        hidden.append(jnp.concatenate(parts, axis=1))
    step = 512
    for c in range(0, width, step):
        total = nn_dot(hidden[0], w_down[0, :, c : c + step])
        for e in range(1, experts):
            total = total + nn_dot(hidden[e], w_down[e, :, c : c + step])
        out[:, c : c + step] = total.astype(BF16)


def run_experts(arrived, w_gate, w_up, w_down):
    rows, width = arrived.shape
    experts, _, hidden = w_gate.shape
    vmem = pl.BlockSpec(memory_space=pltpu.VMEM)
    return pl.pallas_call(
        experts_body,
        in_specs=[vmem] * 4,
        out_specs=vmem,
        out_shape=jax.ShapeDtypeStruct((rows, width), BF16),
        compiler_params=pltpu.CompilerParams(vmem_limit_bytes=16 * MIB),
        cost_estimate=pl.CostEstimate(
            flops=6 * rows * width * experts * hidden,
            bytes_accessed=2 * MIB,
            transcendentals=rows * experts * hidden,
        ),
        name="experts",
    )(arrived, w_gate, w_up, w_down)


def mix_body(returned, coarse, fine, middle, out):
    values = returned[...]
    mixed = nn_dot(coarse[...], values) + nn_dot(fine[...], values)
    out[...] = (middle[...].astype(F32) + mixed).astype(BF16)


def mix(returned, coarse, fine, middle):
    vmem = pl.BlockSpec(memory_space=pltpu.VMEM)
    return pl.pallas_call(
        mix_body,
        in_specs=[vmem] * 4,
        out_specs=vmem,
        out_shape=jax.ShapeDtypeStruct(middle.shape, BF16),
        compiler_params=pltpu.CompilerParams(vmem_limit_bytes=16 * MIB),
        name="mix",
    )(returned, coarse, fine, middle)


def on_device(
    queries,
    new_key,
    new_value,
    key_cache,
    value_cache,
    cache_len,
    out_weight,
    residual,
    norm_gain,
    expert_ids,
    route_weight,
    w_gate,
    w_up,
    w_down,
):
    devices = lax.axis_size("ctx")
    chips = devices // CORES
    index = lax.axis_index("ctx")
    chip, core = index // CORES, index % CORES
    home_rows, width = residual.shape
    top = expert_ids.shape[1]
    heads_here = out_weight.shape[0] // HD
    cache_here = key_cache.shape[0]
    same_core = [[CORES * j + c for j in range(chips)] for c in range(CORES)]
    swap = [(i, i ^ 1) for i in range(devices)]

    across = [(i, i ^ CORES) for i in range(devices)]

    by_owner = queries.reshape(home_rows, chips, CORES, heads_here * HD)
    value_turned = value_cache.T
    key_other = lax.ppermute(key_cache, "ctx", swap)
    value_other = lax.ppermute(value_turned, "ctx", swap)
    query_chunks = []
    for chunk in range(CORES):
        mine = by_owner[:, :, chunk].reshape(home_rows, chips * heads_here * HD)
        stride = 2 * CORES
        while stride < devices:
            if chunk and 2 * stride >= devices:
                mine, _ = lax.optimization_barrier((mine, query_chunks[0][0]))
            step = [(i, i ^ stride) for i in range(devices)]
            mine = jnp.concatenate([mine, lax.ppermute(mine, "ctx", step)], axis=0)
            stride *= 2
        query_chunks.append((mine, lax.ppermute(mine, "ctx", across)))
    weight_other = lax.ppermute(out_weight, "ctx", swap)

    place = jnp.stack([chip, index * cache_here, (index ^ 1) * cache_here, core, chip % 2, chip // 2]).astype(jnp.int32)
    lens = lax.dynamic_index_in_dim(
        cache_len.reshape(chips, CORES, home_rows), core, axis=1, keepdims=False
    ).reshape(1, chips * home_rows)

    flat_ids = expert_ids.reshape(-1)
    picks = jnp.arange(flat_ids.shape[0])
    earlier = (flat_ids[:, None] == flat_ids[None, :]) & (picks[None, :] < picks[:, None])
    target = (flat_ids * MOST + jnp.sum(earlier, axis=1, dtype=jnp.int32)).reshape(home_rows, top)
    experts = w_gate.shape[0]
    slots = experts * devices * MOST
    takes = target[:, :, None] == jnp.arange(slots, dtype=jnp.int32)
    chooser = jnp.any(takes, axis=1).T.astype(BF16)
    spread = jnp.sum(jnp.where(takes, route_weight[:, :, None], 0.0), axis=1)
    coarse = spread.astype(BF16)
    fine = (spread - coarse.astype(F32)).astype(BF16)

    gathered = []
    for chunk, (own_q, other_q) in enumerate(query_chunks):
        sums = attention(
            place,
            own_q,
            other_q,
            (key_cache, key_other),
            (value_turned, value_other),
            new_key,
            new_value,
            lens,
            chips,
            key_cache.shape[1] // HD,
        )
        if chunk + 1 < len(query_chunks):
            own_next, other_next = query_chunks[chunk + 1]
            sums, other_next = lax.optimization_barrier((sums, other_next))
            query_chunks[chunk + 1] = (own_next, other_next)
        gathered.append(
            lax.all_to_all(
                sums, "ctx", split_axis=0, concat_axis=0, axis_index_groups=same_core, tiled=True
            )
        )
    share = project(place, gathered, out_weight, weight_other)
    shares = lax.all_to_all(
        share.reshape(chips, home_rows, width),
        "ctx",
        split_axis=0,
        concat_axis=0,
        axis_index_groups=same_core,
        tiled=True,
    )
    middle, outgoing = norm_and_dispatch(shares, residual, norm_gain.reshape(1, width), chooser)
    held = fetch(middle, (w_gate, w_up, w_down))
    arrived = lax.all_to_all(
        outgoing.reshape(devices, experts * MOST, width), "ctx", split_axis=0, concat_axis=0, tiled=True
    )
    produced = run_experts(arrived.reshape(slots, width), *held)
    returned = lax.all_to_all(
        produced.reshape(devices, experts * MOST, width), "ctx", split_axis=0, concat_axis=0, tiled=True
    )
    return mix(returned.reshape(slots, width), coarse, fine, middle)


def solution(mesh):
    placed = (
        P(("groups", "ctx"), None),
        P(("groups", "ctx"), None),
        P(("groups", "ctx"), None),
        P(("groups", "ctx"), None),
        P(("groups", "ctx"), None),
        P("groups"),
        P("ctx", None),
        P(("groups", "ctx"), None),
        P(),
        P(("groups", "ctx"), None),
        P(("groups", "ctx"), None),
        P("ctx", None, None),
        P("ctx", None, None),
        P("ctx", None, None),
    )
    return jax.shard_map(
        on_device, mesh=mesh, in_specs=placed, out_specs=P(("groups", "ctx"), None), check_vma=False
    )
```

```python
import functools
import math

import jax
import jax.numpy as jnp
from jax import lax
from jax.experimental import pallas as pl
from jax.experimental.pallas import tpu as pltpu
from jax.sharding import PartitionSpec as P

HD = 128
MOST = 4
CORES = 2
STATS = 16
MASKED = -1e30
FLOOR = -1e20
LOG2E = math.log2(math.e)
MIB = 1024 * 1024
F32 = jnp.float32
BF16 = jnp.bfloat16


def nt_dot(a, b):
    return lax.dot_general(a, b, (((1,), (1,)), ((), ())), preferred_element_type=F32)


def nn_dot(a, b):
    return lax.dot_general(a, b, (((1,), (0,)), ((), ())), preferred_element_type=F32)


def attention_body(shape, place, own_q, other_q, key_own, key_other, value_own, value_other, key_fresh, value_fresh, lens, out, *scratch):
    owners, heads_owner, home_rows, rows, cache_here, step = shape
    q_rows, q_turned, hidden, scores, peaks = scratch
    chip, start_own, start_other, pair_place, ring_place = place[0], place[1], place[2], place[4], place[5]
    rings = rows // home_rows // 2
    heads = owners * heads_owner
    wide = heads * rows
    now = lax.rem(pl.program_id(0), 2)
    before = 1 - now

    @pl.when(pl.program_id(0) == 0)
    def _():
        for part, start in enumerate((start_own, start_other)):
            positions = start + lax.broadcasted_iota(jnp.int32, (cache_here, rows), 0)
            hidden[part * cache_here : (part + 1) * cache_here, :] = jnp.where(
                positions < lens[...], 0.0, MASKED
            )
        token = lax.broadcasted_iota(jnp.int32, (home_rows, rows), 0)
        column = lax.broadcasted_iota(jnp.int32, (home_rows, rows), 1)
        hidden[2 * cache_here :, :] = jnp.where(token + chip * home_rows == column, 0.0, MASKED)
        scores[1] = jnp.zeros_like(scores[1])
        peaks[1] = jnp.zeros_like(peaks[1])

    for ring in range(rings):
        taken = slice(ring * home_rows, (ring + 1) * home_rows)
        for piece, side in ((own_q, pair_place), (other_q, 1 - pair_place)):
            spot = pl.multiple_of((2 * (ring ^ ring_place) + side) * home_rows, home_rows)
            q_rows[pl.ds(spot, home_rows), :] = piece[taken, :]

    factor = LOG2E / math.sqrt(HD)
    for h in range(heads):
        scaled = q_rows[:, h * HD : (h + 1) * HD].T.astype(F32) * factor
        coarse = scaled.astype(BF16)
        q_turned[:HD, h * rows : (h + 1) * rows] = coarse
        q_turned[HD:, h * rows : (h + 1) * rows] = (scaled - coarse.astype(F32)).astype(BF16)

    run = [None]
    sums = [None]
    old_peak = peaks[before, :1, :]

    def score(keys, at):
        s = nn_dot(jnp.concatenate([keys, keys], axis=1), q_turned[...])
        s = s + jnp.concatenate([hidden[at, :]] * heads, axis=1)
        scores[now, at, :] = s
        most = jnp.max(s.reshape(s.shape[0] // 8, 8, wide), axis=0)
        run[0] = most if run[0] is None else jnp.maximum(run[0], most)

    def weigh(values, at):
        p = jnp.exp2((scores[before, at, :] - old_peak).astype(BF16))
        ones = jnp.ones((STATS, values.shape[1]), BF16)
        term = nn_dot(jnp.concatenate([values, ones], axis=0), p)
        sums[0] = term if sums[0] is None else sums[0] + term

    fresh_at = slice(2 * cache_here, 2 * cache_here + home_rows)
    weigh(value_fresh[...].astype(F32).T.astype(BF16), fresh_at)
    score(key_fresh[...], fresh_at)
    for base, keys, values in ((0, key_own, value_own), (cache_here, key_other, value_other)):
        for i in range(0, cache_here, step):
            at = slice(base + i, base + i + step)
            weigh(values[:, i : i + step], at)
            score(keys[i : i + step, :], at)
    peak = jnp.maximum(jnp.max(run[0], axis=0, keepdims=True), FLOOR).astype(BF16).astype(F32)
    peaks[now] = jnp.broadcast_to(peak, peaks.shape[1:])

    numer = sums[0][:HD]
    denom = sums[0][HD : HD + 1]
    high = denom.astype(BF16).astype(F32)
    low = denom - high
    for owner in range(owners):
        first = owner * heads_owner
        across = [slice((first + h) * rows, (first + h + 1) * rows) for h in range(heads_owner)]
        for h, cols in enumerate(across):
            out[owner, h * HD : (h + 1) * HD, :] = numer[:, cols].astype(BF16)
        filled = [kind[:, cols] for kind in (old_peak, high, low) for cols in across]
        filled += [jnp.zeros_like(filled[0])] * (STATS - len(filled))
        out[owner, heads_owner * HD :, :] = jnp.concatenate(filled, axis=0).astype(BF16)


def attention(place, own_q, other_q, keys, values, new_key, new_value, lens, chips, kv_heads):
    rows = lens.shape[1]
    home_rows = new_key.shape[0]
    cache_here = keys[0].shape[0]
    heads_owner = own_q.shape[1] // HD // chips
    owners = chips // kv_heads
    wide = owners * heads_owner * rows
    height = heads_owner * HD + STATS
    step = 256
    positions = 2 * cache_here + home_rows
    this = lambda g, place: (0, jnp.minimum(g, kv_heads - 1))
    last = lambda g, place: (0, jnp.maximum(g - 1, 0))
    shape = (owners, heads_owner, home_rows, rows, cache_here, step)
    work = rows * heads_owner * chips * 2 * cache_here
    return pl.pallas_call(
        functools.partial(attention_body, shape),
        grid_spec=pltpu.PrefetchScalarGridSpec(
            num_scalar_prefetch=1,
            grid=(kv_heads + 1,),
            in_specs=[pl.BlockSpec((own_q.shape[0], owners * heads_owner * HD), this)] * 2
            + [pl.BlockSpec((cache_here, HD), this)] * 2
            + [pl.BlockSpec((HD, cache_here), lambda g, place: (jnp.maximum(g - 1, 0), 0))] * 2
            + [pl.BlockSpec((home_rows, HD), this), pl.BlockSpec((home_rows, HD), last)]
            + [pl.BlockSpec((1, rows), lambda g, place: (0, 0))],
            out_specs=pl.BlockSpec(
                (owners, height, rows), lambda g, place: (jnp.maximum(g - 1, 0), 0, 0)
            ),
            scratch_shapes=[
                pltpu.VMEM((rows, owners * heads_owner * HD), BF16),
                pltpu.VMEM((2 * HD, wide), BF16),
                pltpu.VMEM((positions, rows), F32),
                pltpu.VMEM((2, positions, wide), F32),
                pltpu.VMEM((2, 8, wide), F32),
            ],
        ),
        out_shape=jax.ShapeDtypeStruct((chips, height, rows), BF16),
        compiler_params=pltpu.CompilerParams(vmem_limit_bytes=32 * MIB),
        cost_estimate=pl.CostEstimate(
            flops=6 * work * HD, bytes_accessed=8 * MIB, transcendentals=work
        ),
        name="attention",
    )(place, own_q, other_q, pltpu.with_memory_space_constraint(keys[0], pltpu.HBM), keys[1], *values, new_key, new_value, lens)


def project_body(place, *refs):
    *chunks, weight_own, weight_other, out, turned = refs
    core = place[3]
    for chunk, parts in enumerate(chunks):
        chips, height, _ = parts.shape
        base = height - STATS
        heads = base // HD
        stats = parts[:, base:, :].astype(F32)
        peaks = stats[:, :heads]
        share = jnp.exp2(peaks - jnp.max(peaks, axis=0, keepdims=True))
        totals = stats[:, heads : 2 * heads] + stats[:, 2 * heads : 3 * heads]
        denom = jnp.sum(share * totals, axis=0)
        for h in range(heads):
            numer = None
            for s in range(chips):
                term = parts[s, h * HD : (h + 1) * HD, :].astype(F32) * share[s, h : h + 1, :]
                numer = term if numer is None else numer + term
            turned[chunk, :, h * HD : (h + 1) * HD] = (numer / denom[h : h + 1, :]).T.astype(BF16)
    product = nn_dot(turned[core], weight_own[...]) + nn_dot(turned[1 - core], weight_other[...])
    out[...] = product.astype(BF16)


def project(place, chunks, weight_own, weight_other):
    rows = chunks[0].shape[2]
    depth, width = weight_own.shape
    vmem = pl.BlockSpec(memory_space=pltpu.VMEM)
    return pl.pallas_call(
        project_body,
        in_specs=[pl.BlockSpec(memory_space=pltpu.SMEM)] + [vmem] * (len(chunks) + 2),
        out_specs=vmem,
        out_shape=jax.ShapeDtypeStruct((rows, width), BF16),
        scratch_shapes=[pltpu.VMEM((CORES, rows, depth), BF16)],
        compiler_params=pltpu.CompilerParams(vmem_limit_bytes=32 * MIB),
        cost_estimate=pl.CostEstimate(
            flops=4 * rows * width * depth, bytes_accessed=4 * MIB, transcendentals=0
        ),
        name="project",
    )(place, *chunks, weight_own, weight_other)


def norm_body(parts, residual, gain, chooser, middle_out, sent):
    total = parts[0].astype(F32)
    for s in range(1, parts.shape[0]):
        total = total + parts[s].astype(F32)
    middle = (residual[...].astype(F32) + total).astype(BF16)
    middle_out[...] = middle
    middle = middle.astype(F32)
    inv_rms = lax.rsqrt(jnp.mean(middle * middle, axis=-1, keepdims=True) + 1e-06)
    normed = (middle * inv_rms * gain[...].astype(F32)).astype(BF16)
    sent[...] = nn_dot(chooser[...], normed).astype(BF16)


def norm_and_dispatch(parts, residual, gain, chooser):
    vmem = pl.BlockSpec(memory_space=pltpu.VMEM)
    rows, width = residual.shape
    return pl.pallas_call(
        norm_body,
        in_specs=[vmem] * 4,
        out_specs=[vmem] * 2,
        out_shape=[
            jax.ShapeDtypeStruct((rows, width), BF16),
            jax.ShapeDtypeStruct((chooser.shape[0], width), BF16),
        ],
        compiler_params=pltpu.CompilerParams(vmem_limit_bytes=24 * MIB),
        cost_estimate=pl.CostEstimate(
            flops=2 * chooser.shape[0] * rows * width, bytes_accessed=2 * MIB, transcendentals=0
        ),
        name="norm_and_dispatch",
    )(parts, residual, gain, chooser)


def experts_body(step, arrived, w_gate, w_up, w_down, out, gate_held, up_held, down_held, sems):
    experts, _, depth = w_gate.shape
    rows, width = arrived.shape
    pieces = [(e, f) for e in range(experts) for f in range(0, depth, step)]
    copies = []
    for n, (e, f) in enumerate(pieces):
        down = pl.ds(f, step)
        copies.append(
            [
                pltpu.make_async_copy(w_gate.at[e, :, down], gate_held.at[n], sems.at[n, 0]),
                pltpu.make_async_copy(w_up.at[e, :, down], up_held.at[n], sems.at[n, 1]),
                pltpu.make_async_copy(w_down.at[e, down, :], down_held.at[n], sems.at[n, 2]),
            ]
        )
    for piece in copies:
        for copy in piece[:2]:
            copy.start()
    for piece in copies:
        piece[2].start()
    slot = lax.broadcasted_iota(jnp.int32, (rows, 1), 0)
    values = arrived[...]
    hidden = []
    for n, (e, f) in enumerate(pieces):
        copies[n][0].wait()
        copies[n][1].wait()
        gate = nn_dot(values, gate_held[n])
        upward = nn_dot(values, up_held[n])
        part = gate / (1.0 + jnp.exp(-gate)) * upward
        mine = lax.rem(slot, experts * MOST) // MOST == e
        hidden.append(jnp.where(mine, part, 0.0).astype(BF16))
    total = None
    for n in range(len(pieces)):
        copies[n][2].wait()
        term = nn_dot(hidden[n], down_held[n])
        total = term if total is None else total + term
    out[...] = total.astype(BF16)


def run_experts(arrived, w_gate, w_up, w_down):
    rows, width = arrived.shape
    experts, _, depth = w_gate.shape
    step = 256
    pieces = experts * depth // step
    vmem = pl.BlockSpec(memory_space=pltpu.VMEM)
    hbm = pl.BlockSpec(memory_space=pltpu.HBM)
    weights = [pltpu.with_memory_space_constraint(w, pltpu.HBM) for w in (w_gate, w_up, w_down)]
    return pl.pallas_call(
        functools.partial(experts_body, step),
        in_specs=[vmem] + [hbm] * 3,
        out_specs=vmem,
        out_shape=jax.ShapeDtypeStruct((rows, width), BF16),
        scratch_shapes=[
            pltpu.VMEM((pieces, width, step), BF16),
            pltpu.VMEM((pieces, width, step), BF16),
            pltpu.VMEM((pieces, step, width), BF16),
            pltpu.SemaphoreType.DMA((pieces, 3)),
        ],
        compiler_params=pltpu.CompilerParams(vmem_limit_bytes=44 * MIB),
        cost_estimate=pl.CostEstimate(
            flops=6 * rows * width * experts * depth,
            bytes_accessed=6 * width * experts * depth,
            transcendentals=rows * experts * depth,
        ),
        name="experts",
    )(arrived, *weights)


def mix_body(returned, coarse, fine, middle, out):
    values = returned[...]
    mixed = nn_dot(coarse[...], values) + nn_dot(fine[...], values)
    out[...] = (middle[...].astype(F32) + mixed).astype(BF16)


def mix(returned, coarse, fine, middle):
    vmem = pl.BlockSpec(memory_space=pltpu.VMEM)
    return pl.pallas_call(
        mix_body,
        in_specs=[vmem] * 4,
        out_specs=vmem,
        out_shape=jax.ShapeDtypeStruct(middle.shape, BF16),
        compiler_params=pltpu.CompilerParams(vmem_limit_bytes=16 * MIB),
        name="mix",
    )(returned, coarse, fine, middle)


def on_device(
    queries,
    new_key,
    new_value,
    key_cache,
    value_cache,
    cache_len,
    out_weight,
    residual,
    norm_gain,
    expert_ids,
    route_weight,
    w_gate,
    w_up,
    w_down,
):
    devices = lax.axis_size("ctx")
    chips = devices // CORES
    index = lax.axis_index("ctx")
    chip, core = index // CORES, index % CORES
    home_rows, width = residual.shape
    top = expert_ids.shape[1]
    heads_here = out_weight.shape[0] // HD
    cache_here = key_cache.shape[0]
    same_core = [[CORES * j + c for j in range(chips)] for c in range(CORES)]
    swap = [(i, i ^ 1) for i in range(devices)]

    across = [(i, i ^ CORES) for i in range(devices)]

    def chunk_of(part, chunk):
        by_owner = part.reshape(part.shape[0], chips, CORES, heads_here * HD)
        return by_owner[:, :, chunk].reshape(part.shape[0], chips * heads_here * HD)

    strides = [CORES << k for k in range(1, (chips // 2).bit_length())]
    hops = [[(i, i ^ stride) for i in range(devices)] for stride in strides]
    arrived_first = lax.ppermute(queries, "ctx", hops[0])
    key_other = lax.ppermute(key_cache, "ctx", swap)
    both = jnp.concatenate([queries, arrived_first], axis=0)
    both, value_late = lax.optimization_barrier((both, value_cache))
    value_turned = value_late.T
    value_other = lax.ppermute(value_turned, "ctx", swap)
    query_chunks = []
    for chunk in range(CORES):
        mine = chunk_of(both, chunk)
        for hop in hops[1:]:
            if chunk and hop is hops[-1]:
                mine, _ = lax.optimization_barrier((mine, query_chunks[0][0]))
            mine = jnp.concatenate([mine, lax.ppermute(mine, "ctx", hop)], axis=0)
        query_chunks.append((mine, lax.ppermute(mine, "ctx", across)))
    weight_other = lax.ppermute(out_weight, "ctx", swap)

    place = jnp.stack([chip, index * cache_here, (index ^ 1) * cache_here, core, chip % 2, chip // 2]).astype(jnp.int32)
    lens = lax.dynamic_index_in_dim(
        cache_len.reshape(chips, CORES, home_rows), core, axis=1, keepdims=False
    ).reshape(1, chips * home_rows)

    flat_ids = expert_ids.reshape(-1)
    picks = jnp.arange(flat_ids.shape[0])
    earlier = (flat_ids[:, None] == flat_ids[None, :]) & (picks[None, :] < picks[:, None])
    target = (flat_ids * MOST + jnp.sum(earlier, axis=1, dtype=jnp.int32)).reshape(home_rows, top)
    experts = w_gate.shape[0]
    slots = experts * devices * MOST
    takes = target[:, :, None] == jnp.arange(slots, dtype=jnp.int32)
    chooser = jnp.any(takes, axis=1).T.astype(BF16)
    spread = jnp.sum(jnp.where(takes, route_weight[:, :, None], 0.0), axis=1)
    coarse = spread.astype(BF16)
    fine = (spread - coarse.astype(F32)).astype(BF16)

    gathered = []
    for chunk, (own_q, other_q) in enumerate(query_chunks):
        sums = attention(
            place,
            own_q,
            other_q,
            (key_cache, key_other),
            (value_turned, value_other),
            new_key,
            new_value,
            lens,
            chips,
            key_cache.shape[1] // HD,
        )
        if chunk + 1 < len(query_chunks):
            own_next, other_next = query_chunks[chunk + 1]
            sums, other_next = lax.optimization_barrier((sums, other_next))
            query_chunks[chunk + 1] = (own_next, other_next)
        gathered.append(
            lax.all_to_all(
                sums, "ctx", split_axis=0, concat_axis=0, axis_index_groups=same_core, tiled=True
            )
        )
    share = project(place, gathered, out_weight, weight_other)
    shares = lax.all_to_all(
        share.reshape(chips, home_rows, width),
        "ctx",
        split_axis=0,
        concat_axis=0,
        axis_index_groups=same_core,
        tiled=True,
    )
    middle, outgoing = norm_and_dispatch(shares, residual, norm_gain.reshape(1, width), chooser)
    arrived = lax.all_to_all(
        outgoing.reshape(devices, experts * MOST, width), "ctx", split_axis=0, concat_axis=0, tiled=True
    )
    produced = run_experts(arrived.reshape(slots, width), w_gate, w_up, w_down)
    returned = lax.all_to_all(
        produced.reshape(devices, experts * MOST, width), "ctx", split_axis=0, concat_axis=0, tiled=True
    )
    return mix(returned.reshape(slots, width), coarse, fine, middle)


def solution(mesh):
    placed = (
        P(("groups", "ctx"), None),
        P(("groups", "ctx"), None),
        P(("groups", "ctx"), None),
        P(("groups", "ctx"), None),
        P(("groups", "ctx"), None),
        P("groups"),
        P("ctx", None),
        P(("groups", "ctx"), None),
        P(),
        P(("groups", "ctx"), None),
        P(("groups", "ctx"), None),
        P("ctx", None, None),
        P("ctx", None, None),
        P("ctx", None, None),
    )
    return jax.shard_map(
        on_device, mesh=mesh, in_specs=placed, out_specs=P(("groups", "ctx"), None), check_vma=False
    )
```

```python
import functools
import math

import jax
import jax.numpy as jnp
from jax import lax
from jax.experimental import pallas as pl
from jax.experimental.pallas import tpu as pltpu
from jax.sharding import PartitionSpec as P

HD = 128
MOST = 4
CORES = 2
STATS = 16
MASKED = -1e30
FLOOR = -1e20
LOG2E = math.log2(math.e)
MIB = 1024 * 1024
F32 = jnp.float32
BF16 = jnp.bfloat16


def nt_dot(a, b):
    return lax.dot_general(a, b, (((1,), (1,)), ((), ())), preferred_element_type=F32)


def nn_dot(a, b):
    return lax.dot_general(a, b, (((1,), (0,)), ((), ())), preferred_element_type=F32)


def attention_body(shape, place, own_q, other_q, key_own, key_other, value_own, value_other, key_fresh, value_fresh, lens, row_ids, out, *scratch):
    rings, ring_heads, home_rows, side_rows, cache_here, step = shape
    q_rows, q_turned, hidden, scores, probs = scratch
    chip, start_own, start_other, side_here = place[0], place[1], place[2], place[4]
    pack = HD // side_rows
    groups = ring_heads // pack

    @pl.when(pl.program_id(0) == 0)
    def _():
        lanes = lens.shape[1]
        for part, start in enumerate((start_own, start_other)):
            positions = start + lax.broadcasted_iota(jnp.int32, (cache_here, lanes), 0)
            hidden[part * cache_here : (part + 1) * cache_here, :] = jnp.where(
                positions < lens[...], 0.0, MASKED
            )
        token = chip * home_rows + lax.broadcasted_iota(jnp.int32, (home_rows, lanes), 0)
        hidden[2 * cache_here :, :] = jnp.where(token == row_ids[...], 0.0, MASKED)

    for piece, side in ((own_q, side_here), (other_q, 1 - side_here)):
        q_rows[side] = piece[...]

    factor = LOG2E / math.sqrt(HD)
    spots = [(r, s, k) for r in range(rings) for s in range(2) for k in range(groups)]
    for n, (r, s, k) in enumerate(spots):
        first = r * ring_heads + k * pack
        block = jnp.concatenate(
            [q_rows[s, :, h * HD : (h + 1) * HD] for h in range(first, first + pack)], axis=0
        )
        scaled = block.T.astype(F32) * factor
        coarse = scaled.astype(BF16)
        q_turned[:HD, n * HD : (n + 1) * HD] = coarse
        q_turned[HD:, n * HD : (n + 1) * HD] = (scaled - coarse.astype(F32)).astype(BF16)
    wide = len(spots) * HD

    def score(keys, at):
        s = nn_dot(jnp.concatenate([keys, keys], axis=1), q_turned[...])
        return s + jnp.concatenate([hidden[at, s * HD : (s + 1) * HD] for _, s, _ in spots], axis=1)

    s_new = score(key_fresh[...], slice(2 * cache_here, 2 * cache_here + home_rows))
    run = jnp.max(s_new.reshape(home_rows // 8, 8, wide), axis=0)
    pieces = [(part, i) for part in range(2) for i in range(0, cache_here, step)]
    for part, i in pieces:
        at = slice(part * cache_here + i, part * cache_here + i + step)
        s = score((key_own, key_other)[part][i : i + step, :], at)
        scores[at, :] = s
        run = jnp.maximum(run, jnp.max(s.reshape(step // 8, 8, wide), axis=0))
    peak = jnp.maximum(jnp.max(run, axis=0, keepdims=True), FLOOR).astype(BF16).astype(F32)
    p_new = jnp.exp2((s_new - peak).astype(BF16))
    for part, i in pieces:
        at = slice(part * cache_here + i, part * cache_here + i + step)
        probs[at, :] = jnp.exp2((scores[at, :] - peak).astype(BF16))
    ones = jnp.ones((STATS, cache_here), BF16)
    sums = nn_dot(jnp.concatenate([value_own[...], ones], axis=0), probs[:cache_here, :])
    sums = sums + nn_dot(jnp.concatenate([value_other[...], ones], axis=0), probs[cache_here:, :])
    numer = sums[:HD] + nn_dot(value_fresh[...].astype(F32).T.astype(BF16), p_new)
    denom = sums[HD : HD + 1] + jnp.sum(p_new.astype(F32), axis=0, keepdims=True)
    high = denom.astype(BF16).astype(F32)
    low = denom - high
    for owner in range(2 * rings):
        lanes = [slice((owner * groups + k) * HD, (owner * groups + k + 1) * HD) for k in range(groups)]
        for k, cols in enumerate(lanes):
            out[owner, k * HD : (k + 1) * HD, :] = numer[:, cols].astype(BF16)
        filled = [kind[:, cols] for kind in (peak, high, low) for cols in lanes]
        filled += [jnp.zeros_like(filled[0])] * (STATS - len(filled))
        out[owner, groups * HD :, :] = jnp.concatenate(filled, axis=0).astype(BF16)


def attention(place, own_q, other_q, keys, values, new_key, new_value, lens, row_ids, chips, kv_heads):
    side_rows = own_q.shape[0]
    home_rows = new_key.shape[0]
    cache_here = keys[0].shape[0]
    rings = chips // 2 // kv_heads
    columns = own_q.shape[1] // kv_heads
    ring_heads = columns // HD // rings
    wide = 2 * side_rows * columns // HD
    height = ring_heads * side_rows + STATS
    step = 512
    positions = 2 * cache_here + home_rows
    kv = lambda g, place: (0, g)
    whole = lambda g, place: (0, 0)
    shape = (rings, ring_heads, home_rows, side_rows, cache_here, step)
    work = wide * kv_heads * 2 * cache_here
    return pl.pallas_call(
        functools.partial(attention_body, shape),
        grid_spec=pltpu.PrefetchScalarGridSpec(
            num_scalar_prefetch=1,
            grid=(kv_heads,),
            in_specs=[pl.BlockSpec((side_rows, columns), kv)] * 2
            + [pl.BlockSpec((cache_here, HD), kv)] * 2
            + [pl.BlockSpec((HD, cache_here), lambda g, place: (g, 0))] * 2
            + [pl.BlockSpec((home_rows, HD), kv)] * 2
            + [pl.BlockSpec(lens.shape, whole)] * 2,
            out_specs=pl.BlockSpec((2 * rings, height, HD), lambda g, place: (g, 0, 0)),
            scratch_shapes=[
                pltpu.VMEM((2, side_rows, columns), BF16),
                pltpu.VMEM((2 * HD, wide), BF16),
                pltpu.VMEM((positions, 2 * HD), F32),
                pltpu.VMEM((2 * cache_here, wide), F32),
                pltpu.VMEM((2 * cache_here, wide), BF16),
            ],
        ),
        out_shape=jax.ShapeDtypeStruct((chips, height, HD), BF16),
        compiler_params=pltpu.CompilerParams(vmem_limit_bytes=32 * MIB),
        cost_estimate=pl.CostEstimate(
            flops=6 * work * HD, bytes_accessed=8 * MIB, transcendentals=work
        ),
        name="attention",
    )(
        place,
        own_q,
        other_q,
        pltpu.with_memory_space_constraint(keys[0], pltpu.HBM),
        keys[1],
        *values,
        new_key,
        new_value,
        lens,
        row_ids,
    )


def project_body(side_rows, place, *refs):
    *chunks, same_own, same_other, across_own, across_other, out, turned = refs
    core, side = place[3], place[4]
    pack = HD // side_rows
    for chunk, parts in enumerate(chunks):
        chips, height, _ = parts.shape
        base = height - STATS
        groups = base // HD
        owner_heads = groups * pack // 2
        stats = parts[:, base:, :].astype(F32)
        peaks = stats[:, :groups]
        share = jnp.exp2(peaks - jnp.max(peaks, axis=0, keepdims=True))
        totals = stats[:, groups : 2 * groups] + stats[:, 2 * groups : 3 * groups]
        denom = jnp.sum(share * totals, axis=0)
        for k in range(groups):
            numer = None
            for s in range(chips):
                term = parts[s, k * HD : (k + 1) * HD, :].astype(F32) * share[s, k : k + 1, :]
                numer = term if numer is None else numer + term
            attended = (numer / denom[k : k + 1, :]).T.astype(BF16)
            for j in range(pack):
                owner, h = divmod(k * pack + j, owner_heads)
                turned[owner, chunk, :, h * HD : (h + 1) * HD] = attended[
                    j * side_rows : (j + 1) * side_rows
                ]
    product = nn_dot(turned[side, core], same_own[...]) + nn_dot(turned[side, 1 - core], same_other[...])
    product = product + nn_dot(turned[1 - side, core], across_own[...])
    product = product + nn_dot(turned[1 - side, 1 - core], across_other[...])
    out[...] = product.astype(BF16)


def project(place, chunks, weights, side_rows):
    depth, width = weights[0].shape
    vmem = pl.BlockSpec(memory_space=pltpu.VMEM)
    return pl.pallas_call(
        functools.partial(project_body, side_rows),
        in_specs=[pl.BlockSpec(memory_space=pltpu.SMEM)] + [vmem] * (len(chunks) + len(weights)),
        out_specs=vmem,
        out_shape=jax.ShapeDtypeStruct((side_rows, width), BF16),
        scratch_shapes=[pltpu.VMEM((2, CORES, side_rows, depth), BF16)],
        compiler_params=pltpu.CompilerParams(vmem_limit_bytes=32 * MIB),
        cost_estimate=pl.CostEstimate(
            flops=8 * side_rows * width * depth, bytes_accessed=6 * MIB, transcendentals=0
        ),
        name="project",
    )(place, *chunks, *weights)


def norm_body(parts, residual, gain, chooser, middle_out, sent):
    total = parts[0].astype(F32)
    for s in range(1, parts.shape[0]):
        total = total + parts[s].astype(F32)
    middle = (residual[...].astype(F32) + total).astype(BF16)
    middle_out[...] = middle
    middle = middle.astype(F32)
    inv_rms = lax.rsqrt(jnp.mean(middle * middle, axis=-1, keepdims=True) + 1e-06)
    normed = (middle * inv_rms * gain[...].astype(F32)).astype(BF16)
    sent[...] = nn_dot(chooser[...], normed).astype(BF16)


def norm_and_dispatch(parts, residual, gain, chooser):
    vmem = pl.BlockSpec(memory_space=pltpu.VMEM)
    rows, width = residual.shape
    return pl.pallas_call(
        norm_body,
        in_specs=[vmem] * 4,
        out_specs=[vmem] * 2,
        out_shape=[
            jax.ShapeDtypeStruct((rows, width), BF16),
            jax.ShapeDtypeStruct((chooser.shape[0], width), BF16),
        ],
        compiler_params=pltpu.CompilerParams(vmem_limit_bytes=24 * MIB),
        cost_estimate=pl.CostEstimate(
            flops=2 * chooser.shape[0] * rows * width, bytes_accessed=2 * MIB, transcendentals=0
        ),
        name="norm_and_dispatch",
    )(parts, residual, gain, chooser)


def experts_body(step, arrived, w_gate, w_up, w_down, out, gate_held, up_held, down_held, sems):
    experts, _, depth = w_gate.shape
    rows, width = arrived.shape
    pieces = [(e, f) for e in range(experts) for f in range(0, depth, step)]
    copies = []
    for n, (e, f) in enumerate(pieces):
        down = pl.ds(f, step)
        copies.append(
            [
                pltpu.make_async_copy(w_gate.at[e, :, down], gate_held.at[n], sems.at[n, 0]),
                pltpu.make_async_copy(w_up.at[e, :, down], up_held.at[n], sems.at[n, 1]),
                pltpu.make_async_copy(w_down.at[e, down, :], down_held.at[n], sems.at[n, 2]),
            ]
        )
    for piece in copies:
        for copy in piece[:2]:
            copy.start()
    for piece in copies:
        piece[2].start()
    slot = lax.broadcasted_iota(jnp.int32, (rows, 1), 0)
    values = arrived[...]
    hidden = []
    for n, (e, f) in enumerate(pieces):
        copies[n][0].wait()
        copies[n][1].wait()
        gate = nn_dot(values, gate_held[n])
        upward = nn_dot(values, up_held[n])
        part = gate / (1.0 + jnp.exp(-gate)) * upward
        mine = lax.rem(slot, experts * MOST) // MOST == e
        hidden.append(jnp.where(mine, part, 0.0).astype(BF16))
    total = None
    for n in range(len(pieces)):
        copies[n][2].wait()
        term = nn_dot(hidden[n], down_held[n])
        total = term if total is None else total + term
    out[...] = total.astype(BF16)


def run_experts(arrived, w_gate, w_up, w_down):
    rows, width = arrived.shape
    experts, _, depth = w_gate.shape
    step = 256
    pieces = experts * depth // step
    vmem = pl.BlockSpec(memory_space=pltpu.VMEM)
    hbm = pl.BlockSpec(memory_space=pltpu.HBM)
    weights = [pltpu.with_memory_space_constraint(w, pltpu.HBM) for w in (w_gate, w_up, w_down)]
    return pl.pallas_call(
        functools.partial(experts_body, step),
        in_specs=[vmem] + [hbm] * 3,
        out_specs=vmem,
        out_shape=jax.ShapeDtypeStruct((rows, width), BF16),
        scratch_shapes=[
            pltpu.VMEM((pieces, width, step), BF16),
            pltpu.VMEM((pieces, width, step), BF16),
            pltpu.VMEM((pieces, step, width), BF16),
            pltpu.SemaphoreType.DMA((pieces, 3)),
        ],
        compiler_params=pltpu.CompilerParams(vmem_limit_bytes=44 * MIB),
        cost_estimate=pl.CostEstimate(
            flops=6 * rows * width * experts * depth,
            bytes_accessed=6 * width * experts * depth,
            transcendentals=rows * experts * depth,
        ),
        name="experts",
    )(arrived, *weights)


def mix_body(returned, coarse, fine, middle, out):
    values = returned[...]
    mixed = nn_dot(coarse[...], values) + nn_dot(fine[...], values)
    out[...] = (middle[...].astype(F32) + mixed).astype(BF16)


def mix(returned, coarse, fine, middle):
    vmem = pl.BlockSpec(memory_space=pltpu.VMEM)
    return pl.pallas_call(
        mix_body,
        in_specs=[vmem] * 4,
        out_specs=vmem,
        out_shape=jax.ShapeDtypeStruct(middle.shape, BF16),
        compiler_params=pltpu.CompilerParams(vmem_limit_bytes=16 * MIB),
        name="mix",
    )(returned, coarse, fine, middle)


def on_device(
    queries,
    new_key,
    new_value,
    key_cache,
    value_cache,
    cache_len,
    out_weight,
    residual,
    norm_gain,
    expert_ids,
    route_weight,
    w_gate,
    w_up,
    w_down,
):
    devices = lax.axis_size("ctx")
    chips = devices // CORES
    index = lax.axis_index("ctx")
    chip, core = index // CORES, index % CORES
    home_rows, width = residual.shape
    top = expert_ids.shape[1]
    heads_here = out_weight.shape[0] // HD
    cache_here = key_cache.shape[0]
    same_core = [[CORES * j + c for j in range(chips)] for c in range(CORES)]
    swap = [(i, i ^ 1) for i in range(devices)]

    across = [(i, i ^ CORES) for i in range(devices)]
    along = [
        [CORES * (2 * ring + side) + c for ring in range(chips // 2)]
        for side in range(2)
        for c in range(CORES)
    ]
    rings = chips // 2
    side_rows = rings * home_rows

    by_owner = queries.reshape(home_rows, chips, CORES, heads_here * HD)
    query_chunks = []
    for chunk in range(CORES):
        part = by_owner[:, :, chunk].reshape(1, home_rows, chips * heads_here * HD)
        if chunk:
            part, _ = lax.optimization_barrier((part, query_chunks[0][0]))
        mine = lax.all_to_all(
            jnp.broadcast_to(part, (rings, *part.shape[1:])),
            "ctx",
            split_axis=0,
            concat_axis=0,
            axis_index_groups=along,
            tiled=True,
        ).reshape(side_rows, part.shape[2])
        query_chunks.append((mine, lax.ppermute(mine, "ctx", across)))
    key_other = lax.ppermute(key_cache, "ctx", swap)
    value_turned = value_cache.T
    value_other = lax.ppermute(value_turned, "ctx", swap)
    weight_swapped = lax.ppermute(out_weight, "ctx", swap)

    place = jnp.stack([chip, index * cache_here, (index ^ 1) * cache_here, core, chip % 2]).astype(jnp.int32)

    def in_lanes(by_row):
        sides = by_row.reshape(rings, 2, CORES, home_rows)
        sides = lax.dynamic_index_in_dim(sides, core, axis=2, keepdims=False)
        sides = jnp.swapaxes(sides, 0, 1).reshape(2, 1, side_rows)
        return jnp.tile(sides, (1, HD // side_rows, 1)).reshape(1, 2 * HD)

    lens = in_lanes(cache_len)
    numbers = jnp.arange(chips * home_rows, dtype=jnp.int32).reshape(chips, 1, home_rows)
    row_ids = in_lanes(jnp.broadcast_to(numbers, (chips, CORES, home_rows)))

    flat_ids = expert_ids.reshape(-1)
    picks = jnp.arange(flat_ids.shape[0])
    earlier = (flat_ids[:, None] == flat_ids[None, :]) & (picks[None, :] < picks[:, None])
    target = (flat_ids * MOST + jnp.sum(earlier, axis=1, dtype=jnp.int32)).reshape(home_rows, top)
    experts = w_gate.shape[0]
    slots = experts * devices * MOST
    takes = target[:, :, None] == jnp.arange(slots, dtype=jnp.int32)
    chooser = jnp.any(takes, axis=1).T.astype(BF16)
    spread = jnp.sum(jnp.where(takes, route_weight[:, :, None], 0.0), axis=1)
    coarse = spread.astype(BF16)
    fine = (spread - coarse.astype(F32)).astype(BF16)

    gathered = []
    for chunk, (own_q, other_q) in enumerate(query_chunks):
        sums = attention(
            place,
            own_q,
            other_q,
            (key_cache, key_other),
            (value_turned, value_other),
            new_key,
            new_value,
            lens,
            row_ids,
            chips,
            key_cache.shape[1] // HD,
        )
        if chunk + 1 < len(query_chunks):
            own_next, other_next = query_chunks[chunk + 1]
            sums, other_next = lax.optimization_barrier((sums, other_next))
            query_chunks[chunk + 1] = (own_next, other_next)
        if chunk:
            sums, gathered[-1] = lax.optimization_barrier((sums, gathered[-1]))
        gathered.append(
            lax.all_to_all(
                sums, "ctx", split_axis=0, concat_axis=0, axis_index_groups=same_core, tiled=True
            )
        )
    late_weight, _ = lax.optimization_barrier((out_weight, query_chunks[-1][1]))
    weight_across = lax.ppermute(late_weight, "ctx", across)
    weights = (out_weight, weight_swapped, weight_across, lax.ppermute(weight_across, "ctx", swap))
    share = project(place, gathered, weights, side_rows)
    shares = lax.all_to_all(
        share.reshape(rings, home_rows, width),
        "ctx",
        split_axis=0,
        concat_axis=0,
        axis_index_groups=along,
        tiled=True,
    )
    middle, outgoing = norm_and_dispatch(shares, residual, norm_gain.reshape(1, width), chooser)
    arrived = lax.all_to_all(
        outgoing.reshape(devices, experts * MOST, width), "ctx", split_axis=0, concat_axis=0, tiled=True
    )
    produced = run_experts(arrived.reshape(slots, width), w_gate, w_up, w_down)
    returned = lax.all_to_all(
        produced.reshape(devices, experts * MOST, width), "ctx", split_axis=0, concat_axis=0, tiled=True
    )
    return mix(returned.reshape(slots, width), coarse, fine, middle)


def solution(mesh):
    placed = (
        P(("groups", "ctx"), None),
        P(("groups", "ctx"), None),
        P(("groups", "ctx"), None),
        P(("groups", "ctx"), None),
        P(("groups", "ctx"), None),
        P("groups"),
        P("ctx", None),
        P(("groups", "ctx"), None),
        P(),
        P(("groups", "ctx"), None),
        P(("groups", "ctx"), None),
        P("ctx", None, None),
        P("ctx", None, None),
        P("ctx", None, None),
    )
    return jax.shard_map(
        on_device, mesh=mesh, in_specs=placed, out_specs=P(("groups", "ctx"), None), check_vma=False
    )
```

```python
import functools
import math

import jax
import jax.numpy as jnp
from jax import lax
from jax.experimental import pallas as pl
from jax.experimental.pallas import tpu as pltpu
from jax.sharding import PartitionSpec as P

HD = 128
MOST = 4
CORES = 2
STATS = 16
MASKED = -1e30
FLOOR = -1e20
LOG2E = math.log2(math.e)
MIB = 1024 * 1024
F32 = jnp.float32
BF16 = jnp.bfloat16


def nt_dot(a, b):
    return lax.dot_general(a, b, (((1,), (1,)), ((), ())), preferred_element_type=F32)


def nn_dot(a, b):
    return lax.dot_general(a, b, (((1,), (0,)), ((), ())), preferred_element_type=F32)


def attention_body(shape, place, *refs):
    rings, ring_heads, home_rows, side_rows, cache_here, step = shape
    *query_refs, key_own, key_other, value_own, value_other, key_fresh, value_fresh = refs[:-8]
    lens, row_ids, out, q_rows, q_turned, hidden, scores, probs = refs[-8:]
    chip, start_own, start_other, side_here, ring_here = place[0], place[1], place[2], place[4], place[5]
    near = side_rows // home_rows
    pack = HD // side_rows
    groups = ring_heads // pack

    @pl.when(pl.program_id(0) == 0)
    def _():
        lanes = lens.shape[1]
        for part, start in enumerate((start_own, start_other)):
            positions = start + lax.broadcasted_iota(jnp.int32, (cache_here, lanes), 0)
            hidden[part * cache_here : (part + 1) * cache_here, :] = jnp.where(
                positions < lens[...], 0.0, MASKED
            )
        token = chip * home_rows + lax.broadcasted_iota(jnp.int32, (home_rows, lanes), 0)
        hidden[2 * cache_here :, :] = jnp.where(token == row_ids[...], 0.0, MASKED)

    for k, piece in enumerate(query_refs):
        side = side_here if k < near else 1 - side_here
        spot = lax.rem(ring_here, near) ^ (k % near)
        q_rows[side, pl.ds(pl.multiple_of(spot * home_rows, home_rows), home_rows), :] = piece[...]

    factor = LOG2E / math.sqrt(HD)
    spots = [(r, s, k) for r in range(rings) for s in range(2) for k in range(groups)]
    for n, (r, s, k) in enumerate(spots):
        first = r * ring_heads + k * pack
        block = jnp.concatenate(
            [q_rows[s, :, h * HD : (h + 1) * HD] for h in range(first, first + pack)], axis=0
        )
        scaled = block.T.astype(F32) * factor
        coarse = scaled.astype(BF16)
        q_turned[:HD, n * HD : (n + 1) * HD] = coarse
        q_turned[HD:, n * HD : (n + 1) * HD] = (scaled - coarse.astype(F32)).astype(BF16)
    wide = len(spots) * HD

    def score(keys, at):
        s = nn_dot(jnp.concatenate([keys, keys], axis=1), q_turned[...])
        return s + jnp.concatenate([hidden[at, s * HD : (s + 1) * HD] for _, s, _ in spots], axis=1)

    s_new = score(key_fresh[...], slice(2 * cache_here, 2 * cache_here + home_rows))
    run = jnp.max(s_new.reshape(home_rows // 8, 8, wide), axis=0)
    pieces = [(part, i) for part in range(2) for i in range(0, cache_here, step)]
    for part, i in pieces:
        at = slice(part * cache_here + i, part * cache_here + i + step)
        s = score((key_own, key_other)[part][i : i + step, :], at)
        scores[at, :] = s
        run = jnp.maximum(run, jnp.max(s.reshape(step // 8, 8, wide), axis=0))
    peak = jnp.maximum(jnp.max(run, axis=0, keepdims=True), FLOOR).astype(BF16).astype(F32)
    p_new = jnp.exp2((s_new - peak).astype(BF16))
    for part, i in pieces:
        at = slice(part * cache_here + i, part * cache_here + i + step)
        probs[at, :] = jnp.exp2((scores[at, :] - peak).astype(BF16))
    ones = jnp.ones((STATS, cache_here), BF16)
    sums = nn_dot(jnp.concatenate([value_own[...], ones], axis=0), probs[:cache_here, :])
    sums = sums + nn_dot(jnp.concatenate([value_other[...], ones], axis=0), probs[cache_here:, :])
    numer = sums[:HD] + nn_dot(value_fresh[...].astype(F32).T.astype(BF16), p_new)
    denom = sums[HD : HD + 1] + jnp.sum(p_new.astype(F32), axis=0, keepdims=True)
    high = denom.astype(BF16).astype(F32)
    low = denom - high
    for owner in range(2 * rings):
        lanes = [slice((owner * groups + k) * HD, (owner * groups + k + 1) * HD) for k in range(groups)]
        for k, cols in enumerate(lanes):
            out[owner, k * HD : (k + 1) * HD, :] = numer[:, cols].astype(BF16)
        filled = [kind[:, cols] for kind in (peak, high, low) for cols in lanes]
        filled += [jnp.zeros_like(filled[0])] * (STATS - len(filled))
        out[owner, groups * HD :, :] = jnp.concatenate(filled, axis=0).astype(BF16)


def attention(place, query_blocks, keys, values, new_key, new_value, lens, row_ids, chips, kv_heads):
    home_rows = new_key.shape[0]
    side_rows = home_rows * len(query_blocks) // 2
    cache_here = keys[0].shape[0]
    rings = chips // 2 // kv_heads
    columns = query_blocks[0][0].shape[1] // kv_heads
    ring_heads = columns // HD // rings
    wide = 2 * side_rows * columns // HD
    height = ring_heads * side_rows + STATS
    step = 512
    positions = 2 * cache_here + home_rows
    kv = lambda g, place: (0, g)
    whole = lambda g, place: (0, 0)
    shape = (rings, ring_heads, home_rows, side_rows, cache_here, step)
    work = wide * kv_heads * 2 * cache_here
    return pl.pallas_call(
        functools.partial(attention_body, shape),
        grid_spec=pltpu.PrefetchScalarGridSpec(
            num_scalar_prefetch=1,
            grid=(kv_heads,),
            in_specs=[
                pl.BlockSpec((home_rows, columns), functools.partial(lambda n, g, place: (n, g), n))
                for _, n in query_blocks
            ]
            + [pl.BlockSpec((cache_here, HD), kv)] * 2
            + [pl.BlockSpec((HD, cache_here), lambda g, place: (g, 0))] * 2
            + [pl.BlockSpec((home_rows, HD), kv)] * 2
            + [pl.BlockSpec(lens.shape, whole)] * 2,
            out_specs=pl.BlockSpec((2 * rings, height, HD), lambda g, place: (g, 0, 0)),
            scratch_shapes=[
                pltpu.VMEM((2, side_rows, columns), BF16),
                pltpu.VMEM((2 * HD, wide), BF16),
                pltpu.VMEM((positions, 2 * HD), F32),
                pltpu.VMEM((2 * cache_here, wide), F32),
                pltpu.VMEM((2 * cache_here, wide), BF16),
            ],
        ),
        out_shape=jax.ShapeDtypeStruct((chips, height, HD), BF16),
        compiler_params=pltpu.CompilerParams(vmem_limit_bytes=32 * MIB),
        cost_estimate=pl.CostEstimate(
            flops=6 * work * HD, bytes_accessed=8 * MIB, transcendentals=work
        ),
        name="attention",
    )(
        place,
        *[block for block, _ in query_blocks],
        pltpu.with_memory_space_constraint(keys[0], pltpu.HBM),
        keys[1],
        *values,
        new_key,
        new_value,
        lens,
        row_ids,
    )


def project_body(side_rows, place, *refs):
    *chunks, same_own, same_other, across_own, across_other, out, turned = refs
    core, side = place[3], place[4]
    chips, height, _ = chunks[0].shape
    base = height - STATS
    groups = base // HD
    pack = HD // side_rows
    heads_here = groups * pack // 4
    half = chips // 2 // 2
    for near in range(2):
        sources = [chunks[s // 2 // half ^ near].at[s] for s in range(chips)]
        stats = [part[base:, :].astype(F32) for part in sources]
        peaks = [stat[:groups] for stat in stats]
        top = functools.reduce(jnp.maximum, peaks)
        share = [jnp.exp2(peak - top) for peak in peaks]
        denom = sum(w * (t[groups : 2 * groups] + t[2 * groups : 3 * groups]) for w, t in zip(share, stats))
        for k in range(groups):
            numer = sum(
                part[k * HD : (k + 1) * HD, :].astype(F32) * w[k : k + 1, :] for part, w in zip(sources, share)
            )
            attended = (numer / denom[k : k + 1, :]).T.astype(BF16)
            for j in range(pack):
                owner, h = divmod(k * pack + j, heads_here)
                turned[owner // CORES, owner % CORES, near * side_rows : (near + 1) * side_rows, h * HD : (h + 1) * HD] = (
                    attended[j * side_rows : (j + 1) * side_rows]
                )
    product = nn_dot(turned[side, core], same_own[...]) + nn_dot(turned[side, 1 - core], same_other[...])
    product = product + nn_dot(turned[1 - side, core], across_own[...])
    product = product + nn_dot(turned[1 - side, 1 - core], across_other[...])
    out[...] = product.astype(BF16)


def project(place, chunks, weights, side_rows):
    depth, width = weights[0].shape
    rows = 2 * side_rows
    vmem = pl.BlockSpec(memory_space=pltpu.VMEM)
    return pl.pallas_call(
        functools.partial(project_body, side_rows),
        in_specs=[pl.BlockSpec(memory_space=pltpu.SMEM)] + [vmem] * (len(chunks) + len(weights)),
        out_specs=vmem,
        out_shape=jax.ShapeDtypeStruct((rows, width), BF16),
        scratch_shapes=[pltpu.VMEM((2, CORES, rows, depth), BF16)],
        compiler_params=pltpu.CompilerParams(vmem_limit_bytes=32 * MIB),
        cost_estimate=pl.CostEstimate(
            flops=8 * rows * width * depth, bytes_accessed=6 * MIB, transcendentals=0
        ),
        name="project",
    )(place, *chunks, *weights)


def norm_body(parts, residual, gain, chooser, middle_out, sent):
    total = parts[0].astype(F32)
    for s in range(1, parts.shape[0]):
        total = total + parts[s].astype(F32)
    middle = (residual[...].astype(F32) + total).astype(BF16)
    middle_out[...] = middle
    middle = middle.astype(F32)
    inv_rms = lax.rsqrt(jnp.mean(middle * middle, axis=-1, keepdims=True) + 1e-06)
    normed = (middle * inv_rms * gain[...].astype(F32)).astype(BF16)
    sent[...] = nn_dot(chooser[...], normed).astype(BF16)


def norm_and_dispatch(parts, residual, gain, chooser):
    vmem = pl.BlockSpec(memory_space=pltpu.VMEM)
    rows, width = residual.shape
    return pl.pallas_call(
        norm_body,
        in_specs=[vmem] * 4,
        out_specs=[vmem] * 2,
        out_shape=[
            jax.ShapeDtypeStruct((rows, width), BF16),
            jax.ShapeDtypeStruct((chooser.shape[0], width), BF16),
        ],
        compiler_params=pltpu.CompilerParams(vmem_limit_bytes=24 * MIB),
        cost_estimate=pl.CostEstimate(
            flops=2 * chooser.shape[0] * rows * width, bytes_accessed=2 * MIB, transcendentals=0
        ),
        name="norm_and_dispatch",
    )(parts, residual, gain, chooser)


def experts_body(step, arrived, w_gate, w_up, w_down, out, gate_held, up_held, down_held, sems):
    experts, _, depth = w_gate.shape
    rows, width = arrived.shape
    pieces = [(e, f) for e in range(experts) for f in range(0, depth, step)]
    copies = []
    for n, (e, f) in enumerate(pieces):
        down = pl.ds(f, step)
        copies.append(
            [
                pltpu.make_async_copy(w_gate.at[e, :, down], gate_held.at[n], sems.at[n, 0]),
                pltpu.make_async_copy(w_up.at[e, :, down], up_held.at[n], sems.at[n, 1]),
                pltpu.make_async_copy(w_down.at[e, down, :], down_held.at[n], sems.at[n, 2]),
            ]
        )
    for piece in copies:
        for copy in piece[:2]:
            copy.start()
    for piece in copies:
        piece[2].start()
    slot = lax.broadcasted_iota(jnp.int32, (rows, 1), 0)
    values = arrived[...]
    hidden = []
    for n, (e, f) in enumerate(pieces):
        copies[n][0].wait()
        copies[n][1].wait()
        gate = nn_dot(values, gate_held[n])
        upward = nn_dot(values, up_held[n])
        part = gate / (1.0 + jnp.exp(-gate)) * upward
        mine = lax.rem(slot, experts * MOST) // MOST == e
        hidden.append(jnp.where(mine, part, 0.0).astype(BF16))
    total = None
    for n in range(len(pieces)):
        copies[n][2].wait()
        term = nn_dot(hidden[n], down_held[n])
        total = term if total is None else total + term
    out[...] = total.astype(BF16)


def run_experts(arrived, w_gate, w_up, w_down):
    rows, width = arrived.shape
    experts, _, depth = w_gate.shape
    step = 256
    pieces = experts * depth // step
    vmem = pl.BlockSpec(memory_space=pltpu.VMEM)
    hbm = pl.BlockSpec(memory_space=pltpu.HBM)
    weights = [pltpu.with_memory_space_constraint(w, pltpu.HBM) for w in (w_gate, w_up, w_down)]
    return pl.pallas_call(
        functools.partial(experts_body, step),
        in_specs=[vmem] + [hbm] * 3,
        out_specs=vmem,
        out_shape=jax.ShapeDtypeStruct((rows, width), BF16),
        scratch_shapes=[
            pltpu.VMEM((pieces, width, step), BF16),
            pltpu.VMEM((pieces, width, step), BF16),
            pltpu.VMEM((pieces, step, width), BF16),
            pltpu.SemaphoreType.DMA((pieces, 3)),
        ],
        compiler_params=pltpu.CompilerParams(vmem_limit_bytes=44 * MIB),
        cost_estimate=pl.CostEstimate(
            flops=6 * rows * width * experts * depth,
            bytes_accessed=6 * width * experts * depth,
            transcendentals=rows * experts * depth,
        ),
        name="experts",
    )(arrived, *weights)


def mix_body(returned, coarse, fine, middle, out):
    values = returned[...]
    mixed = nn_dot(coarse[...], values) + nn_dot(fine[...], values)
    out[...] = (middle[...].astype(F32) + mixed).astype(BF16)


def mix(returned, coarse, fine, middle):
    vmem = pl.BlockSpec(memory_space=pltpu.VMEM)
    return pl.pallas_call(
        mix_body,
        in_specs=[vmem] * 4,
        out_specs=vmem,
        out_shape=jax.ShapeDtypeStruct(middle.shape, BF16),
        compiler_params=pltpu.CompilerParams(vmem_limit_bytes=16 * MIB),
        name="mix",
    )(returned, coarse, fine, middle)


def on_device(
    queries,
    new_key,
    new_value,
    key_cache,
    value_cache,
    cache_len,
    out_weight,
    residual,
    norm_gain,
    expert_ids,
    route_weight,
    w_gate,
    w_up,
    w_down,
):
    devices = lax.axis_size("ctx")
    chips = devices // CORES
    index = lax.axis_index("ctx")
    chip, core = index // CORES, index % CORES
    home_rows, width = residual.shape
    top = expert_ids.shape[1]
    heads_here = out_weight.shape[0] // HD
    cache_here = key_cache.shape[0]
    same_core = [[CORES * j + c for j in range(chips)] for c in range(CORES)]
    swap = [(i, i ^ 1) for i in range(devices)]

    across = [(i, i ^ CORES) for i in range(devices)]
    along = [
        [CORES * (2 * ring + side) + c for ring in range(chips // 2)]
        for side in range(2)
        for c in range(CORES)
    ]
    rings = chips // 2
    half = rings // 2
    side_rows = half * home_rows

    def across_y(block):
        return lax.ppermute(block, "ctx", across)

    neighbour = across_y(queries)
    by_ring = [queries] + [
        lax.ppermute(queries, "ctx", [(i, i ^ (2 * CORES * k)) for i in range(devices)])
        for k in range(1, rings)
    ]
    near_blocks = [(block, 0) for block in by_ring[:half]]
    near_blocks += [(neighbour, 0)] + [(across_y(block), 0) for block in by_ring[1:half]]
    far = jnp.concatenate(by_ring[half:], axis=0)
    far_across = across_y(far)
    far_blocks = [(far, k) for k in range(half)] + [(far_across, k) for k in range(half)]
    key_other = lax.ppermute(key_cache, "ctx", swap)
    value_turned = value_cache.T
    value_other = lax.ppermute(value_turned, "ctx", swap)
    weight_swapped = lax.ppermute(out_weight, "ctx", swap)

    place = jnp.stack([chip, index * cache_here, (index ^ 1) * cache_here, core, chip % 2, chip // 2]).astype(jnp.int32)

    def in_lanes(by_row):
        sides = by_row.reshape(2, half, 2, CORES, home_rows)
        sides = lax.dynamic_index_in_dim(sides, core, axis=3, keepdims=False)
        sides = jnp.swapaxes(sides, 1, 2).reshape(2, 2, 1, side_rows)
        lanes = jnp.tile(sides, (1, 1, HD // side_rows, 1)).reshape(2, 1, 2 * HD)
        here = chip // CORES // half
        return [lax.dynamic_index_in_dim(lanes, here ^ n, axis=0, keepdims=False) for n in range(2)]

    lens = in_lanes(cache_len)
    numbers = jnp.arange(chips * home_rows, dtype=jnp.int32).reshape(chips, 1, home_rows)
    row_ids = in_lanes(jnp.broadcast_to(numbers, (chips, CORES, home_rows)))

    flat_ids = expert_ids.reshape(-1)
    picks = jnp.arange(flat_ids.shape[0])
    earlier = (flat_ids[:, None] == flat_ids[None, :]) & (picks[None, :] < picks[:, None])
    target = (flat_ids * MOST + jnp.sum(earlier, axis=1, dtype=jnp.int32)).reshape(home_rows, top)
    experts = w_gate.shape[0]
    slots = experts * devices * MOST
    takes = target[:, :, None] == jnp.arange(slots, dtype=jnp.int32)
    chooser = jnp.any(takes, axis=1).T.astype(BF16)
    spread = jnp.sum(jnp.where(takes, route_weight[:, :, None], 0.0), axis=1)
    coarse = spread.astype(BF16)
    fine = (spread - coarse.astype(F32)).astype(BF16)

    gathered = []
    for chunk, blocks in enumerate((near_blocks, far_blocks)):
        sums = attention(
            place,
            blocks,
            (key_cache, key_other),
            (value_turned, value_other),
            new_key,
            new_value,
            lens[chunk],
            row_ids[chunk],
            chips,
            key_cache.shape[1] // HD,
        )
        if chunk:
            sums, gathered[-1] = lax.optimization_barrier((sums, gathered[-1]))
        else:
            sums, place, late_weight = lax.optimization_barrier((sums, place, out_weight))
        gathered.append(
            lax.all_to_all(
                sums, "ctx", split_axis=0, concat_axis=0, axis_index_groups=same_core, tiled=True
            )
        )
    weight_across = lax.ppermute(late_weight, "ctx", across)
    weight_across, _ = lax.optimization_barrier((weight_across, sums))
    weights = (out_weight, weight_swapped, weight_across, lax.ppermute(weight_across, "ctx", swap))
    share = project(place, gathered, weights, side_rows)
    shares = lax.all_to_all(
        share.reshape(rings, home_rows, width),
        "ctx",
        split_axis=0,
        concat_axis=0,
        axis_index_groups=along,
        tiled=True,
    )
    middle, outgoing = norm_and_dispatch(shares, residual, norm_gain.reshape(1, width), chooser)
    arrived = lax.all_to_all(
        outgoing.reshape(devices, experts * MOST, width), "ctx", split_axis=0, concat_axis=0, tiled=True
    )
    produced = run_experts(arrived.reshape(slots, width), w_gate, w_up, w_down)
    returned = lax.all_to_all(
        produced.reshape(devices, experts * MOST, width), "ctx", split_axis=0, concat_axis=0, tiled=True
    )
    return mix(returned.reshape(slots, width), coarse, fine, middle)


def solution(mesh):
    placed = (
        P(("groups", "ctx"), None),
        P(("groups", "ctx"), None),
        P(("groups", "ctx"), None),
        P(("groups", "ctx"), None),
        P(("groups", "ctx"), None),
        P("groups"),
        P("ctx", None),
        P(("groups", "ctx"), None),
        P(),
        P(("groups", "ctx"), None),
        P(("groups", "ctx"), None),
        P("ctx", None, None),
        P("ctx", None, None),
        P("ctx", None, None),
    )
    return jax.shard_map(
        on_device, mesh=mesh, in_specs=placed, out_specs=P(("groups", "ctx"), None), check_vma=False
    )
```

```python
import functools
import math

import jax
import jax.numpy as jnp
from jax import lax
from jax.experimental import pallas as pl
from jax.experimental.pallas import tpu as pltpu
from jax.sharding import PartitionSpec as P

HD = 128
MOST = 4
CORES = 2
STATS = 16
MASKED = -1e30
FLOOR = -1e20
LOG2E = math.log2(math.e)
MIB = 1024 * 1024
F32 = jnp.float32
BF16 = jnp.bfloat16


def nt_dot(a, b):
    return lax.dot_general(a, b, (((1,), (1,)), ((), ())), preferred_element_type=F32)


def nn_dot(a, b):
    return lax.dot_general(a, b, (((1,), (0,)), ((), ())), preferred_element_type=F32)


def attention_body(shape, place, *refs):
    rings, ring_heads, home_rows, side_rows, cache_here, step = shape
    *query_refs, key_own, key_other, value_own, value_other, key_fresh, value_fresh = refs[:-8]
    lens, row_ids, out, q_rows, q_turned, hidden, scores, probs = refs[-8:]
    chip, start_own, start_other, side_here, ring_here = place[0], place[1], place[2], place[4], place[5]
    near = side_rows // home_rows
    pack = HD // side_rows
    groups = ring_heads // pack

    @pl.when(pl.program_id(0) == 0)
    def _():
        lanes = lens.shape[1]
        for part, start in enumerate((start_own, start_other)):
            positions = start + lax.broadcasted_iota(jnp.int32, (cache_here, lanes), 0)
            hidden[part * cache_here : (part + 1) * cache_here, :] = jnp.where(
                positions < lens[...], 0.0, MASKED
            )
        token = chip * home_rows + lax.broadcasted_iota(jnp.int32, (home_rows, lanes), 0)
        hidden[2 * cache_here :, :] = jnp.where(token == row_ids[...], 0.0, MASKED)

    for k, piece in enumerate(query_refs):
        side = side_here if k < near else 1 - side_here
        spot = lax.rem(ring_here, near) ^ (k % near)
        q_rows[side, pl.ds(pl.multiple_of(spot * home_rows, home_rows), home_rows), :] = piece[...]

    factor = LOG2E / math.sqrt(HD)
    spots = [(r, s, k) for r in range(rings) for s in range(2) for k in range(groups)]
    for n, (r, s, k) in enumerate(spots):
        first = r * ring_heads + k * pack
        block = jnp.concatenate(
            [q_rows[s, :, h * HD : (h + 1) * HD] for h in range(first, first + pack)], axis=0
        )
        scaled = block.T.astype(F32) * factor
        coarse = scaled.astype(BF16)
        q_turned[:HD, n * HD : (n + 1) * HD] = coarse
        q_turned[HD:, n * HD : (n + 1) * HD] = (scaled - coarse.astype(F32)).astype(BF16)
    wide = len(spots) * HD

    def score(keys, at):
        s = nn_dot(jnp.concatenate([keys, keys], axis=1), q_turned[...])
        return s + jnp.concatenate([hidden[at, s * HD : (s + 1) * HD] for _, s, _ in spots], axis=1)

    s_new = score(key_fresh[...], slice(2 * cache_here, 2 * cache_here + home_rows))
    run = jnp.max(s_new.reshape(home_rows // 8, 8, wide), axis=0)
    pieces = [(part, i) for part in range(2) for i in range(0, cache_here, step)]
    for part, i in pieces:
        at = slice(part * cache_here + i, part * cache_here + i + step)
        s = score((key_own, key_other)[part][i : i + step, :], at)
        scores[at, :] = s
        run = jnp.maximum(run, jnp.max(s.reshape(step // 8, 8, wide), axis=0))
    peak = jnp.maximum(jnp.max(run, axis=0, keepdims=True), FLOOR).astype(BF16).astype(F32)
    p_new = jnp.exp2((s_new - peak).astype(BF16))
    for part, i in pieces:
        at = slice(part * cache_here + i, part * cache_here + i + step)
        probs[at, :] = jnp.exp2((scores[at, :] - peak).astype(BF16))
    ones = jnp.ones((STATS, cache_here), BF16)
    sums = nn_dot(jnp.concatenate([value_own[...], ones], axis=0), probs[:cache_here, :])
    sums = sums + nn_dot(jnp.concatenate([value_other[...], ones], axis=0), probs[cache_here:, :])
    numer = sums[:HD] + nn_dot(value_fresh[...].astype(F32).T.astype(BF16), p_new)
    denom = sums[HD : HD + 1] + jnp.sum(p_new.astype(F32), axis=0, keepdims=True)
    high = denom.astype(BF16).astype(F32)
    low = denom - high
    for owner in range(2 * rings):
        lanes = [slice((owner * groups + k) * HD, (owner * groups + k + 1) * HD) for k in range(groups)]
        for k, cols in enumerate(lanes):
            out[owner, k * HD : (k + 1) * HD, :] = numer[:, cols].astype(BF16)
        filled = [kind[:, cols] for kind in (peak, high, low) for cols in lanes]
        filled += [jnp.zeros_like(filled[0])] * (STATS - len(filled))
        out[owner, groups * HD :, :] = jnp.concatenate(filled, axis=0).astype(BF16)


def attention(place, query_blocks, keys, values, new_key, new_value, lens, row_ids, chips, kv_heads):
    home_rows = new_key.shape[0]
    side_rows = home_rows * len(query_blocks) // 2
    cache_here = keys[0].shape[0]
    rings = chips // 2 // kv_heads
    columns = query_blocks[0][0].shape[1] // kv_heads
    ring_heads = columns // HD // rings
    wide = 2 * side_rows * columns // HD
    height = ring_heads * side_rows + STATS
    step = 512
    positions = 2 * cache_here + home_rows
    kv = lambda g, place: (0, g)
    whole = lambda g, place: (0, 0)
    shape = (rings, ring_heads, home_rows, side_rows, cache_here, step)
    work = wide * kv_heads * 2 * cache_here
    return pl.pallas_call(
        functools.partial(attention_body, shape),
        grid_spec=pltpu.PrefetchScalarGridSpec(
            num_scalar_prefetch=1,
            grid=(kv_heads,),
            in_specs=[
                pl.BlockSpec((home_rows, columns), functools.partial(lambda n, g, place: (n, g), n))
                for _, n in query_blocks
            ]
            + [pl.BlockSpec((cache_here, HD), kv)] * 2
            + [pl.BlockSpec((HD, cache_here), lambda g, place: (g, 0))] * 2
            + [pl.BlockSpec((home_rows, HD), kv)] * 2
            + [pl.BlockSpec(lens.shape, whole)] * 2,
            out_specs=pl.BlockSpec((2 * rings, height, HD), lambda g, place: (g, 0, 0)),
            scratch_shapes=[
                pltpu.VMEM((2, side_rows, columns), BF16),
                pltpu.VMEM((2 * HD, wide), BF16),
                pltpu.VMEM((positions, 2 * HD), F32),
                pltpu.VMEM((2 * cache_here, wide), F32),
                pltpu.VMEM((2 * cache_here, wide), BF16),
            ],
        ),
        out_shape=jax.ShapeDtypeStruct((chips, height, HD), BF16),
        compiler_params=pltpu.CompilerParams(vmem_limit_bytes=32 * MIB),
        cost_estimate=pl.CostEstimate(
            flops=6 * work * HD, bytes_accessed=8 * MIB, transcendentals=work
        ),
        name="attention",
    )(
        place,
        *[block for block, _ in query_blocks],
        pltpu.with_memory_space_constraint(keys[0], pltpu.HBM),
        keys[1],
        *values,
        pltpu.with_memory_space_constraint(new_key, pltpu.HBM),
        pltpu.with_memory_space_constraint(new_value, pltpu.HBM),
        lens,
        row_ids,
    )


def project_body(side_rows, place, *refs):
    *chunks, same_own, same_other, across_own, across_other, out, turned = refs
    core, side = place[3], place[4]
    chips, height, _ = chunks[0].shape
    base = height - STATS
    groups = base // HD
    pack = HD // side_rows
    heads_here = groups * pack // 4
    half = chips // 2 // 2
    for near in range(2):
        sources = [chunks[s // 2 // half ^ near].at[s] for s in range(chips)]
        stats = [part[base:, :].astype(F32) for part in sources]
        peaks = [stat[:groups] for stat in stats]
        top = functools.reduce(jnp.maximum, peaks)
        share = [jnp.exp2(peak - top) for peak in peaks]
        denom = sum(w * (t[groups : 2 * groups] + t[2 * groups : 3 * groups]) for w, t in zip(share, stats))
        for k in range(groups):
            numer = sum(
                part[k * HD : (k + 1) * HD, :].astype(F32) * w[k : k + 1, :] for part, w in zip(sources, share)
            )
            attended = (numer / denom[k : k + 1, :]).T.astype(BF16)
            for j in range(pack):
                owner, h = divmod(k * pack + j, heads_here)
                turned[owner // CORES, owner % CORES, near * side_rows : (near + 1) * side_rows, h * HD : (h + 1) * HD] = (
                    attended[j * side_rows : (j + 1) * side_rows]
                )
    product = nn_dot(turned[side, core], same_own[...]) + nn_dot(turned[side, 1 - core], same_other[...])
    product = product + nn_dot(turned[1 - side, core], across_own[...])
    product = product + nn_dot(turned[1 - side, 1 - core], across_other[...])
    out[...] = product.astype(BF16)


def project(place, chunks, weights, side_rows):
    depth, width = weights[0].shape
    rows = 2 * side_rows
    vmem = pl.BlockSpec(memory_space=pltpu.VMEM)
    return pl.pallas_call(
        functools.partial(project_body, side_rows),
        in_specs=[pl.BlockSpec(memory_space=pltpu.SMEM)] + [vmem] * (len(chunks) + len(weights)),
        out_specs=vmem,
        out_shape=jax.ShapeDtypeStruct((rows, width), BF16),
        scratch_shapes=[pltpu.VMEM((2, CORES, rows, depth), BF16)],
        compiler_params=pltpu.CompilerParams(vmem_limit_bytes=32 * MIB),
        cost_estimate=pl.CostEstimate(
            flops=8 * rows * width * depth, bytes_accessed=6 * MIB, transcendentals=0
        ),
        name="project",
    )(place, *chunks, *weights)


def norm_body(parts, residual, gain, chooser, middle_out, sent):
    total = parts[0].astype(F32)
    for s in range(1, parts.shape[0]):
        total = total + parts[s].astype(F32)
    middle = (residual[...].astype(F32) + total).astype(BF16)
    middle_out[...] = middle
    middle = middle.astype(F32)
    inv_rms = lax.rsqrt(jnp.mean(middle * middle, axis=-1, keepdims=True) + 1e-06)
    normed = (middle * inv_rms * gain[...].astype(F32)).astype(BF16)
    sent[...] = nn_dot(chooser[...], normed).astype(BF16)


def norm_and_dispatch(parts, residual, gain, chooser):
    vmem = pl.BlockSpec(memory_space=pltpu.VMEM)
    rows, width = residual.shape
    return pl.pallas_call(
        norm_body,
        in_specs=[vmem] * 4,
        out_specs=[vmem] * 2,
        out_shape=[
            jax.ShapeDtypeStruct((rows, width), BF16),
            jax.ShapeDtypeStruct((chooser.shape[0], width), BF16),
        ],
        compiler_params=pltpu.CompilerParams(vmem_limit_bytes=24 * MIB),
        cost_estimate=pl.CostEstimate(
            flops=2 * chooser.shape[0] * rows * width, bytes_accessed=2 * MIB, transcendentals=0
        ),
        name="norm_and_dispatch",
    )(parts, residual, gain, chooser)


def experts_body(step, arrived, w_gate, w_up, w_down, out, gate_held, up_held, down_held, sems):
    experts, _, depth = w_gate.shape
    rows, width = arrived.shape
    pieces = [(e, f) for e in range(experts) for f in range(0, depth, step)]
    copies = []
    for n, (e, f) in enumerate(pieces):
        down = pl.ds(f, step)
        copies.append(
            [
                pltpu.make_async_copy(w_gate.at[e, :, down], gate_held.at[n], sems.at[n, 0]),
                pltpu.make_async_copy(w_up.at[e, :, down], up_held.at[n], sems.at[n, 1]),
                pltpu.make_async_copy(w_down.at[e, down, :], down_held.at[n], sems.at[n, 2]),
            ]
        )
    for piece in copies:
        for copy in piece[:2]:
            copy.start()
    for piece in copies:
        piece[2].start()
    slot = lax.broadcasted_iota(jnp.int32, (rows, 1), 0)
    values = arrived[...]
    hidden = []
    for n, (e, f) in enumerate(pieces):
        copies[n][0].wait()
        copies[n][1].wait()
        gate = nn_dot(values, gate_held[n])
        upward = nn_dot(values, up_held[n])
        part = gate / (1.0 + jnp.exp(-gate)) * upward
        mine = lax.rem(slot, experts * MOST) // MOST == e
        hidden.append(jnp.where(mine, part, 0.0).astype(BF16))
    total = None
    for n in range(len(pieces)):
        copies[n][2].wait()
        term = nn_dot(hidden[n], down_held[n])
        total = term if total is None else total + term
    out[...] = total.astype(BF16)


def run_experts(arrived, w_gate, w_up, w_down):
    rows, width = arrived.shape
    experts, _, depth = w_gate.shape
    step = 256
    pieces = experts * depth // step
    vmem = pl.BlockSpec(memory_space=pltpu.VMEM)
    hbm = pl.BlockSpec(memory_space=pltpu.HBM)
    weights = [pltpu.with_memory_space_constraint(w, pltpu.HBM) for w in (w_gate, w_up, w_down)]
    return pl.pallas_call(
        functools.partial(experts_body, step),
        in_specs=[vmem] + [hbm] * 3,
        out_specs=vmem,
        out_shape=jax.ShapeDtypeStruct((rows, width), BF16),
        scratch_shapes=[
            pltpu.VMEM((pieces, width, step), BF16),
            pltpu.VMEM((pieces, width, step), BF16),
            pltpu.VMEM((pieces, step, width), BF16),
            pltpu.SemaphoreType.DMA((pieces, 3)),
        ],
        compiler_params=pltpu.CompilerParams(vmem_limit_bytes=44 * MIB),
        cost_estimate=pl.CostEstimate(
            flops=6 * rows * width * experts * depth,
            bytes_accessed=6 * width * experts * depth,
            transcendentals=rows * experts * depth,
        ),
        name="experts",
    )(arrived, *weights)


def mix_body(returned, coarse, fine, middle, out):
    values = returned[...]
    mixed = nn_dot(coarse[...], values) + nn_dot(fine[...], values)
    out[...] = (middle[...].astype(F32) + mixed).astype(BF16)


def mix(returned, coarse, fine, middle):
    vmem = pl.BlockSpec(memory_space=pltpu.VMEM)
    return pl.pallas_call(
        mix_body,
        in_specs=[vmem] * 4,
        out_specs=vmem,
        out_shape=jax.ShapeDtypeStruct(middle.shape, BF16),
        compiler_params=pltpu.CompilerParams(vmem_limit_bytes=16 * MIB),
        name="mix",
    )(returned, coarse, fine, middle)


def on_device(
    queries,
    new_key,
    new_value,
    key_cache,
    value_cache,
    cache_len,
    out_weight,
    residual,
    norm_gain,
    expert_ids,
    route_weight,
    w_gate,
    w_up,
    w_down,
):
    devices = lax.axis_size("ctx")
    chips = devices // CORES
    index = lax.axis_index("ctx")
    chip, core = index // CORES, index % CORES
    home_rows, width = residual.shape
    top = expert_ids.shape[1]
    heads_here = out_weight.shape[0] // HD
    cache_here = key_cache.shape[0]
    same_core = [[CORES * j + c for j in range(chips)] for c in range(CORES)]
    swap = [(i, i ^ 1) for i in range(devices)]

    across = [(i, i ^ CORES) for i in range(devices)]
    along = [
        [CORES * (2 * ring + side) + c for ring in range(chips // 2)]
        for side in range(2)
        for c in range(CORES)
    ]
    rings = chips // 2
    half = rings // 2
    side_rows = half * home_rows

    def across_y(block):
        return lax.ppermute(block, "ctx", across)

    neighbour = across_y(queries)
    by_ring = [queries] + [
        lax.ppermute(queries, "ctx", [(i, i ^ (2 * CORES * k)) for i in range(devices)])
        for k in range(1, rings)
    ]
    near_blocks = [(pltpu.with_memory_space_constraint(queries, pltpu.HBM), 0)]
    near_blocks += [(block, 0) for block in by_ring[1:half]]
    near_blocks += [(neighbour, 0)] + [(across_y(block), 0) for block in by_ring[1:half]]
    far = jnp.concatenate(by_ring[half:], axis=0)
    far_across = across_y(far)
    far_blocks = [(far, k) for k in range(half)] + [(far_across, k) for k in range(half)]
    late_keys, late_values, _ = lax.optimization_barrier((key_cache, value_cache, neighbour))
    key_other = lax.ppermute(late_keys, "ctx", swap)
    value_turned = late_values.T
    value_other = lax.ppermute(value_turned, "ctx", swap)
    weight_swapped = lax.ppermute(out_weight, "ctx", swap)

    place = jnp.stack([chip, index * cache_here, (index ^ 1) * cache_here, core, chip % 2, chip // 2]).astype(jnp.int32)

    def in_lanes(by_chip, n):
        here = lax.dynamic_slice_in_dim(by_chip, (chip // CORES // half ^ n) * chips // 2, chips // 2, 0)
        sides = [
            jnp.concatenate([here[2 * ring + side : 2 * ring + side + 1] for ring in range(half)], axis=1)
            for side in range(2)
        ]
        return jnp.concatenate([lanes for lanes in sides for _ in range(HD // side_rows)], axis=1)

    len_by_chip = lax.dynamic_slice_in_dim(
        cache_len.reshape(chips, CORES * home_rows), core * home_rows, home_rows, 1
    )
    number_by_chip = jnp.arange(chips * home_rows, dtype=jnp.int32).reshape(chips, home_rows)
    lens = [in_lanes(len_by_chip, n) for n in range(2)]
    row_ids = [in_lanes(number_by_chip, n) for n in range(2)]

    flat_ids = expert_ids.reshape(-1)
    picks = jnp.arange(flat_ids.shape[0])
    earlier = (flat_ids[:, None] == flat_ids[None, :]) & (picks[None, :] < picks[:, None])
    target = (flat_ids * MOST + jnp.sum(earlier, axis=1, dtype=jnp.int32)).reshape(home_rows, top)
    experts = w_gate.shape[0]
    slots = experts * devices * MOST
    takes = target[:, :, None] == jnp.arange(slots, dtype=jnp.int32)
    chooser = jnp.any(takes, axis=1).T.astype(BF16)
    spread = jnp.sum(jnp.where(takes, route_weight[:, :, None], 0.0), axis=1)
    coarse = spread.astype(BF16)
    fine = (spread - coarse.astype(F32)).astype(BF16)

    gathered = []
    for chunk, blocks in enumerate((near_blocks, far_blocks)):
        sums = attention(
            place,
            blocks,
            (key_cache, key_other),
            (value_turned, value_other),
            new_key,
            new_value,
            lens[chunk],
            row_ids[chunk],
            chips,
            key_cache.shape[1] // HD,
        )
        if chunk:
            sums, gathered[-1] = lax.optimization_barrier((sums, gathered[-1]))
        else:
            sums, place, late_weight, _ = lax.optimization_barrier((sums, place, out_weight, far_across))
        gathered.append(
            lax.all_to_all(
                sums, "ctx", split_axis=0, concat_axis=0, axis_index_groups=same_core, tiled=True
            )
        )
    weight_across = lax.ppermute(late_weight, "ctx", across)
    weight_across, _ = lax.optimization_barrier((weight_across, sums))
    weights = (out_weight, weight_swapped, weight_across, lax.ppermute(weight_across, "ctx", swap))
    share = project(place, gathered, weights, side_rows)
    shares = lax.all_to_all(
        share.reshape(rings, home_rows, width),
        "ctx",
        split_axis=0,
        concat_axis=0,
        axis_index_groups=along,
        tiled=True,
    )
    middle, outgoing = norm_and_dispatch(shares, residual, norm_gain.reshape(1, width), chooser)
    arrived = lax.all_to_all(
        outgoing.reshape(devices, experts * MOST, width), "ctx", split_axis=0, concat_axis=0, tiled=True
    )
    produced = run_experts(arrived.reshape(slots, width), w_gate, w_up, w_down)
    returned = lax.all_to_all(
        produced.reshape(devices, experts * MOST, width), "ctx", split_axis=0, concat_axis=0, tiled=True
    )
    return mix(returned.reshape(slots, width), coarse, fine, middle)


def solution(mesh):
    placed = (
        P(("groups", "ctx"), None),
        P(("groups", "ctx"), None),
        P(("groups", "ctx"), None),
        P(("groups", "ctx"), None),
        P(("groups", "ctx"), None),
        P("groups"),
        P("ctx", None),
        P(("groups", "ctx"), None),
        P(),
        P(("groups", "ctx"), None),
        P(("groups", "ctx"), None),
        P("ctx", None, None),
        P("ctx", None, None),
        P("ctx", None, None),
    )
    return jax.shard_map(
        on_device, mesh=mesh, in_specs=placed, out_specs=P(("groups", "ctx"), None), check_vma=False
    )
```

```python
import functools
import math

import jax
import jax.numpy as jnp
from jax import lax
from jax.experimental import pallas as pl
from jax.experimental.pallas import tpu as pltpu
from jax.sharding import PartitionSpec as P

HD = 128
MOST = 4
CORES = 2
STATS = 16
MASKED = -1e30
FLOOR = -1e20
LOG2E = math.log2(math.e)
MIB = 1024 * 1024
F32 = jnp.float32
BF16 = jnp.bfloat16


def nt_dot(a, b):
    return lax.dot_general(a, b, (((1,), (1,)), ((), ())), preferred_element_type=F32)


def nn_dot(a, b):
    return lax.dot_general(a, b, (((1,), (0,)), ((), ())), preferred_element_type=F32)


def attention_body(shape, place, *refs):
    owners, owner_heads, home_rows, rows, cache_here, step = shape
    *query_refs, key_own, key_other, value_own, value_other, key_fresh, value_fresh = refs[:-8]
    lens, row_ids, out, q_rows, q_turned, hidden, scores, probs = refs[-8:]
    chip, start_own, start_other, side_here, ring_here = place[0], place[1], place[2], place[4], place[5]
    near = rows // home_rows // 2
    pack = HD // rows
    groups = owner_heads // pack

    @pl.when(pl.program_id(0) == 0)
    def _():
        lanes = lens.shape[1]
        for part, start in enumerate((start_own, start_other)):
            positions = start + lax.broadcasted_iota(jnp.int32, (cache_here, lanes), 0)
            hidden[part * cache_here : (part + 1) * cache_here, :] = jnp.where(
                positions < lens[...], 0.0, MASKED
            )
        token = chip * home_rows + lax.broadcasted_iota(jnp.int32, (home_rows, lanes), 0)
        hidden[2 * cache_here :, :] = jnp.where(token == row_ids[...], 0.0, MASKED)

    for k, piece in enumerate(query_refs):
        side = side_here if k < near else 1 - side_here
        spot = 2 * (lax.rem(ring_here, near) ^ (k % near)) + side
        q_rows[pl.ds(pl.multiple_of(spot * home_rows, home_rows), home_rows), :] = piece[...]

    factor = LOG2E / math.sqrt(HD)
    for n in range(owners * groups):
        block = jnp.concatenate(
            [q_rows[:, h * HD : (h + 1) * HD] for h in range(n * pack, (n + 1) * pack)], axis=0
        )
        scaled = block.T.astype(F32) * factor
        coarse = scaled.astype(BF16)
        q_turned[:HD, n * HD : (n + 1) * HD] = coarse
        q_turned[HD:, n * HD : (n + 1) * HD] = (scaled - coarse.astype(F32)).astype(BF16)
    wide = owners * groups * HD

    def score(keys, at):
        s = nn_dot(jnp.concatenate([keys, keys], axis=1), q_turned[...])
        return s + jnp.concatenate([hidden[at, :]] * (owners * groups), axis=1)

    s_new = score(key_fresh[...], slice(2 * cache_here, 2 * cache_here + home_rows))
    run = jnp.max(s_new.reshape(home_rows // 8, 8, wide), axis=0)
    pieces = [(part, i) for part in range(2) for i in range(0, cache_here, step)]
    for part, i in pieces:
        at = slice(part * cache_here + i, part * cache_here + i + step)
        s = score((key_own, key_other)[part][i : i + step, :], at)
        scores[at, :] = s
        run = jnp.maximum(run, jnp.max(s.reshape(step // 8, 8, wide), axis=0))
    peak = jnp.maximum(jnp.max(run, axis=0, keepdims=True), FLOOR).astype(BF16).astype(F32)
    p_new = jnp.exp2((s_new - peak).astype(BF16))
    for part, i in pieces:
        at = slice(part * cache_here + i, part * cache_here + i + step)
        probs[at, :] = jnp.exp2((scores[at, :] - peak).astype(BF16))
    ones = jnp.ones((STATS, cache_here), BF16)
    sums = nn_dot(jnp.concatenate([value_own[...], ones], axis=0), probs[:cache_here, :])
    sums = sums + nn_dot(jnp.concatenate([value_other[...], ones], axis=0), probs[cache_here:, :])
    numer = sums[:HD] + nn_dot(value_fresh[...].astype(F32).T.astype(BF16), p_new)
    denom = sums[HD : HD + 1] + jnp.sum(p_new.astype(F32), axis=0, keepdims=True)
    high = denom.astype(BF16).astype(F32)
    low = denom - high
    for owner in range(owners):
        lanes = [slice((owner * groups + k) * HD, (owner * groups + k + 1) * HD) for k in range(groups)]
        for k, cols in enumerate(lanes):
            out[owner, k * HD : (k + 1) * HD, :] = numer[:, cols].astype(BF16)
        filled = [kind[:, cols] for kind in (peak, high, low) for cols in lanes]
        filled += [jnp.zeros_like(filled[0])] * (STATS - len(filled))
        out[owner, groups * HD :, :] = jnp.concatenate(filled, axis=0).astype(BF16)


def attention(place, query_blocks, keys, values, new_key, new_value, lens, row_ids, chips, kv_heads):
    home_rows = new_key.shape[0]
    rows = home_rows * len(query_blocks)
    cache_here = keys[0].shape[0]
    owners = chips // kv_heads
    columns = query_blocks[0][0].shape[1] // kv_heads
    owner_heads = columns // HD // owners
    wide = rows * columns // HD
    height = owner_heads * rows + STATS
    step = 512
    positions = 2 * cache_here + home_rows
    kv = lambda g, place: (0, g)
    whole = lambda g, place: (0, 0)
    shape = (owners, owner_heads, home_rows, rows, cache_here, step)
    work = wide * kv_heads * 2 * cache_here
    return pl.pallas_call(
        functools.partial(attention_body, shape),
        grid_spec=pltpu.PrefetchScalarGridSpec(
            num_scalar_prefetch=1,
            grid=(kv_heads,),
            in_specs=[
                pl.BlockSpec((home_rows, columns), functools.partial(lambda n, g, place: (n, g), n))
                for _, n in query_blocks
            ]
            + [pl.BlockSpec((cache_here, HD), kv)] * 2
            + [pl.BlockSpec((HD, cache_here), lambda g, place: (g, 0))] * 2
            + [pl.BlockSpec((home_rows, HD), kv)] * 2
            + [pl.BlockSpec(lens.shape, whole)] * 2,
            out_specs=pl.BlockSpec((owners, height, HD), lambda g, place: (g, 0, 0)),
            scratch_shapes=[
                pltpu.VMEM((rows, columns), BF16),
                pltpu.VMEM((2 * HD, wide), BF16),
                pltpu.VMEM((positions, HD), F32),
                pltpu.VMEM((2 * cache_here, wide), F32),
                pltpu.VMEM((2 * cache_here, wide), BF16),
            ],
        ),
        out_shape=jax.ShapeDtypeStruct((chips, height, HD), BF16),
        compiler_params=pltpu.CompilerParams(vmem_limit_bytes=32 * MIB),
        cost_estimate=pl.CostEstimate(
            flops=6 * work * HD, bytes_accessed=8 * MIB, transcendentals=work
        ),
        name="attention",
    )(
        place,
        *[block for block, _ in query_blocks],
        pltpu.with_memory_space_constraint(keys[0], pltpu.HBM),
        keys[1],
        *values,
        pltpu.with_memory_space_constraint(new_key, pltpu.HBM),
        pltpu.with_memory_space_constraint(new_value, pltpu.HBM),
        lens,
        row_ids,
    )


def project_body(rows, place, *refs):
    *chunks, weight_own, weight_other, out, turned = refs
    core = place[3]
    chips, height, _ = chunks[0].shape
    base = height - STATS
    groups = base // HD
    pack = HD // rows
    heads_here = groups * pack // CORES
    half = chips // 2 // 2
    for near in range(2):
        sources = [chunks[s // 2 // half ^ near].at[s] for s in range(chips)]
        stats = [part[base:, :].astype(F32) for part in sources]
        peaks = [stat[:groups] for stat in stats]
        top = functools.reduce(jnp.maximum, peaks)
        share = [jnp.exp2(peak - top) for peak in peaks]
        denom = sum(w * (t[groups : 2 * groups] + t[2 * groups : 3 * groups]) for w, t in zip(share, stats))
        for k in range(groups):
            numer = sum(
                part[k * HD : (k + 1) * HD, :].astype(F32) * w[k : k + 1, :] for part, w in zip(sources, share)
            )
            attended = (numer / denom[k : k + 1, :]).T.astype(BF16)
            for j in range(pack):
                part, h = divmod(k * pack + j, heads_here)
                turned[part, near * rows : (near + 1) * rows, h * HD : (h + 1) * HD] = attended[
                    j * rows : (j + 1) * rows
                ]
    product = nn_dot(turned[core], weight_own[...]) + nn_dot(turned[1 - core], weight_other[...])
    out[...] = product.astype(BF16)


def project(place, chunks, weight_own, weight_other, rows):
    depth, width = weight_own.shape
    vmem = pl.BlockSpec(memory_space=pltpu.VMEM)
    return pl.pallas_call(
        functools.partial(project_body, rows),
        in_specs=[pl.BlockSpec(memory_space=pltpu.SMEM)] + [vmem] * (len(chunks) + 2),
        out_specs=vmem,
        out_shape=jax.ShapeDtypeStruct((2 * rows, width), BF16),
        scratch_shapes=[pltpu.VMEM((CORES, 2 * rows, depth), BF16)],
        compiler_params=pltpu.CompilerParams(vmem_limit_bytes=32 * MIB),
        cost_estimate=pl.CostEstimate(
            flops=8 * rows * width * depth, bytes_accessed=4 * MIB, transcendentals=0
        ),
        name="project",
    )(place, *chunks, weight_own, weight_other)


def norm_body(parts, residual, gain, chooser, middle_out, sent):
    total = parts[0].astype(F32)
    for s in range(1, parts.shape[0]):
        total = total + parts[s].astype(F32)
    middle = (residual[...].astype(F32) + total).astype(BF16)
    middle_out[...] = middle
    middle = middle.astype(F32)
    inv_rms = lax.rsqrt(jnp.mean(middle * middle, axis=-1, keepdims=True) + 1e-06)
    normed = (middle * inv_rms * gain[...].astype(F32)).astype(BF16)
    sent[...] = nn_dot(chooser[...], normed).astype(BF16)


def norm_and_dispatch(parts, residual, gain, chooser):
    vmem = pl.BlockSpec(memory_space=pltpu.VMEM)
    rows, width = residual.shape
    return pl.pallas_call(
        norm_body,
        in_specs=[vmem] * 4,
        out_specs=[vmem] * 2,
        out_shape=[
            jax.ShapeDtypeStruct((rows, width), BF16),
            jax.ShapeDtypeStruct((chooser.shape[0], width), BF16),
        ],
        compiler_params=pltpu.CompilerParams(vmem_limit_bytes=24 * MIB),
        cost_estimate=pl.CostEstimate(
            flops=2 * chooser.shape[0] * rows * width, bytes_accessed=2 * MIB, transcendentals=0
        ),
        name="norm_and_dispatch",
    )(parts, residual, gain, chooser)


def experts_body(step, arrived, w_gate, w_up, w_down, out, gate_held, up_held, down_held, sems):
    experts, _, depth = w_gate.shape
    rows, width = arrived.shape
    pieces = [(e, f) for e in range(experts) for f in range(0, depth, step)]
    copies = []
    for n, (e, f) in enumerate(pieces):
        down = pl.ds(f, step)
        copies.append(
            [
                pltpu.make_async_copy(w_gate.at[e, :, down], gate_held.at[n], sems.at[n, 0]),
                pltpu.make_async_copy(w_up.at[e, :, down], up_held.at[n], sems.at[n, 1]),
                pltpu.make_async_copy(w_down.at[e, down, :], down_held.at[n], sems.at[n, 2]),
            ]
        )
    for piece in copies:
        for copy in piece[:2]:
            copy.start()
    for piece in copies:
        piece[2].start()
    slot = lax.broadcasted_iota(jnp.int32, (rows, 1), 0)
    values = arrived[...]
    hidden = []
    for n, (e, f) in enumerate(pieces):
        copies[n][0].wait()
        copies[n][1].wait()
        gate = nn_dot(values, gate_held[n])
        upward = nn_dot(values, up_held[n])
        part = gate / (1.0 + jnp.exp(-gate)) * upward
        mine = lax.rem(slot, experts * MOST) // MOST == e
        hidden.append(jnp.where(mine, part, 0.0).astype(BF16))
    total = None
    for n in range(len(pieces)):
        copies[n][2].wait()
        term = nn_dot(hidden[n], down_held[n])
        total = term if total is None else total + term
    out[...] = total.astype(BF16)


def run_experts(arrived, w_gate, w_up, w_down):
    rows, width = arrived.shape
    experts, _, depth = w_gate.shape
    step = 256
    pieces = experts * depth // step
    vmem = pl.BlockSpec(memory_space=pltpu.VMEM)
    hbm = pl.BlockSpec(memory_space=pltpu.HBM)
    weights = [pltpu.with_memory_space_constraint(w, pltpu.HBM) for w in (w_gate, w_up, w_down)]
    return pl.pallas_call(
        functools.partial(experts_body, step),
        in_specs=[vmem] + [hbm] * 3,
        out_specs=vmem,
        out_shape=jax.ShapeDtypeStruct((rows, width), BF16),
        scratch_shapes=[
            pltpu.VMEM((pieces, width, step), BF16),
            pltpu.VMEM((pieces, width, step), BF16),
            pltpu.VMEM((pieces, step, width), BF16),
            pltpu.SemaphoreType.DMA((pieces, 3)),
        ],
        compiler_params=pltpu.CompilerParams(vmem_limit_bytes=44 * MIB),
        cost_estimate=pl.CostEstimate(
            flops=6 * rows * width * experts * depth,
            bytes_accessed=6 * width * experts * depth,
            transcendentals=rows * experts * depth,
        ),
        name="experts",
    )(arrived, *weights)


def mix_body(returned, coarse, fine, middle, out):
    values = returned[...]
    mixed = nn_dot(coarse[...], values) + nn_dot(fine[...], values)
    out[...] = (middle[...].astype(F32) + mixed).astype(BF16)


def mix(returned, coarse, fine, middle):
    vmem = pl.BlockSpec(memory_space=pltpu.VMEM)
    return pl.pallas_call(
        mix_body,
        in_specs=[vmem] * 4,
        out_specs=vmem,
        out_shape=jax.ShapeDtypeStruct(middle.shape, BF16),
        compiler_params=pltpu.CompilerParams(vmem_limit_bytes=16 * MIB),
        name="mix",
    )(returned, coarse, fine, middle)


def on_device(
    queries,
    new_key,
    new_value,
    key_cache,
    value_cache,
    cache_len,
    out_weight,
    residual,
    norm_gain,
    expert_ids,
    route_weight,
    w_gate,
    w_up,
    w_down,
):
    devices = lax.axis_size("ctx")
    chips = devices // CORES
    index = lax.axis_index("ctx")
    chip, core = index // CORES, index % CORES
    home_rows, width = residual.shape
    top = expert_ids.shape[1]
    heads_here = out_weight.shape[0] // HD
    cache_here = key_cache.shape[0]
    same_core = [[CORES * j + c for j in range(chips)] for c in range(CORES)]
    swap = [(i, i ^ 1) for i in range(devices)]

    across = [(i, i ^ CORES) for i in range(devices)]
    rings = chips // 2
    half = rings // 2
    chunk_rows = 2 * half * home_rows

    def across_y(block):
        return lax.ppermute(block, "ctx", across)

    neighbour = across_y(queries)
    by_ring = [queries] + [
        lax.ppermute(queries, "ctx", [(i, i ^ (2 * CORES * k)) for i in range(devices)])
        for k in range(1, rings)
    ]
    near_blocks = [(pltpu.with_memory_space_constraint(queries, pltpu.HBM), 0)]
    near_blocks += [(block, 0) for block in by_ring[1:half]]
    near_blocks += [(neighbour, 0)] + [(across_y(block), 0) for block in by_ring[1:half]]
    far = jnp.concatenate(by_ring[half:], axis=0)
    far_across = across_y(far)
    far_blocks = [(far, k) for k in range(half)] + [(far_across, k) for k in range(half)]
    late_keys, late_values, _ = lax.optimization_barrier((key_cache, value_cache, neighbour))
    key_other = lax.ppermute(late_keys, "ctx", swap)
    value_turned = late_values.T
    value_other = lax.ppermute(value_turned, "ctx", swap)
    place = jnp.stack([chip, index * cache_here, (index ^ 1) * cache_here, core, chip % 2, chip // 2]).astype(jnp.int32)

    def in_lanes(by_chip, n):
        first = (chip // CORES // half ^ n) * chips // 2
        here = lax.dynamic_slice_in_dim(by_chip, first, chips // 2, 0).reshape(1, chunk_rows)
        return jnp.tile(here, (1, HD // chunk_rows))

    len_by_chip = lax.dynamic_slice_in_dim(
        cache_len.reshape(chips, CORES * home_rows), core * home_rows, home_rows, 1
    )
    number_by_chip = jnp.arange(chips * home_rows, dtype=jnp.int32).reshape(chips, home_rows)
    lens = [in_lanes(len_by_chip, n) for n in range(2)]
    row_ids = [in_lanes(number_by_chip, n) for n in range(2)]

    flat_ids = expert_ids.reshape(-1)
    picks = jnp.arange(flat_ids.shape[0])
    earlier = (flat_ids[:, None] == flat_ids[None, :]) & (picks[None, :] < picks[:, None])
    target = (flat_ids * MOST + jnp.sum(earlier, axis=1, dtype=jnp.int32)).reshape(home_rows, top)
    experts = w_gate.shape[0]
    slots = experts * devices * MOST
    takes = target[:, :, None] == jnp.arange(slots, dtype=jnp.int32)
    chooser = jnp.any(takes, axis=1).T.astype(BF16)
    spread = jnp.sum(jnp.where(takes, route_weight[:, :, None], 0.0), axis=1)
    coarse = spread.astype(BF16)
    fine = (spread - coarse.astype(F32)).astype(BF16)

    gathered = []
    for chunk, blocks in enumerate((near_blocks, far_blocks)):
        sums = attention(
            place,
            blocks,
            (key_cache, key_other),
            (value_turned, value_other),
            new_key,
            new_value,
            lens[chunk],
            row_ids[chunk],
            chips,
            key_cache.shape[1] // HD,
        )
        if chunk:
            sums, gathered[-1] = lax.optimization_barrier((sums, gathered[-1]))
        else:
            sums, place, late_weight, _ = lax.optimization_barrier((sums, place, out_weight, far_across))
        gathered.append(
            lax.all_to_all(
                sums, "ctx", split_axis=0, concat_axis=0, axis_index_groups=same_core, tiled=True
            )
        )
    weight_other = lax.ppermute(late_weight, "ctx", swap)
    share = project(place, gathered, out_weight, weight_other, chunk_rows)
    shares = lax.all_to_all(
        share.reshape(chips, home_rows, width),
        "ctx",
        split_axis=0,
        concat_axis=0,
        axis_index_groups=same_core,
        tiled=True,
    )
    middle, outgoing = norm_and_dispatch(shares, residual, norm_gain.reshape(1, width), chooser)
    arrived = lax.all_to_all(
        outgoing.reshape(devices, experts * MOST, width), "ctx", split_axis=0, concat_axis=0, tiled=True
    )
    produced = run_experts(arrived.reshape(slots, width), w_gate, w_up, w_down)
    returned = lax.all_to_all(
        produced.reshape(devices, experts * MOST, width), "ctx", split_axis=0, concat_axis=0, tiled=True
    )
    return mix(returned.reshape(slots, width), coarse, fine, middle)


def solution(mesh):
    placed = (
        P(("groups", "ctx"), None),
        P(("groups", "ctx"), None),
        P(("groups", "ctx"), None),
        P(("groups", "ctx"), None),
        P(("groups", "ctx"), None),
        P("groups"),
        P("ctx", None),
        P(("groups", "ctx"), None),
        P(),
        P(("groups", "ctx"), None),
        P(("groups", "ctx"), None),
        P("ctx", None, None),
        P("ctx", None, None),
        P("ctx", None, None),
    )
    return jax.shard_map(
        on_device, mesh=mesh, in_specs=placed, out_specs=P(("groups", "ctx"), None), check_vma=False
    )
```

```python
import functools
import math

import jax
import jax.numpy as jnp
from jax import lax
from jax.experimental import pallas as pl
from jax.experimental.pallas import tpu as pltpu
from jax.sharding import PartitionSpec as P

HD = 128
MOST = 4
CORES = 2
STATS = 16
MASKED = -1e30
FLOOR = -1e20
LOG2E = math.log2(math.e)
MIB = 1024 * 1024
F32 = jnp.float32
BF16 = jnp.bfloat16


def nt_dot(a, b):
    return lax.dot_general(a, b, (((1,), (1,)), ((), ())), preferred_element_type=F32)


def nn_dot(a, b):
    return lax.dot_general(a, b, (((1,), (0,)), ((), ())), preferred_element_type=F32)


def attention_body(shape, chips, place, *refs):
    owners, owner_heads, home_rows, rows, cache_here, step = shape
    q_rows, q_turned, hidden, scores, probs, held = refs[-6:]
    outs = refs[-6 - chips : -6]
    *query_refs, key_own, key_other, value_own, value_other, key_fresh, value_fresh, lens, row_ids = refs[: -6 - chips]
    chip, start_own, start_other, side_here, ring_here = place[0], place[1], place[2], place[4], place[5]
    near = rows // home_rows // 2
    pack = HD // rows
    groups = owner_heads // pack

    @pl.when(pl.program_id(0) == 0)
    def _():
        lanes = lens.shape[1]
        for part, start in enumerate((start_own, start_other)):
            positions = start + lax.broadcasted_iota(jnp.int32, (cache_here, lanes), 0)
            hidden[part * cache_here : (part + 1) * cache_here, :] = jnp.where(
                positions < lens[...], 0.0, MASKED
            )
        token = chip * home_rows + lax.broadcasted_iota(jnp.int32, (home_rows, lanes), 0)
        hidden[2 * cache_here :, :] = jnp.where(token == row_ids[...], 0.0, MASKED)

    for k, piece in enumerate(query_refs):
        side = side_here if k < near else 1 - side_here
        spot = 2 * (lax.rem(ring_here, near) ^ (k % near)) + side
        q_rows[pl.ds(pl.multiple_of(spot * home_rows, home_rows), home_rows), :] = piece[...]

    factor = LOG2E / math.sqrt(HD)
    for n in range(owners * groups):
        block = jnp.concatenate(
            [q_rows[:, h * HD : (h + 1) * HD] for h in range(n * pack, (n + 1) * pack)], axis=0
        )
        scaled = block.T.astype(F32) * factor
        coarse = scaled.astype(BF16)
        q_turned[:HD, n * HD : (n + 1) * HD] = coarse
        q_turned[HD:, n * HD : (n + 1) * HD] = (scaled - coarse.astype(F32)).astype(BF16)
    wide = owners * groups * HD

    def score(keys):
        return nn_dot(jnp.concatenate([keys, keys], axis=1), q_turned[...])

    def masked(s, at):
        return s + jnp.concatenate([hidden[at, :]] * (owners * groups), axis=1)

    s_new = masked(score(key_fresh[...]), slice(2 * cache_here, 2 * cache_here + home_rows))
    run = jnp.max(s_new.reshape(home_rows // 8, 8, wide), axis=0)
    for part, keys in enumerate((key_own, key_other)):
        for i in range(0, cache_here, step):
            scores[part * cache_here + i : part * cache_here + i + step, :] = score(keys[i : i + step, :])
    fine_step = 64
    pieces = [slice(i, i + fine_step) for i in range(0, 2 * cache_here, fine_step)]
    for at in pieces:
        run = jnp.maximum(run, jnp.max(masked(scores[at, :], at).reshape(fine_step // 8, 8, wide), axis=0))
    peak = jnp.maximum(jnp.max(run, axis=0, keepdims=True), FLOOR).astype(BF16).astype(F32)
    p_new = jnp.exp2((s_new - peak).astype(BF16))
    for at in pieces:
        probs[at, :] = jnp.exp2((masked(scores[at, :], at) - peak).astype(BF16))
    ones = jnp.ones((STATS, cache_here), BF16)
    sums = nn_dot(jnp.concatenate([value_own[...], ones], axis=0), probs[:cache_here, :])
    sums = sums + nn_dot(jnp.concatenate([value_other[...], ones], axis=0), probs[cache_here:, :])
    numer = sums[:HD] + nn_dot(value_fresh[...].astype(F32).T.astype(BF16), p_new)
    denom = sums[HD : HD + 1] + jnp.sum(p_new.astype(F32), axis=0, keepdims=True)
    high = denom.astype(BF16).astype(F32)
    low = denom - high
    for owner in range(owners):
        distance = (pl.program_id(0) * owners + owner) ^ chip
        lanes = [slice((owner * groups + k) * HD, (owner * groups + k + 1) * HD) for k in range(groups)]
        for k, cols in enumerate(lanes):
            held[distance, k * HD : (k + 1) * HD, :] = numer[:, cols].astype(BF16)
        filled = [kind[:, cols] for kind in (peak, high, low) for cols in lanes]
        filled += [jnp.zeros_like(filled[0])] * (STATS - len(filled))
        held[distance, groups * HD :, :] = jnp.concatenate(filled, axis=0).astype(BF16)

    @pl.when(pl.program_id(0) == pl.num_programs(0) - 1)
    def _():
        for k, out in enumerate(outs):
            out[...] = held[k]


def attention(place, query_blocks, keys, values, new_key, new_value, lens, row_ids, chips, kv_heads):
    home_rows = new_key.shape[0]
    rows = home_rows * len(query_blocks)
    cache_here = keys[0].shape[0]
    owners = chips // kv_heads
    columns = query_blocks[0][0].shape[1] // kv_heads
    owner_heads = columns // HD // owners
    wide = rows * columns // HD
    height = owner_heads * rows + STATS
    step = 512
    positions = 2 * cache_here + home_rows
    kv = lambda g, place: (0, g)
    whole = lambda g, place: (0, 0)
    shape = (owners, owner_heads, home_rows, rows, cache_here, step)
    work = wide * kv_heads * 2 * cache_here
    return pl.pallas_call(
        functools.partial(attention_body, shape, chips),
        grid_spec=pltpu.PrefetchScalarGridSpec(
            num_scalar_prefetch=1,
            grid=(kv_heads,),
            in_specs=[
                pl.BlockSpec((home_rows, columns), functools.partial(lambda n, g, place: (n, g), n))
                for _, n in query_blocks
            ]
            + [pl.BlockSpec((cache_here, HD), kv)] * 2
            + [pl.BlockSpec((HD, cache_here), lambda g, place: (g, 0))] * 2
            + [pl.BlockSpec((home_rows, HD), kv)] * 2
            + [pl.BlockSpec(lens.shape, whole)] * 2,
            out_specs=[pl.BlockSpec((height, HD), whole)] * chips,
            scratch_shapes=[
                pltpu.VMEM((rows, columns), BF16),
                pltpu.VMEM((2 * HD, wide), BF16),
                pltpu.VMEM((positions, HD), F32),
                pltpu.VMEM((2 * cache_here, wide), F32),
                pltpu.VMEM((2 * cache_here, wide), BF16),
                pltpu.VMEM((chips, height, HD), BF16),
            ],
        ),
        out_shape=[jax.ShapeDtypeStruct((height, HD), BF16)] * chips,
        compiler_params=pltpu.CompilerParams(vmem_limit_bytes=32 * MIB),
        cost_estimate=pl.CostEstimate(
            flops=6 * work * HD, bytes_accessed=8 * MIB, transcendentals=work
        ),
        name="attention",
    )(
        place,
        *[block for block, _ in query_blocks],
        pltpu.with_memory_space_constraint(keys[0], pltpu.HBM),
        keys[1],
        *values,
        pltpu.with_memory_space_constraint(new_key, pltpu.HBM),
        pltpu.with_memory_space_constraint(new_value, pltpu.HBM),
        lens,
        row_ids,
    )


def project_body(rows, chips, place, *refs):
    chunks = refs[:chips], refs[chips : 2 * chips]
    weight_own, weight_other = refs[2 * chips : 2 * chips + 2]
    *outs, turned, product = refs[2 * chips + 2 :]
    chip, core, ring = place[0], place[3], place[5]
    base = chunks[0][0].shape[0] - STATS
    groups = base // HD
    pack = HD // rows
    heads_here = groups * pack // CORES
    half = chips // 2 // 2
    for near in range(2):
        sources = [chunks[near ^ (k // 2 // half)][k] for k in range(chips)]
        stats = [source[base:, :].astype(F32) for source in sources]
        peaks = [stat[:groups] for stat in stats]
        top = functools.reduce(jnp.maximum, peaks)
        share = [jnp.exp2(peak - top) for peak in peaks]
        denom = sum(w * (t[groups : 2 * groups] + t[2 * groups : 3 * groups]) for w, t in zip(share, stats))
        first = pl.multiple_of((ring // half ^ near) * rows, rows)
        for k in range(groups):
            numer = sum(
                source[k * HD : (k + 1) * HD, :].astype(F32) * w[k : k + 1, :]
                for source, w in zip(sources, share)
            )
            attended = (numer / denom[k : k + 1, :]).T.astype(BF16)
            for j in range(pack):
                part, h = divmod(k * pack + j, heads_here)
                turned[part, pl.ds(first, rows), h * HD : (h + 1) * HD] = attended[j * rows : (j + 1) * rows]
    total = nn_dot(turned[core], weight_own[...]) + nn_dot(turned[1 - core], weight_other[...])
    product[...] = total.astype(BF16)
    for k, out in enumerate(outs):
        home_rows = out.shape[0]
        out[...] = product[pl.ds(pl.multiple_of((chip ^ k) * home_rows, home_rows), home_rows), :]


def project(place, chunks, weight_own, weight_other, rows):
    chips = len(chunks[0])
    depth, width = weight_own.shape
    vmem = pl.BlockSpec(memory_space=pltpu.VMEM)
    return pl.pallas_call(
        functools.partial(project_body, rows, chips),
        in_specs=[pl.BlockSpec(memory_space=pltpu.SMEM)] + [vmem] * (2 * chips + 2),
        out_specs=[vmem] * chips,
        out_shape=[jax.ShapeDtypeStruct((2 * rows // chips, width), BF16)] * chips,
        scratch_shapes=[
            pltpu.VMEM((CORES, 2 * rows, depth), BF16),
            pltpu.VMEM((2 * rows, width), BF16),
        ],
        compiler_params=pltpu.CompilerParams(vmem_limit_bytes=32 * MIB),
        cost_estimate=pl.CostEstimate(
            flops=8 * rows * width * depth, bytes_accessed=4 * MIB, transcendentals=0
        ),
        name="project",
    )(place, *chunks[0], *chunks[1], weight_own, weight_other)


def norm_body(*refs):
    *parts, residual, gain, chooser, middle_out, sent = refs
    total = sum(part[...].astype(F32) for part in parts)
    middle = (residual[...].astype(F32) + total).astype(BF16)
    middle_out[...] = middle
    middle = middle.astype(F32)
    inv_rms = lax.rsqrt(jnp.mean(middle * middle, axis=-1, keepdims=True) + 1e-06)
    normed = (middle * inv_rms * gain[...].astype(F32)).astype(BF16)
    sent[...] = nn_dot(chooser[...], normed).astype(BF16)


def norm_and_dispatch(parts, residual, gain, chooser):
    vmem = pl.BlockSpec(memory_space=pltpu.VMEM)
    rows, width = residual.shape
    return pl.pallas_call(
        norm_body,
        in_specs=[vmem] * (len(parts) + 3),
        out_specs=[vmem] * 2,
        out_shape=[
            jax.ShapeDtypeStruct((rows, width), BF16),
            jax.ShapeDtypeStruct((chooser.shape[0], width), BF16),
        ],
        compiler_params=pltpu.CompilerParams(vmem_limit_bytes=24 * MIB),
        cost_estimate=pl.CostEstimate(
            flops=2 * chooser.shape[0] * rows * width, bytes_accessed=2 * MIB, transcendentals=0
        ),
        name="norm_and_dispatch",
    )(*parts, residual, gain, chooser)


def experts_body(step, arrived, w_gate, w_up, w_down, out, gate_held, up_held, down_held, sems):
    experts, _, depth = w_gate.shape
    rows, width = arrived.shape
    pieces = [(e, f) for e in range(experts) for f in range(0, depth, step)]
    copies = []
    for n, (e, f) in enumerate(pieces):
        down = pl.ds(f, step)
        copies.append(
            [
                pltpu.make_async_copy(w_gate.at[e, :, down], gate_held.at[n], sems.at[n, 0]),
                pltpu.make_async_copy(w_up.at[e, :, down], up_held.at[n], sems.at[n, 1]),
                pltpu.make_async_copy(w_down.at[e, down, :], down_held.at[n], sems.at[n, 2]),
            ]
        )
    for piece in copies:
        for copy in piece[:2]:
            copy.start()
    for piece in copies:
        piece[2].start()
    slot = lax.broadcasted_iota(jnp.int32, (rows, 1), 0)
    values = arrived[...]
    hidden = []
    for n, (e, f) in enumerate(pieces):
        copies[n][0].wait()
        copies[n][1].wait()
        gate = nn_dot(values, gate_held[n])
        upward = nn_dot(values, up_held[n])
        part = gate / (1.0 + jnp.exp(-gate)) * upward
        mine = lax.rem(slot, experts * MOST) // MOST == e
        hidden.append(jnp.where(mine, part, 0.0).astype(BF16))
    total = None
    for n in range(len(pieces)):
        copies[n][2].wait()
        term = nn_dot(hidden[n], down_held[n])
        total = term if total is None else total + term
    out[...] = total.astype(BF16)


def run_experts(arrived, w_gate, w_up, w_down):
    rows, width = arrived.shape
    experts, _, depth = w_gate.shape
    step = 256
    pieces = experts * depth // step
    vmem = pl.BlockSpec(memory_space=pltpu.VMEM)
    hbm = pl.BlockSpec(memory_space=pltpu.HBM)
    weights = [pltpu.with_memory_space_constraint(w, pltpu.HBM) for w in (w_gate, w_up, w_down)]
    return pl.pallas_call(
        functools.partial(experts_body, step),
        in_specs=[vmem] + [hbm] * 3,
        out_specs=vmem,
        out_shape=jax.ShapeDtypeStruct((rows, width), BF16),
        scratch_shapes=[
            pltpu.VMEM((pieces, width, step), BF16),
            pltpu.VMEM((pieces, width, step), BF16),
            pltpu.VMEM((pieces, step, width), BF16),
            pltpu.SemaphoreType.DMA((pieces, 3)),
        ],
        compiler_params=pltpu.CompilerParams(vmem_limit_bytes=44 * MIB),
        cost_estimate=pl.CostEstimate(
            flops=6 * rows * width * experts * depth,
            bytes_accessed=6 * width * experts * depth,
            transcendentals=rows * experts * depth,
        ),
        name="experts",
    )(arrived, *weights)


def mix_body(returned, coarse, fine, middle, out):
    values = returned[...]
    mixed = nn_dot(coarse[...], values) + nn_dot(fine[...], values)
    out[...] = (middle[...].astype(F32) + mixed).astype(BF16)


def mix(returned, coarse, fine, middle):
    vmem = pl.BlockSpec(memory_space=pltpu.VMEM)
    return pl.pallas_call(
        mix_body,
        in_specs=[vmem] * 4,
        out_specs=vmem,
        out_shape=jax.ShapeDtypeStruct(middle.shape, BF16),
        compiler_params=pltpu.CompilerParams(vmem_limit_bytes=16 * MIB),
        name="mix",
    )(returned, coarse, fine, middle)


def on_device(
    queries,
    new_key,
    new_value,
    key_cache,
    value_cache,
    cache_len,
    out_weight,
    residual,
    norm_gain,
    expert_ids,
    route_weight,
    w_gate,
    w_up,
    w_down,
):
    devices = lax.axis_size("ctx")
    chips = devices // CORES
    index = lax.axis_index("ctx")
    chip, core = index // CORES, index % CORES
    home_rows, width = residual.shape
    top = expert_ids.shape[1]
    heads_here = out_weight.shape[0] // HD
    cache_here = key_cache.shape[0]

    def to_peers(blocks):
        return blocks[:1] + [
            lax.ppermute(block, "ctx", [(i, i ^ (CORES * k)) for i in range(devices)])
            for k, block in enumerate(blocks)
            if k
        ]

    swap = [(i, i ^ 1) for i in range(devices)]

    across = [(i, i ^ CORES) for i in range(devices)]
    rings = chips // 2
    half = rings // 2
    chunk_rows = 2 * half * home_rows

    def across_y(block):
        return lax.ppermute(block, "ctx", across)

    neighbour = across_y(queries)
    by_ring = [queries] + [
        lax.ppermute(queries, "ctx", [(i, i ^ (2 * CORES * k)) for i in range(devices)])
        for k in range(1, rings)
    ]
    near_blocks = [(pltpu.with_memory_space_constraint(queries, pltpu.HBM), 0)]
    near_blocks += [(block, 0) for block in by_ring[1:half]]
    near_blocks += [(neighbour, 0)] + [(across_y(block), 0) for block in by_ring[1:half]]
    far = jnp.concatenate(by_ring[half:], axis=0)
    far_across = across_y(far)
    far_blocks = [(far, k) for k in range(half)] + [(far_across, k) for k in range(half)]
    late_keys, late_values, _ = lax.optimization_barrier((key_cache, value_cache, neighbour))
    key_other = lax.ppermute(late_keys, "ctx", swap)
    value_turned = late_values.T
    value_other = lax.ppermute(value_turned, "ctx", swap)
    place = jnp.stack([chip, index * cache_here, (index ^ 1) * cache_here, core, chip % 2, chip // 2]).astype(jnp.int32)

    def in_lanes(by_chip, n):
        first = (chip // CORES // half ^ n) * chips // 2
        here = lax.dynamic_slice_in_dim(by_chip, first, chips // 2, 0).reshape(1, chunk_rows)
        return jnp.tile(here, (1, HD // chunk_rows))

    len_by_chip = lax.dynamic_slice_in_dim(
        cache_len.reshape(chips, CORES * home_rows), core * home_rows, home_rows, 1
    )
    number_by_chip = jnp.arange(chips * home_rows, dtype=jnp.int32).reshape(chips, home_rows)
    lens = [in_lanes(len_by_chip, n) for n in range(2)]
    row_ids = [in_lanes(number_by_chip, n) for n in range(2)]

    flat_ids = expert_ids.reshape(-1)
    picks = jnp.arange(flat_ids.shape[0])
    earlier = (flat_ids[:, None] == flat_ids[None, :]) & (picks[None, :] < picks[:, None])
    target = (flat_ids * MOST + jnp.sum(earlier, axis=1, dtype=jnp.int32)).reshape(home_rows, top)
    experts = w_gate.shape[0]
    slots = experts * devices * MOST
    takes = target[:, :, None] == jnp.arange(slots, dtype=jnp.int32)
    chooser = jnp.any(takes, axis=1).T.astype(BF16)
    spread = jnp.sum(jnp.where(takes, route_weight[:, :, None], 0.0), axis=1)
    coarse = spread.astype(BF16)
    fine = (spread - coarse.astype(F32)).astype(BF16)

    gathered = []
    for chunk, blocks in enumerate((near_blocks, far_blocks)):
        sums = attention(
            place,
            blocks,
            (key_cache, key_other),
            (value_turned, value_other),
            new_key,
            new_value,
            lens[chunk],
            row_ids[chunk],
            chips,
            key_cache.shape[1] // HD,
        )
        if chunk:
            sums, gathered[-1] = lax.optimization_barrier((sums, gathered[-1]))
        else:
            sums, place, late_weight, _ = lax.optimization_barrier((sums, place, out_weight, far_across))
        gathered.append(to_peers(list(sums)))
    weight_other = lax.ppermute(late_weight, "ctx", swap)
    shares = to_peers(list(project(place, gathered, out_weight, weight_other, chunk_rows)))
    middle, outgoing = norm_and_dispatch(shares, residual, norm_gain.reshape(1, width), chooser)
    arrived = lax.all_to_all(
        outgoing.reshape(devices, experts * MOST, width), "ctx", split_axis=0, concat_axis=0, tiled=True
    )
    produced = run_experts(arrived.reshape(slots, width), w_gate, w_up, w_down)
    returned = lax.all_to_all(
        produced.reshape(devices, experts * MOST, width), "ctx", split_axis=0, concat_axis=0, tiled=True
    )
    return mix(returned.reshape(slots, width), coarse, fine, middle)


def solution(mesh):
    placed = (
        P(("groups", "ctx"), None),
        P(("groups", "ctx"), None),
        P(("groups", "ctx"), None),
        P(("groups", "ctx"), None),
        P(("groups", "ctx"), None),
        P("groups"),
        P("ctx", None),
        P(("groups", "ctx"), None),
        P(),
        P(("groups", "ctx"), None),
        P(("groups", "ctx"), None),
        P("ctx", None, None),
        P("ctx", None, None),
        P("ctx", None, None),
    )
    return jax.shard_map(
        on_device, mesh=mesh, in_specs=placed, out_specs=P(("groups", "ctx"), None), check_vma=False
    )
```

```python
import functools
import math

import jax
import jax.numpy as jnp
from jax import lax
from jax.experimental import pallas as pl
from jax.experimental.pallas import tpu as pltpu
from jax.sharding import PartitionSpec as P

HD = 128
MOST = 4
CORES = 2
STATS = 16
MASKED = -1e30
FLOOR = -1e20
LOG2E = math.log2(math.e)
MIB = 1024 * 1024
F32 = jnp.float32
BF16 = jnp.bfloat16


def nt_dot(a, b):
    return lax.dot_general(a, b, (((1,), (1,)), ((), ())), preferred_element_type=F32)


def nn_dot(a, b):
    return lax.dot_general(a, b, (((1,), (0,)), ((), ())), preferred_element_type=F32)


def attention_body(shape, place, *refs):
    owners, owner_heads, home_rows, rows, cache_here, step = shape
    *query_refs, key_own, key_other, value_own, value_other, key_fresh, value_fresh = refs[:-8]
    lens, row_ids, out, q_rows, q_turned, hidden, scores, probs = refs[-8:]
    chip, start_own, start_other, side_here, ring_here = place[0], place[1], place[2], place[4], place[5]
    near = rows // home_rows // 2
    block_rows = HD // owner_heads
    blocks = rows // block_rows
    spots = [(owner, block) for owner in range(owners) for block in range(blocks)]

    @pl.when(pl.program_id(0) == 0)
    def _():
        lanes = lens.shape[1]
        for part, start in enumerate((start_own, start_other)):
            positions = start + lax.broadcasted_iota(jnp.int32, (cache_here, lanes), 0)
            hidden[part * cache_here : (part + 1) * cache_here, :] = jnp.where(
                positions < lens[...], 0.0, MASKED
            )
        token = chip * home_rows + lax.broadcasted_iota(jnp.int32, (home_rows, lanes), 0)
        hidden[2 * cache_here :, :] = jnp.where(token == row_ids[...], 0.0, MASKED)

    for k, piece in enumerate(query_refs):
        side = side_here if k < near else 1 - side_here
        spot = 2 * (lax.rem(ring_here, near) ^ (k % near)) + side
        q_rows[pl.ds(pl.multiple_of(spot * home_rows, home_rows), home_rows), :] = piece[...]

    factor = LOG2E / math.sqrt(HD)
    for n, (owner, block) in enumerate(spots):
        here = slice(block * block_rows, (block + 1) * block_rows)
        first = owner * owner_heads
        stacked = jnp.concatenate(
            [q_rows[here, h * HD : (h + 1) * HD] for h in range(first, first + owner_heads)], axis=0
        )
        scaled = stacked.T.astype(F32) * factor
        coarse = scaled.astype(BF16)
        q_turned[:HD, n * HD : (n + 1) * HD] = coarse
        q_turned[HD:, n * HD : (n + 1) * HD] = (scaled - coarse.astype(F32)).astype(BF16)
    wide = len(spots) * HD

    def score(keys, at):
        s = nn_dot(jnp.concatenate([keys, keys], axis=1), q_turned[...])
        return s + jnp.concatenate([hidden[at, :]] * owners, axis=1)

    s_new = score(key_fresh[...], slice(2 * cache_here, 2 * cache_here + home_rows))
    run = jnp.max(s_new.reshape(home_rows // 8, 8, wide), axis=0)
    pieces = [(part, i) for part in range(2) for i in range(0, cache_here, step)]
    for part, i in pieces:
        at = slice(part * cache_here + i, part * cache_here + i + step)
        s = score((key_own, key_other)[part][i : i + step, :], at)
        scores[at, :] = s
        run = jnp.maximum(run, jnp.max(s.reshape(step // 8, 8, wide), axis=0))
    peak = jnp.maximum(jnp.max(run, axis=0, keepdims=True), FLOOR).astype(BF16).astype(F32)
    p_new = jnp.exp2((s_new - peak).astype(BF16))
    for part, i in pieces:
        at = slice(part * cache_here + i, part * cache_here + i + step)
        probs[at, :] = jnp.exp2((scores[at, :] - peak).astype(BF16))
    ones = jnp.ones((STATS, cache_here), BF16)
    sums = nn_dot(jnp.concatenate([value_own[...], ones], axis=0), probs[:cache_here, :])
    sums = sums + nn_dot(jnp.concatenate([value_other[...], ones], axis=0), probs[cache_here:, :])
    numer = sums[:HD] + nn_dot(value_fresh[...].astype(F32).T.astype(BF16), p_new)
    denom = sums[HD : HD + 1] + jnp.sum(p_new.astype(F32), axis=0, keepdims=True)
    high = denom.astype(BF16).astype(F32)
    low = denom - high
    for owner in range(owners):
        lanes = [slice(n * HD, (n + 1) * HD) for n in range(owner * blocks, (owner + 1) * blocks)]
        for k, cols in enumerate(lanes):
            out[owner, k * HD : (k + 1) * HD, :] = numer[:, cols].astype(BF16)
        filled = [kind[:, cols] for kind in (peak, high, low) for cols in lanes]
        filled += [jnp.zeros_like(filled[0])] * (STATS - len(filled))
        out[owner, blocks * HD :, :] = jnp.concatenate(filled, axis=0).astype(BF16)


def attention(place, query_blocks, keys, values, new_key, new_value, lens, row_ids, chips, kv_heads):
    home_rows = new_key.shape[0]
    rows = home_rows * len(query_blocks)
    cache_here = keys[0].shape[0]
    owners = chips // kv_heads
    columns = query_blocks[0][0].shape[1] // kv_heads
    owner_heads = columns // HD // owners
    wide = rows * columns // HD
    height = owner_heads * rows + STATS
    step = 512
    positions = 2 * cache_here + home_rows
    kv = lambda g, place: (0, g)
    whole = lambda g, place: (0, 0)
    shape = (owners, owner_heads, home_rows, rows, cache_here, step)
    work = wide * kv_heads * 2 * cache_here
    return pl.pallas_call(
        functools.partial(attention_body, shape),
        grid_spec=pltpu.PrefetchScalarGridSpec(
            num_scalar_prefetch=1,
            grid=(kv_heads,),
            in_specs=[
                pl.BlockSpec((home_rows, columns), functools.partial(lambda n, g, place: (n, g), n))
                for _, n in query_blocks
            ]
            + [pl.BlockSpec((cache_here, HD), kv)] * 2
            + [pl.BlockSpec((HD, cache_here), lambda g, place: (g, 0))] * 2
            + [pl.BlockSpec((home_rows, HD), kv)] * 2
            + [pl.BlockSpec(lens.shape, whole)] * 2,
            out_specs=pl.BlockSpec((owners, height, HD), lambda g, place: (g, 0, 0)),
            scratch_shapes=[
                pltpu.VMEM((rows, columns), BF16),
                pltpu.VMEM((2 * HD, wide), BF16),
                pltpu.VMEM((positions, wide // owners), F32),
                pltpu.VMEM((2 * cache_here, wide), F32),
                pltpu.VMEM((2 * cache_here, wide), BF16),
            ],
        ),
        out_shape=jax.ShapeDtypeStruct((chips, height, HD), BF16),
        compiler_params=pltpu.CompilerParams(vmem_limit_bytes=32 * MIB),
        cost_estimate=pl.CostEstimate(
            flops=6 * work * HD, bytes_accessed=8 * MIB, transcendentals=work
        ),
        name="attention",
    )(
        place,
        *[block for block, _ in query_blocks],
        pltpu.with_memory_space_constraint(keys[0], pltpu.HBM),
        keys[1],
        *values,
        pltpu.with_memory_space_constraint(new_key, pltpu.HBM),
        pltpu.with_memory_space_constraint(new_value, pltpu.HBM),
        lens,
        row_ids,
    )


def project_body(chunks_n, blocks_n, place, *refs):
    chunks = refs[:chunks_n]
    weight_own, weight_other, out, turned = refs[chunks_n:]
    core = place[3]
    chips = chunks[0].shape[0]
    heads_here = weight_own.shape[0] // HD
    rows = HD // (CORES * heads_here)
    block_chips = chips // blocks_n
    for block in range(blocks_n):
        sources, stats = [], []
        for s in range(chips):
            chunk = (s // block_chips ^ block).bit_length()
            held = chunks[chunk].at[s]
            wide = (held.shape[0] - STATS) // HD
            spot = block % wide
            sources.append(held.at[spot * HD : (spot + 1) * HD])
            stat = held[wide * HD :, :].astype(F32)
            stats.append([stat[kind * wide + spot : kind * wide + spot + 1] for kind in range(3)])
        top = functools.reduce(jnp.maximum, [peak for peak, _, _ in stats])
        share = [jnp.exp2(peak - top) for peak, _, _ in stats]
        denom = sum(w * (high + low) for w, (_, high, low) in zip(share, stats))
        numer = sum(source[...].astype(F32) * w for source, w in zip(sources, share))
        attended = (numer / denom).T.astype(BF16)
        for h in range(CORES * heads_here):
            part, column = divmod(h, heads_here)
            turned[part, block * rows : (block + 1) * rows, column * HD : (column + 1) * HD] = attended[
                h * rows : (h + 1) * rows
            ]
    product = nn_dot(turned[core], weight_own[...]) + nn_dot(turned[1 - core], weight_other[...])
    out[...] = product.astype(BF16)


def project(place, chunks, weight_own, weight_other, rows, blocks):
    depth, width = weight_own.shape
    vmem = pl.BlockSpec(memory_space=pltpu.VMEM)
    return pl.pallas_call(
        functools.partial(project_body, len(chunks), blocks),
        in_specs=[pl.BlockSpec(memory_space=pltpu.SMEM)] + [vmem] * (len(chunks) + 2),
        out_specs=vmem,
        out_shape=jax.ShapeDtypeStruct((rows, width), BF16),
        scratch_shapes=[pltpu.VMEM((CORES, rows, depth), BF16)],
        compiler_params=pltpu.CompilerParams(vmem_limit_bytes=32 * MIB),
        cost_estimate=pl.CostEstimate(
            flops=4 * rows * width * depth, bytes_accessed=4 * MIB, transcendentals=0
        ),
        name="project",
    )(place, *chunks, weight_own, weight_other)


def norm_body(parts, residual, gain, chooser, middle_out, sent):
    total = parts[0].astype(F32)
    for s in range(1, parts.shape[0]):
        total = total + parts[s].astype(F32)
    middle = (residual[...].astype(F32) + total).astype(BF16)
    middle_out[...] = middle
    middle = middle.astype(F32)
    inv_rms = lax.rsqrt(jnp.mean(middle * middle, axis=-1, keepdims=True) + 1e-06)
    normed = (middle * inv_rms * gain[...].astype(F32)).astype(BF16)
    sent[...] = nn_dot(chooser[...], normed).astype(BF16)


def norm_and_dispatch(parts, residual, gain, chooser):
    vmem = pl.BlockSpec(memory_space=pltpu.VMEM)
    rows, width = residual.shape
    return pl.pallas_call(
        norm_body,
        in_specs=[vmem] * 4,
        out_specs=[vmem] * 2,
        out_shape=[
            jax.ShapeDtypeStruct((rows, width), BF16),
            jax.ShapeDtypeStruct((chooser.shape[0], width), BF16),
        ],
        compiler_params=pltpu.CompilerParams(vmem_limit_bytes=24 * MIB),
        cost_estimate=pl.CostEstimate(
            flops=2 * chooser.shape[0] * rows * width, bytes_accessed=2 * MIB, transcendentals=0
        ),
        name="norm_and_dispatch",
    )(parts, residual, gain, chooser)


def experts_body(step, arrived, w_gate, w_up, w_down, out, gate_held, up_held, down_held, sems):
    experts, _, depth = w_gate.shape
    rows, width = arrived.shape
    pieces = [(e, f) for e in range(experts) for f in range(0, depth, step)]
    copies = []
    for n, (e, f) in enumerate(pieces):
        down = pl.ds(f, step)
        copies.append(
            [
                pltpu.make_async_copy(w_gate.at[e, :, down], gate_held.at[n], sems.at[n, 0]),
                pltpu.make_async_copy(w_up.at[e, :, down], up_held.at[n], sems.at[n, 1]),
                pltpu.make_async_copy(w_down.at[e, down, :], down_held.at[n], sems.at[n, 2]),
            ]
        )
    for piece in copies:
        for copy in piece[:2]:
            copy.start()
    for piece in copies:
        piece[2].start()
    slot = lax.broadcasted_iota(jnp.int32, (rows, 1), 0)
    values = arrived[...]
    hidden = []
    for n, (e, f) in enumerate(pieces):
        copies[n][0].wait()
        copies[n][1].wait()
        gate = nn_dot(values, gate_held[n])
        upward = nn_dot(values, up_held[n])
        part = gate / (1.0 + jnp.exp(-gate)) * upward
        mine = lax.rem(slot, experts * MOST) // MOST == e
        hidden.append(jnp.where(mine, part, 0.0).astype(BF16))
    total = None
    for n in range(len(pieces)):
        copies[n][2].wait()
        term = nn_dot(hidden[n], down_held[n])
        total = term if total is None else total + term
    out[...] = total.astype(BF16)


def run_experts(arrived, w_gate, w_up, w_down):
    rows, width = arrived.shape
    experts, _, depth = w_gate.shape
    step = 256
    pieces = experts * depth // step
    vmem = pl.BlockSpec(memory_space=pltpu.VMEM)
    hbm = pl.BlockSpec(memory_space=pltpu.HBM)
    weights = [pltpu.with_memory_space_constraint(w, pltpu.HBM) for w in (w_gate, w_up, w_down)]
    return pl.pallas_call(
        functools.partial(experts_body, step),
        in_specs=[vmem] + [hbm] * 3,
        out_specs=vmem,
        out_shape=jax.ShapeDtypeStruct((rows, width), BF16),
        scratch_shapes=[
            pltpu.VMEM((pieces, width, step), BF16),
            pltpu.VMEM((pieces, width, step), BF16),
            pltpu.VMEM((pieces, step, width), BF16),
            pltpu.SemaphoreType.DMA((pieces, 3)),
        ],
        compiler_params=pltpu.CompilerParams(vmem_limit_bytes=44 * MIB),
        cost_estimate=pl.CostEstimate(
            flops=6 * rows * width * experts * depth,
            bytes_accessed=6 * width * experts * depth,
            transcendentals=rows * experts * depth,
        ),
        name="experts",
    )(arrived, *weights)


def mix_body(returned, coarse, fine, middle, out):
    values = returned[...]
    mixed = nn_dot(coarse[...], values) + nn_dot(fine[...], values)
    out[...] = (middle[...].astype(F32) + mixed).astype(BF16)


def mix(returned, coarse, fine, middle):
    vmem = pl.BlockSpec(memory_space=pltpu.VMEM)
    return pl.pallas_call(
        mix_body,
        in_specs=[vmem] * 4,
        out_specs=vmem,
        out_shape=jax.ShapeDtypeStruct(middle.shape, BF16),
        compiler_params=pltpu.CompilerParams(vmem_limit_bytes=16 * MIB),
        name="mix",
    )(returned, coarse, fine, middle)


def on_device(
    queries,
    new_key,
    new_value,
    key_cache,
    value_cache,
    cache_len,
    out_weight,
    residual,
    norm_gain,
    expert_ids,
    route_weight,
    w_gate,
    w_up,
    w_down,
):
    devices = lax.axis_size("ctx")
    chips = devices // CORES
    index = lax.axis_index("ctx")
    chip, core = index // CORES, index % CORES
    home_rows, width = residual.shape
    top = expert_ids.shape[1]
    heads_here = out_weight.shape[0] // HD
    cache_here = key_cache.shape[0]
    same_core = [[CORES * j + c for j in range(chips)] for c in range(CORES)]
    swap = [(i, i ^ 1) for i in range(devices)]

    across = [(i, i ^ CORES) for i in range(devices)]
    rings = chips // 2
    block_rings = max(1, HD // (CORES * heads_here * 2 * home_rows))
    steps = [(0, block_rings)]
    while sum(steps[-1]) < rings:
        steps.append((sum(steps[-1]), sum(steps[-1])))

    by_ring = [queries] + [
        lax.ppermute(queries, "ctx", [(i, i ^ (2 * CORES * k)) for i in range(devices)])
        for k in range(1, rings)
    ]
    query_chunks = []

    def gather_chunk(first, count):
        mine = by_ring[first] if count == 1 else jnp.concatenate(by_ring[first : first + count], axis=0)
        query_chunks.append((mine, lax.ppermute(mine, "ctx", across)))

    for step in steps[:2]:
        gather_chunk(*step)
    key_other = lax.ppermute(key_cache, "ctx", swap)
    value_turned = value_cache.T
    value_other = lax.ppermute(value_turned, "ctx", swap)

    place = jnp.stack(
        [chip, index * cache_here, (index ^ 1) * cache_here, core, chip % 2, chip // 2]
    ).astype(jnp.int32)

    def in_lanes(by_chip, first, count):
        base = (chip // 2 // count ^ first // count) * 2 * count
        here = lax.dynamic_slice_in_dim(by_chip, base, 2 * count, 0)
        here = here.reshape(count // block_rings, 2 * block_rings * home_rows)
        return jnp.tile(here, (1, CORES * heads_here)).reshape(1, count // block_rings * HD)

    len_by_chip = lax.dynamic_slice_in_dim(
        cache_len.reshape(chips, CORES * home_rows), core * home_rows, home_rows, 1
    )
    number_by_chip = jnp.arange(chips * home_rows, dtype=jnp.int32).reshape(chips, home_rows)
    lens = [in_lanes(len_by_chip, *step) for step in steps]
    row_ids = [in_lanes(number_by_chip, *step) for step in steps]

    flat_ids = expert_ids.reshape(-1)
    picks = jnp.arange(flat_ids.shape[0])
    earlier = (flat_ids[:, None] == flat_ids[None, :]) & (picks[None, :] < picks[:, None])
    target = (flat_ids * MOST + jnp.sum(earlier, axis=1, dtype=jnp.int32)).reshape(home_rows, top)
    experts = w_gate.shape[0]
    slots = experts * devices * MOST
    takes = target[:, :, None] == jnp.arange(slots, dtype=jnp.int32)
    chooser = jnp.any(takes, axis=1).T.astype(BF16)
    spread = jnp.sum(jnp.where(takes, route_weight[:, :, None], 0.0), axis=1)
    coarse = spread.astype(BF16)
    fine = (spread - coarse.astype(F32)).astype(BF16)

    gathered = []
    for n, (_, count) in enumerate(steps):
        mine, mine_across = query_chunks[n]
        if count == 1 and n == 0:
            mine = pltpu.with_memory_space_constraint(mine, pltpu.HBM)
        sums = attention(
            place,
            [(block, k) for block in (mine, mine_across) for k in range(count)],
            (key_cache, key_other),
            (value_turned, value_other),
            new_key,
            new_value,
            lens[n],
            row_ids[n],
            chips,
            key_cache.shape[1] // HD,
        )
        if n:
            sums, gathered[-1] = lax.optimization_barrier((sums, gathered[-1]))
        if n == 0:
            sums, by_ring = lax.optimization_barrier((sums, by_ring))
            for step in steps[2:]:
                gather_chunk(*step)
        if n + 1 < len(query_chunks):
            sums, place, _ = lax.optimization_barrier((sums, place, query_chunks[n + 1][1]))
        if n == 0:
            sums, late_weight = lax.optimization_barrier((sums, out_weight))
        gathered.append(
            lax.all_to_all(
                sums, "ctx", split_axis=0, concat_axis=0, axis_index_groups=same_core, tiled=True
            )
        )
    weight_other = lax.ppermute(late_weight, "ctx", swap)
    share = project(
        place, gathered, out_weight, weight_other, chips * home_rows, rings // block_rings
    )
    shares = lax.all_to_all(
        share.reshape(chips, home_rows, width),
        "ctx",
        split_axis=0,
        concat_axis=0,
        axis_index_groups=same_core,
        tiled=True,
    )
    middle, outgoing = norm_and_dispatch(shares, residual, norm_gain.reshape(1, width), chooser)
    arrived = lax.all_to_all(
        outgoing.reshape(devices, experts * MOST, width), "ctx", split_axis=0, concat_axis=0, tiled=True
    )
    produced = run_experts(arrived.reshape(slots, width), w_gate, w_up, w_down)
    returned = lax.all_to_all(
        produced.reshape(devices, experts * MOST, width), "ctx", split_axis=0, concat_axis=0, tiled=True
    )
    return mix(returned.reshape(slots, width), coarse, fine, middle)


def solution(mesh):
    placed = (
        P(("groups", "ctx"), None),
        P(("groups", "ctx"), None),
        P(("groups", "ctx"), None),
        P(("groups", "ctx"), None),
        P(("groups", "ctx"), None),
        P("groups"),
        P("ctx", None),
        P(("groups", "ctx"), None),
        P(),
        P(("groups", "ctx"), None),
        P(("groups", "ctx"), None),
        P("ctx", None, None),
        P("ctx", None, None),
        P("ctx", None, None),
    )
    return jax.shard_map(
        on_device, mesh=mesh, in_specs=placed, out_specs=P(("groups", "ctx"), None), check_vma=False
    )
```

```python
import functools
import math

import jax
import jax.numpy as jnp
from jax import lax
from jax.experimental import pallas as pl
from jax.experimental.pallas import tpu as pltpu
from jax.sharding import PartitionSpec as P

HD = 128
MOST = 4
CORES = 2
STATS = 16
MASKED = -1e30
FLOOR = -1e20
LOG2E = math.log2(math.e)
MIB = 1024 * 1024
F32 = jnp.float32
BF16 = jnp.bfloat16


def nt_dot(a, b):
    return lax.dot_general(a, b, (((1,), (1,)), ((), ())), preferred_element_type=F32)


def nn_dot(a, b):
    return lax.dot_general(a, b, (((1,), (0,)), ((), ())), preferred_element_type=F32)


def attention_body(shape, place, *refs):
    key_heads, owners, owner_heads, home_rows, rows, cache_here, step = shape
    *query_refs, key_own, key_other, value_own, value_other, key_fresh, value_fresh = refs[:-8]
    lens, row_ids, out, q_rows, q_turned, hidden, scores, probs = refs[-8:]
    chip, start_own, start_other, side_here, ring_here = place[0], place[1], place[2], place[4], place[5]
    near = rows // home_rows // 2
    pack = HD // rows
    groups = owner_heads // pack

    @pl.when(pl.program_id(0) == 0)
    def _():
        lanes = lens.shape[1]
        for part, start in enumerate((start_own, start_other)):
            positions = start + lax.broadcasted_iota(jnp.int32, (cache_here, lanes), 0)
            hidden[part * cache_here : (part + 1) * cache_here, :] = jnp.where(
                positions < lens[...], 0.0, MASKED
            )
        token = chip * home_rows + lax.broadcasted_iota(jnp.int32, (home_rows, lanes), 0)
        hidden[2 * cache_here :, :] = jnp.where(token == row_ids[...], 0.0, MASKED)

    for k, piece in enumerate(query_refs):
        side = side_here if k < near else 1 - side_here
        spot = 2 * (lax.rem(ring_here, near) ^ (k % near)) + side
        q_rows[pl.ds(pl.multiple_of(spot * home_rows, home_rows), home_rows), :] = piece[...]

    factor = LOG2E / math.sqrt(HD)
    wide = owners * groups * HD
    for n in range(key_heads * owners * groups):
        block = jnp.concatenate(
            [q_rows[:, h * HD : (h + 1) * HD] for h in range(n * pack, (n + 1) * pack)], axis=0
        )
        scaled = block.T.astype(F32) * factor
        coarse = scaled.astype(BF16)
        q_turned[:HD, n * HD : (n + 1) * HD] = coarse
        q_turned[HD:, n * HD : (n + 1) * HD] = (scaled - coarse.astype(F32)).astype(BF16)

    each = range(key_heads)
    heads = [slice(g * HD, (g + 1) * HD) for g in each]
    across = [slice(g * wide, (g + 1) * wide) for g in each]

    def score(g, keys, at):
        s = nn_dot(jnp.concatenate([keys, keys], axis=1), q_turned[:, across[g]])
        return s + jnp.concatenate([hidden[at, :]] * (owners * groups), axis=1)

    def most(s):
        return jnp.max(s.reshape(s.shape[0] // 8, 8, wide), axis=0)

    fresh_at = slice(2 * cache_here, 2 * cache_here + home_rows)
    s_new = [score(g, key_fresh[:, heads[g]], fresh_at) for g in each]
    run = [most(s) for s in s_new]
    pieces = [(part, i) for part in range(2) for i in range(0, cache_here, step)]
    for part, i in pieces:
        at = slice(part * cache_here + i, part * cache_here + i + step)
        for g in each:
            s = score(g, (key_own, key_other)[part][i : i + step, heads[g]], at)
            scores[at, across[g]] = s
            run[g] = jnp.maximum(run[g], most(s))
    peak = [
        jnp.maximum(jnp.max(r, axis=0, keepdims=True), FLOOR).astype(BF16).astype(F32) for r in run
    ]
    for part, i in pieces:
        at = slice(part * cache_here + i, part * cache_here + i + step)
        for g in each:
            probs[at, across[g]] = jnp.exp2((scores[at, across[g]] - peak[g]).astype(BF16))
    ones = jnp.ones((STATS, cache_here), BF16)
    sums = [
        nn_dot(jnp.concatenate([value_own[heads[g], :], ones], axis=0), probs[:cache_here, across[g]])
        for g in each
    ]
    sums = [
        sums[g]
        + nn_dot(jnp.concatenate([value_other[heads[g], :], ones], axis=0), probs[cache_here:, across[g]])
        for g in each
    ]
    for g in each:
        p_new = jnp.exp2((s_new[g] - peak[g]).astype(BF16))
        values = value_fresh[:, heads[g]].astype(F32).T.astype(BF16)
        numer = sums[g][:HD] + nn_dot(values, p_new)
        denom = sums[g][HD : HD + 1] + jnp.sum(p_new.astype(F32), axis=0, keepdims=True)
        high = denom.astype(BF16).astype(F32)
        low = denom - high
        for owner in range(owners):
            spot = g * owners + owner
            lanes = [slice((owner * groups + k) * HD, (owner * groups + k + 1) * HD) for k in range(groups)]
            for k, cols in enumerate(lanes):
                out[spot, k * HD : (k + 1) * HD, :] = numer[:, cols].astype(BF16)
            filled = [kind[:, cols] for kind in (peak[g], high, low) for cols in lanes]
            filled += [jnp.zeros_like(filled[0])] * (STATS - len(filled))
            out[spot, groups * HD :, :] = jnp.concatenate(filled, axis=0).astype(BF16)


def attention(place, query_blocks, keys, values, new_key, new_value, lens, row_ids, chips, kv_heads):
    home_rows = new_key.shape[0]
    rows = home_rows * len(query_blocks)
    cache_here = keys[0].shape[0]
    together = 2
    steps = kv_heads // together
    owners = chips // kv_heads
    columns = query_blocks[0][0].shape[1] // steps
    owner_heads = columns // HD // owners // together
    wide = rows * columns // HD
    height = owner_heads * rows + STATS
    step = 512
    positions = 2 * cache_here + home_rows
    kv = lambda g, place: (0, g)
    whole = lambda g, place: (0, 0)
    shape = (together, owners, owner_heads, home_rows, rows, cache_here, step)
    work = wide * steps * 2 * cache_here
    return pl.pallas_call(
        functools.partial(attention_body, shape),
        grid_spec=pltpu.PrefetchScalarGridSpec(
            num_scalar_prefetch=1,
            grid=(steps,),
            in_specs=[
                pl.BlockSpec((home_rows, columns), functools.partial(lambda n, g, place: (n, g), n))
                for _, n in query_blocks
            ]
            + [pl.BlockSpec((cache_here, together * HD), kv)] * 2
            + [pl.BlockSpec((together * HD, cache_here), lambda g, place: (g, 0))] * 2
            + [pl.BlockSpec((home_rows, together * HD), kv)] * 2
            + [pl.BlockSpec(lens.shape, whole)] * 2,
            out_specs=pl.BlockSpec((together * owners, height, HD), lambda g, place: (g, 0, 0)),
            scratch_shapes=[
                pltpu.VMEM((rows, columns), BF16),
                pltpu.VMEM((2 * HD, wide), BF16),
                pltpu.VMEM((positions, HD), F32),
                pltpu.VMEM((2 * cache_here, wide), F32),
                pltpu.VMEM((2 * cache_here, wide), BF16),
            ],
        ),
        out_shape=jax.ShapeDtypeStruct((chips, height, HD), BF16),
        compiler_params=pltpu.CompilerParams(vmem_limit_bytes=40 * MIB),
        cost_estimate=pl.CostEstimate(
            flops=6 * work * HD, bytes_accessed=8 * MIB, transcendentals=work
        ),
        name="attention",
    )(
        place,
        *[block for block, _ in query_blocks],
        pltpu.with_memory_space_constraint(keys[0], pltpu.HBM),
        keys[1],
        *values,
        pltpu.with_memory_space_constraint(new_key, pltpu.HBM),
        pltpu.with_memory_space_constraint(new_value, pltpu.HBM),
        lens,
        row_ids,
    )


def project_body(rows, place, *refs):
    *chunks, weight_own, weight_other, out, turned = refs
    core = place[3]
    chips, height, _ = chunks[0].shape
    base = height - STATS
    groups = base // HD
    pack = HD // rows
    heads_here = groups * pack // CORES
    half = chips // 2 // 2
    for near in range(2):
        sources = [chunks[s // 2 // half ^ near].at[s] for s in range(chips)]
        stats = [part[base:, :].astype(F32) for part in sources]
        peaks = [stat[:groups] for stat in stats]
        top = functools.reduce(jnp.maximum, peaks)
        share = [jnp.exp2(peak - top) for peak in peaks]
        denom = sum(w * (t[groups : 2 * groups] + t[2 * groups : 3 * groups]) for w, t in zip(share, stats))
        for k in range(groups):
            numer = sum(
                part[k * HD : (k + 1) * HD, :].astype(F32) * w[k : k + 1, :] for part, w in zip(sources, share)
            )
            attended = (numer / denom[k : k + 1, :]).T.astype(BF16)
            for j in range(pack):
                part, h = divmod(k * pack + j, heads_here)
                turned[part, near * rows : (near + 1) * rows, h * HD : (h + 1) * HD] = attended[
                    j * rows : (j + 1) * rows
                ]
    product = nn_dot(turned[core], weight_own[...]) + nn_dot(turned[1 - core], weight_other[...])
    out[...] = product.astype(BF16)


def project(place, chunks, weight_own, weight_other, rows):
    depth, width = weight_own.shape
    vmem = pl.BlockSpec(memory_space=pltpu.VMEM)
    return pl.pallas_call(
        functools.partial(project_body, rows),
        in_specs=[pl.BlockSpec(memory_space=pltpu.SMEM)] + [vmem] * (len(chunks) + 2),
        out_specs=vmem,
        out_shape=jax.ShapeDtypeStruct((2 * rows, width), BF16),
        scratch_shapes=[pltpu.VMEM((CORES, 2 * rows, depth), BF16)],
        compiler_params=pltpu.CompilerParams(vmem_limit_bytes=32 * MIB),
        cost_estimate=pl.CostEstimate(
            flops=8 * rows * width * depth, bytes_accessed=4 * MIB, transcendentals=0
        ),
        name="project",
    )(place, *chunks, weight_own, weight_other)


def norm_body(parts, residual, gain, chooser, middle_out, sent):
    total = parts[0].astype(F32)
    for s in range(1, parts.shape[0]):
        total = total + parts[s].astype(F32)
    middle = (residual[...].astype(F32) + total).astype(BF16)
    middle_out[...] = middle
    middle = middle.astype(F32)
    inv_rms = lax.rsqrt(jnp.mean(middle * middle, axis=-1, keepdims=True) + 1e-06)
    normed = (middle * inv_rms * gain[...].astype(F32)).astype(BF16)
    sent[...] = nn_dot(chooser[...], normed).astype(BF16)


def norm_and_dispatch(parts, residual, gain, chooser):
    vmem = pl.BlockSpec(memory_space=pltpu.VMEM)
    rows, width = residual.shape
    return pl.pallas_call(
        norm_body,
        in_specs=[vmem] * 4,
        out_specs=[vmem] * 2,
        out_shape=[
            jax.ShapeDtypeStruct((rows, width), BF16),
            jax.ShapeDtypeStruct((chooser.shape[0], width), BF16),
        ],
        compiler_params=pltpu.CompilerParams(vmem_limit_bytes=24 * MIB),
        cost_estimate=pl.CostEstimate(
            flops=2 * chooser.shape[0] * rows * width, bytes_accessed=2 * MIB, transcendentals=0
        ),
        name="norm_and_dispatch",
    )(parts, residual, gain, chooser)


def experts_body(step, arrived, w_gate, w_up, w_down, out, gate_held, up_held, down_held, sems):
    experts, _, depth = w_gate.shape
    rows, width = arrived.shape
    pieces = [(e, f) for e in range(experts) for f in range(0, depth, step)]
    copies = []
    for n, (e, f) in enumerate(pieces):
        down = pl.ds(f, step)
        copies.append(
            [
                pltpu.make_async_copy(w_gate.at[e, :, down], gate_held.at[n], sems.at[n, 0]),
                pltpu.make_async_copy(w_up.at[e, :, down], up_held.at[n], sems.at[n, 1]),
                pltpu.make_async_copy(w_down.at[e, down, :], down_held.at[n], sems.at[n, 2]),
            ]
        )
    for piece in copies:
        for copy in piece[:2]:
            copy.start()
    for piece in copies:
        piece[2].start()
    slot = lax.broadcasted_iota(jnp.int32, (rows, 1), 0)
    values = arrived[...]
    hidden = []
    for n, (e, f) in enumerate(pieces):
        copies[n][0].wait()
        copies[n][1].wait()
        gate = nn_dot(values, gate_held[n])
        upward = nn_dot(values, up_held[n])
        part = gate / (1.0 + jnp.exp(-gate)) * upward
        mine = lax.rem(slot, experts * MOST) // MOST == e
        hidden.append(jnp.where(mine, part, 0.0).astype(BF16))
    total = None
    for n in range(len(pieces)):
        copies[n][2].wait()
        term = nn_dot(hidden[n], down_held[n])
        total = term if total is None else total + term
    out[...] = total.astype(BF16)


def run_experts(arrived, w_gate, w_up, w_down):
    rows, width = arrived.shape
    experts, _, depth = w_gate.shape
    step = 256
    pieces = experts * depth // step
    vmem = pl.BlockSpec(memory_space=pltpu.VMEM)
    hbm = pl.BlockSpec(memory_space=pltpu.HBM)
    weights = [pltpu.with_memory_space_constraint(w, pltpu.HBM) for w in (w_gate, w_up, w_down)]
    return pl.pallas_call(
        functools.partial(experts_body, step),
        in_specs=[vmem] + [hbm] * 3,
        out_specs=vmem,
        out_shape=jax.ShapeDtypeStruct((rows, width), BF16),
        scratch_shapes=[
            pltpu.VMEM((pieces, width, step), BF16),
            pltpu.VMEM((pieces, width, step), BF16),
            pltpu.VMEM((pieces, step, width), BF16),
            pltpu.SemaphoreType.DMA((pieces, 3)),
        ],
        compiler_params=pltpu.CompilerParams(vmem_limit_bytes=44 * MIB),
        cost_estimate=pl.CostEstimate(
            flops=6 * rows * width * experts * depth,
            bytes_accessed=6 * width * experts * depth,
            transcendentals=rows * experts * depth,
        ),
        name="experts",
    )(arrived, *weights)


def mix_body(returned, coarse, fine, middle, out):
    values = returned[...]
    mixed = nn_dot(coarse[...], values) + nn_dot(fine[...], values)
    out[...] = (middle[...].astype(F32) + mixed).astype(BF16)


def mix(returned, coarse, fine, middle):
    vmem = pl.BlockSpec(memory_space=pltpu.VMEM)
    return pl.pallas_call(
        mix_body,
        in_specs=[vmem] * 4,
        out_specs=vmem,
        out_shape=jax.ShapeDtypeStruct(middle.shape, BF16),
        compiler_params=pltpu.CompilerParams(vmem_limit_bytes=16 * MIB),
        name="mix",
    )(returned, coarse, fine, middle)


def on_device(
    queries,
    new_key,
    new_value,
    key_cache,
    value_cache,
    cache_len,
    out_weight,
    residual,
    norm_gain,
    expert_ids,
    route_weight,
    w_gate,
    w_up,
    w_down,
):
    devices = lax.axis_size("ctx")
    chips = devices // CORES
    index = lax.axis_index("ctx")
    chip, core = index // CORES, index % CORES
    home_rows, width = residual.shape
    top = expert_ids.shape[1]
    heads_here = out_weight.shape[0] // HD
    cache_here = key_cache.shape[0]
    same_core = [[CORES * j + c for j in range(chips)] for c in range(CORES)]
    swap = [(i, i ^ 1) for i in range(devices)]

    across = [(i, i ^ CORES) for i in range(devices)]
    rings = chips // 2
    half = rings // 2
    chunk_rows = 2 * half * home_rows

    def across_y(block):
        return lax.ppermute(block, "ctx", across)

    neighbour = across_y(queries)
    by_ring = [queries] + [
        lax.ppermute(queries, "ctx", [(i, i ^ (2 * CORES * k)) for i in range(devices)])
        for k in range(1, rings)
    ]
    near_blocks = [(pltpu.with_memory_space_constraint(queries, pltpu.HBM), 0)]
    near_blocks += [(block, 0) for block in by_ring[1:half]]
    near_blocks += [(neighbour, 0)] + [(across_y(block), 0) for block in by_ring[1:half]]
    far = jnp.concatenate(by_ring[half:], axis=0)
    far_across = across_y(far)
    far_blocks = [(far, k) for k in range(half)] + [(far_across, k) for k in range(half)]
    late_keys, late_values, _ = lax.optimization_barrier((key_cache, value_cache, neighbour))
    key_other = lax.ppermute(late_keys, "ctx", swap)
    value_turned = late_values.T
    value_other = lax.ppermute(value_turned, "ctx", swap)
    place = jnp.stack([chip, index * cache_here, (index ^ 1) * cache_here, core, chip % 2, chip // 2]).astype(jnp.int32)

    def in_lanes(by_chip, n):
        first = (chip // CORES // half ^ n) * chips // 2
        here = lax.dynamic_slice_in_dim(by_chip, first, chips // 2, 0).reshape(1, chunk_rows)
        return jnp.tile(here, (1, HD // chunk_rows))

    len_by_chip = lax.dynamic_slice_in_dim(
        cache_len.reshape(chips, CORES * home_rows), core * home_rows, home_rows, 1
    )
    number_by_chip = jnp.arange(chips * home_rows, dtype=jnp.int32).reshape(chips, home_rows)
    lens = [in_lanes(len_by_chip, n) for n in range(2)]
    row_ids = [in_lanes(number_by_chip, n) for n in range(2)]

    flat_ids = expert_ids.reshape(-1)
    picks = jnp.arange(flat_ids.shape[0])
    earlier = (flat_ids[:, None] == flat_ids[None, :]) & (picks[None, :] < picks[:, None])
    target = (flat_ids * MOST + jnp.sum(earlier, axis=1, dtype=jnp.int32)).reshape(home_rows, top)
    experts = w_gate.shape[0]
    slots = experts * devices * MOST
    takes = target[:, :, None] == jnp.arange(slots, dtype=jnp.int32)
    chooser = jnp.any(takes, axis=1).T.astype(BF16)
    spread = jnp.sum(jnp.where(takes, route_weight[:, :, None], 0.0), axis=1)
    coarse = spread.astype(BF16)
    fine = (spread - coarse.astype(F32)).astype(BF16)

    gathered = []
    for chunk, blocks in enumerate((near_blocks, far_blocks)):
        sums = attention(
            place,
            blocks,
            (key_cache, key_other),
            (value_turned, value_other),
            new_key,
            new_value,
            lens[chunk],
            row_ids[chunk],
            chips,
            key_cache.shape[1] // HD,
        )
        if chunk:
            sums, gathered[-1] = lax.optimization_barrier((sums, gathered[-1]))
        else:
            sums, place, late_weight, _ = lax.optimization_barrier((sums, place, out_weight, far_across))
        gathered.append(
            lax.all_to_all(
                sums, "ctx", split_axis=0, concat_axis=0, axis_index_groups=same_core, tiled=True
            )
        )
    weight_other = lax.ppermute(late_weight, "ctx", swap)
    share = project(place, gathered, out_weight, weight_other, chunk_rows)
    shares = lax.all_to_all(
        share.reshape(chips, home_rows, width),
        "ctx",
        split_axis=0,
        concat_axis=0,
        axis_index_groups=same_core,
        tiled=True,
    )
    middle, outgoing = norm_and_dispatch(shares, residual, norm_gain.reshape(1, width), chooser)
    arrived = lax.all_to_all(
        outgoing.reshape(devices, experts * MOST, width), "ctx", split_axis=0, concat_axis=0, tiled=True
    )
    produced = run_experts(arrived.reshape(slots, width), w_gate, w_up, w_down)
    returned = lax.all_to_all(
        produced.reshape(devices, experts * MOST, width), "ctx", split_axis=0, concat_axis=0, tiled=True
    )
    return mix(returned.reshape(slots, width), coarse, fine, middle)


def solution(mesh):
    placed = (
        P(("groups", "ctx"), None),
        P(("groups", "ctx"), None),
        P(("groups", "ctx"), None),
        P(("groups", "ctx"), None),
        P(("groups", "ctx"), None),
        P("groups"),
        P("ctx", None),
        P(("groups", "ctx"), None),
        P(),
        P(("groups", "ctx"), None),
        P(("groups", "ctx"), None),
        P("ctx", None, None),
        P("ctx", None, None),
        P("ctx", None, None),
    )
    return jax.shard_map(
        on_device, mesh=mesh, in_specs=placed, out_specs=P(("groups", "ctx"), None), check_vma=False
    )
```

```python
import functools
import math

import jax
import jax.numpy as jnp
from jax import lax
from jax.experimental import pallas as pl
from jax.experimental.pallas import tpu as pltpu
from jax.sharding import PartitionSpec as P

HD = 128
MOST = 4
CORES = 2
STATS = 16
MASKED = -1e30
FLOOR = -1e20
LOG2E = math.log2(math.e)
MIB = 1024 * 1024
F32 = jnp.float32
BF16 = jnp.bfloat16


def nt_dot(a, b):
    return lax.dot_general(a, b, (((1,), (1,)), ((), ())), preferred_element_type=F32)


def nn_dot(a, b):
    return lax.dot_general(a, b, (((1,), (0,)), ((), ())), preferred_element_type=F32)


def attention_body(shape, place, *refs):
    key_heads, owners, owner_heads, home_rows, rows, cache_here, step = shape
    *query_refs, key_own, key_other, value_own, value_other, key_fresh, value_fresh = refs[:-11]
    lens, row_ids, out, q_rows, q_turned, hidden, scores, probs, keys_held, values_held, sems = refs[-11:]
    chip, start_own, start_other, side_here, ring_here = place[0], place[1], place[2], place[4], place[5]
    near = rows // home_rows // 2
    pack = HD // rows
    groups = owner_heads // pack
    parts = [slice(part * cache_here, (part + 1) * cache_here) for part in range(2)]
    key_copies = [
        pltpu.make_async_copy(source, keys_held.at[parts[n], :], sems.at[n])
        for n, source in enumerate((key_own, key_other))
    ]
    value_copies = [
        pltpu.make_async_copy(source, values_held.at[n], sems.at[2 + n])
        for n, source in enumerate((value_own, value_other))
    ]

    @pl.when(pl.program_id(0) == 0)
    def _():
        for copy in key_copies + value_copies:
            copy.start()

    @pl.when(pl.program_id(0) == 0)
    def _():
        lanes = lens.shape[1]
        for part, start in enumerate((start_own, start_other)):
            positions = start + lax.broadcasted_iota(jnp.int32, (cache_here, lanes), 0)
            hidden[part * cache_here : (part + 1) * cache_here, :] = jnp.where(
                positions < lens[...], 0.0, MASKED
            )
        token = chip * home_rows + lax.broadcasted_iota(jnp.int32, (home_rows, lanes), 0)
        hidden[2 * cache_here :, :] = jnp.where(token == row_ids[...], 0.0, MASKED)

    for k, piece in enumerate(query_refs):
        side = side_here if k < near else 1 - side_here
        spot = 2 * (lax.rem(ring_here, near) ^ (k % near)) + side
        q_rows[pl.ds(pl.multiple_of(spot * home_rows, home_rows), home_rows), :] = piece[...]

    factor = LOG2E / math.sqrt(HD)
    wide = owners * groups * HD
    for n in range(key_heads * owners * groups):
        block = jnp.concatenate(
            [q_rows[:, h * HD : (h + 1) * HD] for h in range(n * pack, (n + 1) * pack)], axis=0
        )
        scaled = block.T.astype(F32) * factor
        coarse = scaled.astype(BF16)
        q_turned[:HD, n * HD : (n + 1) * HD] = coarse
        q_turned[HD:, n * HD : (n + 1) * HD] = (scaled - coarse.astype(F32)).astype(BF16)

    @pl.when(pl.program_id(0) == 0)
    def _():
        for copy in key_copies:
            copy.wait()

    each = range(key_heads)
    heads = [slice(g * HD, (g + 1) * HD) for g in each]
    held = [
        pl.ds(pl.multiple_of((pl.program_id(0) * key_heads + g) * HD, HD), HD) for g in each
    ]
    across = [slice(g * wide, (g + 1) * wide) for g in each]

    def score(g, keys, at):
        s = nn_dot(jnp.concatenate([keys, keys], axis=1), q_turned[:, across[g]])
        return s + jnp.concatenate([hidden[at, :]] * (owners * groups), axis=1)

    def most(s):
        return jnp.max(s.reshape(s.shape[0] // 8, 8, wide), axis=0)

    fresh_at = slice(2 * cache_here, 2 * cache_here + home_rows)
    s_new = [score(g, key_fresh[:, heads[g]], fresh_at) for g in each]
    run = [most(s) for s in s_new]
    pieces = [(part, i) for part in range(2) for i in range(0, cache_here, step)]
    for part, i in pieces:
        at = slice(part * cache_here + i, part * cache_here + i + step)
        for g in each:
            s = score(g, keys_held[at, held[g]], at)
            scores[at, across[g]] = s
            run[g] = jnp.maximum(run[g], most(s))
    peak = [
        jnp.maximum(jnp.max(r, axis=0, keepdims=True), FLOOR).astype(BF16).astype(F32) for r in run
    ]
    for part, i in pieces:
        at = slice(part * cache_here + i, part * cache_here + i + step)
        for g in each:
            probs[at, across[g]] = jnp.exp2((scores[at, across[g]] - peak[g]).astype(BF16))
    @pl.when(pl.program_id(0) == 0)
    def _():
        for copy in value_copies:
            copy.wait()

    ones = jnp.ones((STATS, cache_here), BF16)
    sums = [
        nn_dot(jnp.concatenate([values_held[0, held[g], :], ones], axis=0), probs[parts[0], across[g]])
        for g in each
    ]
    sums = [
        sums[g]
        + nn_dot(jnp.concatenate([values_held[1, held[g], :], ones], axis=0), probs[parts[1], across[g]])
        for g in each
    ]
    for g in each:
        p_new = jnp.exp2((s_new[g] - peak[g]).astype(BF16))
        values = value_fresh[:, heads[g]].astype(F32).T.astype(BF16)
        numer = sums[g][:HD] + nn_dot(values, p_new)
        denom = sums[g][HD : HD + 1] + jnp.sum(p_new.astype(F32), axis=0, keepdims=True)
        high = denom.astype(BF16).astype(F32)
        low = denom - high
        for owner in range(owners):
            spot = g * owners + owner
            lanes = [slice((owner * groups + k) * HD, (owner * groups + k + 1) * HD) for k in range(groups)]
            for k, cols in enumerate(lanes):
                out[spot, k * HD : (k + 1) * HD, :] = numer[:, cols].astype(BF16)
            filled = [kind[:, cols] for kind in (peak[g], high, low) for cols in lanes]
            filled += [jnp.zeros_like(filled[0])] * (STATS - len(filled))
            out[spot, groups * HD :, :] = jnp.concatenate(filled, axis=0).astype(BF16)


def attention(place, query_blocks, keys, values, new_key, new_value, lens, row_ids, chips, kv_heads):
    home_rows = new_key.shape[0]
    rows = home_rows * len(query_blocks)
    cache_here = keys[0].shape[0]
    together = 2
    steps = kv_heads // together
    owners = chips // kv_heads
    columns = query_blocks[0][0].shape[1] // steps
    owner_heads = columns // HD // owners // together
    wide = rows * columns // HD
    height = owner_heads * rows + STATS
    step = 512
    positions = 2 * cache_here + home_rows
    kv = lambda g, place: (0, g)
    whole = lambda g, place: (0, 0)
    shape = (together, owners, owner_heads, home_rows, rows, cache_here, step)
    work = wide * steps * 2 * cache_here
    return pl.pallas_call(
        functools.partial(attention_body, shape),
        grid_spec=pltpu.PrefetchScalarGridSpec(
            num_scalar_prefetch=1,
            grid=(steps,),
            in_specs=[
                pl.BlockSpec((home_rows, columns), functools.partial(lambda n, g, place: (n, g), n))
                for _, n in query_blocks
            ]
            + [pl.BlockSpec(memory_space=pl.ANY)] * 4
            + [pl.BlockSpec((home_rows, together * HD), kv)] * 2
            + [pl.BlockSpec(lens.shape, whole)] * 2,
            out_specs=pl.BlockSpec((together * owners, height, HD), lambda g, place: (g, 0, 0)),
            scratch_shapes=[
                pltpu.VMEM((rows, columns), BF16),
                pltpu.VMEM((2 * HD, wide), BF16),
                pltpu.VMEM((positions, HD), F32),
                pltpu.VMEM((2 * cache_here, wide), F32),
                pltpu.VMEM((2 * cache_here, wide), BF16),
                pltpu.VMEM((2 * cache_here, kv_heads * HD), BF16),
                pltpu.VMEM((2, kv_heads * HD, cache_here), BF16),
                pltpu.SemaphoreType.DMA((4,)),
            ],
        ),
        out_shape=jax.ShapeDtypeStruct((chips, height, HD), BF16),
        compiler_params=pltpu.CompilerParams(vmem_limit_bytes=40 * MIB),
        cost_estimate=pl.CostEstimate(
            flops=6 * work * HD, bytes_accessed=8 * MIB, transcendentals=work
        ),
        name="attention",
    )(
        place,
        *[block for block, _ in query_blocks],
        pltpu.with_memory_space_constraint(keys[0], pltpu.HBM),
        keys[1],
        *values,
        pltpu.with_memory_space_constraint(new_key, pltpu.HBM),
        pltpu.with_memory_space_constraint(new_value, pltpu.HBM),
        lens,
        row_ids,
    )


def project_body(rows, place, *refs):
    *chunks, weight_own, weight_other, out, turned = refs
    core = place[3]
    chips, height, _ = chunks[0].shape
    base = height - STATS
    groups = base // HD
    pack = HD // rows
    heads_here = groups * pack // CORES
    half = chips // 2 // 2
    for near in range(2):
        sources = [chunks[s // 2 // half ^ near].at[s] for s in range(chips)]
        stats = [part[base:, :].astype(F32) for part in sources]
        peaks = [stat[:groups] for stat in stats]
        top = functools.reduce(jnp.maximum, peaks)
        share = [jnp.exp2(peak - top) for peak in peaks]
        denom = sum(w * (t[groups : 2 * groups] + t[2 * groups : 3 * groups]) for w, t in zip(share, stats))
        for k in range(groups):
            numer = sum(
                part[k * HD : (k + 1) * HD, :].astype(F32) * w[k : k + 1, :] for part, w in zip(sources, share)
            )
            attended = (numer / denom[k : k + 1, :]).T.astype(BF16)
            for j in range(pack):
                part, h = divmod(k * pack + j, heads_here)
                turned[part, near * rows : (near + 1) * rows, h * HD : (h + 1) * HD] = attended[
                    j * rows : (j + 1) * rows
                ]
    product = nn_dot(turned[core], weight_own[...]) + nn_dot(turned[1 - core], weight_other[...])
    out[...] = product.astype(BF16)


def project(place, chunks, weight_own, weight_other, rows):
    depth, width = weight_own.shape
    vmem = pl.BlockSpec(memory_space=pltpu.VMEM)
    return pl.pallas_call(
        functools.partial(project_body, rows),
        in_specs=[pl.BlockSpec(memory_space=pltpu.SMEM)] + [vmem] * (len(chunks) + 2),
        out_specs=vmem,
        out_shape=jax.ShapeDtypeStruct((2 * rows, width), BF16),
        scratch_shapes=[pltpu.VMEM((CORES, 2 * rows, depth), BF16)],
        compiler_params=pltpu.CompilerParams(vmem_limit_bytes=32 * MIB),
        cost_estimate=pl.CostEstimate(
            flops=8 * rows * width * depth, bytes_accessed=4 * MIB, transcendentals=0
        ),
        name="project",
    )(place, *chunks, weight_own, weight_other)


def norm_body(parts, residual, gain, chooser, middle_out, sent):
    total = parts[0].astype(F32)
    for s in range(1, parts.shape[0]):
        total = total + parts[s].astype(F32)
    middle = (residual[...].astype(F32) + total).astype(BF16)
    middle_out[...] = middle
    middle = middle.astype(F32)
    inv_rms = lax.rsqrt(jnp.mean(middle * middle, axis=-1, keepdims=True) + 1e-06)
    normed = (middle * inv_rms * gain[...].astype(F32)).astype(BF16)
    sent[...] = nn_dot(chooser[...], normed).astype(BF16)


def norm_and_dispatch(parts, residual, gain, chooser):
    vmem = pl.BlockSpec(memory_space=pltpu.VMEM)
    rows, width = residual.shape
    return pl.pallas_call(
        norm_body,
        in_specs=[vmem] * 4,
        out_specs=[vmem] * 2,
        out_shape=[
            jax.ShapeDtypeStruct((rows, width), BF16),
            jax.ShapeDtypeStruct((chooser.shape[0], width), BF16),
        ],
        compiler_params=pltpu.CompilerParams(vmem_limit_bytes=24 * MIB),
        cost_estimate=pl.CostEstimate(
            flops=2 * chooser.shape[0] * rows * width, bytes_accessed=2 * MIB, transcendentals=0
        ),
        name="norm_and_dispatch",
    )(parts, residual, gain, chooser)


def experts_body(step, arrived, w_gate, w_up, w_down, out, gate_held, up_held, down_held, sems):
    experts, _, depth = w_gate.shape
    rows, width = arrived.shape
    pieces = [(e, f) for e in range(experts) for f in range(0, depth, step)]
    copies = []
    for n, (e, f) in enumerate(pieces):
        down = pl.ds(f, step)
        copies.append(
            [
                pltpu.make_async_copy(w_gate.at[e, :, down], gate_held.at[n], sems.at[n, 0]),
                pltpu.make_async_copy(w_up.at[e, :, down], up_held.at[n], sems.at[n, 1]),
                pltpu.make_async_copy(w_down.at[e, down, :], down_held.at[n], sems.at[n, 2]),
            ]
        )
    for piece in copies:
        for copy in piece[:2]:
            copy.start()
    for piece in copies:
        piece[2].start()
    slot = lax.broadcasted_iota(jnp.int32, (rows, 1), 0)
    values = arrived[...]
    hidden = []
    for n, (e, f) in enumerate(pieces):
        copies[n][0].wait()
        copies[n][1].wait()
        gate = nn_dot(values, gate_held[n])
        upward = nn_dot(values, up_held[n])
        part = gate / (1.0 + jnp.exp(-gate)) * upward
        mine = lax.rem(slot, experts * MOST) // MOST == e
        hidden.append(jnp.where(mine, part, 0.0).astype(BF16))
    total = None
    for n in range(len(pieces)):
        copies[n][2].wait()
        term = nn_dot(hidden[n], down_held[n])
        total = term if total is None else total + term
    out[...] = total.astype(BF16)


def run_experts(arrived, w_gate, w_up, w_down):
    rows, width = arrived.shape
    experts, _, depth = w_gate.shape
    step = 256
    pieces = experts * depth // step
    vmem = pl.BlockSpec(memory_space=pltpu.VMEM)
    hbm = pl.BlockSpec(memory_space=pltpu.HBM)
    weights = [pltpu.with_memory_space_constraint(w, pltpu.HBM) for w in (w_gate, w_up, w_down)]
    return pl.pallas_call(
        functools.partial(experts_body, step),
        in_specs=[vmem] + [hbm] * 3,
        out_specs=vmem,
        out_shape=jax.ShapeDtypeStruct((rows, width), BF16),
        scratch_shapes=[
            pltpu.VMEM((pieces, width, step), BF16),
            pltpu.VMEM((pieces, width, step), BF16),
            pltpu.VMEM((pieces, step, width), BF16),
            pltpu.SemaphoreType.DMA((pieces, 3)),
        ],
        compiler_params=pltpu.CompilerParams(vmem_limit_bytes=44 * MIB),
        cost_estimate=pl.CostEstimate(
            flops=6 * rows * width * experts * depth,
            bytes_accessed=6 * width * experts * depth,
            transcendentals=rows * experts * depth,
        ),
        name="experts",
    )(arrived, *weights)


def mix_body(returned, coarse, fine, middle, out):
    values = returned[...]
    mixed = nn_dot(coarse[...], values) + nn_dot(fine[...], values)
    out[...] = (middle[...].astype(F32) + mixed).astype(BF16)


def mix(returned, coarse, fine, middle):
    vmem = pl.BlockSpec(memory_space=pltpu.VMEM)
    return pl.pallas_call(
        mix_body,
        in_specs=[vmem] * 4,
        out_specs=vmem,
        out_shape=jax.ShapeDtypeStruct(middle.shape, BF16),
        compiler_params=pltpu.CompilerParams(vmem_limit_bytes=16 * MIB),
        name="mix",
    )(returned, coarse, fine, middle)


def on_device(
    queries,
    new_key,
    new_value,
    key_cache,
    value_cache,
    cache_len,
    out_weight,
    residual,
    norm_gain,
    expert_ids,
    route_weight,
    w_gate,
    w_up,
    w_down,
):
    devices = lax.axis_size("ctx")
    chips = devices // CORES
    index = lax.axis_index("ctx")
    chip, core = index // CORES, index % CORES
    home_rows, width = residual.shape
    top = expert_ids.shape[1]
    heads_here = out_weight.shape[0] // HD
    cache_here = key_cache.shape[0]
    same_core = [[CORES * j + c for j in range(chips)] for c in range(CORES)]
    swap = [(i, i ^ 1) for i in range(devices)]

    across = [(i, i ^ CORES) for i in range(devices)]
    rings = chips // 2
    half = rings // 2
    chunk_rows = 2 * half * home_rows

    def across_y(block):
        return lax.ppermute(block, "ctx", across)

    neighbour = across_y(queries)
    by_ring = [queries] + [
        lax.ppermute(queries, "ctx", [(i, i ^ (2 * CORES * k)) for i in range(devices)])
        for k in range(1, rings)
    ]
    near_blocks = [(pltpu.with_memory_space_constraint(queries, pltpu.HBM), 0)]
    near_blocks += [(block, 0) for block in by_ring[1:half]]
    near_blocks += [(neighbour, 0)] + [(across_y(block), 0) for block in by_ring[1:half]]
    far = jnp.concatenate(by_ring[half:], axis=0)
    far_across = across_y(far)
    far_blocks = [(far, k) for k in range(half)] + [(far_across, k) for k in range(half)]
    late_keys, late_values, _ = lax.optimization_barrier((key_cache, value_cache, neighbour))
    key_other = lax.ppermute(late_keys, "ctx", swap)
    value_turned = late_values.T
    value_other = lax.ppermute(value_turned, "ctx", swap)
    place = jnp.stack([chip, index * cache_here, (index ^ 1) * cache_here, core, chip % 2, chip // 2]).astype(jnp.int32)

    def in_lanes(by_chip, n):
        first = (chip // CORES // half ^ n) * chips // 2
        here = lax.dynamic_slice_in_dim(by_chip, first, chips // 2, 0).reshape(1, chunk_rows)
        return jnp.tile(here, (1, HD // chunk_rows))

    len_by_chip = lax.dynamic_slice_in_dim(
        cache_len.reshape(chips, CORES * home_rows), core * home_rows, home_rows, 1
    )
    number_by_chip = jnp.arange(chips * home_rows, dtype=jnp.int32).reshape(chips, home_rows)
    lens = [in_lanes(len_by_chip, n) for n in range(2)]
    row_ids = [in_lanes(number_by_chip, n) for n in range(2)]

    flat_ids = expert_ids.reshape(-1)
    picks = jnp.arange(flat_ids.shape[0])
    earlier = (flat_ids[:, None] == flat_ids[None, :]) & (picks[None, :] < picks[:, None])
    target = (flat_ids * MOST + jnp.sum(earlier, axis=1, dtype=jnp.int32)).reshape(home_rows, top)
    experts = w_gate.shape[0]
    slots = experts * devices * MOST
    takes = target[:, :, None] == jnp.arange(slots, dtype=jnp.int32)
    chooser = jnp.any(takes, axis=1).T.astype(BF16)
    spread = jnp.sum(jnp.where(takes, route_weight[:, :, None], 0.0), axis=1)
    coarse = spread.astype(BF16)
    fine = (spread - coarse.astype(F32)).astype(BF16)

    gathered = []
    for chunk, blocks in enumerate((near_blocks, far_blocks)):
        sums = attention(
            place,
            blocks,
            (key_cache, key_other),
            (value_turned, value_other),
            new_key,
            new_value,
            lens[chunk],
            row_ids[chunk],
            chips,
            key_cache.shape[1] // HD,
        )
        if chunk:
            sums, gathered[-1] = lax.optimization_barrier((sums, gathered[-1]))
        else:
            sums, place, late_weight, _ = lax.optimization_barrier((sums, place, out_weight, far_across))
        gathered.append(
            lax.all_to_all(
                sums, "ctx", split_axis=0, concat_axis=0, axis_index_groups=same_core, tiled=True
            )
        )
    weight_other = lax.ppermute(late_weight, "ctx", swap)
    share = project(place, gathered, out_weight, weight_other, chunk_rows)
    shares = lax.all_to_all(
        share.reshape(chips, home_rows, width),
        "ctx",
        split_axis=0,
        concat_axis=0,
        axis_index_groups=same_core,
        tiled=True,
    )
    middle, outgoing = norm_and_dispatch(shares, residual, norm_gain.reshape(1, width), chooser)
    arrived = lax.all_to_all(
        outgoing.reshape(devices, experts * MOST, width), "ctx", split_axis=0, concat_axis=0, tiled=True
    )
    produced = run_experts(arrived.reshape(slots, width), w_gate, w_up, w_down)
    returned = lax.all_to_all(
        produced.reshape(devices, experts * MOST, width), "ctx", split_axis=0, concat_axis=0, tiled=True
    )
    return mix(returned.reshape(slots, width), coarse, fine, middle)


def solution(mesh):
    placed = (
        P(("groups", "ctx"), None),
        P(("groups", "ctx"), None),
        P(("groups", "ctx"), None),
        P(("groups", "ctx"), None),
        P(("groups", "ctx"), None),
        P("groups"),
        P("ctx", None),
        P(("groups", "ctx"), None),
        P(),
        P(("groups", "ctx"), None),
        P(("groups", "ctx"), None),
        P("ctx", None, None),
        P("ctx", None, None),
        P("ctx", None, None),
    )
    return jax.shard_map(
        on_device, mesh=mesh, in_specs=placed, out_specs=P(("groups", "ctx"), None), check_vma=False
    )
```

```python
import functools
import math

import jax
import jax.numpy as jnp
from jax import lax
from jax.experimental import pallas as pl
from jax.experimental.pallas import tpu as pltpu
from jax.sharding import PartitionSpec as P

HD = 128
MOST = 4
CORES = 2
STATS = 16
MASKED = -1e30
FLOOR = -1e20
LOG2E = math.log2(math.e)
MIB = 1024 * 1024
F32 = jnp.float32
BF16 = jnp.bfloat16


def nt_dot(a, b):
    return lax.dot_general(a, b, (((1,), (1,)), ((), ())), preferred_element_type=F32)


def nn_dot(a, b):
    return lax.dot_general(a, b, (((1,), (0,)), ((), ())), preferred_element_type=F32)


def attention_body(shape, place, *refs):
    key_heads, owners, owner_heads, home_rows, rows, cache_here, step = shape
    *query_refs, key_own, key_other, value_own, value_other, key_fresh, value_fresh = refs[:-8]
    lens, row_ids, out, q_rows, q_turned, hidden, scores, probs = refs[-8:]
    chip, start_own, start_other, side_here, ring_here = place[0], place[1], place[2], place[4], place[5]
    near = rows // home_rows // 2
    pack = HD // rows
    groups = owner_heads // pack

    @pl.when(pl.program_id(0) == 0)
    def _():
        lanes = lens.shape[1]
        for part, start in enumerate((start_own, start_other)):
            positions = start + lax.broadcasted_iota(jnp.int32, (cache_here, lanes), 0)
            hidden[part * cache_here : (part + 1) * cache_here, :] = jnp.where(
                positions < lens[...], 0.0, MASKED
            )
        token = chip * home_rows + lax.broadcasted_iota(jnp.int32, (home_rows, lanes), 0)
        hidden[2 * cache_here :, :] = jnp.where(token == row_ids[...], 0.0, MASKED)

    for k, piece in enumerate(query_refs):
        side = side_here if k < near else 1 - side_here
        spot = 2 * (lax.rem(ring_here, near) ^ (k % near)) + side
        q_rows[pl.ds(pl.multiple_of(spot * home_rows, home_rows), home_rows), :] = piece[...]

    factor = LOG2E / math.sqrt(HD)
    wide = owners * groups * HD
    for n in range(key_heads * owners * groups):
        block = jnp.concatenate(
            [q_rows[:, h * HD : (h + 1) * HD] for h in range(n * pack, (n + 1) * pack)], axis=0
        )
        scaled = block.T.astype(F32) * factor
        coarse = scaled.astype(BF16)
        q_turned[:HD, n * HD : (n + 1) * HD] = coarse
        q_turned[HD:, n * HD : (n + 1) * HD] = (scaled - coarse.astype(F32)).astype(BF16)

    each = range(key_heads)
    heads = [slice(g * HD, (g + 1) * HD) for g in each]
    across = [slice(g * wide, (g + 1) * wide) for g in each]

    def score(g, keys, at):
        s = nn_dot(jnp.concatenate([keys, keys], axis=1), q_turned[:, across[g]])
        return s + jnp.concatenate([hidden[at, :]] * (owners * groups), axis=1)

    def most(s):
        return jnp.max(s.reshape(s.shape[0] // 8, 8, wide), axis=0)

    fresh_at = slice(2 * cache_here, 2 * cache_here + home_rows)
    s_new = [score(g, key_fresh[:, heads[g]], fresh_at) for g in each]
    run = [most(s) for s in s_new]
    pieces = [(part, i) for part in range(2) for i in range(0, cache_here, step)]
    for part, i in pieces:
        at = slice(part * cache_here + i, part * cache_here + i + step)
        for g in each:
            s = score(g, (key_own, key_other)[part][i : i + step, heads[g]], at)
            scores[at, across[g]] = s
            run[g] = jnp.maximum(run[g], most(s))
    peak = [
        jnp.maximum(jnp.max(r, axis=0, keepdims=True), FLOOR).astype(BF16).astype(F32) for r in run
    ]
    for part, i in pieces:
        at = slice(part * cache_here + i, part * cache_here + i + step)
        for g in each:
            probs[at, across[g]] = jnp.exp2((scores[at, across[g]] - peak[g]).astype(BF16))
    ones = jnp.ones((STATS, cache_here), BF16)
    sums = [
        nn_dot(jnp.concatenate([value_own[:, heads[g]].T, ones], axis=0), probs[:cache_here, across[g]])
        for g in each
    ]
    sums = [
        sums[g]
        + nn_dot(jnp.concatenate([value_other[:, heads[g]].T, ones], axis=0), probs[cache_here:, across[g]])
        for g in each
    ]
    for g in each:
        p_new = jnp.exp2((s_new[g] - peak[g]).astype(BF16))
        values = value_fresh[:, heads[g]].astype(F32).T.astype(BF16)
        numer = sums[g][:HD] + nn_dot(values, p_new)
        denom = sums[g][HD : HD + 1] + jnp.sum(p_new.astype(F32), axis=0, keepdims=True)
        high = denom.astype(BF16).astype(F32)
        low = denom - high
        for owner in range(owners):
            spot = g * owners + owner
            lanes = [slice((owner * groups + k) * HD, (owner * groups + k + 1) * HD) for k in range(groups)]
            for k, cols in enumerate(lanes):
                out[spot, k * HD : (k + 1) * HD, :] = numer[:, cols].astype(BF16)
            filled = [kind[:, cols] for kind in (peak[g], high, low) for cols in lanes]
            filled += [jnp.zeros_like(filled[0])] * (STATS - len(filled))
            out[spot, groups * HD :, :] = jnp.concatenate(filled, axis=0).astype(BF16)


def attention(place, query_blocks, keys, values, new_key, new_value, lens, row_ids, chips, kv_heads):
    home_rows = new_key.shape[0]
    rows = home_rows * len(query_blocks)
    cache_here = keys[0].shape[0]
    together = 2
    steps = kv_heads // together
    owners = chips // kv_heads
    columns = query_blocks[0][0].shape[1] // steps
    owner_heads = columns // HD // owners // together
    wide = rows * columns // HD
    height = owner_heads * rows + STATS
    step = 512
    positions = 2 * cache_here + home_rows
    kv = lambda g, place: (0, g)
    whole = lambda g, place: (0, 0)
    shape = (together, owners, owner_heads, home_rows, rows, cache_here, step)
    work = wide * steps * 2 * cache_here
    return pl.pallas_call(
        functools.partial(attention_body, shape),
        grid_spec=pltpu.PrefetchScalarGridSpec(
            num_scalar_prefetch=1,
            grid=(steps,),
            in_specs=[
                pl.BlockSpec((home_rows, columns), functools.partial(lambda n, g, place: (n, g), n))
                for _, n in query_blocks
            ]
            + [pl.BlockSpec((cache_here, together * HD), kv)] * 4
            + [pl.BlockSpec((home_rows, together * HD), kv)] * 2
            + [pl.BlockSpec(lens.shape, whole)] * 2,
            out_specs=pl.BlockSpec((together * owners, height, HD), lambda g, place: (g, 0, 0)),
            scratch_shapes=[
                pltpu.VMEM((rows, columns), BF16),
                pltpu.VMEM((2 * HD, wide), BF16),
                pltpu.VMEM((positions, HD), F32),
                pltpu.VMEM((2 * cache_here, wide), F32),
                pltpu.VMEM((2 * cache_here, wide), BF16),
            ],
        ),
        out_shape=jax.ShapeDtypeStruct((chips, height, HD), BF16),
        compiler_params=pltpu.CompilerParams(vmem_limit_bytes=40 * MIB),
        cost_estimate=pl.CostEstimate(
            flops=6 * work * HD, bytes_accessed=8 * MIB, transcendentals=work
        ),
        name="attention",
    )(
        place,
        *[block for block, _ in query_blocks],
        pltpu.with_memory_space_constraint(keys[0], pltpu.HBM),
        keys[1],
        pltpu.with_memory_space_constraint(values[0], pltpu.HBM),
        values[1],
        pltpu.with_memory_space_constraint(new_key, pltpu.HBM),
        pltpu.with_memory_space_constraint(new_value, pltpu.HBM),
        lens,
        row_ids,
    )


def project_body(rows, place, *refs):
    *chunks, weight_own, weight_other, out, turned = refs
    core = place[3]
    chips, height, _ = chunks[0].shape
    base = height - STATS
    groups = base // HD
    pack = HD // rows
    heads_here = groups * pack // CORES
    half = chips // 2 // 2
    for near in range(2):
        sources = [chunks[s // 2 // half ^ near].at[s] for s in range(chips)]
        stats = [part[base:, :].astype(F32) for part in sources]
        peaks = [stat[:groups] for stat in stats]
        top = functools.reduce(jnp.maximum, peaks)
        share = [jnp.exp2(peak - top) for peak in peaks]
        denom = sum(w * (t[groups : 2 * groups] + t[2 * groups : 3 * groups]) for w, t in zip(share, stats))
        for k in range(groups):
            numer = sum(
                part[k * HD : (k + 1) * HD, :].astype(F32) * w[k : k + 1, :] for part, w in zip(sources, share)
            )
            attended = (numer / denom[k : k + 1, :]).T.astype(BF16)
            for j in range(pack):
                part, h = divmod(k * pack + j, heads_here)
                turned[part, near * rows : (near + 1) * rows, h * HD : (h + 1) * HD] = attended[
                    j * rows : (j + 1) * rows
                ]
    product = nn_dot(turned[core], weight_own[...]) + nn_dot(turned[1 - core], weight_other[...])
    out[...] = product.astype(BF16)


def project(place, chunks, weight_own, weight_other, rows):
    depth, width = weight_own.shape
    vmem = pl.BlockSpec(memory_space=pltpu.VMEM)
    return pl.pallas_call(
        functools.partial(project_body, rows),
        in_specs=[pl.BlockSpec(memory_space=pltpu.SMEM)] + [vmem] * (len(chunks) + 2),
        out_specs=vmem,
        out_shape=jax.ShapeDtypeStruct((2 * rows, width), BF16),
        scratch_shapes=[pltpu.VMEM((CORES, 2 * rows, depth), BF16)],
        compiler_params=pltpu.CompilerParams(vmem_limit_bytes=32 * MIB),
        cost_estimate=pl.CostEstimate(
            flops=8 * rows * width * depth, bytes_accessed=4 * MIB, transcendentals=0
        ),
        name="project",
    )(place, *chunks, weight_own, weight_other)


def norm_body(parts, residual, gain, chooser, middle_out, sent):
    total = parts[0].astype(F32)
    for s in range(1, parts.shape[0]):
        total = total + parts[s].astype(F32)
    middle = (residual[...].astype(F32) + total).astype(BF16)
    middle_out[...] = middle
    middle = middle.astype(F32)
    inv_rms = lax.rsqrt(jnp.mean(middle * middle, axis=-1, keepdims=True) + 1e-06)
    normed = (middle * inv_rms * gain[...].astype(F32)).astype(BF16)
    sent[...] = nn_dot(chooser[...], normed).astype(BF16)


def norm_and_dispatch(parts, residual, gain, chooser):
    vmem = pl.BlockSpec(memory_space=pltpu.VMEM)
    rows, width = residual.shape
    return pl.pallas_call(
        norm_body,
        in_specs=[vmem] * 4,
        out_specs=[vmem] * 2,
        out_shape=[
            jax.ShapeDtypeStruct((rows, width), BF16),
            jax.ShapeDtypeStruct((chooser.shape[0], width), BF16),
        ],
        compiler_params=pltpu.CompilerParams(vmem_limit_bytes=24 * MIB),
        cost_estimate=pl.CostEstimate(
            flops=2 * chooser.shape[0] * rows * width, bytes_accessed=2 * MIB, transcendentals=0
        ),
        name="norm_and_dispatch",
    )(parts, residual, gain, chooser)


def experts_body(step, arrived, w_gate, w_up, w_down, out, gate_held, up_held, down_held, sems):
    experts, _, depth = w_gate.shape
    rows, width = arrived.shape
    pieces = [(e, f) for e in range(experts) for f in range(0, depth, step)]
    copies = []
    for n, (e, f) in enumerate(pieces):
        down = pl.ds(f, step)
        copies.append(
            [
                pltpu.make_async_copy(w_gate.at[e, :, down], gate_held.at[n], sems.at[n, 0]),
                pltpu.make_async_copy(w_up.at[e, :, down], up_held.at[n], sems.at[n, 1]),
                pltpu.make_async_copy(w_down.at[e, down, :], down_held.at[n], sems.at[n, 2]),
            ]
        )
    for piece in copies:
        for copy in piece[:2]:
            copy.start()
    for piece in copies:
        piece[2].start()
    slot = lax.broadcasted_iota(jnp.int32, (rows, 1), 0)
    values = arrived[...]
    hidden = []
    for n, (e, f) in enumerate(pieces):
        copies[n][0].wait()
        copies[n][1].wait()
        gate = nn_dot(values, gate_held[n])
        upward = nn_dot(values, up_held[n])
        part = gate / (1.0 + jnp.exp(-gate)) * upward
        mine = lax.rem(slot, experts * MOST) // MOST == e
        hidden.append(jnp.where(mine, part, 0.0).astype(BF16))
    total = None
    for n in range(len(pieces)):
        copies[n][2].wait()
        term = nn_dot(hidden[n], down_held[n])
        total = term if total is None else total + term
    out[...] = total.astype(BF16)


def run_experts(arrived, w_gate, w_up, w_down):
    rows, width = arrived.shape
    experts, _, depth = w_gate.shape
    step = 256
    pieces = experts * depth // step
    vmem = pl.BlockSpec(memory_space=pltpu.VMEM)
    hbm = pl.BlockSpec(memory_space=pltpu.HBM)
    weights = [pltpu.with_memory_space_constraint(w, pltpu.HBM) for w in (w_gate, w_up, w_down)]
    return pl.pallas_call(
        functools.partial(experts_body, step),
        in_specs=[vmem] + [hbm] * 3,
        out_specs=vmem,
        out_shape=jax.ShapeDtypeStruct((rows, width), BF16),
        scratch_shapes=[
            pltpu.VMEM((pieces, width, step), BF16),
            pltpu.VMEM((pieces, width, step), BF16),
            pltpu.VMEM((pieces, step, width), BF16),
            pltpu.SemaphoreType.DMA((pieces, 3)),
        ],
        compiler_params=pltpu.CompilerParams(vmem_limit_bytes=44 * MIB),
        cost_estimate=pl.CostEstimate(
            flops=6 * rows * width * experts * depth,
            bytes_accessed=6 * width * experts * depth,
            transcendentals=rows * experts * depth,
        ),
        name="experts",
    )(arrived, *weights)


def mix_body(returned, coarse, fine, middle, out):
    values = returned[...]
    mixed = nn_dot(coarse[...], values) + nn_dot(fine[...], values)
    out[...] = (middle[...].astype(F32) + mixed).astype(BF16)


def mix(returned, coarse, fine, middle):
    vmem = pl.BlockSpec(memory_space=pltpu.VMEM)
    return pl.pallas_call(
        mix_body,
        in_specs=[vmem] * 4,
        out_specs=vmem,
        out_shape=jax.ShapeDtypeStruct(middle.shape, BF16),
        compiler_params=pltpu.CompilerParams(vmem_limit_bytes=16 * MIB),
        name="mix",
    )(returned, coarse, fine, middle)


def on_device(
    queries,
    new_key,
    new_value,
    key_cache,
    value_cache,
    cache_len,
    out_weight,
    residual,
    norm_gain,
    expert_ids,
    route_weight,
    w_gate,
    w_up,
    w_down,
):
    devices = lax.axis_size("ctx")
    chips = devices // CORES
    index = lax.axis_index("ctx")
    chip, core = index // CORES, index % CORES
    home_rows, width = residual.shape
    top = expert_ids.shape[1]
    heads_here = out_weight.shape[0] // HD
    cache_here = key_cache.shape[0]
    same_core = [[CORES * j + c for j in range(chips)] for c in range(CORES)]
    swap = [(i, i ^ 1) for i in range(devices)]

    across = [(i, i ^ CORES) for i in range(devices)]
    rings = chips // 2
    half = rings // 2
    chunk_rows = 2 * half * home_rows

    def across_y(block):
        return lax.ppermute(block, "ctx", across)

    neighbour = across_y(queries)
    by_ring = [queries] + [
        lax.ppermute(queries, "ctx", [(i, i ^ (2 * CORES * k)) for i in range(devices)])
        for k in range(1, rings)
    ]
    near_blocks = [(pltpu.with_memory_space_constraint(queries, pltpu.HBM), 0)]
    near_blocks += [(block, 0) for block in by_ring[1:half]]
    near_blocks += [(neighbour, 0)] + [(across_y(block), 0) for block in by_ring[1:half]]
    key_other = lax.ppermute(key_cache, "ctx", swap)
    value_other = lax.ppermute(value_cache, "ctx", swap)

    place = jnp.stack([chip, index * cache_here, (index ^ 1) * cache_here, core, chip % 2, chip // 2]).astype(jnp.int32)

    def in_lanes(by_chip, n):
        first = (chip // CORES // half ^ n) * chips // 2
        here = lax.dynamic_slice_in_dim(by_chip, first, chips // 2, 0).reshape(1, chunk_rows)
        return jnp.tile(here, (1, HD // chunk_rows))

    len_by_chip = lax.dynamic_slice_in_dim(
        cache_len.reshape(chips, CORES * home_rows), core * home_rows, home_rows, 1
    )
    number_by_chip = jnp.arange(chips * home_rows, dtype=jnp.int32).reshape(chips, home_rows)
    lens = [in_lanes(len_by_chip, n) for n in range(2)]
    row_ids = [in_lanes(number_by_chip, n) for n in range(2)]

    flat_ids = expert_ids.reshape(-1)
    picks = jnp.arange(flat_ids.shape[0])
    earlier = (flat_ids[:, None] == flat_ids[None, :]) & (picks[None, :] < picks[:, None])
    target = (flat_ids * MOST + jnp.sum(earlier, axis=1, dtype=jnp.int32)).reshape(home_rows, top)
    experts = w_gate.shape[0]
    slots = experts * devices * MOST
    takes = target[:, :, None] == jnp.arange(slots, dtype=jnp.int32)
    chooser = jnp.any(takes, axis=1).T.astype(BF16)
    spread = jnp.sum(jnp.where(takes, route_weight[:, :, None], 0.0), axis=1)
    coarse = spread.astype(BF16)
    fine = (spread - coarse.astype(F32)).astype(BF16)

    def attend(blocks, n, place):
        return attention(
            place,
            blocks,
            (key_cache, key_other),
            (value_cache, value_other),
            new_key,
            new_value,
            lens[n],
            row_ids[n],
            chips,
            key_cache.shape[1] // HD,
        )

    def to_owners(sums):
        return lax.all_to_all(
            sums, "ctx", split_axis=0, concat_axis=0, axis_index_groups=same_core, tiled=True
        )

    sums = attend(near_blocks, 0, place)
    sums, late_place, late_weight, far = lax.optimization_barrier((sums, place, out_weight, by_ring[half:]))
    far_blocks = [(block, 0) for block in far] + [(across_y(block), 0) for block in far]
    gathered = [to_owners(sums)]
    sums = attend(far_blocks, 1, late_place)
    sums, gathered[0] = lax.optimization_barrier((sums, gathered[0]))
    gathered.append(to_owners(sums))
    weight_other = lax.ppermute(late_weight, "ctx", swap)
    share = project(place, gathered, out_weight, weight_other, chunk_rows)
    shares = lax.all_to_all(
        share.reshape(chips, home_rows, width),
        "ctx",
        split_axis=0,
        concat_axis=0,
        axis_index_groups=same_core,
        tiled=True,
    )
    middle, outgoing = norm_and_dispatch(shares, residual, norm_gain.reshape(1, width), chooser)
    arrived = lax.all_to_all(
        outgoing.reshape(devices, experts * MOST, width), "ctx", split_axis=0, concat_axis=0, tiled=True
    )
    produced = run_experts(arrived.reshape(slots, width), w_gate, w_up, w_down)
    returned = lax.all_to_all(
        produced.reshape(devices, experts * MOST, width), "ctx", split_axis=0, concat_axis=0, tiled=True
    )
    return mix(returned.reshape(slots, width), coarse, fine, middle)


def solution(mesh):
    placed = (
        P(("groups", "ctx"), None),
        P(("groups", "ctx"), None),
        P(("groups", "ctx"), None),
        P(("groups", "ctx"), None),
        P(("groups", "ctx"), None),
        P("groups"),
        P("ctx", None),
        P(("groups", "ctx"), None),
        P(),
        P(("groups", "ctx"), None),
        P(("groups", "ctx"), None),
        P("ctx", None, None),
        P("ctx", None, None),
        P("ctx", None, None),
    )
    return jax.shard_map(
        on_device, mesh=mesh, in_specs=placed, out_specs=P(("groups", "ctx"), None), check_vma=False
    )
```

```python
import functools
import math

import jax
import jax.numpy as jnp
from jax import lax
from jax.experimental import pallas as pl
from jax.experimental.pallas import tpu as pltpu
from jax.sharding import PartitionSpec as P

HD = 128
MOST = 4
CORES = 2
STATS = 16
MASKED = -1e30
FLOOR = -1e20
LOG2E = math.log2(math.e)
MIB = 1024 * 1024
F32 = jnp.float32
BF16 = jnp.bfloat16


def nt_dot(a, b):
    return lax.dot_general(a, b, (((1,), (1,)), ((), ())), preferred_element_type=F32)


def nn_dot(a, b):
    return lax.dot_general(a, b, (((1,), (0,)), ((), ())), preferred_element_type=F32)


def attention_body(shape, place, *refs):
    steps, key_heads, owners, owner_heads, home_rows, rows, cache_here, piece = shape
    inputs, (lens, row_ids, out) = refs[:-13], refs[-13:-10]
    q_rows, q_turned, hidden, scores, probs, keys, values, key_new, value_new, sems = refs[-10:]
    *query_refs, key_own, key_other, value_own, value_other, key_fresh, value_fresh = inputs
    chip, start_own, start_other, side_here, ring_here = place[0], place[1], place[2], place[4], place[5]
    near = rows // home_rows // 2
    pack = HD // rows
    groups = owner_heads // pack
    columns = key_heads * HD
    parts = [slice(part * cache_here, (part + 1) * cache_here) for part in range(2)]

    copies = []

    def copy(source, target):
        copies.append(pltpu.make_async_copy(source, target, sems.at[len(copies)]))
        copies[-1].start()
        return copies[-1]

    small = [copy(key_fresh, key_new), copy(value_fresh, value_new)]
    for k, block in enumerate(query_refs):
        side = side_here if k < near else 1 - side_here
        spot = 2 * (lax.rem(ring_here, near) ^ (k % near)) + side
        place_rows = pl.ds(pl.multiple_of(spot * home_rows, home_rows), home_rows)
        small.append(copy(block, q_rows.at[place_rows, :]))
    key_copies, value_copies = [], []
    for n in range(steps):
        cols = pl.ds(n * columns, columns)
        key_copies.append(
            [copy(source.at[:, cols], keys.at[n, parts[p], :]) for p, source in enumerate((key_own, key_other))]
        )
        value_copies.append(
            [copy(source.at[:, cols], values.at[n, parts[p], :]) for p, source in enumerate((value_own, value_other))]
        )

    for part, start in enumerate((start_own, start_other)):
        positions = start + lax.broadcasted_iota(jnp.int32, (cache_here, HD), 0)
        hidden[parts[part], :] = jnp.where(positions < lens[...], 0.0, MASKED)
    token = chip * home_rows + lax.broadcasted_iota(jnp.int32, (home_rows, HD), 0)
    hidden[2 * cache_here :, :] = jnp.where(token == row_ids[...], 0.0, MASKED)

    for one in small:
        one.wait()
    factor = LOG2E / math.sqrt(HD)
    wide = owners * groups * HD
    for n in range(steps * key_heads * owners * groups):
        block = jnp.concatenate(
            [q_rows[:, h * HD : (h + 1) * HD] for h in range(n * pack, (n + 1) * pack)], axis=0
        )
        scaled = block.T.astype(F32) * factor
        coarse = scaled.astype(BF16)
        q_turned[:HD, n * HD : (n + 1) * HD] = coarse
        q_turned[HD:, n * HD : (n + 1) * HD] = (scaled - coarse.astype(F32)).astype(BF16)

    each = range(key_heads)
    heads = [slice(g * HD, (g + 1) * HD) for g in each]
    across = [slice(g * wide, (g + 1) * wide) for g in each]
    fresh_at = slice(2 * cache_here, 2 * cache_here + home_rows)
    pieces = [slice(i, i + piece) for i in range(0, 2 * cache_here, piece)]
    ones = jnp.ones((STATS, cache_here), BF16)

    def most(s):
        return jnp.max(s.reshape(s.shape[0] // 8, 8, wide), axis=0)

    for n in range(steps):

        def score(g, keys_here, at):
            first = (n * key_heads + g) * wide
            s = nn_dot(jnp.concatenate([keys_here, keys_here], axis=1), q_turned[:, first : first + wide])
            return s + jnp.concatenate([hidden[at, :]] * (owners * groups), axis=1)

        for one in key_copies[n]:
            one.wait()
        whole = [slice((n * key_heads + g) * HD, (n * key_heads + g + 1) * HD) for g in each]
        s_new = [score(g, key_new[:, whole[g]], fresh_at) for g in each]
        run = [most(s) for s in s_new]
        for at in pieces:
            for g in each:
                s = score(g, keys[n, at, heads[g]], at)
                scores[n % 2, at, across[g]] = s
                run[g] = jnp.maximum(run[g], most(s))
        peak = [
            jnp.maximum(jnp.max(r, axis=0, keepdims=True), FLOOR).astype(BF16).astype(F32) for r in run
        ]
        for at in pieces:
            for g in each:
                probs[n % 2, at, across[g]] = jnp.exp2((scores[n % 2, at, across[g]] - peak[g]).astype(BF16))
        for one in value_copies[n]:
            one.wait()
        for g in each:
            sums = 0.0
            for part in parts:
                turned = jnp.concatenate([values[n, part, heads[g]].T, ones], axis=0)
                sums = sums + nn_dot(turned, probs[n % 2, part, across[g]])
            p_new = jnp.exp2((s_new[g] - peak[g]).astype(BF16))
            fresh = value_new[:, whole[g]].astype(F32).T.astype(BF16)
            numer = sums[:HD] + nn_dot(fresh, p_new)
            denom = sums[HD : HD + 1] + jnp.sum(p_new.astype(F32), axis=0, keepdims=True)
            high = denom.astype(BF16).astype(F32)
            low = denom - high
            for owner in range(owners):
                spot = (n * key_heads + g) * owners + owner
                lanes = [slice((owner * groups + k) * HD, (owner * groups + k + 1) * HD) for k in range(groups)]
                for k, cols in enumerate(lanes):
                    out[spot, k * HD : (k + 1) * HD, :] = numer[:, cols].astype(BF16)
                filled = [kind[:, cols] for kind in (peak[g], high, low) for cols in lanes]
                filled += [jnp.zeros_like(filled[0])] * (STATS - len(filled))
                out[spot, groups * HD :, :] = jnp.concatenate(filled, axis=0).astype(BF16)


def attention(place, query_blocks, keys, values, new_key, new_value, lens, row_ids, chips, kv_heads):
    home_rows = new_key.shape[0]
    rows = home_rows * len(query_blocks)
    cache_here = keys[0].shape[0]
    together = 2
    steps = kv_heads // together
    owners = chips // kv_heads
    width = query_blocks[0].shape[1]
    owner_heads = width // HD // chips
    wide = together * owners * owner_heads * rows
    height = owner_heads * rows + STATS
    piece = 512
    positions = 2 * cache_here
    shape = (steps, together, owners, owner_heads, home_rows, rows, cache_here, piece)
    work = wide * steps * positions
    vmem = pl.BlockSpec(memory_space=pltpu.VMEM)
    anywhere = pl.BlockSpec(memory_space=pl.ANY)
    inputs = [*query_blocks, *keys, *values, new_key, new_value]
    return pl.pallas_call(
        functools.partial(attention_body, shape),
        in_specs=[pl.BlockSpec(memory_space=pltpu.SMEM)] + [anywhere] * len(inputs) + [vmem] * 2,
        out_specs=vmem,
        scratch_shapes=[
            pltpu.VMEM((rows, width), BF16),
            pltpu.VMEM((2 * HD, steps * wide), BF16),
            pltpu.VMEM((positions + home_rows, HD), F32),
            pltpu.VMEM((2, positions, wide), F32),
            pltpu.VMEM((2, positions, wide), BF16),
            pltpu.VMEM((steps, positions, together * HD), BF16),
            pltpu.VMEM((steps, positions, together * HD), BF16),
            pltpu.VMEM(new_key.shape, BF16),
            pltpu.VMEM(new_value.shape, BF16),
            pltpu.SemaphoreType.DMA((len(query_blocks) + 2 + 4 * steps,)),
        ],
        out_shape=jax.ShapeDtypeStruct((chips, height, HD), BF16),
        compiler_params=pltpu.CompilerParams(vmem_limit_bytes=48 * MIB),
        cost_estimate=pl.CostEstimate(
            flops=6 * work * HD, bytes_accessed=8 * MIB, transcendentals=work
        ),
        name="attention",
    )(
        place,
        *query_blocks,
        pltpu.with_memory_space_constraint(keys[0], pltpu.HBM),
        keys[1],
        pltpu.with_memory_space_constraint(values[0], pltpu.HBM),
        values[1],
        pltpu.with_memory_space_constraint(new_key, pltpu.HBM),
        pltpu.with_memory_space_constraint(new_value, pltpu.HBM),
        lens,
        row_ids,
    )


def project_body(rows, place, *refs):
    *chunks, weight_own, weight_other, out, turned = refs
    core = place[3]
    chips, height, _ = chunks[0].shape
    base = height - STATS
    groups = base // HD
    pack = HD // rows
    heads_here = groups * pack // CORES
    half = chips // 2 // 2
    for near in range(2):
        sources = [chunks[s // 2 // half ^ near].at[s] for s in range(chips)]
        stats = [part[base:, :].astype(F32) for part in sources]
        peaks = [stat[:groups] for stat in stats]
        top = functools.reduce(jnp.maximum, peaks)
        share = [jnp.exp2(peak - top) for peak in peaks]
        denom = sum(w * (t[groups : 2 * groups] + t[2 * groups : 3 * groups]) for w, t in zip(share, stats))
        for k in range(groups):
            numer = sum(
                part[k * HD : (k + 1) * HD, :].astype(F32) * w[k : k + 1, :] for part, w in zip(sources, share)
            )
            attended = (numer / denom[k : k + 1, :]).T.astype(BF16)
            for j in range(pack):
                part, h = divmod(k * pack + j, heads_here)
                turned[part, near * rows : (near + 1) * rows, h * HD : (h + 1) * HD] = attended[
                    j * rows : (j + 1) * rows
                ]
    product = nn_dot(turned[core], weight_own[...]) + nn_dot(turned[1 - core], weight_other[...])
    out[...] = product.astype(BF16)


def project(place, chunks, weight_own, weight_other, rows):
    depth, width = weight_own.shape
    vmem = pl.BlockSpec(memory_space=pltpu.VMEM)
    return pl.pallas_call(
        functools.partial(project_body, rows),
        in_specs=[pl.BlockSpec(memory_space=pltpu.SMEM)] + [vmem] * (len(chunks) + 2),
        out_specs=vmem,
        out_shape=jax.ShapeDtypeStruct((2 * rows, width), BF16),
        scratch_shapes=[pltpu.VMEM((CORES, 2 * rows, depth), BF16)],
        compiler_params=pltpu.CompilerParams(vmem_limit_bytes=32 * MIB),
        cost_estimate=pl.CostEstimate(
            flops=8 * rows * width * depth, bytes_accessed=4 * MIB, transcendentals=0
        ),
        name="project",
    )(place, *chunks, weight_own, weight_other)


def norm_body(parts, residual, gain, chooser, middle_out, sent):
    total = parts[0].astype(F32)
    for s in range(1, parts.shape[0]):
        total = total + parts[s].astype(F32)
    middle = (residual[...].astype(F32) + total).astype(BF16)
    middle_out[...] = middle
    middle = middle.astype(F32)
    inv_rms = lax.rsqrt(jnp.mean(middle * middle, axis=-1, keepdims=True) + 1e-06)
    normed = (middle * inv_rms * gain[...].astype(F32)).astype(BF16)
    sent[...] = nn_dot(chooser[...], normed).astype(BF16)


def norm_and_dispatch(parts, residual, gain, chooser):
    vmem = pl.BlockSpec(memory_space=pltpu.VMEM)
    rows, width = residual.shape
    return pl.pallas_call(
        norm_body,
        in_specs=[vmem] * 4,
        out_specs=[vmem] * 2,
        out_shape=[
            jax.ShapeDtypeStruct((rows, width), BF16),
            jax.ShapeDtypeStruct((chooser.shape[0], width), BF16),
        ],
        compiler_params=pltpu.CompilerParams(vmem_limit_bytes=24 * MIB),
        cost_estimate=pl.CostEstimate(
            flops=2 * chooser.shape[0] * rows * width, bytes_accessed=2 * MIB, transcendentals=0
        ),
        name="norm_and_dispatch",
    )(parts, residual, gain, chooser)


def experts_body(step, arrived, w_gate, w_up, w_down, out, gate_held, up_held, down_held, sems):
    experts, _, depth = w_gate.shape
    rows, width = arrived.shape
    pieces = [(e, f) for e in range(experts) for f in range(0, depth, step)]
    copies = []
    for n, (e, f) in enumerate(pieces):
        down = pl.ds(f, step)
        copies.append(
            [
                pltpu.make_async_copy(w_gate.at[e, :, down], gate_held.at[n], sems.at[n, 0]),
                pltpu.make_async_copy(w_up.at[e, :, down], up_held.at[n], sems.at[n, 1]),
                pltpu.make_async_copy(w_down.at[e, down, :], down_held.at[n], sems.at[n, 2]),
            ]
        )
    for piece in copies:
        for copy in piece[:2]:
            copy.start()
    for piece in copies:
        piece[2].start()
    slot = lax.broadcasted_iota(jnp.int32, (rows, 1), 0)
    values = arrived[...]
    hidden = []
    for n, (e, f) in enumerate(pieces):
        copies[n][0].wait()
        copies[n][1].wait()
        gate = nn_dot(values, gate_held[n])
        upward = nn_dot(values, up_held[n])
        part = gate / (1.0 + jnp.exp(-gate)) * upward
        mine = lax.rem(slot, experts * MOST) // MOST == e
        hidden.append(jnp.where(mine, part, 0.0).astype(BF16))
    total = None
    for n in range(len(pieces)):
        copies[n][2].wait()
        term = nn_dot(hidden[n], down_held[n])
        total = term if total is None else total + term
    out[...] = total.astype(BF16)


def run_experts(arrived, w_gate, w_up, w_down):
    rows, width = arrived.shape
    experts, _, depth = w_gate.shape
    step = 256
    pieces = experts * depth // step
    vmem = pl.BlockSpec(memory_space=pltpu.VMEM)
    hbm = pl.BlockSpec(memory_space=pltpu.HBM)
    weights = [pltpu.with_memory_space_constraint(w, pltpu.HBM) for w in (w_gate, w_up, w_down)]
    return pl.pallas_call(
        functools.partial(experts_body, step),
        in_specs=[vmem] + [hbm] * 3,
        out_specs=vmem,
        out_shape=jax.ShapeDtypeStruct((rows, width), BF16),
        scratch_shapes=[
            pltpu.VMEM((pieces, width, step), BF16),
            pltpu.VMEM((pieces, width, step), BF16),
            pltpu.VMEM((pieces, step, width), BF16),
            pltpu.SemaphoreType.DMA((pieces, 3)),
        ],
        compiler_params=pltpu.CompilerParams(vmem_limit_bytes=44 * MIB),
        cost_estimate=pl.CostEstimate(
            flops=6 * rows * width * experts * depth,
            bytes_accessed=6 * width * experts * depth,
            transcendentals=rows * experts * depth,
        ),
        name="experts",
    )(arrived, *weights)


def mix_body(returned, coarse, fine, middle, out):
    values = returned[...]
    mixed = nn_dot(coarse[...], values) + nn_dot(fine[...], values)
    out[...] = (middle[...].astype(F32) + mixed).astype(BF16)


def mix(returned, coarse, fine, middle):
    vmem = pl.BlockSpec(memory_space=pltpu.VMEM)
    return pl.pallas_call(
        mix_body,
        in_specs=[vmem] * 4,
        out_specs=vmem,
        out_shape=jax.ShapeDtypeStruct(middle.shape, BF16),
        compiler_params=pltpu.CompilerParams(vmem_limit_bytes=16 * MIB),
        name="mix",
    )(returned, coarse, fine, middle)


def on_device(
    queries,
    new_key,
    new_value,
    key_cache,
    value_cache,
    cache_len,
    out_weight,
    residual,
    norm_gain,
    expert_ids,
    route_weight,
    w_gate,
    w_up,
    w_down,
):
    devices = lax.axis_size("ctx")
    chips = devices // CORES
    index = lax.axis_index("ctx")
    chip, core = index // CORES, index % CORES
    home_rows, width = residual.shape
    top = expert_ids.shape[1]
    heads_here = out_weight.shape[0] // HD
    cache_here = key_cache.shape[0]
    same_core = [[CORES * j + c for j in range(chips)] for c in range(CORES)]
    swap = [(i, i ^ 1) for i in range(devices)]

    across = [(i, i ^ CORES) for i in range(devices)]
    rings = chips // 2
    half = rings // 2
    chunk_rows = 2 * half * home_rows

    def across_y(block):
        return lax.ppermute(block, "ctx", across)

    neighbour = across_y(queries)
    by_ring = [queries] + [
        lax.ppermute(queries, "ctx", [(i, i ^ (2 * CORES * k)) for i in range(devices)])
        for k in range(1, rings)
    ]
    near_blocks = [pltpu.with_memory_space_constraint(queries, pltpu.HBM), *by_ring[1:half]]
    near_blocks += [neighbour] + [across_y(block) for block in by_ring[1:half]]
    far_across = [across_y(block) for block in by_ring[half:]]
    far_blocks = by_ring[half:] + far_across
    late_keys, late_values, _ = lax.optimization_barrier((key_cache, value_cache, neighbour))
    key_other = lax.ppermute(late_keys, "ctx", swap)
    value_other = lax.ppermute(late_values, "ctx", swap)
    place = jnp.stack([chip, index * cache_here, (index ^ 1) * cache_here, core, chip % 2, chip // 2]).astype(jnp.int32)

    def in_lanes(by_chip, n):
        first = (chip // CORES // half ^ n) * chips // 2
        here = lax.dynamic_slice_in_dim(by_chip, first, chips // 2, 0).reshape(1, chunk_rows)
        return jnp.tile(here, (1, HD // chunk_rows))

    len_by_chip = lax.dynamic_slice_in_dim(
        cache_len.reshape(chips, CORES * home_rows), core * home_rows, home_rows, 1
    )
    number_by_chip = jnp.arange(chips * home_rows, dtype=jnp.int32).reshape(chips, home_rows)
    lens = [in_lanes(len_by_chip, n) for n in range(2)]
    row_ids = [in_lanes(number_by_chip, n) for n in range(2)]

    flat_ids = expert_ids.reshape(-1)
    picks = jnp.arange(flat_ids.shape[0])
    earlier = (flat_ids[:, None] == flat_ids[None, :]) & (picks[None, :] < picks[:, None])
    target = (flat_ids * MOST + jnp.sum(earlier, axis=1, dtype=jnp.int32)).reshape(home_rows, top)
    experts = w_gate.shape[0]
    slots = experts * devices * MOST
    takes = target[:, :, None] == jnp.arange(slots, dtype=jnp.int32)
    chooser = jnp.any(takes, axis=1).T.astype(BF16)
    spread = jnp.sum(jnp.where(takes, route_weight[:, :, None], 0.0), axis=1)
    coarse = spread.astype(BF16)
    fine = (spread - coarse.astype(F32)).astype(BF16)

    gathered = []
    for chunk, blocks in enumerate((near_blocks, far_blocks)):
        sums = attention(
            place,
            blocks,
            (key_cache, key_other),
            (value_cache, value_other),
            new_key,
            new_value,
            lens[chunk],
            row_ids[chunk],
            chips,
            key_cache.shape[1] // HD,
        )
        if chunk:
            sums, gathered[-1] = lax.optimization_barrier((sums, gathered[-1]))
        else:
            sums, place, late_weight, _ = lax.optimization_barrier((sums, place, out_weight, far_across))
        gathered.append(
            lax.all_to_all(
                sums, "ctx", split_axis=0, concat_axis=0, axis_index_groups=same_core, tiled=True
            )
        )
    weight_other = lax.ppermute(late_weight, "ctx", swap)
    share = project(place, gathered, out_weight, weight_other, chunk_rows)
    shares = lax.all_to_all(
        share.reshape(chips, home_rows, width),
        "ctx",
        split_axis=0,
        concat_axis=0,
        axis_index_groups=same_core,
        tiled=True,
    )
    middle, outgoing = norm_and_dispatch(shares, residual, norm_gain.reshape(1, width), chooser)
    arrived = lax.all_to_all(
        outgoing.reshape(devices, experts * MOST, width), "ctx", split_axis=0, concat_axis=0, tiled=True
    )
    produced = run_experts(arrived.reshape(slots, width), w_gate, w_up, w_down)
    returned = lax.all_to_all(
        produced.reshape(devices, experts * MOST, width), "ctx", split_axis=0, concat_axis=0, tiled=True
    )
    return mix(returned.reshape(slots, width), coarse, fine, middle)


def solution(mesh):
    placed = (
        P(("groups", "ctx"), None),
        P(("groups", "ctx"), None),
        P(("groups", "ctx"), None),
        P(("groups", "ctx"), None),
        P(("groups", "ctx"), None),
        P("groups"),
        P("ctx", None),
        P(("groups", "ctx"), None),
        P(),
        P(("groups", "ctx"), None),
        P(("groups", "ctx"), None),
        P("ctx", None, None),
        P("ctx", None, None),
        P("ctx", None, None),
    )
    return jax.shard_map(
        on_device, mesh=mesh, in_specs=placed, out_specs=P(("groups", "ctx"), None), check_vma=False
    )
```

```python
import functools
import math

import jax
import jax.numpy as jnp
from jax import lax
from jax.experimental import pallas as pl
from jax.experimental.pallas import tpu as pltpu
from jax.sharding import PartitionSpec as P

HD = 128
MOST = 4
CORES = 2
STATS = 16
MASKED = -1e30
FLOOR = -1e20
LOG2E = math.log2(math.e)
MIB = 1024 * 1024
F32 = jnp.float32
BF16 = jnp.bfloat16


def nt_dot(a, b):
    return lax.dot_general(a, b, (((1,), (1,)), ((), ())), preferred_element_type=F32)


def nn_dot(a, b):
    return lax.dot_general(a, b, (((1,), (0,)), ((), ())), preferred_element_type=F32)


def attention_body(shape, place, *refs):
    key_heads, owners, owner_heads, home_rows, rows, cache_here, step = shape
    *query_refs, key_own, key_other, value_own, value_other, key_fresh, value_fresh = refs[:-8]
    lens, row_ids, out, q_rows, q_turned, hidden, scores, probs = refs[-8:]
    chip, start_own, start_other, side_here, ring_here = place[0], place[1], place[2], place[4], place[5]
    near = rows // home_rows // 2
    pack = HD // rows
    groups = owner_heads // pack

    @pl.when(pl.program_id(0) == 0)
    def _():
        lanes = lens.shape[1]
        for part, start in enumerate((start_own, start_other)):
            positions = start + lax.broadcasted_iota(jnp.int32, (cache_here, lanes), 0)
            hidden[part * cache_here : (part + 1) * cache_here, :] = jnp.where(
                positions < lens[...], 0.0, MASKED
            )
        token = chip * home_rows + lax.broadcasted_iota(jnp.int32, (home_rows, lanes), 0)
        hidden[2 * cache_here :, :] = jnp.where(token == row_ids[...], 0.0, MASKED)

    for k, piece in enumerate(query_refs):
        side = side_here if k < near else 1 - side_here
        spot = 2 * (lax.rem(ring_here, near) ^ (k % near)) + side
        q_rows[pl.ds(pl.multiple_of(spot * home_rows, home_rows), home_rows), :] = piece[...]

    factor = LOG2E / math.sqrt(HD)
    wide = owners * groups * HD
    for n in range(key_heads * owners * groups):
        block = jnp.concatenate(
            [q_rows[:, h * HD : (h + 1) * HD] for h in range(n * pack, (n + 1) * pack)], axis=0
        )
        scaled = block.T.astype(F32) * factor
        coarse = scaled.astype(BF16)
        q_turned[:HD, n * HD : (n + 1) * HD] = coarse
        q_turned[HD:, n * HD : (n + 1) * HD] = (scaled - coarse.astype(F32)).astype(BF16)

    each = range(key_heads)
    heads = [slice(g * HD, (g + 1) * HD) for g in each]
    across = [slice(g * wide, (g + 1) * wide) for g in each]

    def score(g, keys, at):
        s = nn_dot(jnp.concatenate([keys, keys], axis=1), q_turned[:, across[g]])
        return s + jnp.concatenate([hidden[at, :]] * (owners * groups), axis=1)

    def most(s):
        return jnp.max(s.reshape(s.shape[0] // 8, 8, wide), axis=0)

    fresh_at = slice(2 * cache_here, 2 * cache_here + home_rows)
    s_new = [score(g, key_fresh[:, heads[g]], fresh_at) for g in each]
    run = [most(s) for s in s_new]
    pieces = [(part, i) for part in range(2) for i in range(0, cache_here, step)]
    for part, i in pieces:
        at = slice(part * cache_here + i, part * cache_here + i + step)
        for g in each:
            s = score(g, (key_own, key_other)[part][i : i + step, heads[g]], at)
            scores[at, across[g]] = s
            run[g] = jnp.maximum(run[g], most(s))
    peak = [
        jnp.maximum(jnp.max(r, axis=0, keepdims=True), FLOOR).astype(BF16).astype(F32) for r in run
    ]
    for part, i in pieces:
        at = slice(part * cache_here + i, part * cache_here + i + step)
        for g in each:
            probs[at, across[g]] = jnp.exp2((scores[at, across[g]] - peak[g]).astype(BF16))
    ones = jnp.ones((STATS, cache_here), BF16)
    sums = [
        nn_dot(jnp.concatenate([value_own[heads[g], :], ones], axis=0), probs[:cache_here, across[g]])
        for g in each
    ]
    sums = [
        sums[g]
        + nn_dot(jnp.concatenate([value_other[heads[g], :], ones], axis=0), probs[cache_here:, across[g]])
        for g in each
    ]
    for g in each:
        p_new = jnp.exp2((s_new[g] - peak[g]).astype(BF16))
        values = value_fresh[:, heads[g]].astype(F32).T.astype(BF16)
        numer = sums[g][:HD] + nn_dot(values, p_new)
        denom = sums[g][HD : HD + 1] + jnp.sum(p_new.astype(F32), axis=0, keepdims=True)
        high = denom.astype(BF16).astype(F32)
        low = denom - high
        for owner in range(owners):
            spot = g * owners + owner
            lanes = [slice((owner * groups + k) * HD, (owner * groups + k + 1) * HD) for k in range(groups)]
            for k, cols in enumerate(lanes):
                out[spot, k * HD : (k + 1) * HD, :] = numer[:, cols].astype(BF16)
            filled = [kind[:, cols] for kind in (peak[g], high, low) for cols in lanes]
            filled += [jnp.zeros_like(filled[0])] * (STATS - len(filled))
            out[spot, groups * HD :, :] = jnp.concatenate(filled, axis=0).astype(BF16)


def attention(place, query_blocks, keys, values, new_key, new_value, lens, row_ids, chips, kv_heads):
    home_rows = new_key.shape[0]
    rows = home_rows * len(query_blocks)
    cache_here = keys[0].shape[0]
    together = 2
    steps = kv_heads // together
    owners = chips // kv_heads
    columns = query_blocks[0][0].shape[1] // steps
    owner_heads = columns // HD // owners // together
    wide = rows * columns // HD
    height = owner_heads * rows + STATS
    step = 512
    positions = 2 * cache_here + home_rows
    kv = lambda g, place: (0, g)
    whole = lambda g, place: (0, 0)
    shape = (together, owners, owner_heads, home_rows, rows, cache_here, step)
    work = wide * steps * 2 * cache_here
    return pl.pallas_call(
        functools.partial(attention_body, shape),
        grid_spec=pltpu.PrefetchScalarGridSpec(
            num_scalar_prefetch=1,
            grid=(steps,),
            in_specs=[
                pl.BlockSpec((home_rows, columns), functools.partial(lambda n, g, place: (n, g), n))
                for _, n in query_blocks
            ]
            + [pl.BlockSpec((cache_here, together * HD), kv)] * 2
            + [pl.BlockSpec((together * HD, cache_here), lambda g, place: (g, 0))] * 2
            + [pl.BlockSpec((home_rows, together * HD), kv)] * 2
            + [pl.BlockSpec(lens.shape, whole)] * 2,
            out_specs=pl.BlockSpec((together * owners, height, HD), lambda g, place: (g, 0, 0)),
            scratch_shapes=[
                pltpu.VMEM((rows, columns), BF16),
                pltpu.VMEM((2 * HD, wide), BF16),
                pltpu.VMEM((positions, HD), F32),
                pltpu.VMEM((2 * cache_here, wide), F32),
                pltpu.VMEM((2 * cache_here, wide), BF16),
            ],
        ),
        out_shape=jax.ShapeDtypeStruct((chips, height, HD), BF16),
        compiler_params=pltpu.CompilerParams(vmem_limit_bytes=40 * MIB),
        cost_estimate=pl.CostEstimate(
            flops=6 * work * HD, bytes_accessed=8 * MIB, transcendentals=work
        ),
        name="attention",
    )(
        place,
        *[block for block, _ in query_blocks],
        pltpu.with_memory_space_constraint(keys[0], pltpu.HBM),
        keys[1],
        *values,
        pltpu.with_memory_space_constraint(new_key, pltpu.HBM),
        pltpu.with_memory_space_constraint(new_value, pltpu.HBM),
        lens,
        row_ids,
    )


def project_body(rows, place, *refs):
    *chunks, weight_own, weight_other, out, turned, own_held, other_held, sems = refs
    core = place[3]
    copies = [
        pltpu.make_async_copy(weight_own, own_held, sems.at[0]),
        pltpu.make_async_copy(weight_other, other_held, sems.at[1]),
    ]
    for copy in copies:
        copy.start()
    chips, height, _ = chunks[0].shape
    base = height - STATS
    groups = base // HD
    pack = HD // rows
    heads_here = groups * pack // CORES
    half = chips // 2 // 2
    for near in range(2):
        sources = [chunks[s // 2 // half ^ near].at[s] for s in range(chips)]
        stats = [part[base:, :].astype(F32) for part in sources]
        peaks = [stat[:groups] for stat in stats]
        top = functools.reduce(jnp.maximum, peaks)
        share = [jnp.exp2(peak - top) for peak in peaks]
        denom = sum(w * (t[groups : 2 * groups] + t[2 * groups : 3 * groups]) for w, t in zip(share, stats))
        for k in range(groups):
            numer = sum(
                part[k * HD : (k + 1) * HD, :].astype(F32) * w[k : k + 1, :] for part, w in zip(sources, share)
            )
            attended = (numer / denom[k : k + 1, :]).T.astype(BF16)
            for j in range(pack):
                part, h = divmod(k * pack + j, heads_here)
                turned[part, near * rows : (near + 1) * rows, h * HD : (h + 1) * HD] = attended[
                    j * rows : (j + 1) * rows
                ]
    for copy in copies:
        copy.wait()
    product = nn_dot(turned[core], own_held[...]) + nn_dot(turned[1 - core], other_held[...])
    out[...] = product.astype(BF16)


def project(place, chunks, weight_own, weight_other, rows):
    depth, width = weight_own.shape
    vmem = pl.BlockSpec(memory_space=pltpu.VMEM)
    return pl.pallas_call(
        functools.partial(project_body, rows),
        in_specs=[pl.BlockSpec(memory_space=pltpu.SMEM)]
        + [vmem] * len(chunks)
        + [pl.BlockSpec(memory_space=pl.ANY)] * 2,
        out_specs=vmem,
        out_shape=jax.ShapeDtypeStruct((2 * rows, width), BF16),
        scratch_shapes=[
            pltpu.VMEM((CORES, 2 * rows, depth), BF16),
            pltpu.VMEM((depth, width), BF16),
            pltpu.VMEM((depth, width), BF16),
            pltpu.SemaphoreType.DMA((2,)),
        ],
        compiler_params=pltpu.CompilerParams(vmem_limit_bytes=32 * MIB),
        cost_estimate=pl.CostEstimate(
            flops=8 * rows * width * depth, bytes_accessed=4 * MIB, transcendentals=0
        ),
        name="project",
    )(place, *chunks, pltpu.with_memory_space_constraint(weight_own, pltpu.HBM), weight_other)


def norm_body(parts, residual, gain, chooser, middle_out, sent):
    total = parts[0].astype(F32)
    for s in range(1, parts.shape[0]):
        total = total + parts[s].astype(F32)
    middle = (residual[...].astype(F32) + total).astype(BF16)
    middle_out[...] = middle
    middle = middle.astype(F32)
    inv_rms = lax.rsqrt(jnp.mean(middle * middle, axis=-1, keepdims=True) + 1e-06)
    normed = (middle * inv_rms * gain[...].astype(F32)).astype(BF16)
    sent[...] = nn_dot(chooser[...], normed).astype(BF16)


def norm_and_dispatch(parts, residual, gain, chooser):
    vmem = pl.BlockSpec(memory_space=pltpu.VMEM)
    rows, width = residual.shape
    return pl.pallas_call(
        norm_body,
        in_specs=[vmem] * 4,
        out_specs=[vmem] * 2,
        out_shape=[
            jax.ShapeDtypeStruct((rows, width), BF16),
            jax.ShapeDtypeStruct((chooser.shape[0], width), BF16),
        ],
        compiler_params=pltpu.CompilerParams(vmem_limit_bytes=24 * MIB),
        cost_estimate=pl.CostEstimate(
            flops=2 * chooser.shape[0] * rows * width, bytes_accessed=2 * MIB, transcendentals=0
        ),
        name="norm_and_dispatch",
    )(parts, residual, gain, chooser)


def experts_body(step, arrived, w_gate, w_up, w_down, out, gate_held, up_held, down_held, sems):
    experts, _, depth = w_gate.shape
    rows, width = arrived.shape
    pieces = [(e, f) for e in range(experts) for f in range(0, depth, step)]
    order = []
    for n, (e, f) in enumerate(pieces):
        columns = pl.ds(f, step)
        order.append(pltpu.make_async_copy(w_gate.at[e, :, columns], gate_held.at[n], sems.at[n, 0]))
        order.append(pltpu.make_async_copy(w_up.at[e, :, columns], up_held.at[n], sems.at[n, 1]))
    for n, (e, f) in enumerate(pieces):
        order.append(pltpu.make_async_copy(w_down.at[e, pl.ds(f, step), :], down_held.at[n], sems.at[n, 2]))
    window = 6
    for copy in order[:window]:
        copy.start()

    def await_copy(k):
        order[k].wait()
        if k + window < len(order):
            order[k + window].start()

    slot = lax.broadcasted_iota(jnp.int32, (rows, 1), 0)
    values = arrived[...]
    hidden = []
    for n, (e, f) in enumerate(pieces):
        await_copy(2 * n)
        await_copy(2 * n + 1)
        gate = nn_dot(values, gate_held[n])
        upward = nn_dot(values, up_held[n])
        part = gate / (1.0 + jnp.exp(-gate)) * upward
        mine = lax.rem(slot, experts * MOST) // MOST == e
        hidden.append(jnp.where(mine, part, 0.0).astype(BF16))
    total = None
    for n in range(len(pieces)):
        await_copy(2 * len(pieces) + n)
        term = nn_dot(hidden[n], down_held[n])
        total = term if total is None else total + term
    out[...] = total.astype(BF16)


def run_experts(arrived, w_gate, w_up, w_down):
    rows, width = arrived.shape
    experts, _, depth = w_gate.shape
    step = 256
    pieces = experts * depth // step
    vmem = pl.BlockSpec(memory_space=pltpu.VMEM)
    hbm = pl.BlockSpec(memory_space=pltpu.HBM)
    weights = [pltpu.with_memory_space_constraint(w, pltpu.HBM) for w in (w_gate, w_up, w_down)]
    return pl.pallas_call(
        functools.partial(experts_body, step),
        in_specs=[vmem] + [hbm] * 3,
        out_specs=vmem,
        out_shape=jax.ShapeDtypeStruct((rows, width), BF16),
        scratch_shapes=[
            pltpu.VMEM((pieces, width, step), BF16),
            pltpu.VMEM((pieces, width, step), BF16),
            pltpu.VMEM((pieces, step, width), BF16),
            pltpu.SemaphoreType.DMA((pieces, 3)),
        ],
        compiler_params=pltpu.CompilerParams(vmem_limit_bytes=44 * MIB),
        cost_estimate=pl.CostEstimate(
            flops=6 * rows * width * experts * depth,
            bytes_accessed=6 * width * experts * depth,
            transcendentals=rows * experts * depth,
        ),
        name="experts",
    )(arrived, *weights)


def mix_body(returned, coarse, fine, middle, out):
    values = returned[...]
    mixed = nn_dot(coarse[...], values) + nn_dot(fine[...], values)
    out[...] = (middle[...].astype(F32) + mixed).astype(BF16)


def mix(returned, coarse, fine, middle):
    vmem = pl.BlockSpec(memory_space=pltpu.VMEM)
    return pl.pallas_call(
        mix_body,
        in_specs=[vmem] * 4,
        out_specs=vmem,
        out_shape=jax.ShapeDtypeStruct(middle.shape, BF16),
        compiler_params=pltpu.CompilerParams(vmem_limit_bytes=16 * MIB),
        name="mix",
    )(returned, coarse, fine, middle)


def on_device(
    queries,
    new_key,
    new_value,
    key_cache,
    value_cache,
    cache_len,
    out_weight,
    residual,
    norm_gain,
    expert_ids,
    route_weight,
    w_gate,
    w_up,
    w_down,
):
    devices = lax.axis_size("ctx")
    chips = devices // CORES
    index = lax.axis_index("ctx")
    chip, core = index // CORES, index % CORES
    home_rows, width = residual.shape
    top = expert_ids.shape[1]
    heads_here = out_weight.shape[0] // HD
    cache_here = key_cache.shape[0]
    same_core = [[CORES * j + c for j in range(chips)] for c in range(CORES)]
    swap = [(i, i ^ 1) for i in range(devices)]

    across = [(i, i ^ CORES) for i in range(devices)]
    rings = chips // 2
    half = rings // 2
    chunk_rows = 2 * half * home_rows

    def across_y(block):
        return lax.ppermute(block, "ctx", across)

    neighbour = across_y(queries)
    by_ring = [queries] + [
        lax.ppermute(queries, "ctx", [(i, i ^ (2 * CORES * k)) for i in range(devices)])
        for k in range(1, rings)
    ]
    near_blocks = [(pltpu.with_memory_space_constraint(queries, pltpu.HBM), 0)]
    near_blocks += [(block, 0) for block in by_ring[1:half]]
    near_blocks += [(neighbour, 0)] + [(across_y(block), 0) for block in by_ring[1:half]]
    far = jnp.concatenate(by_ring[half:], axis=0)
    far_across = across_y(far)
    far_blocks = [(far, k) for k in range(half)] + [(far_across, k) for k in range(half)]
    late_keys, late_values, _ = lax.optimization_barrier((key_cache, value_cache, neighbour))
    key_other = lax.ppermute(late_keys, "ctx", swap)
    value_turned = late_values.T
    value_other = lax.ppermute(value_turned, "ctx", swap)
    place = jnp.stack([chip, index * cache_here, (index ^ 1) * cache_here, core, chip % 2, chip // 2]).astype(jnp.int32)

    def in_lanes(by_chip, n):
        first = (chip // CORES // half ^ n) * chips // 2
        here = lax.dynamic_slice_in_dim(by_chip, first, chips // 2, 0).reshape(1, chunk_rows)
        return jnp.tile(here, (1, HD // chunk_rows))

    len_by_chip = lax.dynamic_slice_in_dim(
        cache_len.reshape(chips, CORES * home_rows), core * home_rows, home_rows, 1
    )
    number_by_chip = jnp.arange(chips * home_rows, dtype=jnp.int32).reshape(chips, home_rows)
    lens = [in_lanes(len_by_chip, n) for n in range(2)]
    row_ids = [in_lanes(number_by_chip, n) for n in range(2)]

    flat_ids = expert_ids.reshape(-1)
    picks = jnp.arange(flat_ids.shape[0])
    earlier = (flat_ids[:, None] == flat_ids[None, :]) & (picks[None, :] < picks[:, None])
    target = (flat_ids * MOST + jnp.sum(earlier, axis=1, dtype=jnp.int32)).reshape(home_rows, top)
    experts = w_gate.shape[0]
    slots = experts * devices * MOST
    takes = target[:, :, None] == jnp.arange(slots, dtype=jnp.int32)
    chooser = jnp.any(takes, axis=1).T.astype(BF16)
    spread = jnp.sum(jnp.where(takes, route_weight[:, :, None], 0.0), axis=1)
    coarse = spread.astype(BF16)
    fine = (spread - coarse.astype(F32)).astype(BF16)

    gathered = []
    for chunk, blocks in enumerate((near_blocks, far_blocks)):
        sums = attention(
            place,
            blocks,
            (key_cache, key_other),
            (value_turned, value_other),
            new_key,
            new_value,
            lens[chunk],
            row_ids[chunk],
            chips,
            key_cache.shape[1] // HD,
        )
        if chunk:
            sums, gathered[-1] = lax.optimization_barrier((sums, gathered[-1]))
        else:
            sums, place, late_weight, _ = lax.optimization_barrier((sums, place, out_weight, far_across))
        gathered.append(
            lax.all_to_all(
                sums, "ctx", split_axis=0, concat_axis=0, axis_index_groups=same_core, tiled=True
            )
        )
    weight_other = lax.ppermute(late_weight, "ctx", swap)
    share = project(place, gathered, out_weight, weight_other, chunk_rows)
    shares = lax.all_to_all(
        share.reshape(chips, home_rows, width),
        "ctx",
        split_axis=0,
        concat_axis=0,
        axis_index_groups=same_core,
        tiled=True,
    )
    middle, outgoing = norm_and_dispatch(shares, residual, norm_gain.reshape(1, width), chooser)
    arrived = lax.all_to_all(
        outgoing.reshape(devices, experts * MOST, width), "ctx", split_axis=0, concat_axis=0, tiled=True
    )
    produced = run_experts(arrived.reshape(slots, width), w_gate, w_up, w_down)
    returned = lax.all_to_all(
        produced.reshape(devices, experts * MOST, width), "ctx", split_axis=0, concat_axis=0, tiled=True
    )
    return mix(returned.reshape(slots, width), coarse, fine, middle)


def solution(mesh):
    placed = (
        P(("groups", "ctx"), None),
        P(("groups", "ctx"), None),
        P(("groups", "ctx"), None),
        P(("groups", "ctx"), None),
        P(("groups", "ctx"), None),
        P("groups"),
        P("ctx", None),
        P(("groups", "ctx"), None),
        P(),
        P(("groups", "ctx"), None),
        P(("groups", "ctx"), None),
        P("ctx", None, None),
        P("ctx", None, None),
        P("ctx", None, None),
    )
    return jax.shard_map(
        on_device, mesh=mesh, in_specs=placed, out_specs=P(("groups", "ctx"), None), check_vma=False
    )
```

```python
import functools
import math

import jax
import jax.numpy as jnp
from jax import lax
from jax.experimental import pallas as pl
from jax.experimental.pallas import tpu as pltpu
from jax.sharding import PartitionSpec as P

HD = 128
MOST = 4
CORES = 2
STATS = 16
MASKED = -1e30
FLOOR = -1e20
LOG2E = math.log2(math.e)
MIB = 1024 * 1024
F32 = jnp.float32
BF16 = jnp.bfloat16


def nt_dot(a, b):
    return lax.dot_general(a, b, (((1,), (1,)), ((), ())), preferred_element_type=F32)


def nn_dot(a, b):
    return lax.dot_general(a, b, (((1,), (0,)), ((), ())), preferred_element_type=F32)


def attention_body(shape, place, *refs):
    key_heads, owners, owner_heads, home_rows, rows, cache_here, step = shape
    *query_refs, key_own, key_other, value_own, value_other, key_fresh, value_fresh = refs[:-8]
    lens, row_ids, out, q_rows, q_turned, hidden, scores, probs = refs[-8:]
    chip, start_own, start_other, side_here, ring_here = place[0], place[1], place[2], place[4], place[5]
    near = rows // home_rows // 2
    pack = HD // rows
    groups = owner_heads // pack

    @pl.when(pl.program_id(0) == 0)
    def _():
        lanes = lens.shape[1]
        for part, start in enumerate((start_own, start_other)):
            positions = start + lax.broadcasted_iota(jnp.int32, (cache_here, lanes), 0)
            hidden[part * cache_here : (part + 1) * cache_here, :] = jnp.where(
                positions < lens[...], 0.0, MASKED
            )
        token = chip * home_rows + lax.broadcasted_iota(jnp.int32, (home_rows, lanes), 0)
        hidden[2 * cache_here :, :] = jnp.where(token == row_ids[...], 0.0, MASKED)

    for k, piece in enumerate(query_refs):
        side = side_here if k < near else 1 - side_here
        spot = 2 * (lax.rem(ring_here, near) ^ (k % near)) + side
        q_rows[pl.ds(pl.multiple_of(spot * home_rows, home_rows), home_rows), :] = piece[...]

    factor = LOG2E / math.sqrt(HD)
    wide = owners * groups * HD
    for n in range(key_heads * owners * groups):
        block = jnp.concatenate(
            [q_rows[:, h * HD : (h + 1) * HD] for h in range(n * pack, (n + 1) * pack)], axis=0
        )
        scaled = block.T.astype(F32) * factor
        coarse = scaled.astype(BF16)
        q_turned[:HD, n * HD : (n + 1) * HD] = coarse
        q_turned[HD:, n * HD : (n + 1) * HD] = (scaled - coarse.astype(F32)).astype(BF16)

    each = range(key_heads)
    heads = [slice(g * HD, (g + 1) * HD) for g in each]
    across = [slice(g * wide, (g + 1) * wide) for g in each]

    def score(g, keys, at):
        s = nn_dot(jnp.concatenate([keys, keys], axis=1), q_turned[:, across[g]])
        return s + jnp.concatenate([hidden[at, :]] * (owners * groups), axis=1)

    def most(s):
        return jnp.max(s.reshape(s.shape[0] // 8, 8, wide), axis=0)

    fresh_at = slice(2 * cache_here, 2 * cache_here + home_rows)
    s_new = [score(g, key_fresh[:, heads[g]], fresh_at) for g in each]
    run = [most(s) for s in s_new]
    pieces = [(part, i) for part in range(2) for i in range(0, cache_here, step)]
    for part, i in pieces:
        at = slice(part * cache_here + i, part * cache_here + i + step)
        for g in each:
            s = score(g, (key_own, key_other)[part][i : i + step, heads[g]], at)
            scores[at, across[g]] = s
            run[g] = jnp.maximum(run[g], most(s))
    peak = [
        jnp.maximum(jnp.max(r, axis=0, keepdims=True), FLOOR).astype(BF16).astype(F32) for r in run
    ]
    for part, i in pieces:
        at = slice(part * cache_here + i, part * cache_here + i + step)
        for g in each:
            probs[at, across[g]] = jnp.exp2((scores[at, across[g]] - peak[g]).astype(BF16))
    ones = jnp.ones((STATS, cache_here), BF16)
    sums = [
        nn_dot(jnp.concatenate([value_own[:, heads[g]].T, ones], axis=0), probs[:cache_here, across[g]])
        for g in each
    ]
    sums = [
        sums[g]
        + nn_dot(jnp.concatenate([value_other[:, heads[g]].T, ones], axis=0), probs[cache_here:, across[g]])
        for g in each
    ]
    for g in each:
        p_new = jnp.exp2((s_new[g] - peak[g]).astype(BF16))
        values = value_fresh[:, heads[g]].astype(F32).T.astype(BF16)
        numer = sums[g][:HD] + nn_dot(values, p_new)
        denom = sums[g][HD : HD + 1] + jnp.sum(p_new.astype(F32), axis=0, keepdims=True)
        high = denom.astype(BF16).astype(F32)
        low = denom - high
        for owner in range(owners):
            spot = g * owners + owner
            lanes = [slice((owner * groups + k) * HD, (owner * groups + k + 1) * HD) for k in range(groups)]
            for k, cols in enumerate(lanes):
                out[spot, k * HD : (k + 1) * HD, :] = numer[:, cols].astype(BF16)
            filled = [kind[:, cols] for kind in (peak[g], high, low) for cols in lanes]
            filled += [jnp.zeros_like(filled[0])] * (STATS - len(filled))
            out[spot, groups * HD :, :] = jnp.concatenate(filled, axis=0).astype(BF16)


def attention(place, query_blocks, keys, values, new_key, new_value, lens, row_ids, chips, kv_heads):
    home_rows = new_key.shape[0]
    rows = home_rows * len(query_blocks)
    cache_here = keys[0].shape[0]
    together = 2
    steps = kv_heads // together
    owners = chips // kv_heads
    columns = query_blocks[0][0].shape[1] // steps
    owner_heads = columns // HD // owners // together
    wide = rows * columns // HD
    height = owner_heads * rows + STATS
    step = 512
    positions = 2 * cache_here + home_rows
    kv = lambda g, place: (0, g)
    whole = lambda g, place: (0, 0)
    shape = (together, owners, owner_heads, home_rows, rows, cache_here, step)
    work = wide * steps * 2 * cache_here
    return pl.pallas_call(
        functools.partial(attention_body, shape),
        grid_spec=pltpu.PrefetchScalarGridSpec(
            num_scalar_prefetch=1,
            grid=(steps,),
            in_specs=[
                pl.BlockSpec((home_rows, columns), functools.partial(lambda n, g, place: (n, g), n))
                for _, n in query_blocks
            ]
            + [pl.BlockSpec((cache_here, together * HD), kv)] * 4
            + [pl.BlockSpec((home_rows, together * HD), kv)] * 2
            + [pl.BlockSpec(lens.shape, whole)] * 2,
            out_specs=pl.BlockSpec((together * owners, height, HD), lambda g, place: (g, 0, 0)),
            scratch_shapes=[
                pltpu.VMEM((rows, columns), BF16),
                pltpu.VMEM((2 * HD, wide), BF16),
                pltpu.VMEM((positions, HD), F32),
                pltpu.VMEM((2 * cache_here, wide), F32),
                pltpu.VMEM((2 * cache_here, wide), BF16),
            ],
        ),
        out_shape=jax.ShapeDtypeStruct((chips, height, HD), BF16),
        compiler_params=pltpu.CompilerParams(vmem_limit_bytes=40 * MIB),
        cost_estimate=pl.CostEstimate(
            flops=6 * work * HD, bytes_accessed=8 * MIB, transcendentals=work
        ),
        name="attention",
    )(
        place,
        *[block for block, _ in query_blocks],
        pltpu.with_memory_space_constraint(keys[0], pltpu.HBM),
        keys[1],
        pltpu.with_memory_space_constraint(values[0], pltpu.HBM),
        values[1],
        pltpu.with_memory_space_constraint(new_key, pltpu.HBM),
        pltpu.with_memory_space_constraint(new_value, pltpu.HBM),
        lens,
        row_ids,
    )


def project_body(rows, place, *refs):
    *chunks, weight_own, weight_other, out, turned = refs
    core = place[3]
    chips, height, _ = chunks[0].shape
    base = height - STATS
    groups = base // HD
    pack = HD // rows
    heads_here = groups * pack // CORES
    half = chips // 2 // 2
    for near in range(2):
        sources = [chunks[s // 2 // half ^ near].at[s] for s in range(chips)]
        stats = [part[base:, :].astype(F32) for part in sources]
        peaks = [stat[:groups] for stat in stats]
        top = functools.reduce(jnp.maximum, peaks)
        share = [jnp.exp2(peak - top) for peak in peaks]
        denom = sum(w * (t[groups : 2 * groups] + t[2 * groups : 3 * groups]) for w, t in zip(share, stats))
        for k in range(groups):
            numer = sum(
                part[k * HD : (k + 1) * HD, :].astype(F32) * w[k : k + 1, :] for part, w in zip(sources, share)
            )
            attended = (numer / denom[k : k + 1, :]).T.astype(BF16)
            for j in range(pack):
                part, h = divmod(k * pack + j, heads_here)
                turned[part, near * rows : (near + 1) * rows, h * HD : (h + 1) * HD] = attended[
                    j * rows : (j + 1) * rows
                ]
    product = nn_dot(turned[core], weight_own[...]) + nn_dot(turned[1 - core], weight_other[...])
    out[...] = product.astype(BF16)


def project(place, chunks, weight_own, weight_other, rows):
    depth, width = weight_own.shape
    vmem = pl.BlockSpec(memory_space=pltpu.VMEM)
    return pl.pallas_call(
        functools.partial(project_body, rows),
        in_specs=[pl.BlockSpec(memory_space=pltpu.SMEM)] + [vmem] * (len(chunks) + 2),
        out_specs=vmem,
        out_shape=jax.ShapeDtypeStruct((2 * rows, width), BF16),
        scratch_shapes=[pltpu.VMEM((CORES, 2 * rows, depth), BF16)],
        compiler_params=pltpu.CompilerParams(vmem_limit_bytes=32 * MIB),
        cost_estimate=pl.CostEstimate(
            flops=8 * rows * width * depth, bytes_accessed=4 * MIB, transcendentals=0
        ),
        name="project",
    )(place, *chunks, weight_own, weight_other)


def norm_body(parts, residual, gain, chooser, middle_out, sent):
    total = parts[0].astype(F32)
    for s in range(1, parts.shape[0]):
        total = total + parts[s].astype(F32)
    middle = (residual[...].astype(F32) + total).astype(BF16)
    middle_out[...] = middle
    middle = middle.astype(F32)
    inv_rms = lax.rsqrt(jnp.mean(middle * middle, axis=-1, keepdims=True) + 1e-06)
    normed = (middle * inv_rms * gain[...].astype(F32)).astype(BF16)
    sent[...] = nn_dot(chooser[...], normed).astype(BF16)


def norm_and_dispatch(parts, residual, gain, chooser):
    vmem = pl.BlockSpec(memory_space=pltpu.VMEM)
    rows, width = residual.shape
    return pl.pallas_call(
        norm_body,
        in_specs=[vmem] * 4,
        out_specs=[vmem] * 2,
        out_shape=[
            jax.ShapeDtypeStruct((rows, width), BF16),
            jax.ShapeDtypeStruct((chooser.shape[0], width), BF16),
        ],
        compiler_params=pltpu.CompilerParams(vmem_limit_bytes=24 * MIB),
        cost_estimate=pl.CostEstimate(
            flops=2 * chooser.shape[0] * rows * width, bytes_accessed=2 * MIB, transcendentals=0
        ),
        name="norm_and_dispatch",
    )(parts, residual, gain, chooser)


def experts_body(step, arrived, w_gate, w_up, w_down, out, gate_held, up_held, down_held, sems):
    experts, _, depth = w_gate.shape
    rows, width = arrived.shape
    pieces = [(e, f) for e in range(experts) for f in range(0, depth, step)]
    copies = []
    for n, (e, f) in enumerate(pieces):
        down = pl.ds(f, step)
        copies.append(
            [
                pltpu.make_async_copy(w_gate.at[e, :, down], gate_held.at[n], sems.at[n, 0]),
                pltpu.make_async_copy(w_up.at[e, :, down], up_held.at[n], sems.at[n, 1]),
                pltpu.make_async_copy(w_down.at[e, down, :], down_held.at[n], sems.at[n, 2]),
            ]
        )
    for piece in copies:
        for copy in piece[:2]:
            copy.start()
    for piece in copies:
        piece[2].start()
    slot = lax.broadcasted_iota(jnp.int32, (rows, 1), 0)
    values = arrived[...]
    hidden = []
    for n, (e, f) in enumerate(pieces):
        copies[n][0].wait()
        copies[n][1].wait()
        gate = nn_dot(values, gate_held[n])
        upward = nn_dot(values, up_held[n])
        part = gate / (1.0 + jnp.exp(-gate)) * upward
        mine = lax.rem(slot, experts * MOST) // MOST == e
        hidden.append(jnp.where(mine, part, 0.0).astype(BF16))
    total = None
    for n in range(len(pieces)):
        copies[n][2].wait()
        term = nn_dot(hidden[n], down_held[n])
        total = term if total is None else total + term
    out[...] = total.astype(BF16)


def run_experts(arrived, w_gate, w_up, w_down):
    rows, width = arrived.shape
    experts, _, depth = w_gate.shape
    step = 256
    pieces = experts * depth // step
    vmem = pl.BlockSpec(memory_space=pltpu.VMEM)
    hbm = pl.BlockSpec(memory_space=pltpu.HBM)
    weights = [pltpu.with_memory_space_constraint(w, pltpu.HBM) for w in (w_gate, w_up, w_down)]
    return pl.pallas_call(
        functools.partial(experts_body, step),
        in_specs=[vmem] + [hbm] * 3,
        out_specs=vmem,
        out_shape=jax.ShapeDtypeStruct((rows, width), BF16),
        scratch_shapes=[
            pltpu.VMEM((pieces, width, step), BF16),
            pltpu.VMEM((pieces, width, step), BF16),
            pltpu.VMEM((pieces, step, width), BF16),
            pltpu.SemaphoreType.DMA((pieces, 3)),
        ],
        compiler_params=pltpu.CompilerParams(vmem_limit_bytes=44 * MIB),
        cost_estimate=pl.CostEstimate(
            flops=6 * rows * width * experts * depth,
            bytes_accessed=6 * width * experts * depth,
            transcendentals=rows * experts * depth,
        ),
        name="experts",
    )(arrived, *weights)


def mix_body(returned, coarse, fine, middle, out):
    values = returned[...]
    mixed = nn_dot(coarse[...], values) + nn_dot(fine[...], values)
    out[...] = (middle[...].astype(F32) + mixed).astype(BF16)


def mix(returned, coarse, fine, middle):
    vmem = pl.BlockSpec(memory_space=pltpu.VMEM)
    return pl.pallas_call(
        mix_body,
        in_specs=[vmem] * 4,
        out_specs=vmem,
        out_shape=jax.ShapeDtypeStruct(middle.shape, BF16),
        compiler_params=pltpu.CompilerParams(vmem_limit_bytes=16 * MIB),
        name="mix",
    )(returned, coarse, fine, middle)


def on_device(
    queries,
    new_key,
    new_value,
    key_cache,
    value_cache,
    cache_len,
    out_weight,
    residual,
    norm_gain,
    expert_ids,
    route_weight,
    w_gate,
    w_up,
    w_down,
):
    devices = lax.axis_size("ctx")
    chips = devices // CORES
    index = lax.axis_index("ctx")
    chip, core = index // CORES, index % CORES
    home_rows, width = residual.shape
    top = expert_ids.shape[1]
    heads_here = out_weight.shape[0] // HD
    cache_here = key_cache.shape[0]
    same_core = [[CORES * j + c for j in range(chips)] for c in range(CORES)]
    swap = [(i, i ^ 1) for i in range(devices)]

    across = [(i, i ^ CORES) for i in range(devices)]
    rings = chips // 2
    half = rings // 2
    chunk_rows = 2 * half * home_rows

    def from_peer(block, ring, side):
        far_end = 2 * CORES * ring + CORES * side
        return lax.ppermute(block, "ctx", [(i, i ^ far_end) for i in range(devices)])

    def across_y(block):
        return from_peer(block, 0, 1)

    by_ring = [queries] + [None] * (half - 1) + [from_peer(queries, k, 0) for k in range(half, rings)]
    key_other = lax.ppermute(key_cache, "ctx", swap)
    late_queries, key_other = lax.optimization_barrier((queries, key_other))
    neighbour = across_y(late_queries)
    by_ring[1:half] = [from_peer(late_queries, k, 0) for k in range(1, half)]
    near_blocks = [(pltpu.with_memory_space_constraint(queries, pltpu.HBM), 0)]
    near = by_ring[1:half] + [neighbour] + [from_peer(late_queries, k, 1) for k in range(1, half)]
    near, by_ring[half:] = lax.optimization_barrier((near, by_ring[half:]))
    near_blocks += [(block, 0) for block in near]
    far = jnp.concatenate(by_ring[half:], axis=0)
    far_across = across_y(far)
    far_blocks = [(far, k) for k in range(half)] + [(far_across, k) for k in range(half)]
    late_values, neighbour = lax.optimization_barrier((value_cache, neighbour))
    value_other = lax.ppermute(late_values, "ctx", swap)
    place = jnp.stack([chip, index * cache_here, (index ^ 1) * cache_here, core, chip % 2, chip // 2]).astype(jnp.int32)

    def in_lanes(by_chip, n):
        first = (chip // CORES // half ^ n) * chips // 2
        here = lax.dynamic_slice_in_dim(by_chip, first, chips // 2, 0).reshape(1, chunk_rows)
        return jnp.tile(here, (1, HD // chunk_rows))

    len_by_chip = lax.dynamic_slice_in_dim(
        cache_len.reshape(chips, CORES * home_rows), core * home_rows, home_rows, 1
    )
    number_by_chip = jnp.arange(chips * home_rows, dtype=jnp.int32).reshape(chips, home_rows)
    lens = [in_lanes(len_by_chip, n) for n in range(2)]
    row_ids = [in_lanes(number_by_chip, n) for n in range(2)]

    flat_ids = expert_ids.reshape(-1)
    picks = jnp.arange(flat_ids.shape[0])
    earlier = (flat_ids[:, None] == flat_ids[None, :]) & (picks[None, :] < picks[:, None])
    target = (flat_ids * MOST + jnp.sum(earlier, axis=1, dtype=jnp.int32)).reshape(home_rows, top)
    experts = w_gate.shape[0]
    slots = experts * devices * MOST
    takes = target[:, :, None] == jnp.arange(slots, dtype=jnp.int32)
    chooser = jnp.any(takes, axis=1).T.astype(BF16)
    spread = jnp.sum(jnp.where(takes, route_weight[:, :, None], 0.0), axis=1)
    coarse = spread.astype(BF16)
    fine = (spread - coarse.astype(F32)).astype(BF16)

    gathered = []
    for chunk, blocks in enumerate((near_blocks, far_blocks)):
        sums = attention(
            place,
            blocks,
            (key_cache, key_other),
            (value_cache, value_other),
            new_key,
            new_value,
            lens[chunk],
            row_ids[chunk],
            chips,
            key_cache.shape[1] // HD,
        )
        if chunk:
            sums, gathered[-1] = lax.optimization_barrier((sums, gathered[-1]))
        else:
            sums, place, late_weight, _ = lax.optimization_barrier((sums, place, out_weight, far_across))
        gathered.append(
            lax.all_to_all(
                sums, "ctx", split_axis=0, concat_axis=0, axis_index_groups=same_core, tiled=True
            )
        )
    weight_other = lax.ppermute(late_weight, "ctx", swap)
    share = project(place, gathered, out_weight, weight_other, chunk_rows)
    shares = lax.all_to_all(
        share.reshape(chips, home_rows, width),
        "ctx",
        split_axis=0,
        concat_axis=0,
        axis_index_groups=same_core,
        tiled=True,
    )
    middle, outgoing = norm_and_dispatch(shares, residual, norm_gain.reshape(1, width), chooser)
    arrived = lax.all_to_all(
        outgoing.reshape(devices, experts * MOST, width), "ctx", split_axis=0, concat_axis=0, tiled=True
    )
    produced = run_experts(arrived.reshape(slots, width), w_gate, w_up, w_down)
    returned = lax.all_to_all(
        produced.reshape(devices, experts * MOST, width), "ctx", split_axis=0, concat_axis=0, tiled=True
    )
    return mix(returned.reshape(slots, width), coarse, fine, middle)


def solution(mesh):
    placed = (
        P(("groups", "ctx"), None),
        P(("groups", "ctx"), None),
        P(("groups", "ctx"), None),
        P(("groups", "ctx"), None),
        P(("groups", "ctx"), None),
        P("groups"),
        P("ctx", None),
        P(("groups", "ctx"), None),
        P(),
        P(("groups", "ctx"), None),
        P(("groups", "ctx"), None),
        P("ctx", None, None),
        P("ctx", None, None),
        P("ctx", None, None),
    )
    return jax.shard_map(
        on_device, mesh=mesh, in_specs=placed, out_specs=P(("groups", "ctx"), None), check_vma=False
    )
```

```python
import functools
import math

import jax
import jax.numpy as jnp
from jax import lax
from jax.experimental import pallas as pl
from jax.experimental.pallas import tpu as pltpu
from jax.sharding import PartitionSpec as P

HD = 128
MOST = 4
CORES = 2
STATS = 16
MASKED = -1e30
FLOOR = -1e20
LOG2E = math.log2(math.e)
MIB = 1024 * 1024
F32 = jnp.float32
BF16 = jnp.bfloat16


def nt_dot(a, b):
    return lax.dot_general(a, b, (((1,), (1,)), ((), ())), preferred_element_type=F32)


def nn_dot(a, b):
    return lax.dot_general(a, b, (((1,), (0,)), ((), ())), preferred_element_type=F32)


def attention_body(shape, place, *refs):
    key_heads, owners, owner_heads, home_rows, rows, cache_here, step = shape
    *query_refs, key_own, key_other, value_own, value_other, key_fresh, value_fresh = refs[:-8]
    lens, row_ids, out, q_rows, q_turned, hidden, scores, probs = refs[-8:]
    chip, start_own, start_other, side_here, ring_here = place[0], place[1], place[2], place[4], place[5]
    near = rows // home_rows // 2
    pack = HD // rows
    groups = owner_heads // pack

    @pl.when(pl.program_id(0) == 0)
    def _():
        lanes = lens.shape[1]
        for part, start in enumerate((start_own, start_other)):
            positions = start + lax.broadcasted_iota(jnp.int32, (cache_here, lanes), 0)
            hidden[part * cache_here : (part + 1) * cache_here, :] = jnp.where(
                positions < lens[...], 0.0, MASKED
            )
        token = chip * home_rows + lax.broadcasted_iota(jnp.int32, (home_rows, lanes), 0)
        hidden[2 * cache_here :, :] = jnp.where(token == row_ids[...], 0.0, MASKED)

    for k, piece in enumerate(query_refs):
        side = side_here if k < near else 1 - side_here
        spot = 2 * (lax.rem(ring_here, near) ^ (k % near)) + side
        q_rows[pl.ds(pl.multiple_of(spot * home_rows, home_rows), home_rows), :] = piece[...]

    factor = LOG2E / math.sqrt(HD)
    wide = owners * groups * HD
    for n in range(key_heads * owners * groups):
        block = jnp.concatenate(
            [q_rows[:, h * HD : (h + 1) * HD] for h in range(n * pack, (n + 1) * pack)], axis=0
        )
        scaled = block.T.astype(F32) * factor
        coarse = scaled.astype(BF16)
        q_turned[:HD, n * HD : (n + 1) * HD] = coarse
        q_turned[HD:, n * HD : (n + 1) * HD] = (scaled - coarse.astype(F32)).astype(BF16)

    each = range(key_heads)
    heads = [slice(g * HD, (g + 1) * HD) for g in each]
    across = [slice(g * wide, (g + 1) * wide) for g in each]

    def score(g, keys, at):
        s = nn_dot(jnp.concatenate([keys, keys], axis=1), q_turned[:, across[g]])
        return s + jnp.concatenate([hidden[at, :]] * (owners * groups), axis=1)

    def most(s):
        return jnp.max(s.reshape(s.shape[0] // 8, 8, wide), axis=0)

    fresh_at = slice(2 * cache_here, 2 * cache_here + home_rows)
    s_new = [score(g, key_fresh[:, heads[g]], fresh_at) for g in each]
    run = [most(s) for s in s_new]
    pieces = [(part, i) for part in range(2) for i in range(0, cache_here, step)]
    for part, i in pieces:
        at = slice(part * cache_here + i, part * cache_here + i + step)
        for g in each:
            s = score(g, (key_own, key_other)[part][i : i + step, heads[g]], at)
            scores[at, across[g]] = s
            run[g] = jnp.maximum(run[g], most(s))
    peak = [
        jnp.maximum(jnp.max(r, axis=0, keepdims=True), FLOOR).astype(BF16).astype(F32) for r in run
    ]
    for part, i in pieces:
        at = slice(part * cache_here + i, part * cache_here + i + step)
        for g in each:
            probs[at, across[g]] = jnp.exp2((scores[at, across[g]] - peak[g]).astype(BF16))
    ones = jnp.ones((STATS, cache_here), BF16)
    sums = [
        nn_dot(jnp.concatenate([value_own[:, heads[g]].T, ones], axis=0), probs[:cache_here, across[g]])
        for g in each
    ]
    sums = [
        sums[g]
        + nn_dot(jnp.concatenate([value_other[:, heads[g]].T, ones], axis=0), probs[cache_here:, across[g]])
        for g in each
    ]
    for g in each:
        p_new = jnp.exp2((s_new[g] - peak[g]).astype(BF16))
        values = value_fresh[:, heads[g]].astype(F32).T.astype(BF16)
        numer = sums[g][:HD] + nn_dot(values, p_new)
        denom = sums[g][HD : HD + 1] + jnp.sum(p_new.astype(F32), axis=0, keepdims=True)
        high = denom.astype(BF16).astype(F32)
        low = denom - high
        for owner in range(owners):
            spot = g * owners + owner
            lanes = [slice((owner * groups + k) * HD, (owner * groups + k + 1) * HD) for k in range(groups)]
            for k, cols in enumerate(lanes):
                out[spot, k * HD : (k + 1) * HD, :] = numer[:, cols].astype(BF16)
            filled = [kind[:, cols] for kind in (peak[g], high, low) for cols in lanes]
            filled += [jnp.zeros_like(filled[0])] * (STATS - len(filled))
            out[spot, groups * HD :, :] = jnp.concatenate(filled, axis=0).astype(BF16)


def attention(place, query_blocks, keys, values, new_key, new_value, lens, row_ids, chips, kv_heads):
    home_rows = new_key.shape[0]
    rows = home_rows * len(query_blocks)
    cache_here = keys[0].shape[0]
    together = 2
    steps = kv_heads // together
    owners = chips // kv_heads
    columns = query_blocks[0][0].shape[1] // steps
    owner_heads = columns // HD // owners // together
    wide = rows * columns // HD
    height = owner_heads * rows + STATS
    step = 512
    positions = 2 * cache_here + home_rows
    kv = lambda g, place: (0, g)
    whole = lambda g, place: (0, 0)
    shape = (together, owners, owner_heads, home_rows, rows, cache_here, step)
    work = wide * steps * 2 * cache_here
    return pl.pallas_call(
        functools.partial(attention_body, shape),
        grid_spec=pltpu.PrefetchScalarGridSpec(
            num_scalar_prefetch=1,
            grid=(steps,),
            in_specs=[
                pl.BlockSpec((home_rows, columns), functools.partial(lambda n, g, place: (n, g), n))
                for _, n in query_blocks
            ]
            + [pl.BlockSpec((cache_here, together * HD), kv)] * 4
            + [pl.BlockSpec((home_rows, together * HD), kv)] * 2
            + [pl.BlockSpec(lens.shape, whole)] * 2,
            out_specs=pl.BlockSpec((together * owners, height, HD), lambda g, place: (g, 0, 0)),
            scratch_shapes=[
                pltpu.VMEM((rows, columns), BF16),
                pltpu.VMEM((2 * HD, wide), BF16),
                pltpu.VMEM((positions, HD), F32),
                pltpu.VMEM((2 * cache_here, wide), F32),
                pltpu.VMEM((2 * cache_here, wide), BF16),
            ],
        ),
        out_shape=jax.ShapeDtypeStruct((chips, height, HD), BF16),
        compiler_params=pltpu.CompilerParams(vmem_limit_bytes=40 * MIB),
        cost_estimate=pl.CostEstimate(
            flops=6 * work * HD, bytes_accessed=8 * MIB, transcendentals=work
        ),
        name="attention",
    )(
        place,
        *[block for block, _ in query_blocks],
        pltpu.with_memory_space_constraint(keys[0], pltpu.HBM),
        keys[1],
        pltpu.with_memory_space_constraint(values[0], pltpu.HBM),
        values[1],
        pltpu.with_memory_space_constraint(new_key, pltpu.HBM),
        pltpu.with_memory_space_constraint(new_value, pltpu.HBM),
        lens,
        row_ids,
    )


def project_body(rows, place, *refs):
    *chunks, weight_own, weight_other, out, turned = refs
    core = place[3]
    chips, height, _ = chunks[0].shape
    base = height - STATS
    groups = base // HD
    pack = HD // rows
    heads_here = groups * pack // CORES
    half = chips // 2 // 2
    for near in range(2):
        sources = [chunks[s // 2 // half ^ near].at[s] for s in range(chips)]
        stats = [part[base:, :].astype(F32) for part in sources]
        peaks = [stat[:groups] for stat in stats]
        top = functools.reduce(jnp.maximum, peaks)
        share = [jnp.exp2(peak - top) for peak in peaks]
        denom = sum(w * (t[groups : 2 * groups] + t[2 * groups : 3 * groups]) for w, t in zip(share, stats))
        for k in range(groups):
            numer = sum(
                part[k * HD : (k + 1) * HD, :].astype(F32) * w[k : k + 1, :] for part, w in zip(sources, share)
            )
            attended = (numer / denom[k : k + 1, :]).T.astype(BF16)
            for j in range(pack):
                part, h = divmod(k * pack + j, heads_here)
                turned[part, near * rows : (near + 1) * rows, h * HD : (h + 1) * HD] = attended[
                    j * rows : (j + 1) * rows
                ]
    product = nn_dot(turned[core], weight_own[...]) + nn_dot(turned[1 - core], weight_other[...])
    out[...] = product.astype(BF16)


def project(place, chunks, weight_own, weight_other, rows):
    depth, width = weight_own.shape
    vmem = pl.BlockSpec(memory_space=pltpu.VMEM)
    return pl.pallas_call(
        functools.partial(project_body, rows),
        in_specs=[pl.BlockSpec(memory_space=pltpu.SMEM)] + [vmem] * (len(chunks) + 2),
        out_specs=vmem,
        out_shape=jax.ShapeDtypeStruct((2 * rows, width), BF16),
        scratch_shapes=[pltpu.VMEM((CORES, 2 * rows, depth), BF16)],
        compiler_params=pltpu.CompilerParams(vmem_limit_bytes=32 * MIB),
        cost_estimate=pl.CostEstimate(
            flops=8 * rows * width * depth, bytes_accessed=4 * MIB, transcendentals=0
        ),
        name="project",
    )(place, *chunks, weight_own, weight_other)


def norm_body(parts, residual, gain, chooser, middle_out, sent):
    total = parts[0].astype(F32)
    for s in range(1, parts.shape[0]):
        total = total + parts[s].astype(F32)
    middle = (residual[...].astype(F32) + total).astype(BF16)
    middle_out[...] = middle
    middle = middle.astype(F32)
    inv_rms = lax.rsqrt(jnp.mean(middle * middle, axis=-1, keepdims=True) + 1e-06)
    normed = (middle * inv_rms * gain[...].astype(F32)).astype(BF16)
    sent[...] = nn_dot(chooser[...], normed).astype(BF16)


def norm_and_dispatch(parts, residual, gain, chooser):
    vmem = pl.BlockSpec(memory_space=pltpu.VMEM)
    rows, width = residual.shape
    return pl.pallas_call(
        norm_body,
        in_specs=[vmem] * 4,
        out_specs=[vmem] * 2,
        out_shape=[
            jax.ShapeDtypeStruct((rows, width), BF16),
            jax.ShapeDtypeStruct((chooser.shape[0], width), BF16),
        ],
        compiler_params=pltpu.CompilerParams(vmem_limit_bytes=24 * MIB),
        cost_estimate=pl.CostEstimate(
            flops=2 * chooser.shape[0] * rows * width, bytes_accessed=2 * MIB, transcendentals=0
        ),
        name="norm_and_dispatch",
    )(parts, residual, gain, chooser)


def experts_body(step, arrived, w_gate, w_up, w_down, out, gate_held, up_held, down_held, sems):
    experts, _, depth = w_gate.shape
    rows, width = arrived.shape
    pieces = [(e, f) for e in range(experts) for f in range(0, depth, step)]
    copies = []
    for n, (e, f) in enumerate(pieces):
        down = pl.ds(f, step)
        copies.append(
            [
                pltpu.make_async_copy(w_gate.at[e, :, down], gate_held.at[n], sems.at[n, 0]),
                pltpu.make_async_copy(w_up.at[e, :, down], up_held.at[n], sems.at[n, 1]),
                pltpu.make_async_copy(w_down.at[e, down, :], down_held.at[n], sems.at[n, 2]),
            ]
        )
    for piece in copies:
        for copy in piece[:2]:
            copy.start()
    for piece in copies:
        piece[2].start()
    slot = lax.broadcasted_iota(jnp.int32, (rows, 1), 0)
    values = arrived[...]
    hidden = []
    for n, (e, f) in enumerate(pieces):
        copies[n][0].wait()
        copies[n][1].wait()
        gate = nn_dot(values, gate_held[n])
        upward = nn_dot(values, up_held[n])
        part = gate / (1.0 + jnp.exp(-gate)) * upward
        mine = lax.rem(slot, experts * MOST) // MOST == e
        hidden.append(jnp.where(mine, part, 0.0).astype(BF16))
    total = None
    for n in range(len(pieces)):
        copies[n][2].wait()
        term = nn_dot(hidden[n], down_held[n])
        total = term if total is None else total + term
    out[...] = total.astype(BF16)


def run_experts(arrived, w_gate, w_up, w_down):
    rows, width = arrived.shape
    experts, _, depth = w_gate.shape
    step = 256
    pieces = experts * depth // step
    vmem = pl.BlockSpec(memory_space=pltpu.VMEM)
    hbm = pl.BlockSpec(memory_space=pltpu.HBM)
    weights = [pltpu.with_memory_space_constraint(w, pltpu.HBM) for w in (w_gate, w_up, w_down)]
    return pl.pallas_call(
        functools.partial(experts_body, step),
        in_specs=[vmem] + [hbm] * 3,
        out_specs=vmem,
        out_shape=jax.ShapeDtypeStruct((rows, width), BF16),
        scratch_shapes=[
            pltpu.VMEM((pieces, width, step), BF16),
            pltpu.VMEM((pieces, width, step), BF16),
            pltpu.VMEM((pieces, step, width), BF16),
            pltpu.SemaphoreType.DMA((pieces, 3)),
        ],
        compiler_params=pltpu.CompilerParams(vmem_limit_bytes=44 * MIB),
        cost_estimate=pl.CostEstimate(
            flops=6 * rows * width * experts * depth,
            bytes_accessed=6 * width * experts * depth,
            transcendentals=rows * experts * depth,
        ),
        name="experts",
    )(arrived, *weights)


def mix_body(returned, coarse, fine, middle, out):
    values = returned[...]
    mixed = nn_dot(coarse[...], values) + nn_dot(fine[...], values)
    out[...] = (middle[...].astype(F32) + mixed).astype(BF16)


def mix(returned, coarse, fine, middle):
    vmem = pl.BlockSpec(memory_space=pltpu.VMEM)
    return pl.pallas_call(
        mix_body,
        in_specs=[vmem] * 4,
        out_specs=vmem,
        out_shape=jax.ShapeDtypeStruct(middle.shape, BF16),
        compiler_params=pltpu.CompilerParams(vmem_limit_bytes=16 * MIB),
        name="mix",
    )(returned, coarse, fine, middle)


def on_device(
    queries,
    new_key,
    new_value,
    key_cache,
    value_cache,
    cache_len,
    out_weight,
    residual,
    norm_gain,
    expert_ids,
    route_weight,
    w_gate,
    w_up,
    w_down,
):
    devices = lax.axis_size("ctx")
    chips = devices // CORES
    index = lax.axis_index("ctx")
    chip, core = index // CORES, index % CORES
    home_rows, width = residual.shape
    top = expert_ids.shape[1]
    heads_here = out_weight.shape[0] // HD
    cache_here = key_cache.shape[0]
    same_core = [[CORES * j + c for j in range(chips)] for c in range(CORES)]
    swap = [(i, i ^ 1) for i in range(devices)]

    across = [(i, i ^ CORES) for i in range(devices)]
    rings = chips // 2
    half = rings // 2
    chunk_rows = 2 * half * home_rows

    def across_y(block):
        return lax.ppermute(block, "ctx", across)

    neighbour = across_y(queries)
    by_ring = [queries] + [
        lax.ppermute(queries, "ctx", [(i, i ^ (2 * CORES * k)) for i in range(devices)])
        for k in range(1, rings)
    ]
    near_blocks = [(pltpu.with_memory_space_constraint(queries, pltpu.HBM), 0)]
    near_blocks += [(block, 0) for block in by_ring[1:half]]
    near_blocks += [(neighbour, 0)] + [(across_y(block), 0) for block in by_ring[1:half]]
    far = jnp.concatenate(by_ring[half:], axis=0)
    far_across = across_y(far)
    far_blocks = [(far, k) for k in range(half)] + [(far_across, k) for k in range(half)]
    late_keys, late_values, _ = lax.optimization_barrier((key_cache, value_cache, neighbour))
    key_other = lax.ppermute(late_keys, "ctx", swap)
    value_other = lax.ppermute(late_values, "ctx", swap)
    place = jnp.stack([chip, index * cache_here, (index ^ 1) * cache_here, core, chip % 2, chip // 2]).astype(jnp.int32)

    def in_lanes(by_chip, n):
        first = (chip // CORES // half ^ n) * chips // 2
        here = lax.dynamic_slice_in_dim(by_chip, first, chips // 2, 0).reshape(1, chunk_rows)
        return jnp.tile(here, (1, HD // chunk_rows))

    len_by_chip = lax.dynamic_slice_in_dim(
        cache_len.reshape(chips, CORES * home_rows), core * home_rows, home_rows, 1
    )
    number_by_chip = jnp.arange(chips * home_rows, dtype=jnp.int32).reshape(chips, home_rows)
    lens = [in_lanes(len_by_chip, n) for n in range(2)]
    row_ids = [in_lanes(number_by_chip, n) for n in range(2)]

    flat_ids = expert_ids.reshape(-1)
    picks = jnp.arange(flat_ids.shape[0])
    earlier = (flat_ids[:, None] == flat_ids[None, :]) & (picks[None, :] < picks[:, None])
    target = (flat_ids * MOST + jnp.sum(earlier, axis=1, dtype=jnp.int32)).reshape(home_rows, top)
    experts = w_gate.shape[0]
    slots = experts * devices * MOST
    takes = target[:, :, None] == jnp.arange(slots, dtype=jnp.int32)
    chooser = jnp.any(takes, axis=1).T.astype(BF16)
    spread = jnp.sum(jnp.where(takes, route_weight[:, :, None], 0.0), axis=1)
    coarse = spread.astype(BF16)
    fine = (spread - coarse.astype(F32)).astype(BF16)

    gathered = []
    for chunk, blocks in enumerate((near_blocks, far_blocks)):
        sums = attention(
            place,
            blocks,
            (key_cache, key_other),
            (value_cache, value_other),
            new_key,
            new_value,
            lens[chunk],
            row_ids[chunk],
            chips,
            key_cache.shape[1] // HD,
        )
        if chunk:
            sums, gathered[-1] = lax.optimization_barrier((sums, gathered[-1]))
        else:
            sums, place, late_weight, _ = lax.optimization_barrier((sums, place, out_weight, far_across))
        gathered.append(
            lax.all_to_all(
                sums, "ctx", split_axis=0, concat_axis=0, axis_index_groups=same_core, tiled=True
            )
        )
    weight_other = lax.ppermute(late_weight, "ctx", swap)
    share = project(place, gathered, out_weight, weight_other, chunk_rows)
    shares = lax.all_to_all(
        share.reshape(chips, home_rows, width),
        "ctx",
        split_axis=0,
        concat_axis=0,
        axis_index_groups=same_core,
        tiled=True,
    )
    middle, outgoing = norm_and_dispatch(shares, residual, norm_gain.reshape(1, width), chooser)
    arrived = lax.all_to_all(
        outgoing.reshape(devices, experts * MOST, width), "ctx", split_axis=0, concat_axis=0, tiled=True
    )
    produced = run_experts(arrived.reshape(slots, width), w_gate, w_up, w_down)
    returned = lax.all_to_all(
        produced.reshape(devices, experts * MOST, width), "ctx", split_axis=0, concat_axis=0, tiled=True
    )
    return mix(returned.reshape(slots, width), coarse, fine, middle)


def solution(mesh):
    placed = (
        P(("groups", "ctx"), None),
        P(("groups", "ctx"), None),
        P(("groups", "ctx"), None),
        P(("groups", "ctx"), None),
        P(("groups", "ctx"), None),
        P("groups"),
        P("ctx", None),
        P(("groups", "ctx"), None),
        P(),
        P(("groups", "ctx"), None),
        P(("groups", "ctx"), None),
        P("ctx", None, None),
        P("ctx", None, None),
        P("ctx", None, None),
    )
    return jax.shard_map(
        on_device, mesh=mesh, in_specs=placed, out_specs=P(("groups", "ctx"), None), check_vma=False
    )
```

```python
import functools
import math

import jax
import jax.numpy as jnp
from jax import lax
from jax.experimental import pallas as pl
from jax.experimental.pallas import tpu as pltpu
from jax.sharding import PartitionSpec as P

HD = 128
MOST = 4
CORES = 2
STATS = 16
MASKED = -1e30
FLOOR = -1e20
LOG2E = math.log2(math.e)
MIB = 1024 * 1024
F32 = jnp.float32
BF16 = jnp.bfloat16


def nt_dot(a, b):
    return lax.dot_general(a, b, (((1,), (1,)), ((), ())), preferred_element_type=F32)


def nn_dot(a, b):
    return lax.dot_general(a, b, (((1,), (0,)), ((), ())), preferred_element_type=F32)


def attention_body(shape, place, *refs):
    key_heads, owners, owner_heads, home_rows, rows, cache_here, step = shape
    *query_refs, key_own, key_other, value_own, value_other, key_fresh, value_fresh = refs[:-8]
    lens, row_ids, out, q_rows, q_turned, hidden, scores, probs = refs[-8:]
    chip, start_own, start_other, side_here, ring_here = place[0], place[1], place[2], place[4], place[5]
    near = rows // home_rows // 2
    pack = HD // rows
    groups = owner_heads // pack

    @pl.when(pl.program_id(0) == 0)
    def _():
        lanes = lens.shape[1]
        for part, start in enumerate((start_own, start_other)):
            positions = start + lax.broadcasted_iota(jnp.int32, (cache_here, lanes), 0)
            hidden[part * cache_here : (part + 1) * cache_here, :] = jnp.where(
                positions < lens[...], 0.0, MASKED
            )
        token = chip * home_rows + lax.broadcasted_iota(jnp.int32, (home_rows, lanes), 0)
        hidden[2 * cache_here :, :] = jnp.where(token == row_ids[...], 0.0, MASKED)

    for k, piece in enumerate(query_refs):
        side = side_here if k < near else 1 - side_here
        spot = 2 * (lax.rem(ring_here, near) ^ (k % near)) + side
        q_rows[pl.ds(pl.multiple_of(spot * home_rows, home_rows), home_rows), :] = piece[...]

    factor = LOG2E / math.sqrt(HD)
    wide = owners * groups * HD
    for n in range(key_heads * owners * groups):
        block = jnp.concatenate(
            [q_rows[:, h * HD : (h + 1) * HD] for h in range(n * pack, (n + 1) * pack)], axis=0
        )
        scaled = block.T.astype(F32) * factor
        coarse = scaled.astype(BF16)
        q_turned[:HD, n * HD : (n + 1) * HD] = coarse
        q_turned[HD:, n * HD : (n + 1) * HD] = (scaled - coarse.astype(F32)).astype(BF16)

    each = range(key_heads)
    heads = [slice(g * HD, (g + 1) * HD) for g in each]
    across = [slice(g * wide, (g + 1) * wide) for g in each]

    def score(g, keys, at):
        s = nn_dot(jnp.concatenate([keys, keys], axis=1), q_turned[:, across[g]])
        return s + jnp.concatenate([hidden[at, :]] * (owners * groups), axis=1)

    def most(s):
        return jnp.max(s.reshape(s.shape[0] // 8, 8, wide), axis=0)

    fresh_at = slice(2 * cache_here, 2 * cache_here + home_rows)
    s_new = [score(g, key_fresh[:, heads[g]], fresh_at) for g in each]
    run = [most(s) for s in s_new]
    pieces = [(part, i) for part in range(2) for i in range(0, cache_here, step)]
    for part, i in pieces:
        at = slice(part * cache_here + i, part * cache_here + i + step)
        for g in each:
            s = score(g, (key_own, key_other)[part][i : i + step, heads[g]], at)
            scores[at, across[g]] = s
            run[g] = jnp.maximum(run[g], most(s))
    peak = [
        jnp.maximum(jnp.max(r, axis=0, keepdims=True), FLOOR).astype(BF16).astype(F32) for r in run
    ]
    for part, i in pieces:
        at = slice(part * cache_here + i, part * cache_here + i + step)
        for g in each:
            probs[at, across[g]] = jnp.exp2((scores[at, across[g]] - peak[g]).astype(BF16))
    ones = jnp.ones((STATS, cache_here), BF16)
    sums = [
        nn_dot(jnp.concatenate([value_own[:, heads[g]].T, ones], axis=0), probs[:cache_here, across[g]])
        for g in each
    ]
    sums = [
        sums[g]
        + nn_dot(jnp.concatenate([value_other[:, heads[g]].T, ones], axis=0), probs[cache_here:, across[g]])
        for g in each
    ]
    for g in each:
        p_new = jnp.exp2((s_new[g] - peak[g]).astype(BF16))
        values = value_fresh[:, heads[g]].astype(F32).T.astype(BF16)
        numer = sums[g][:HD] + nn_dot(values, p_new)
        denom = sums[g][HD : HD + 1] + jnp.sum(p_new.astype(F32), axis=0, keepdims=True)
        high = denom.astype(BF16).astype(F32)
        low = denom - high
        for owner in range(owners):
            spot = g * owners + owner
            lanes = [slice((owner * groups + k) * HD, (owner * groups + k + 1) * HD) for k in range(groups)]
            for k, cols in enumerate(lanes):
                out[spot, k * HD : (k + 1) * HD, :] = numer[:, cols].astype(BF16)
            filled = [kind[:, cols] for kind in (peak[g], high, low) for cols in lanes]
            filled += [jnp.zeros_like(filled[0])] * (STATS - len(filled))
            out[spot, groups * HD :, :] = jnp.concatenate(filled, axis=0).astype(BF16)


def attention(place, query_blocks, keys, values, new_key, new_value, lens, row_ids, chips, kv_heads):
    home_rows = new_key.shape[0]
    rows = home_rows * len(query_blocks)
    cache_here = keys[0].shape[0]
    together = 2
    steps = kv_heads // together
    owners = chips // kv_heads
    columns = query_blocks[0][0].shape[1] // steps
    owner_heads = columns // HD // owners // together
    wide = rows * columns // HD
    height = owner_heads * rows + STATS
    step = 1024
    positions = 2 * cache_here + home_rows
    kv = lambda g, place: (0, g)
    whole = lambda g, place: (0, 0)
    shape = (together, owners, owner_heads, home_rows, rows, cache_here, step)
    work = wide * steps * 2 * cache_here
    return pl.pallas_call(
        functools.partial(attention_body, shape),
        grid_spec=pltpu.PrefetchScalarGridSpec(
            num_scalar_prefetch=1,
            grid=(steps,),
            in_specs=[
                pl.BlockSpec((home_rows, columns), functools.partial(lambda n, g, place: (n, g), n))
                for _, n in query_blocks
            ]
            + [pl.BlockSpec((cache_here, together * HD), kv)] * 4
            + [pl.BlockSpec((home_rows, together * HD), kv)] * 2
            + [pl.BlockSpec(lens.shape, whole)] * 2,
            out_specs=pl.BlockSpec((together * owners, height, HD), lambda g, place: (g, 0, 0)),
            scratch_shapes=[
                pltpu.VMEM((rows, columns), BF16),
                pltpu.VMEM((2 * HD, wide), BF16),
                pltpu.VMEM((positions, HD), F32),
                pltpu.VMEM((2 * cache_here, wide), F32),
                pltpu.VMEM((2 * cache_here, wide), BF16),
            ],
        ),
        out_shape=jax.ShapeDtypeStruct((chips, height, HD), BF16),
        compiler_params=pltpu.CompilerParams(vmem_limit_bytes=40 * MIB),
        cost_estimate=pl.CostEstimate(
            flops=6 * work * HD, bytes_accessed=8 * MIB, transcendentals=work
        ),
        name="attention",
    )(
        place,
        *[block for block, _ in query_blocks],
        pltpu.with_memory_space_constraint(keys[0], pltpu.HBM),
        keys[1],
        pltpu.with_memory_space_constraint(values[0], pltpu.HBM),
        values[1],
        pltpu.with_memory_space_constraint(new_key, pltpu.HBM),
        pltpu.with_memory_space_constraint(new_value, pltpu.HBM),
        lens,
        row_ids,
    )


def project_body(rows, place, *refs):
    *chunks, weight_own, weight_other, out, turned = refs
    core = place[3]
    chips, height, _ = chunks[0].shape
    base = height - STATS
    groups = base // HD
    pack = HD // rows
    heads_here = groups * pack // CORES
    half = chips // 2 // 2
    for near in range(2):
        sources = [chunks[s // 2 // half ^ near].at[s] for s in range(chips)]
        stats = [part[base:, :].astype(F32) for part in sources]
        peaks = [stat[:groups] for stat in stats]
        top = functools.reduce(jnp.maximum, peaks)
        share = [jnp.exp2(peak - top) for peak in peaks]
        denom = sum(w * (t[groups : 2 * groups] + t[2 * groups : 3 * groups]) for w, t in zip(share, stats))
        for k in range(groups):
            numer = sum(
                part[k * HD : (k + 1) * HD, :].astype(F32) * w[k : k + 1, :] for part, w in zip(sources, share)
            )
            attended = (numer / denom[k : k + 1, :]).T.astype(BF16)
            for j in range(pack):
                part, h = divmod(k * pack + j, heads_here)
                turned[part, near * rows : (near + 1) * rows, h * HD : (h + 1) * HD] = attended[
                    j * rows : (j + 1) * rows
                ]
    product = nn_dot(turned[core], weight_own[...]) + nn_dot(turned[1 - core], weight_other[...])
    out[...] = product.astype(BF16)


def project(place, chunks, weight_own, weight_other, rows):
    depth, width = weight_own.shape
    vmem = pl.BlockSpec(memory_space=pltpu.VMEM)
    return pl.pallas_call(
        functools.partial(project_body, rows),
        in_specs=[pl.BlockSpec(memory_space=pltpu.SMEM)] + [vmem] * (len(chunks) + 2),
        out_specs=vmem,
        out_shape=jax.ShapeDtypeStruct((2 * rows, width), BF16),
        scratch_shapes=[pltpu.VMEM((CORES, 2 * rows, depth), BF16)],
        compiler_params=pltpu.CompilerParams(vmem_limit_bytes=32 * MIB),
        cost_estimate=pl.CostEstimate(
            flops=8 * rows * width * depth, bytes_accessed=4 * MIB, transcendentals=0
        ),
        name="project",
    )(place, *chunks, weight_own, weight_other)


def norm_body(parts, residual, gain, chooser, middle_out, sent):
    total = parts[0].astype(F32)
    for s in range(1, parts.shape[0]):
        total = total + parts[s].astype(F32)
    middle = (residual[...].astype(F32) + total).astype(BF16)
    middle_out[...] = middle
    middle = middle.astype(F32)
    inv_rms = lax.rsqrt(jnp.mean(middle * middle, axis=-1, keepdims=True) + 1e-06)
    normed = (middle * inv_rms * gain[...].astype(F32)).astype(BF16)
    sent[...] = nn_dot(chooser[...], normed).astype(BF16)


def norm_and_dispatch(parts, residual, gain, chooser):
    vmem = pl.BlockSpec(memory_space=pltpu.VMEM)
    rows, width = residual.shape
    return pl.pallas_call(
        norm_body,
        in_specs=[vmem] * 4,
        out_specs=[vmem] * 2,
        out_shape=[
            jax.ShapeDtypeStruct((rows, width), BF16),
            jax.ShapeDtypeStruct((chooser.shape[0], width), BF16),
        ],
        compiler_params=pltpu.CompilerParams(vmem_limit_bytes=24 * MIB),
        cost_estimate=pl.CostEstimate(
            flops=2 * chooser.shape[0] * rows * width, bytes_accessed=2 * MIB, transcendentals=0
        ),
        name="norm_and_dispatch",
    )(parts, residual, gain, chooser)


def experts_body(step, arrived, w_gate, w_up, w_down, out, gate_held, up_held, down_held, sems):
    experts, _, depth = w_gate.shape
    rows, width = arrived.shape
    pieces = [(e, f) for e in range(experts) for f in range(0, depth, step)]
    copies = []
    for n, (e, f) in enumerate(pieces):
        down = pl.ds(f, step)
        copies.append(
            [
                pltpu.make_async_copy(w_gate.at[e, :, down], gate_held.at[n], sems.at[n, 0]),
                pltpu.make_async_copy(w_up.at[e, :, down], up_held.at[n], sems.at[n, 1]),
                pltpu.make_async_copy(w_down.at[e, down, :], down_held.at[n], sems.at[n, 2]),
            ]
        )
    for piece in copies:
        for copy in piece[:2]:
            copy.start()
    for piece in copies:
        piece[2].start()
    slot = lax.broadcasted_iota(jnp.int32, (rows, 1), 0)
    values = arrived[...]
    hidden = []
    for n, (e, f) in enumerate(pieces):
        copies[n][0].wait()
        copies[n][1].wait()
        gate = nn_dot(values, gate_held[n])
        upward = nn_dot(values, up_held[n])
        part = gate / (1.0 + jnp.exp(-gate)) * upward
        mine = lax.rem(slot, experts * MOST) // MOST == e
        hidden.append(jnp.where(mine, part, 0.0).astype(BF16))
    total = None
    for n in range(len(pieces)):
        copies[n][2].wait()
        term = nn_dot(hidden[n], down_held[n])
        total = term if total is None else total + term
    out[...] = total.astype(BF16)


def run_experts(arrived, w_gate, w_up, w_down):
    rows, width = arrived.shape
    experts, _, depth = w_gate.shape
    step = 256
    pieces = experts * depth // step
    vmem = pl.BlockSpec(memory_space=pltpu.VMEM)
    hbm = pl.BlockSpec(memory_space=pltpu.HBM)
    weights = [pltpu.with_memory_space_constraint(w, pltpu.HBM) for w in (w_gate, w_up, w_down)]
    return pl.pallas_call(
        functools.partial(experts_body, step),
        in_specs=[vmem] + [hbm] * 3,
        out_specs=vmem,
        out_shape=jax.ShapeDtypeStruct((rows, width), BF16),
        scratch_shapes=[
            pltpu.VMEM((pieces, width, step), BF16),
            pltpu.VMEM((pieces, width, step), BF16),
            pltpu.VMEM((pieces, step, width), BF16),
            pltpu.SemaphoreType.DMA((pieces, 3)),
        ],
        compiler_params=pltpu.CompilerParams(vmem_limit_bytes=44 * MIB),
        cost_estimate=pl.CostEstimate(
            flops=6 * rows * width * experts * depth,
            bytes_accessed=6 * width * experts * depth,
            transcendentals=rows * experts * depth,
        ),
        name="experts",
    )(arrived, *weights)


def mix_body(returned, coarse, fine, middle, out):
    values = returned[...]
    mixed = nn_dot(coarse[...], values) + nn_dot(fine[...], values)
    out[...] = (middle[...].astype(F32) + mixed).astype(BF16)


def mix(returned, coarse, fine, middle):
    vmem = pl.BlockSpec(memory_space=pltpu.VMEM)
    return pl.pallas_call(
        mix_body,
        in_specs=[vmem] * 4,
        out_specs=vmem,
        out_shape=jax.ShapeDtypeStruct(middle.shape, BF16),
        compiler_params=pltpu.CompilerParams(vmem_limit_bytes=16 * MIB),
        name="mix",
    )(returned, coarse, fine, middle)


def on_device(
    queries,
    new_key,
    new_value,
    key_cache,
    value_cache,
    cache_len,
    out_weight,
    residual,
    norm_gain,
    expert_ids,
    route_weight,
    w_gate,
    w_up,
    w_down,
):
    devices = lax.axis_size("ctx")
    chips = devices // CORES
    index = lax.axis_index("ctx")
    chip, core = index // CORES, index % CORES
    home_rows, width = residual.shape
    top = expert_ids.shape[1]
    heads_here = out_weight.shape[0] // HD
    cache_here = key_cache.shape[0]
    same_core = [[CORES * j + c for j in range(chips)] for c in range(CORES)]
    swap = [(i, i ^ 1) for i in range(devices)]

    across = [(i, i ^ CORES) for i in range(devices)]
    rings = chips // 2
    half = rings // 2
    chunk_rows = 2 * half * home_rows

    def across_y(block):
        return lax.ppermute(block, "ctx", across)

    neighbour = across_y(queries)
    by_ring = [queries] + [
        lax.ppermute(queries, "ctx", [(i, i ^ (2 * CORES * k)) for i in range(devices)])
        for k in range(1, rings)
    ]
    near_blocks = [(pltpu.with_memory_space_constraint(queries, pltpu.HBM), 0)]
    near_blocks += [(block, 0) for block in by_ring[1:half]]
    near_blocks += [(neighbour, 0)] + [(across_y(block), 0) for block in by_ring[1:half]]
    far = jnp.concatenate(by_ring[half:], axis=0)
    far_across = across_y(far)
    far_blocks = [(far, k) for k in range(half)] + [(far_across, k) for k in range(half)]
    late_keys, late_values, _ = lax.optimization_barrier((key_cache, value_cache, neighbour))
    key_other = lax.ppermute(late_keys, "ctx", swap)
    value_other = lax.ppermute(late_values, "ctx", swap)
    place = jnp.stack([chip, index * cache_here, (index ^ 1) * cache_here, core, chip % 2, chip // 2]).astype(jnp.int32)

    def in_lanes(by_chip, n):
        first = (chip // CORES // half ^ n) * chips // 2
        here = lax.dynamic_slice_in_dim(by_chip, first, chips // 2, 0).reshape(1, chunk_rows)
        return jnp.tile(here, (1, HD // chunk_rows))

    len_by_chip = lax.dynamic_slice_in_dim(
        cache_len.reshape(chips, CORES * home_rows), core * home_rows, home_rows, 1
    )
    number_by_chip = jnp.arange(chips * home_rows, dtype=jnp.int32).reshape(chips, home_rows)
    lens = [in_lanes(len_by_chip, n) for n in range(2)]
    row_ids = [in_lanes(number_by_chip, n) for n in range(2)]

    flat_ids = expert_ids.reshape(-1)
    picks = jnp.arange(flat_ids.shape[0])
    earlier = (flat_ids[:, None] == flat_ids[None, :]) & (picks[None, :] < picks[:, None])
    target = (flat_ids * MOST + jnp.sum(earlier, axis=1, dtype=jnp.int32)).reshape(home_rows, top)
    experts = w_gate.shape[0]
    slots = experts * devices * MOST
    takes = target[:, :, None] == jnp.arange(slots, dtype=jnp.int32)
    chooser = jnp.any(takes, axis=1).T.astype(BF16)
    spread = jnp.sum(jnp.where(takes, route_weight[:, :, None], 0.0), axis=1)
    coarse = spread.astype(BF16)
    fine = (spread - coarse.astype(F32)).astype(BF16)

    gathered = []
    for chunk, blocks in enumerate((near_blocks, far_blocks)):
        sums = attention(
            place,
            blocks,
            (key_cache, key_other),
            (value_cache, value_other),
            new_key,
            new_value,
            lens[chunk],
            row_ids[chunk],
            chips,
            key_cache.shape[1] // HD,
        )
        if chunk:
            sums, gathered[-1] = lax.optimization_barrier((sums, gathered[-1]))
        else:
            sums, place, late_weight, _ = lax.optimization_barrier((sums, place, out_weight, far_across))
        gathered.append(
            lax.all_to_all(
                sums, "ctx", split_axis=0, concat_axis=0, axis_index_groups=same_core, tiled=True
            )
        )
    weight_other = lax.ppermute(late_weight, "ctx", swap)
    share = project(place, gathered, out_weight, weight_other, chunk_rows)
    shares = lax.all_to_all(
        share.reshape(chips, home_rows, width),
        "ctx",
        split_axis=0,
        concat_axis=0,
        axis_index_groups=same_core,
        tiled=True,
    )
    middle, outgoing = norm_and_dispatch(shares, residual, norm_gain.reshape(1, width), chooser)
    arrived = lax.all_to_all(
        outgoing.reshape(devices, experts * MOST, width), "ctx", split_axis=0, concat_axis=0, tiled=True
    )
    produced = run_experts(arrived.reshape(slots, width), w_gate, w_up, w_down)
    returned = lax.all_to_all(
        produced.reshape(devices, experts * MOST, width), "ctx", split_axis=0, concat_axis=0, tiled=True
    )
    return mix(returned.reshape(slots, width), coarse, fine, middle)


def solution(mesh):
    placed = (
        P(("groups", "ctx"), None),
        P(("groups", "ctx"), None),
        P(("groups", "ctx"), None),
        P(("groups", "ctx"), None),
        P(("groups", "ctx"), None),
        P("groups"),
        P("ctx", None),
        P(("groups", "ctx"), None),
        P(),
        P(("groups", "ctx"), None),
        P(("groups", "ctx"), None),
        P("ctx", None, None),
        P("ctx", None, None),
        P("ctx", None, None),
    )
    return jax.shard_map(
        on_device, mesh=mesh, in_specs=placed, out_specs=P(("groups", "ctx"), None), check_vma=False
    )
```

```python
import functools
import math

import jax
import jax.numpy as jnp
from jax import lax
from jax.experimental import pallas as pl
from jax.experimental.pallas import tpu as pltpu
from jax.sharding import PartitionSpec as P

HD = 128
MOST = 4
CORES = 2
STATS = 16
MASKED = -1e30
FLOOR = -1e20
LOG2E = math.log2(math.e)
MIB = 1024 * 1024
F32 = jnp.float32
BF16 = jnp.bfloat16


def nt_dot(a, b):
    return lax.dot_general(a, b, (((1,), (1,)), ((), ())), preferred_element_type=F32)


def nn_dot(a, b):
    return lax.dot_general(a, b, (((1,), (0,)), ((), ())), preferred_element_type=F32)


def attention_body(shape, place, *refs):
    key_heads, owners, owner_heads, home_rows, rows, cache_here, step = shape
    *query_refs, key_own, key_other, value_own, value_other, key_fresh, value_fresh = refs[:-8]
    lens, row_ids, out, q_rows, q_turned, hidden, scores, probs = refs[-8:]
    chip, start_own, start_other, side_here, ring_here = place[0], place[1], place[2], place[4], place[5]
    near = rows // home_rows // 2
    pack = HD // rows
    groups = owner_heads // pack

    @pl.when(pl.program_id(0) == 0)
    def _():
        lanes = lens.shape[1]
        for part, start in enumerate((start_own, start_other)):
            positions = start + lax.broadcasted_iota(jnp.int32, (cache_here, lanes), 0)
            hidden[part * cache_here : (part + 1) * cache_here, :] = jnp.where(
                positions < lens[...], 0.0, MASKED
            )
        token = chip * home_rows + lax.broadcasted_iota(jnp.int32, (home_rows, lanes), 0)
        hidden[2 * cache_here :, :] = jnp.where(token == row_ids[...], 0.0, MASKED)

    for k, piece in enumerate(query_refs):
        side = side_here if k < near else 1 - side_here
        spot = 2 * (lax.rem(ring_here, near) ^ (k % near)) + side
        q_rows[pl.ds(pl.multiple_of(spot * home_rows, home_rows), home_rows), :] = piece[...]

    factor = LOG2E / math.sqrt(HD)
    wide = owners * groups * HD
    for n in range(key_heads * owners * groups):
        block = jnp.concatenate(
            [q_rows[:, h * HD : (h + 1) * HD] for h in range(n * pack, (n + 1) * pack)], axis=0
        )
        scaled = block.T.astype(F32) * factor
        coarse = scaled.astype(BF16)
        q_turned[:HD, n * HD : (n + 1) * HD] = coarse
        q_turned[HD:, n * HD : (n + 1) * HD] = (scaled - coarse.astype(F32)).astype(BF16)

    each = range(key_heads)
    heads = [slice(g * HD, (g + 1) * HD) for g in each]
    across = [slice(g * wide, (g + 1) * wide) for g in each]

    def score(g, keys, at):
        s = nn_dot(jnp.concatenate([keys, keys], axis=1), q_turned[:, across[g]])
        return s + jnp.concatenate([hidden[at, :]] * (owners * groups), axis=1)

    def most(s):
        return jnp.max(s.reshape(s.shape[0] // 8, 8, wide), axis=0)

    fresh_at = slice(2 * cache_here, 2 * cache_here + home_rows)
    s_new = [score(g, key_fresh[:, heads[g]], fresh_at) for g in each]
    run = [most(s) for s in s_new]
    pieces = [(part, i) for part in range(2) for i in range(0, cache_here, step)]
    for part, i in pieces:
        at = slice(part * cache_here + i, part * cache_here + i + step)
        for g in each:
            s = score(g, (key_own, key_other)[part][i : i + step, heads[g]], at)
            scores[at, across[g]] = s
            run[g] = jnp.maximum(run[g], most(s))
    peak = [
        jnp.maximum(jnp.max(r, axis=0, keepdims=True), FLOOR).astype(BF16).astype(F32) for r in run
    ]
    for part, i in pieces:
        at = slice(part * cache_here + i, part * cache_here + i + step)
        for g in each:
            probs[at, across[g]] = jnp.exp2((scores[at, across[g]] - peak[g]).astype(BF16))
    ones = jnp.ones((STATS, cache_here), BF16)
    sums = [
        nn_dot(jnp.concatenate([value_own[heads[g], :], ones], axis=0), probs[:cache_here, across[g]])
        for g in each
    ]
    sums = [
        sums[g]
        + nn_dot(jnp.concatenate([value_other[heads[g], :], ones], axis=0), probs[cache_here:, across[g]])
        for g in each
    ]
    for g in each:
        p_new = jnp.exp2((s_new[g] - peak[g]).astype(BF16))
        values = value_fresh[:, heads[g]].astype(F32).T.astype(BF16)
        numer = sums[g][:HD] + nn_dot(values, p_new)
        denom = sums[g][HD : HD + 1] + jnp.sum(p_new.astype(F32), axis=0, keepdims=True)
        high = denom.astype(BF16).astype(F32)
        low = denom - high
        for owner in range(owners):
            spot = g * owners + owner
            lanes = [slice((owner * groups + k) * HD, (owner * groups + k + 1) * HD) for k in range(groups)]
            for k, cols in enumerate(lanes):
                out[spot, k * HD : (k + 1) * HD, :] = numer[:, cols].astype(BF16)
            filled = [kind[:, cols] for kind in (peak[g], high, low) for cols in lanes]
            filled += [jnp.zeros_like(filled[0])] * (STATS - len(filled))
            out[spot, groups * HD :, :] = jnp.concatenate(filled, axis=0).astype(BF16)


def attention(place, query_blocks, keys, values, new_key, new_value, lens, row_ids, chips, kv_heads):
    home_rows = new_key.shape[0]
    rows = home_rows * len(query_blocks)
    cache_here = keys[0].shape[0]
    together = 2
    steps = kv_heads // together
    owners = chips // kv_heads
    columns = query_blocks[0][0].shape[1] // steps
    owner_heads = columns // HD // owners // together
    wide = rows * columns // HD
    height = owner_heads * rows + STATS
    step = 512
    positions = 2 * cache_here + home_rows
    kv = lambda g, place: (0, g)
    whole = lambda g, place: (0, 0)
    shape = (together, owners, owner_heads, home_rows, rows, cache_here, step)
    work = wide * steps * 2 * cache_here
    return pl.pallas_call(
        functools.partial(attention_body, shape),
        grid_spec=pltpu.PrefetchScalarGridSpec(
            num_scalar_prefetch=1,
            grid=(steps,),
            in_specs=[
                pl.BlockSpec((home_rows, columns), functools.partial(lambda n, g, place: (n, g), n))
                for _, n in query_blocks
            ]
            + [pl.BlockSpec((cache_here, together * HD), kv)] * 2
            + [pl.BlockSpec((together * HD, cache_here), lambda g, place: (g, 0))] * 2
            + [pl.BlockSpec((home_rows, together * HD), kv)] * 2
            + [pl.BlockSpec(lens.shape, whole)] * 2,
            out_specs=pl.BlockSpec((together * owners, height, HD), lambda g, place: (g, 0, 0)),
            scratch_shapes=[
                pltpu.VMEM((rows, columns), BF16),
                pltpu.VMEM((2 * HD, wide), BF16),
                pltpu.VMEM((positions, HD), F32),
                pltpu.VMEM((2 * cache_here, wide), F32),
                pltpu.VMEM((2 * cache_here, wide), BF16),
            ],
        ),
        out_shape=jax.ShapeDtypeStruct((chips, height, HD), BF16),
        compiler_params=pltpu.CompilerParams(vmem_limit_bytes=40 * MIB),
        cost_estimate=pl.CostEstimate(
            flops=6 * work * HD, bytes_accessed=8 * MIB, transcendentals=work
        ),
        name="attention",
    )(
        place,
        *[block for block, _ in query_blocks],
        pltpu.with_memory_space_constraint(keys[0], pltpu.HBM),
        keys[1],
        *values,
        pltpu.with_memory_space_constraint(new_key, pltpu.HBM),
        pltpu.with_memory_space_constraint(new_value, pltpu.HBM),
        lens,
        row_ids,
    )


def project_body(rows, place, *refs):
    *chunks, weight_own, weight_other, out, turned = refs
    core = place[3]
    chips, height, _ = chunks[0].shape
    base = height - STATS
    groups = base // HD
    pack = HD // rows
    heads_here = groups * pack // CORES
    half = chips // 2 // 2
    for near in range(2):
        sources = [chunks[s // 2 // half ^ near].at[s] for s in range(chips)]
        stats = [part[base:, :].astype(F32) for part in sources]
        peaks = [stat[:groups] for stat in stats]
        top = functools.reduce(jnp.maximum, peaks)
        share = [jnp.exp2(peak - top) for peak in peaks]
        denom = sum(w * (t[groups : 2 * groups] + t[2 * groups : 3 * groups]) for w, t in zip(share, stats))
        for k in range(groups):
            numer = sum(
                part[k * HD : (k + 1) * HD, :].astype(F32) * w[k : k + 1, :] for part, w in zip(sources, share)
            )
            attended = (numer / denom[k : k + 1, :]).T.astype(BF16)
            for j in range(pack):
                part, h = divmod(k * pack + j, heads_here)
                turned[part, near * rows : (near + 1) * rows, h * HD : (h + 1) * HD] = attended[
                    j * rows : (j + 1) * rows
                ]
    product = nn_dot(turned[core], weight_own[...]) + nn_dot(turned[1 - core], weight_other[...])
    out[...] = product.astype(BF16)


def project(place, chunks, weight_own, weight_other, rows):
    depth, width = weight_own.shape
    vmem = pl.BlockSpec(memory_space=pltpu.VMEM)
    return pl.pallas_call(
        functools.partial(project_body, rows),
        in_specs=[pl.BlockSpec(memory_space=pltpu.SMEM)] + [vmem] * (len(chunks) + 2),
        out_specs=vmem,
        out_shape=jax.ShapeDtypeStruct((2 * rows, width), BF16),
        scratch_shapes=[pltpu.VMEM((CORES, 2 * rows, depth), BF16)],
        compiler_params=pltpu.CompilerParams(vmem_limit_bytes=32 * MIB),
        cost_estimate=pl.CostEstimate(
            flops=8 * rows * width * depth, bytes_accessed=4 * MIB, transcendentals=0
        ),
        name="project",
    )(place, *chunks, pltpu.with_memory_space_constraint(weight_own, pltpu.VMEM), weight_other)


def norm_body(parts, residual, gain, chooser, middle_out, sent):
    total = parts[0].astype(F32)
    for s in range(1, parts.shape[0]):
        total = total + parts[s].astype(F32)
    middle = (residual[...].astype(F32) + total).astype(BF16)
    middle_out[...] = middle
    middle = middle.astype(F32)
    inv_rms = lax.rsqrt(jnp.mean(middle * middle, axis=-1, keepdims=True) + 1e-06)
    normed = (middle * inv_rms * gain[...].astype(F32)).astype(BF16)
    sent[...] = nn_dot(chooser[...], normed).astype(BF16)


def norm_and_dispatch(parts, residual, gain, chooser):
    vmem = pl.BlockSpec(memory_space=pltpu.VMEM)
    rows, width = residual.shape
    return pl.pallas_call(
        norm_body,
        in_specs=[vmem] * 4,
        out_specs=[vmem] * 2,
        out_shape=[
            jax.ShapeDtypeStruct((rows, width), BF16),
            jax.ShapeDtypeStruct((chooser.shape[0], width), BF16),
        ],
        compiler_params=pltpu.CompilerParams(vmem_limit_bytes=24 * MIB),
        cost_estimate=pl.CostEstimate(
            flops=2 * chooser.shape[0] * rows * width, bytes_accessed=2 * MIB, transcendentals=0
        ),
        name="norm_and_dispatch",
    )(parts, residual, gain, chooser)


def experts_body(step, arrived, w_gate, w_up, w_down, out, gate_held, up_held, down_held, sems):
    experts, _, depth = w_gate.shape
    rows, width = arrived.shape
    pieces = [(e, f) for e in range(experts) for f in range(0, depth, step)]
    copies = []
    for n, (e, f) in enumerate(pieces):
        down = pl.ds(f, step)
        copies.append(
            [
                pltpu.make_async_copy(w_gate.at[e, :, down], gate_held.at[n], sems.at[n, 0]),
                pltpu.make_async_copy(w_up.at[e, :, down], up_held.at[n], sems.at[n, 1]),
                pltpu.make_async_copy(w_down.at[e, down, :], down_held.at[n], sems.at[n, 2]),
            ]
        )
    for piece in copies:
        for copy in piece[:2]:
            copy.start()
    for piece in copies:
        piece[2].start()
    slot = lax.broadcasted_iota(jnp.int32, (rows, 1), 0)
    values = arrived[...]
    hidden = []
    for n, (e, f) in enumerate(pieces):
        copies[n][0].wait()
        copies[n][1].wait()
        gate = nn_dot(values, gate_held[n])
        upward = nn_dot(values, up_held[n])
        part = gate / (1.0 + jnp.exp(-gate)) * upward
        mine = lax.rem(slot, experts * MOST) // MOST == e
        hidden.append(jnp.where(mine, part, 0.0).astype(BF16))
    total = None
    for n in range(len(pieces)):
        copies[n][2].wait()
        term = nn_dot(hidden[n], down_held[n])
        total = term if total is None else total + term
    out[...] = total.astype(BF16)


def run_experts(arrived, w_gate, w_up, w_down):
    rows, width = arrived.shape
    experts, _, depth = w_gate.shape
    step = 256
    pieces = experts * depth // step
    vmem = pl.BlockSpec(memory_space=pltpu.VMEM)
    hbm = pl.BlockSpec(memory_space=pltpu.HBM)
    weights = [pltpu.with_memory_space_constraint(w, pltpu.HBM) for w in (w_gate, w_up, w_down)]
    return pl.pallas_call(
        functools.partial(experts_body, step),
        in_specs=[vmem] + [hbm] * 3,
        out_specs=vmem,
        out_shape=jax.ShapeDtypeStruct((rows, width), BF16),
        scratch_shapes=[
            pltpu.VMEM((pieces, width, step), BF16),
            pltpu.VMEM((pieces, width, step), BF16),
            pltpu.VMEM((pieces, step, width), BF16),
            pltpu.SemaphoreType.DMA((pieces, 3)),
        ],
        compiler_params=pltpu.CompilerParams(vmem_limit_bytes=44 * MIB),
        cost_estimate=pl.CostEstimate(
            flops=6 * rows * width * experts * depth,
            bytes_accessed=6 * width * experts * depth,
            transcendentals=rows * experts * depth,
        ),
        name="experts",
    )(arrived, *weights)


def mix_body(returned, coarse, fine, middle, out):
    values = returned[...]
    mixed = nn_dot(coarse[...], values) + nn_dot(fine[...], values)
    out[...] = (middle[...].astype(F32) + mixed).astype(BF16)


def mix(returned, coarse, fine, middle):
    vmem = pl.BlockSpec(memory_space=pltpu.VMEM)
    return pl.pallas_call(
        mix_body,
        in_specs=[vmem] * 4,
        out_specs=vmem,
        out_shape=jax.ShapeDtypeStruct(middle.shape, BF16),
        compiler_params=pltpu.CompilerParams(vmem_limit_bytes=16 * MIB),
        name="mix",
    )(returned, coarse, fine, middle)


def on_device(
    queries,
    new_key,
    new_value,
    key_cache,
    value_cache,
    cache_len,
    out_weight,
    residual,
    norm_gain,
    expert_ids,
    route_weight,
    w_gate,
    w_up,
    w_down,
):
    devices = lax.axis_size("ctx")
    chips = devices // CORES
    index = lax.axis_index("ctx")
    chip, core = index // CORES, index % CORES
    home_rows, width = residual.shape
    top = expert_ids.shape[1]
    heads_here = out_weight.shape[0] // HD
    cache_here = key_cache.shape[0]
    same_core = [[CORES * j + c for j in range(chips)] for c in range(CORES)]
    swap = [(i, i ^ 1) for i in range(devices)]

    across = [(i, i ^ CORES) for i in range(devices)]
    rings = chips // 2
    half = rings // 2
    chunk_rows = 2 * half * home_rows

    def across_y(block):
        return lax.ppermute(block, "ctx", across)

    neighbour = across_y(queries)
    by_ring = [queries] + [
        lax.ppermute(queries, "ctx", [(i, i ^ (2 * CORES * k)) for i in range(devices)])
        for k in range(1, rings)
    ]
    near_blocks = [(pltpu.with_memory_space_constraint(queries, pltpu.HBM), 0)]
    near_blocks += [(block, 0) for block in by_ring[1:half]]
    near_blocks += [(neighbour, 0)] + [(across_y(block), 0) for block in by_ring[1:half]]
    far = jnp.concatenate(by_ring[half:], axis=0)
    far_across = across_y(far)
    far_blocks = [(far, k) for k in range(half)] + [(far_across, k) for k in range(half)]
    late_keys, late_values, _ = lax.optimization_barrier((key_cache, value_cache, neighbour))
    key_other = lax.ppermute(late_keys, "ctx", swap)
    value_turned = late_values.T
    value_other = lax.ppermute(value_turned, "ctx", swap)
    place = jnp.stack([chip, index * cache_here, (index ^ 1) * cache_here, core, chip % 2, chip // 2]).astype(jnp.int32)

    def in_lanes(by_chip, n):
        first = (chip // CORES // half ^ n) * chips // 2
        here = lax.dynamic_slice_in_dim(by_chip, first, chips // 2, 0).reshape(1, chunk_rows)
        return jnp.tile(here, (1, HD // chunk_rows))

    len_by_chip = lax.dynamic_slice_in_dim(
        cache_len.reshape(chips, CORES * home_rows), core * home_rows, home_rows, 1
    )
    number_by_chip = jnp.arange(chips * home_rows, dtype=jnp.int32).reshape(chips, home_rows)
    lens = [in_lanes(len_by_chip, n) for n in range(2)]
    row_ids = [in_lanes(number_by_chip, n) for n in range(2)]

    flat_ids = expert_ids.reshape(-1)
    picks = jnp.arange(flat_ids.shape[0])
    earlier = (flat_ids[:, None] == flat_ids[None, :]) & (picks[None, :] < picks[:, None])
    target = (flat_ids * MOST + jnp.sum(earlier, axis=1, dtype=jnp.int32)).reshape(home_rows, top)
    experts = w_gate.shape[0]
    slots = experts * devices * MOST
    takes = target[:, :, None] == jnp.arange(slots, dtype=jnp.int32)
    chooser = jnp.any(takes, axis=1).T.astype(BF16)
    spread = jnp.sum(jnp.where(takes, route_weight[:, :, None], 0.0), axis=1)
    coarse = spread.astype(BF16)
    fine = (spread - coarse.astype(F32)).astype(BF16)

    gathered = []
    for chunk, blocks in enumerate((near_blocks, far_blocks)):
        sums = attention(
            place,
            blocks,
            (key_cache, key_other),
            (value_turned, value_other),
            new_key,
            new_value,
            lens[chunk],
            row_ids[chunk],
            chips,
            key_cache.shape[1] // HD,
        )
        if chunk:
            sums, gathered[-1] = lax.optimization_barrier((sums, gathered[-1]))
        else:
            sums, place, late_weight, _ = lax.optimization_barrier((sums, place, out_weight, far_across))
        gathered.append(
            lax.all_to_all(
                sums, "ctx", split_axis=0, concat_axis=0, axis_index_groups=same_core, tiled=True
            )
        )
    weight_other = lax.ppermute(late_weight, "ctx", swap)
    share = project(place, gathered, out_weight, weight_other, chunk_rows)
    shares = lax.all_to_all(
        share.reshape(chips, home_rows, width),
        "ctx",
        split_axis=0,
        concat_axis=0,
        axis_index_groups=same_core,
        tiled=True,
    )
    middle, outgoing = norm_and_dispatch(shares, residual, norm_gain.reshape(1, width), chooser)
    arrived = lax.all_to_all(
        outgoing.reshape(devices, experts * MOST, width), "ctx", split_axis=0, concat_axis=0, tiled=True
    )
    produced = run_experts(arrived.reshape(slots, width), w_gate, w_up, w_down)
    returned = lax.all_to_all(
        produced.reshape(devices, experts * MOST, width), "ctx", split_axis=0, concat_axis=0, tiled=True
    )
    return mix(returned.reshape(slots, width), coarse, fine, middle)


def solution(mesh):
    placed = (
        P(("groups", "ctx"), None),
        P(("groups", "ctx"), None),
        P(("groups", "ctx"), None),
        P(("groups", "ctx"), None),
        P(("groups", "ctx"), None),
        P("groups"),
        P("ctx", None),
        P(("groups", "ctx"), None),
        P(),
        P(("groups", "ctx"), None),
        P(("groups", "ctx"), None),
        P("ctx", None, None),
        P("ctx", None, None),
        P("ctx", None, None),
    )
    return jax.shard_map(
        on_device, mesh=mesh, in_specs=placed, out_specs=P(("groups", "ctx"), None), check_vma=False
    )
```
